32 devices in a mesh: dp: 2 (over x), seq: 16 (over z, y, core).
Axes of the slice: x: 2, y: 2, z: 4, core: 2. Of those that a mesh axis runs over, the one named last changes fastest.
Arguments:
- inputs: bfloat16 [15360, 1152], P(('dp', 'seq')), may hold values from -6 to 6
- image_ids: int32 [15360], P(('dp', 'seq')), may hold values from 0 to 19, as said below
- token_mask: int32 [15360], P(('dp', 'seq')), may hold values from 0 to 1, as said below
- cotangent: bfloat16 [15360, 1152], P(('dp', 'seq')), may hold values from -6 to 6
- w_qkv: bfloat16 [2, 1152, 3456], P(None, ('dp', 'seq')), may hold values from -0.1875 to 0.1875
- w_out: bfloat16 [2, 1152, 1152], P(None, ('dp', 'seq')), may hold values from -1.5 to 1.5
- w_up: bfloat16 [2, 1152, 4304], P(None, ('dp', 'seq')), may hold values from -0.1875 to 0.1875
- w_down: bfloat16 [2, 4304, 1152], P(None, None, ('dp', 'seq')), may hold values from -0.09375 to 0.09375
- norm_gains: bfloat16 [2, 2, 1152], P(None, None, ('dp', 'seq')), may hold values from 0.5 to 1.5
- bias_rows: bfloat16 [2, 6, 1152], P(None, None, ('dp', 'seq')), may hold values from -1.1953125 to 1.1953125
- up_bias: bfloat16 [2, 4304], replicated, may hold values from -1.1953125 to 1.1953125
- first_qkv: float32 [2, 1152, 3456], P(None, ('dp', 'seq')), may hold values from -160 to 160
- first_out: float32 [2, 1152, 1152], P(None, ('dp', 'seq')), may hold values from -160 to 160
- first_up: float32 [2, 1152, 4304], P(None, ('dp', 'seq')), may hold values from -160 to 160
- first_down: float32 [2, 4304, 1152], P(None, None, ('dp', 'seq')), may hold values from -160 to 160
- first_gains: float32 [2, 2, 1152], P(None, None, ('dp', 'seq')), may hold values from -160 to 160
- first_bias: float32 [2, 6, 1152], P(None, None, ('dp', 'seq')), may hold values from -160 to 160
- first_upbias: float32 [2, 4304], replicated, may hold values from -160 to 160
- second_qkv: float32 [2, 1152, 3456], P(None, ('dp', 'seq')), may hold values from 1000 to 10000
- second_out: float32 [2, 1152, 1152], P(None, ('dp', 'seq')), may hold values from 1000 to 10000
- second_up: float32 [2, 1152, 4304], P(None, ('dp', 'seq')), may hold values from 1000 to 10000
- second_down: float32 [2, 4304, 1152], P(None, None, ('dp', 'seq')), may hold values from 1000 to 10000
- second_gains: float32 [2, 2, 1152], P(None, None, ('dp', 'seq')), may hold values from 1000 to 10000
- second_bias: float32 [2, 6, 1152], P(None, None, ('dp', 'seq')), may hold values from 245760 to 3932160
- second_upbias: float32 [2, 4304], replicated, may hold values from 1000 to 10000
Outputs:
- block_out: float32 [15360, 1152], P(('dp', 'seq'))
- input_grad: float32 [15360, 1152], P(('dp', 'seq'))
- grad_qkv: float32 [2, 1152, 3456], P(None, ('dp', 'seq'))
- grad_out: float32 [2, 1152, 1152], P(None, ('dp', 'seq'))
- grad_up: float32 [2, 1152, 4304], P(None, ('dp', 'seq'))
- grad_down: float32 [2, 4304, 1152], P(None, None, ('dp', 'seq'))
- grad_gains: float32 [2, 2, 1152], P(None, None, ('dp', 'seq'))
- grad_bias: float32 [2, 6, 1152], P(None, None, ('dp', 'seq'))
- grad_upbias: float32 [2, 4304], replicated
- new_first_qkv: float32 [2, 1152, 3456], P(None, ('dp', 'seq'))
- new_first_out: float32 [2, 1152, 1152], P(None, ('dp', 'seq'))
- new_first_up: float32 [2, 1152, 4304], P(None, ('dp', 'seq'))
- new_first_down: float32 [2, 4304, 1152], P(None, None, ('dp', 'seq'))
- new_first_gains: float32 [2, 2, 1152], P(None, None, ('dp', 'seq'))
- new_first_bias: float32 [2, 6, 1152], P(None, None, ('dp', 'seq'))
- new_first_upbias: float32 [2, 4304], replicated
- new_second_qkv: float32 [2, 1152, 3456], P(None, ('dp', 'seq'))
- new_second_out: float32 [2, 1152, 1152], P(None, ('dp', 'seq'))
- new_second_up: float32 [2, 1152, 4304], P(None, ('dp', 'seq'))
- new_second_down: float32 [2, 4304, 1152], P(None, None, ('dp', 'seq'))
- new_second_gains: float32 [2, 2, 1152], P(None, None, ('dp', 'seq'))
- new_second_bias: float32 [2, 6, 1152], P(None, None, ('dp', 'seq'))
- new_second_upbias: float32 [2, 4304], replicated
- step_qkv: float32 [2, 1152, 3456], P(None, ('dp', 'seq'))
- step_out: float32 [2, 1152, 1152], P(None, ('dp', 'seq'))
- step_up: float32 [2, 1152, 4304], P(None, ('dp', 'seq'))
- step_down: float32 [2, 4304, 1152], P(None, None, ('dp', 'seq'))
- step_gains: float32 [2, 2, 1152], P(None, None, ('dp', 'seq'))
- step_bias: float32 [2, 6, 1152], P(None, None, ('dp', 'seq'))
- step_upbias: float32 [2, 4304], replicated
The draws below stay inside these ranges and needn't reach their ends.
Inputs may be any that keep to these rules, and one draw needn't show every extreme that they name: `image_ids`: group g (tokens g * 7680 to (g + 1) * 7680 - 1) holds images g * 10 to (g + 1) * 10 - 1 in rising order; the valid tokens of each image are one run of 729 consecutive positions, starting with the group's first token for its first image; padding tokens follow an image and carry its id. `token_mask`: each group has 390 padding tokens.
All inputs are finite; a program needn't handle non-finite values.
Results may differ from the reference program's by a relative error of at most 0.012.
Values may be sent and summed in bfloat16 or wider, within the bound.
A program may use at most 448 MiB of HBM per device.

```python
import math
import jax
import jax.numpy as jnp
from jax import lax

D = 1152
HEADS = 16
HEAD_DIM = 72
FF = 4304
IMG = 729
LAYERS = 2
STEP = 8
TOK_DEV = 480
TOKENS = 15360
N_DP = 2
N_SEQ = 16


def layout_draw(key):
    group_tok = TOK_DEV * N_SEQ
    images = group_tok // IMG
    spare_count = group_tok - images * IMG
    cut_points = jnp.sort(jax.random.randint(jax.random.fold_in(key, 17), (N_DP, images - 1), 0, spare_count + 1), axis=1)
    edge_points = jnp.concatenate([jnp.zeros((N_DP, 1), jnp.int32), cut_points.astype(jnp.int32), jnp.full((N_DP, 1), spare_count, jnp.int32)], axis=1)
    gap_sizes = edge_points[:, 1:] - edge_points[:, :-1]
    before = jnp.cumsum(gap_sizes, axis=1) - gap_sizes
    starts = jnp.arange(images, dtype=jnp.int32)[None, :] * IMG + before
    positions = jnp.arange(group_tok, dtype=jnp.int32)
    owner_local = jnp.sum((starts[:, None, :] <= positions[None, :, None]).astype(jnp.int32), axis=2) - 1
    run_begin = jnp.take_along_axis(starts, owner_local, axis=1)
    is_valid = (positions[None, :] < run_begin + IMG).astype(jnp.int32)
    owner_ids = owner_local + images * jnp.arange(N_DP, dtype=jnp.int32)[:, None]
    return (owner_ids.reshape(-1).astype(jnp.int32), is_valid.reshape(-1))


def draw_image_ids(key, part):
    return layout_draw(key)[0]


def draw_token_mask(key, part):
    return layout_draw(key)[1]


def steps_of(own_key, dims, split, smallest, high):
    level, own = 1.0, jax.random.fold_in(own_key, 6)
    for position, blocks in split:
        draws = jnp.exp(jax.random.uniform(jax.random.fold_in(own, position), (blocks,), jnp.float32, smallest / len(split), high / len(split)))
        level = level * jnp.repeat(draws, dims[position] // blocks).reshape([-1 if axis == position else 1 for axis in range(len(dims))])
    return level


def gaussian(key, dims, deviation, bound, split=(), kind=jnp.bfloat16):
    array = deviation * jax.random.normal(key, dims, jnp.float32)
    if split:
        array = array * steps_of(key, dims, split, -0.22, 0.18)
    return jnp.clip(array, -bound, bound).astype(kind)


def setup_inputs(seed: int = 0) -> dict:
    key_list = jax.random.split(jax.random.key(seed), 26)
    inputs = gaussian(key_list[0], (TOKENS, D), 1.0, 6.0, ((0, 32),))
    image_ids = draw_image_ids(jax.random.fold_in(key_list[25], 71), 0)
    token_mask = draw_token_mask(jax.random.fold_in(key_list[25], 71), 0)
    cotangent = gaussian(key_list[3], (TOKENS, D), 1.0, 6.0, ((0, 32),))
    w_qkv = gaussian(key_list[4], (LAYERS, D, 3 * D), D ** -0.5, 0.1875, ((1, 32),))
    w_out = gaussian(key_list[5], (LAYERS, D, D), (max(1, D // 64)) ** -0.5, 1.5, ((1, 32),))
    w_up = gaussian(key_list[6], (LAYERS, D, FF), D ** -0.5, 0.1875, ((1, 32),))
    w_down = gaussian(key_list[7], (LAYERS, FF, D), FF ** -0.5, 0.09375, ((2, 32),))
    norm_gains = jnp.clip(1.0 + 0.1 * jax.random.normal(key_list[8], (LAYERS, 2, D), jnp.float32), 0.5, 1.5).astype(jnp.bfloat16)
    bias_rows = gaussian(key_list[9], (LAYERS, 6, D), 0.2, 1.1953125, ((2, 32),))
    up_bias = gaussian(key_list[10], (LAYERS, FF), 0.2, 1.1953125)
    first_qkv = gaussian(key_list[11], (LAYERS, D, 3 * D), 25.0, 160.0, ((1, 32),), jnp.float32)
    first_out = gaussian(key_list[12], (LAYERS, D, D), 25.0, 160.0, ((1, 32),), jnp.float32)
    first_up = gaussian(key_list[13], (LAYERS, D, FF), 25.0, 160.0, ((1, 32),), jnp.float32)
    first_down = gaussian(key_list[14], (LAYERS, FF, D), 25.0, 160.0, ((2, 32),), jnp.float32)
    first_gains = gaussian(key_list[15], (LAYERS, 2, D), 25.0, 160.0, ((2, 32),), jnp.float32)
    first_bias = gaussian(key_list[16], (LAYERS, 6, D), 25.0, 160.0, ((2, 32),), jnp.float32)
    first_upbias = gaussian(key_list[17], (LAYERS, FF), 25.0, 160.0, (), jnp.float32)
    second_qkv = jnp.clip(jnp.exp(math.log(10000.0) - 2.3025851 * jax.random.uniform(key_list[18], (LAYERS, D, 3 * D), jnp.float32) ** steps_of(key_list[18], (LAYERS, D, 3 * D), ((1, 32),), -0.2, 0.2)), 1000.0, 10000.0)
    second_out = jnp.clip(jnp.exp(math.log(10000.0) - 2.3025851 * jax.random.uniform(key_list[19], (LAYERS, D, D), jnp.float32) ** steps_of(key_list[19], (LAYERS, D, D), ((1, 32),), -0.2, 0.2)), 1000.0, 10000.0)
    second_up = jnp.clip(jnp.exp(math.log(10000.0) - 2.3025851 * jax.random.uniform(key_list[20], (LAYERS, D, FF), jnp.float32) ** steps_of(key_list[20], (LAYERS, D, FF), ((1, 32),), -0.2, 0.2)), 1000.0, 10000.0)
    second_down = jnp.clip(jnp.exp(math.log(10000.0) - 2.3025851 * jax.random.uniform(key_list[21], (LAYERS, FF, D), jnp.float32) ** steps_of(key_list[21], (LAYERS, FF, D), ((2, 32),), -0.2, 0.2)), 1000.0, 10000.0)
    second_gains = jnp.clip(jnp.exp(math.log(10000.0) - 2.3025851 * jax.random.uniform(key_list[22], (LAYERS, 2, D), jnp.float32) ** steps_of(key_list[22], (LAYERS, 2, D), ((2, 32),), -0.2, 0.2)), 1000.0, 10000.0)
    second_bias = jnp.clip(jnp.exp(math.log(3932160) - 2.7725887 * jax.random.uniform(key_list[23], (LAYERS, 6, D), jnp.float32) ** steps_of(key_list[23], (LAYERS, 6, D), ((2, 32),), -0.2, 0.2)), 245760.0, 3932160)
    second_upbias = jnp.clip(jnp.exp(jax.random.uniform(key_list[24], (LAYERS, FF), jnp.float32, math.log(1000.0), math.log(10000.0))), 1000.0, 10000.0)
    return dict(inputs=inputs, image_ids=image_ids, token_mask=token_mask, cotangent=cotangent, w_qkv=w_qkv, w_out=w_out, w_up=w_up, w_down=w_down, norm_gains=norm_gains, bias_rows=bias_rows, up_bias=up_bias, first_qkv=first_qkv, first_out=first_out, first_up=first_up, first_down=first_down, first_gains=first_gains, first_bias=first_bias, first_upbias=first_upbias, second_qkv=second_qkv, second_out=second_out, second_up=second_up, second_down=second_down, second_gains=second_gains, second_bias=second_bias, second_upbias=second_upbias)


@jax.custom_vjp
def low(v):
    return lax.optimization_barrier(v.astype(jnp.bfloat16)).astype(jnp.float32)

@jax.custom_vjp
def low_back(v):
    return v

def low_keep(v):
    return (low(v), None)

def low_pass(kept, grad):
    return (grad,)

def back_keep(v):
    return (v, None)

def back_low(kept, grad):
    return (low(grad),)
low.defvjp(low_keep, low_pass)
low_back.defvjp(back_keep, back_low)
eps_norm = 1e-06
beta_first = 0.9
beta_second = 0.95
learn_rate = 0.025
weight_decay = 0.1
eps_adam = 1e-08
masked_score = -1e+30
highest = lax.Precision.HIGHEST

def matmul_high(left_op, right_op):
    return jnp.dot(left_op, right_op, precision=highest, preferred_element_type=jnp.float32)

def layer_norm(source, gain_row, shift_row):
    row_mean = lax.optimization_barrier(jnp.mean(source, axis=-1, keepdims=True))
    centred = source - row_mean
    variance = lax.optimization_barrier(jnp.mean(centred * centred, axis=-1, keepdims=True))
    return centred * lax.rsqrt(variance + eps_norm) * gain_row + shift_row

def attention(queries, key_rows, value_rows, image_ids, token_mask):
    group_tok = TOK_DEV * N_SEQ
    spare_count = group_tok - group_tok // IMG * IMG
    reach_hops = (IMG - 1 + spare_count + TOK_DEV - 1) // TOK_DEV
    border = reach_hops * TOK_DEV
    wide = (2 * reach_hops + 1) * TOK_DEV
    score_scale = 1.0 / jnp.sqrt(jnp.float32(HEAD_DIM))
    key_code = jnp.where(token_mask > 0, image_ids + 1, 0).astype(jnp.int32).reshape(N_DP, group_tok)
    code_pad = jnp.pad(key_code, ((0, 0), (border, border)))
    query_code = (image_ids + 1).astype(jnp.int32).reshape(N_DP, group_tok)
    query_all = queries.reshape(N_DP, group_tok, HEADS, HEAD_DIM)
    key_all = jnp.pad(key_rows.reshape(N_DP, group_tok, HEADS, HEAD_DIM), ((0, 0), (border, border), (0, 0), (0, 0)))
    value_all = jnp.pad(value_rows.reshape(N_DP, group_tok, HEADS, HEAD_DIM), ((0, 0), (border, border), (0, 0), (0, 0)))
    diagonal = jnp.arange(TOK_DEV)[:, None] + border == jnp.arange(wide)[None, :]

    def one_block(index):
        group = (index // N_SEQ).astype(jnp.int32)
        start = (index % N_SEQ * TOK_DEV).astype(jnp.int32)
        zero = jnp.int32(0)
        query_blk = lax.dynamic_slice(query_all, (group, start, zero, zero), (1, TOK_DEV, HEADS, HEAD_DIM))[0]
        key_blk = lax.dynamic_slice(key_all, (group, start, zero, zero), (1, wide, HEADS, HEAD_DIM))[0]
        value_blk = lax.dynamic_slice(value_all, (group, start, zero, zero), (1, wide, HEADS, HEAD_DIM))[0]
        query_cb = lax.dynamic_slice(query_code, (group, start), (1, TOK_DEV))[0]
        key_cb = lax.dynamic_slice(code_pad, (group, start), (1, wide))[0]
        allowed = (query_cb[:, None] == key_cb[None, :]) | diagonal
        scores = low_back(jnp.einsum('bhd,whd->hbw', query_blk, key_blk, precision=highest) * score_scale)
        scores = jnp.where(allowed[None], scores, masked_score)
        row_top = lax.optimization_barrier(jnp.max(scores, axis=-1, keepdims=True))
        powers = jnp.exp(scores - row_top)
        attn_prob = low(powers / lax.optimization_barrier(jnp.sum(powers, axis=-1, keepdims=True)))
        mixed = jnp.einsum('hbw,whd->bhd', attn_prob, value_blk, precision=highest)
        return mixed.reshape(TOK_DEV, HEADS * HEAD_DIM)
    blocks_out = lax.map(jax.checkpoint(one_block), jnp.arange(N_DP * N_SEQ, dtype=jnp.int32))
    return blocks_out.reshape(N_DP * group_tok, HEADS * HEAD_DIM)

def adam_step(weight_now, gradient, first_old, second_old):
    first_new = beta_first * first_old + (1.0 - beta_first) * gradient
    second_new = beta_second * second_old + (1.0 - beta_second) * gradient * gradient
    first_hat = first_new / (1.0 - beta_first ** STEP)
    second_hat = second_new / (1.0 - beta_second ** STEP)
    update = -learn_rate * (first_hat / (jnp.sqrt(second_hat) + eps_adam) + weight_decay * weight_now)
    return (first_new, second_new, update)

def reference(inputs, image_ids, token_mask, cotangent, w_qkv, w_out, w_up, w_down, norm_gains, bias_rows, up_bias, first_qkv, first_out, first_up, first_down, first_gains, first_bias, first_upbias, second_qkv, second_out, second_up, second_down, second_gains, second_bias, second_upbias):

    def forward(inputs_f, qkv_all, out_all, up_all, down_all, gains_all, shifts_all, upbias_all):
        residual = inputs_f
        for layer_index in range(LAYERS):
            normed = low(layer_norm(residual, gains_all[layer_index, 0], shifts_all[layer_index, 0]))
            projected = matmul_high(normed, qkv_all[layer_index])
            queries = low(low_back(projected[:, :D] + shifts_all[layer_index, 2]))
            key_rows = low(low_back(projected[:, D:2 * D]))
            value_rows = low(low_back(projected[:, 2 * D:] + shifts_all[layer_index, 3]))
            attended = low(low_back(attention(queries, key_rows, value_rows, image_ids, token_mask)))
            residual = residual + low_back(matmul_high(attended, out_all[layer_index]) + shifts_all[layer_index, 4])
            hidden = low(layer_norm(residual, gains_all[layer_index, 1], shifts_all[layer_index, 1]))
            pre_act = low_back(matmul_high(hidden, up_all[layer_index]) + upbias_all[layer_index])
            active = low(jax.nn.gelu(pre_act, approximate=True))
            residual = residual + low_back(matmul_high(active, down_all[layer_index]) + shifts_all[layer_index, 5])
        return residual
    params = (w_qkv.astype(jnp.float32), w_out.astype(jnp.float32), w_up.astype(jnp.float32), w_down.astype(jnp.float32), norm_gains.astype(jnp.float32), bias_rows.astype(jnp.float32), up_bias.astype(jnp.float32))
    block_out, pullback = jax.vjp(forward, inputs.astype(jnp.float32), params[0], params[1], params[2], params[3], params[4], params[5], params[6])
    grads = pullback(cotangent.astype(jnp.float32))
    firsts = (first_qkv, first_out, first_up, first_down, first_gains, first_bias, first_upbias)
    seconds = (second_qkv, second_out, second_up, second_down, second_gains, second_bias, second_upbias)
    results = [adam_step(params[member], grads[member + 1], firsts[member], seconds[member]) for member in range(7)]
    return (block_out, grads[0], grads[1], grads[2], grads[3], grads[4], grads[5], grads[6], grads[7], results[0][0], results[1][0], results[2][0], results[3][0], results[4][0], results[5][0], results[6][0], results[0][1], results[1][1], results[2][1], results[3][1], results[4][1], results[5][1], results[6][1], results[0][2], results[1][2], results[2][2], results[3][2], results[4][2], results[5][2], results[6][2])
```

```python
import functools
import math

import jax
import jax.numpy as jnp
from jax import lax
from jax.experimental import pallas as pl
from jax.experimental.pallas import tpu as pltpu
from jax.sharding import PartitionSpec as P

HEADS = 16
IMG = 729
STEP = 8

eps_norm = 1e-06
beta_first = 0.9
beta_second = 0.95
learn_rate = 0.025
weight_decay = 0.1
eps_adam = 1e-08
span_len = 768
lane_pair = 256
masked_score = -1e30
mib = 2**20


def head_lanes(head, head_size, width):
    low = head * head_size
    first = jnp.minimum(low // 128 * 128, width - lane_pair)
    lanes = lax.broadcasted_iota(jnp.int32, (1, lane_pair), 1)
    inside = (lanes >= low - first) & (lanes < low - first + head_size)
    keys = pl.ds(pl.multiple_of(first, 128), lane_pair)
    values = pl.ds(pl.multiple_of(first + width, 128), lane_pair)
    return keys, values, inside


def dot_nn(left, right):
    return lax.dot_general(left, right, (((1,), (0,)), ((), ())), preferred_element_type=jnp.float32)


def dot_nt(left, right):
    return lax.dot_general(left, right, (((1,), (1,)), ((), ())), preferred_element_type=jnp.float32)


def dot_tn(left, right):
    return lax.dot_general(left, right, (((0,), (0,)), ((), ())), preferred_element_type=jnp.float32)


def attention_forward_kernel(
    tile, left, exp_scale, plan, query, window, own_code, span_code, out, lse_out, bias, mix
):
    tok, width = query.shape
    head_size = width // HEADS

    def one_span(tile_index, which):
        offset = pl.multiple_of(plan[4 * tile_index + which], 16)
        image = plan[4 * tile_index + 2 + which]
        rows = pl.ds(pl.multiple_of(tile_index * tile, 16), tile)
        own_rows = pl.ds(pl.multiple_of(left + tile_index * tile, 16), tile)
        span = pl.ds(offset, span_len)
        code = own_code[rows, :]
        row_image = jnp.maximum(code, -code)
        mine = row_image == image
        bias[...] = jnp.where(row_image == span_code[2 * tile_index + which], 0.0, masked_score)
        self_bias = jnp.where(code < 0, 0.0, masked_score)
        lse_lane = lax.broadcasted_iota(jnp.int32, (tile, lse_out.shape[1]), 1)

        def one_head(head, carry):
            lanes, value_lanes, inside = head_lanes(head, head_size, width)
            queries = jnp.where(inside, query[rows, lanes], 0)
            scores = dot_nt(queries, window[span, lanes]) * exp_scale + bias[...]
            own_key = window[own_rows, lanes].astype(jnp.float32)
            own_value = window[own_rows, value_lanes].astype(jnp.float32)
            self_score = (
                jnp.sum(queries.astype(jnp.float32) * own_key, axis=1, keepdims=True) * exp_scale
                + self_bias
            )
            top = jnp.maximum(jnp.max(scores, axis=1, keepdims=True), self_score)
            powers = jnp.exp2(scores - top)
            self_power = jnp.exp2(self_score - top)
            total = jnp.sum(powers, axis=1, keepdims=True) + self_power
            mixed = dot_nn(powers.astype(jnp.bfloat16), window[span, value_lanes])
            mixed = (mixed + self_power * own_value) / total
            mix[rows, lanes] = jnp.where(inside & mine, mixed, mix[rows, lanes])
            lse_out[rows, :] = jnp.where(
                (lse_lane == head) & mine, top + jnp.log2(total), lse_out[rows, :]
            )
            return carry

        lax.fori_loop(0, HEADS, one_head, 0)

    def one_tile(tile_index, carry):
        one_span(tile_index, 0)

        @pl.when(plan[4 * tile_index + 2] != plan[4 * tile_index + 3])
        def _():
            one_span(tile_index, 1)

        return carry

    lax.fori_loop(0, tok // tile, one_tile, 0)
    out[...] = mix[...].astype(out.dtype)


def attention_backward_kernel(
    tile, left, exp_scale, plan, query, window, grad, lse_in, own_code, span_code,
    grad_query, grad_window, bias, acc_query, acc_window,
):
    tok, width = query.shape
    head_size = width // HEADS
    scale = 1.0 / math.sqrt(head_size)
    acc_query[...] = jnp.zeros_like(acc_query)
    acc_window[...] = jnp.zeros_like(acc_window)

    def one_span(tile_index, which):
        offset = pl.multiple_of(plan[4 * tile_index + which], 16)
        image = plan[4 * tile_index + 2 + which]
        rows = pl.ds(pl.multiple_of(tile_index * tile, 16), tile)
        own_rows = pl.ds(pl.multiple_of(left + tile_index * tile, 16), tile)
        span = pl.ds(offset, span_len)
        code = own_code[rows, :]
        row_image = jnp.maximum(code, -code)
        mine = row_image == image
        bias[...] = jnp.where(
            mine & (span_code[2 * tile_index + which] == image), 0.0, masked_score
        )
        self_bias = jnp.where((code < 0) & mine, 0.0, masked_score)
        lse_lane = lax.broadcasted_iota(jnp.int32, (tile, lse_in.shape[1]), 1)

        def one_head(head, carry):
            lanes, value_lanes, inside = head_lanes(head, head_size, width)
            queries = jnp.where(inside, query[rows, lanes], 0)
            grads = jnp.where(inside, grad[rows, lanes], 0)
            lse = jnp.sum(jnp.where(lse_lane == head, lse_in[rows, :], 0.0), axis=1, keepdims=True)
            keys = window[span, lanes]
            own_key = window[own_rows, lanes].astype(jnp.float32)
            own_value = window[own_rows, value_lanes].astype(jnp.float32)
            queries_wide = queries.astype(jnp.float32)
            grads_wide = grads.astype(jnp.float32)
            prob = jnp.exp2(dot_nt(queries, keys) * exp_scale + bias[...] - lse)
            self_score = jnp.sum(queries_wide * own_key, axis=1, keepdims=True) * exp_scale
            self_prob = jnp.exp2(self_score + self_bias - lse)
            grad_prob = dot_nt(grads, window[span, value_lanes])
            self_grad = jnp.sum(grads_wide * own_value, axis=1, keepdims=True)
            inner = jnp.sum(prob * grad_prob, axis=1, keepdims=True) + self_prob * self_grad
            grad_scores = (prob * (grad_prob - inner)).astype(jnp.bfloat16)
            self_grad_score = self_prob * (self_grad - inner)
            part = dot_nn(grad_scores, keys) + self_grad_score * own_key
            acc_query[rows, lanes] += jnp.where(inside, part, 0.0)
            acc_window[span, lanes] += dot_tn(grad_scores, queries)
            acc_window[span, value_lanes] += dot_tn(prob.astype(jnp.bfloat16), grads)
            acc_window[own_rows, lanes] += self_grad_score * queries_wide
            acc_window[own_rows, value_lanes] += self_prob * grads_wide
            return carry

        lax.fori_loop(0, HEADS, one_head, 0)

    def one_tile(tile_index, carry):
        one_span(tile_index, 0)

        @pl.when(plan[4 * tile_index + 2] != plan[4 * tile_index + 3])
        def _():
            one_span(tile_index, 1)

        return carry

    lax.fori_loop(0, tok // tile, one_tile, 0)
    grad_query[...] = (acc_query[...] * scale).astype(grad_query.dtype)
    step = 16

    def narrow(index, carry):
        rows = pl.ds(pl.multiple_of(index * step, step), step)
        grad_window[rows, :width] = (acc_window[rows, :width] * scale).astype(grad_window.dtype)
        grad_window[rows, width:] = acc_window[rows, width:].astype(grad_window.dtype)
        return carry

    lax.fori_loop(0, acc_window.shape[0] // step, narrow, 0)


def in_vmem():
    return pl.BlockSpec(memory_space=pltpu.VMEM)


def attention_forward(tile, left, plan, query, window, own_code, span_code):
    tok, width = query.shape
    exp_scale = math.log2(math.e) / math.sqrt(width // HEADS)
    return pl.pallas_call(
        functools.partial(attention_forward_kernel, tile, left, exp_scale),
        name="attention_forward",
        out_shape=[
            jax.ShapeDtypeStruct((tok, width), jnp.bfloat16),
            jax.ShapeDtypeStruct((tok, 128), jnp.float32),
        ],
        in_specs=[pl.BlockSpec(memory_space=pltpu.SMEM)] + [in_vmem()] * 4,
        out_specs=[in_vmem()] * 2,
        scratch_shapes=[
            pltpu.VMEM((tile, span_len), jnp.float32),
            pltpu.VMEM((tok, width), jnp.float32),
        ],
        compiler_params=pltpu.CompilerParams(vmem_limit_bytes=60 * mib),
    )(plan, query, window, own_code, span_code)


def attention_backward(tile, left, plan, query, window, grad, lse, own_code, span_code):
    tok, width = query.shape
    exp_scale = math.log2(math.e) / math.sqrt(width // HEADS)
    return pl.pallas_call(
        functools.partial(attention_backward_kernel, tile, left, exp_scale),
        name="attention_backward",
        out_shape=[
            jax.ShapeDtypeStruct((tok, width), jnp.bfloat16),
            jax.ShapeDtypeStruct(window.shape, jnp.bfloat16),
        ],
        in_specs=[pl.BlockSpec(memory_space=pltpu.SMEM)] + [in_vmem()] * 6,
        out_specs=[in_vmem()] * 2,
        scratch_shapes=[
            pltpu.VMEM((tile, span_len), jnp.float32),
            pltpu.VMEM((tok, width), jnp.float32),
            pltpu.VMEM(window.shape, jnp.float32),
        ],
        compiler_params=pltpu.CompilerParams(vmem_limit_bytes=62 * mib),
    )(plan, query, window, grad, lse, own_code, span_code)


def attention_plan(tile, left, right, own_ids, own_mask, window_ids, window_mask, place, places):
    tok = own_ids.shape[0]
    window_len = left + tok + right
    room = jnp.minimum(window_len, left + (places - place) * tok) - span_len
    position = jnp.arange(window_len)
    present = (position >= left - place * tok) & (position < left + (places - place) * tok)
    floor_ids = jnp.where(position < left, -1, window_ids + 0)
    ids = jnp.where(present, window_ids, floor_ids)
    codes = jnp.where((window_mask > 0) & present, window_ids + 1, 0)
    plans, spans = [], []
    for index in range(tok // tile):
        images = (own_ids[index * tile], own_ids[(index + 1) * tile - 1])
        offsets = []
        for image in images:
            start = jnp.sum((ids < image) & (position < left + tok)).astype(jnp.int32)
            offset = jnp.minimum(start // 16 * 16, room)
            offsets.append(offset)
            spans.append(lax.dynamic_slice(codes, (offset,), (span_len,)))
        plans += offsets + [image + 1 for image in images]
    plan = jnp.stack(plans).astype(jnp.int32)
    own_code = jnp.where(own_mask > 0, own_ids + 1, -(own_ids + 1)).astype(jnp.int32)[:, None]
    return plan, own_code, jnp.stack(spans)[:, None, :].astype(jnp.int32)


class Layout:
    def __init__(self, groups, seats, model_width):
        self.rows = model_width // (groups * seats)
        self.members = 2
        while self.members * self.rows % 16:
            self.members *= 2
        self.sides = self.members // 2
        self.lines = seats // self.members
        self.slab = self.members * self.rows
        self.padded = -(-self.rows // 16) * 16
        self.near = model_width // groups
        self.model_width = model_width

    def width(self, columns, shared):
        blocks = 2 if shared else 2 * self.sides
        return -(-columns // (128 * blocks)) * 128

    def columns(self, columns, shared):
        return self.width(columns, shared) * (2 if shared else 2 * self.sides)


class Mail:
    def __init__(self, layout, send, recv, slots):
        self.layout, self.send_sems, self.recv_sems, self.slots = layout, send, recv, slots
        self.group = lax.axis_index("dp")
        seat = lax.axis_index("seq")
        self.line = seat // layout.members
        self.member = seat % layout.members
        self.side = self.member // 2
        self.core = self.member % 2
        self.started = []

    def at(self, group=None, line=None, side=None, core=None):
        group = self.group if group is None else group
        line = self.line if line is None else line
        side = self.side if side is None else side
        core = self.core if core is None else core
        return (group, line * self.layout.members + side * 2 + core)

    def copy(self, slot, source, target, device, shift=0):
        index = self.slots[slot] + shift
        return pltpu.make_async_remote_copy(
            src_ref=source,
            dst_ref=target,
            send_sem=self.send_sems.at[index],
            recv_sem=self.recv_sems.at[index],
            device_id=device,
            device_id_type=pl.DeviceIdType.MESH,
        )

    def send(self, slot, source, target, device, when=None):
        copy = self.copy(slot, source, target, device)
        self.started.append((copy, when))
        guarded(when, copy.start)

    def wait(self, slot, target, shift=0):
        self.copy(slot, target, target, self.at(core=1 - self.core), shift).wait_recv()

    def finish(self):
        for copy, when in self.started:
            guarded(when, copy.wait_send)


def guarded(when, action):
    if when is None:
        action()
    else:
        pl.when(when)(action)


def all_of(*conditions):
    kept = [condition for condition in conditions if condition is not None]
    return functools.reduce(jnp.logical_and, kept) if kept else None


def run_steps(works, lag):
    waiting = [(index, work) for index, work in enumerate(works)]
    for _, work in waiting:
        next(work)
    clock = 0
    while waiting:
        for entry in list(waiting):
            if clock >= lag * entry[0]:
                try:
                    next(entry[1])
                except StopIteration:
                    waiting.remove(entry)
        clock += 1


def number(names):
    return {name: index for index, name in enumerate(names)}


def gather_slots(layout, shared):
    names = []
    steps = range(1, layout.lines)
    sources = ["own"] + [f"{way}{t}" for t in steps for way in ("below", "above")]
    for index, one_block in enumerate(shared):
        names += [(index, "mix", j) for j in range(1, layout.members)]
        names += [(index, way, t) for way in ("up", "down") for t in range(layout.lines)]
        names += [(index, "cross", source) for source in sources]
        if not one_block:
            for j in range(1, layout.sides):
                names += [
                    (index, "side", half, source, j) for half in (0, 1) for source in sources
                ]
        names += [(index, "core", j) for j in range(layout.sides)]
    return number(names)


def gather_kernel(layout, shared, widths, lag, *refs):
    count = len(shared)
    shards, outs = refs[:count], refs[count : 2 * count]
    landings, slabs = refs[2 * count : 3 * count], refs[3 * count : 4 * count]
    wide, send, recv, local = refs[4 * count :]
    mail = Mail(layout, send, recv, gather_slots(layout, shared))
    group, line, member, side, core = mail.group, mail.line, mail.member, mail.side, mail.core
    lines, members, sides = layout.lines, layout.members, layout.sides
    has_up, has_down = line < lines - 1, line > 0

    def work(index):
        shard, out, landing, slab = shards[index], outs[index], landings[index], slabs[index]
        width, one_block = widths[index], shared[index]

        def columns(side_of, core_of):
            block = core_of if one_block else core_of * sides + side_of
            return pl.ds(pl.multiple_of(block * width, 128), width)

        own = columns(side, core)

        def place(group_of, line_of):
            first = (group_of * lines + line_of) * layout.slab
            return out.at[pl.ds(pl.multiple_of(first, 16), layout.slab), own]

        for j in range(1, members):
            other = (member + j) % members
            mail.send(
                (index, "mix", j),
                shard.at[:, columns(other // 2, other % 2)],
                landing.at[member],
                mail.at(side=other // 2, core=other % 2),
            )
        mine = pltpu.make_async_copy(shard.at[:, own], landing.at[member], local.at[index, 0])
        mine.start()
        yield
        for j in range(1, members):
            mail.wait((index, "mix", j), landing.at[(member + members - j) % members])
        mine.wait()
        for m in range(members):
            rows = slice(m * layout.rows, (m + 1) * layout.rows)
            wide[rows, :width] = landing[m, : layout.rows, :].astype(jnp.float32)
        slab[...] = wide[:, :width].astype(slab.dtype)
        keep = pltpu.make_async_copy(slab, place(group, line), local.at[index, 1])
        keep.start()

        def pass_on(source, what, half, where, when=None):
            if half == 0:
                mail.send(
                    (index, "cross", source), what, where, mail.at(group=1 - group), when
                )
            if not one_block:
                for j in range(1, sides):
                    mail.send(
                        (index, "side", half, source, j),
                        what,
                        where,
                        mail.at(side=(side + j) % sides),
                        when,
                    )

        home = place(group, line)
        mail.send((index, "up", 0), slab, home, mail.at(line=line + 1), has_up)
        mail.send((index, "down", 0), slab, home, mail.at(line=line - 1), has_down)
        pass_on("own", slab, 0, home)
        yield
        for t in range(1, lines):
            below, above = line >= t, line < lines - t

            @pl.when(below)
            def _():
                mail.wait((index, "up", t - 1), place(group, line - t))

            where = place(group, line - t)
            mail.send(
                (index, "up", t), where, where, mail.at(line=line + 1), all_of(below, has_up)
            )
            pass_on(f"below{t}", where, 0, where, below)

            @pl.when(above)
            def _():
                mail.wait((index, "down", t - 1), place(group, line + t))

            where = place(group, line + t)
            mail.send(
                (index, "down", t), where, where, mail.at(line=line - 1), all_of(above, has_down)
            )
            pass_on(f"above{t}", where, 0, where, above)
            if t == 1:
                where = place(1 - group, line)
                mail.wait((index, "cross", "own"), where)
                pass_on("own", where, 1, where)
            yield
        for t in range(1, lines):
            for way, step, when in (("below", -t, line >= t), ("above", t, line < lines - t)):
                where = place(1 - group, line + step)

                @pl.when(when)
                def _():
                    mail.wait((index, "cross", f"{way}{t}"), where)

                pass_on(f"{way}{t}", where, 1, where, when)
            yield
        keep.wait()
        partner = mail.at(core=1 - core)
        mail.send((index, "core", 0), out.at[:, own], out.at[:, own], partner)
        if not one_block:
            yield
            for j in range(1, sides):
                source_side = (side + sides - j) % sides
                theirs = columns(source_side, core)
                for half, group_of in ((0, group), (1, 1 - group)):
                    for source, step, when in [("own", 0, None)] + [
                        (f"{way}{t}", sign * t, line >= t if sign < 0 else line < lines - t)
                        for t in range(1, lines)
                        for way, sign in (("below", -1), ("above", 1))
                    ]:
                        first = (group_of * lines + line + step) * layout.slab
                        where = out.at[pl.ds(pl.multiple_of(first, 16), layout.slab), theirs]
                        slot = (index, "side", half, source, j)
                        guarded(when, functools.partial(mail.wait, slot, where))
                mail.send((index, "core", j), out.at[:, theirs], out.at[:, theirs], partner)
        yield
        mail.wait((index, "core", 0), out.at[:, columns(side, 1 - core)])
        if not one_block:
            for j in range(1, sides):
                source_side = (side + sides - j) % sides
                mail.wait((index, "core", j), out.at[:, columns(source_side, 1 - core)])

    run_steps([work(index) for index in range(count)], lag)
    mail.finish()


def gather_parameters(layout, shards, shared, lag=2):
    widths = [
        shard.shape[1] // (2 if one_block else 2 * layout.sides)
        for shard, one_block in zip(shards, shared)
    ]
    slots = len(gather_slots(layout, shared))
    anywhere = pl.BlockSpec(memory_space=pl.ANY)
    return pl.pallas_call(
        functools.partial(gather_kernel, layout, shared, widths, lag),
        name="gather_parameters",
        out_shape=[
            jax.ShapeDtypeStruct((layout.model_width, shard.shape[1]), shard.dtype)
            for shard in shards
        ],
        in_specs=[anywhere] * len(shards),
        out_specs=[anywhere] * len(shards),
        scratch_shapes=[
            pltpu.VMEM((layout.members, layout.padded, width), jnp.bfloat16) for width in widths
        ]
        + [pltpu.VMEM((layout.slab, width), jnp.bfloat16) for width in widths]
        + [
            pltpu.VMEM((layout.slab, max(widths)), jnp.float32),
            pltpu.SemaphoreType.DMA((slots,)),
            pltpu.SemaphoreType.DMA((slots,)),
            pltpu.SemaphoreType.DMA((len(shards), 2)),
        ],
        compiler_params=pltpu.CompilerParams(
            has_side_effects=True, vmem_limit_bytes=40 * mib
        ),
    )(*shards)


def reduce_slots(layout, shared):
    names = []
    for index, one_block in enumerate(shared):
        names += [(index, "core", half) for half in (0, 1)]
        if not one_block:
            names += [(index, "side", half, j) for half in (0, 1) for j in range(1, layout.sides)]
        names += [(index, "cross")]
        names += [(index, way, t) for way in ("up", "down") for t in range(layout.lines)]
        names += [(index, "mix", j) for j in range(1, layout.members)]
    return number(names)


def add_rows(target, first, target_columns, source, source_columns, count, source_first=0):
    step = 48

    def one(index, carry):
        rows = pl.ds(pl.multiple_of(first + index * step, 16), step)
        theirs = pl.ds(pl.multiple_of(source_first + index * step, 16), step)
        total = target[rows, target_columns].astype(jnp.float32)
        total += source[theirs, source_columns].astype(jnp.float32)
        target[rows, target_columns] = total.astype(target.dtype)
        return carry

    lax.fori_loop(0, count // step, one, 0)


def reduce_kernel(layout, shared, widths, lag, *refs):
    count = len(shared)
    take = iter(range(0, len(refs), count))
    grads, outs, cores, sums, crosses, ups, downs, pieces, landings = (
        refs[first : first + count] for first in [next(take) for _ in range(9)]
    )
    rest = list(refs[9 * count :])
    sides_in = [None if one_block else rest.pop(0) for one_block in shared]
    wide, spare, send, recv, local = rest
    mail = Mail(layout, send, recv, reduce_slots(layout, shared))
    group, line, member, side, core = mail.group, mail.line, mail.member, mail.side, mail.core
    lines, members, sides = layout.lines, layout.members, layout.sides
    near_rows, slab_rows = layout.near, layout.slab
    far_first = pl.multiple_of((1 - group) * near_rows, 16)
    near_first = pl.multiple_of(group * near_rows, 16)

    def work(index):
        grad, out, from_core, total = grads[index], outs[index], cores[index], sums[index]
        cross, up, down = crosses[index], ups[index], downs[index]
        piece, landing, from_side = pieces[index], landings[index], sides_in[index]
        width, one_block = widths[index], shared[index]
        half = width if one_block else width * sides
        first_own = 0 if one_block else pl.multiple_of(side * width, 128)
        own = pl.ds(first_own, width)
        halves = ((0, far_first), (1, near_first))
        loads = []
        for tag, first in halves:
            rows = pl.ds(first, near_rows)
            away = pl.ds(pl.multiple_of((1 - core) * half, 128), half)
            stay = pl.ds(pl.multiple_of(core * half, 128), half)
            mail.send(
                (index, "core", tag), grad.at[rows, away], from_core.at[rows], mail.at(core=1 - core)
            )
            load = pltpu.make_async_copy(grad.at[rows, stay], total.at[rows], local.at[index, tag])
            load.start()
            loads.append(load)
        yield
        for tag, first in halves:
            rows = pl.ds(first, near_rows)
            mail.wait((index, "core", tag), from_core.at[rows])
            fetch = pltpu.make_async_copy(
                from_core.at[rows], spare.at[:, pl.ds(0, half)], local.at[index, 2]
            )
            fetch.start()
            loads[tag].wait()
            fetch.wait()
            add_rows(total, first, pl.ds(0, half), spare, pl.ds(0, half), near_rows)
            if not one_block:
                for j in range(1, sides):
                    other = (side + j) % sides
                    theirs = pl.ds(pl.multiple_of(other * width, 128), width)
                    mail.send(
                        (index, "side", tag, j),
                        total.at[rows, theirs],
                        from_side.at[j - 1, rows],
                        mail.at(side=other),
                    )
            elif tag == 0:
                mail.send((index, "cross"), total.at[rows, own], cross, mail.at(group=1 - group))
            yield
        if not one_block:
            for tag, first in halves:
                rows = pl.ds(first, near_rows)
                for j in range(1, sides):
                    mail.wait((index, "side", tag, j), from_side.at[j - 1, rows])
                    add_rows(
                        total, first, own, from_side.at[j - 1], pl.ds(0, width), near_rows, first
                    )
                if tag == 0:
                    mail.send(
                        (index, "cross"), total.at[rows, own], cross, mail.at(group=1 - group)
                    )
                yield
        mail.wait((index, "cross"), cross)
        add_rows(total, near_first, own, cross, pl.ds(0, width), near_rows)

        def slab_first(line_of):
            return pl.multiple_of(near_first + line_of * slab_rows, 16)

        for t in range(lines - 1):
            for way, buffer, goal, going, fed, to in (
                ("up", up, lines - 1 - t, line < lines - 1 - t, line > 0, line + 1),
                ("down", down, t, line > t, line < lines - 1, line - 1),
            ):
                slot = (index, way, goal)
                first = slab_first(goal)

                @pl.when(all_of(going, fed))
                def _():
                    mail.wait(slot, buffer.at[goal])
                    add_rows(total, first, own, buffer.at[goal], pl.ds(0, width), slab_rows)

                mail.send(
                    slot,
                    total.at[pl.ds(first, slab_rows), own],
                    buffer.at[goal],
                    mail.at(line=to),
                    going,
                )
            yield
        first = slab_first(line)
        wide[:, :width] = total[pl.ds(first, slab_rows), own].astype(jnp.float32)
        for way, buffer, fed in (("up", up, line > 0), ("down", down, line < lines - 1)):

            @pl.when(fed)
            def _():
                mail.wait((index, way, 0), buffer.at[line], line)
                wide[:, :width] += buffer[line].astype(jnp.float32)

        for m in range(members):
            rows = slice(m * layout.rows, (m + 1) * layout.rows)
            piece[m] = jnp.zeros(piece.shape[1:], piece.dtype)
            piece[m, : layout.rows, :] = wide[rows, :width].astype(piece.dtype)
        seat = core * sides + side
        for j in range(1, members):
            other = (member + j) % members
            mail.send(
                (index, "mix", j),
                piece.at[other],
                landing.at[seat],
                mail.at(side=other // 2, core=other % 2),
            )
        landing[seat] = piece[member]
        yield
        for j in range(1, members):
            other = (member + members - j) % members
            mail.wait((index, "mix", j), landing.at[other % 2 * sides + other // 2])
        if one_block:
            for c in range(2):
                block = landing[c * sides].astype(jnp.float32)
                for s in range(1, sides):
                    block += landing[c * sides + s].astype(jnp.float32)
                out[:, c * width : (c + 1) * width] = block
        else:
            for b in range(2 * sides):
                out[:, b * width : (b + 1) * width] = landing[b].astype(jnp.float32)

    run_steps([work(index) for index in range(count)], lag)
    mail.finish()


def reduce_gradients(layout, grads, shared, lag=1):
    blocks = [2 if one_block else 2 * layout.sides for one_block in shared]
    widths = [grad.shape[1] // block for grad, block in zip(grads, blocks)]
    slots = len(reduce_slots(layout, shared))
    anywhere = pl.BlockSpec(memory_space=pl.ANY)
    count, rows, slab = len(grads), layout.model_width, layout.slab
    low = jnp.bfloat16
    members, padded, lines = layout.members, layout.padded, layout.lines
    halves = [grad.shape[1] // 2 for grad in grads]
    results = pl.pallas_call(
        functools.partial(reduce_kernel, layout, shared, widths, lag),
        name="reduce_gradients",
        out_shape=[jax.ShapeDtypeStruct((padded, grad.shape[1]), jnp.float32) for grad in grads]
        + [jax.ShapeDtypeStruct((rows, half), low) for half in halves],
        in_specs=[anywhere] * count,
        out_specs=[in_vmem()] * count + [anywhere] * count,
        scratch_shapes=[pltpu.VMEM((rows, half), low) for half in halves]
        + [pltpu.VMEM((layout.near, width), low) for width in widths]
        + [pltpu.VMEM((lines, slab, width), low) for _ in range(2) for width in widths]
        + [pltpu.VMEM((members, padded, width), low) for _ in range(2) for width in widths]
        + [
            pltpu.VMEM((layout.sides - 1, rows, width), low)
            for width, one_block in zip(widths, shared)
            if not one_block
        ]
        + [
            pltpu.VMEM((slab, max(widths)), jnp.float32),
            pltpu.VMEM((layout.near, max(halves)), low),
            pltpu.SemaphoreType.DMA((slots,)),
            pltpu.SemaphoreType.DMA((slots,)),
            pltpu.SemaphoreType.DMA((count, 3)),
        ],
        compiler_params=pltpu.CompilerParams(
            has_side_effects=True, vmem_limit_bytes=60 * mib
        ),
    )(*grads)
    return results[:count]


def shifted(array, by):
    devices = lax.axis_size("seq")
    pairs = [(i, i + by) for i in range(devices) if 0 <= i + by < devices]
    return lax.ppermute(array, "seq", pairs)


def column_sum(source):
    return jnp.sum(source.astype(jnp.float32), axis=0)


def norm_forward(source, gain_row, shift_row):
    row_mean = jnp.mean(source, axis=-1, keepdims=True)
    centred = source - row_mean
    variance = jnp.mean(centred * centred, axis=-1, keepdims=True)
    inv_scale = lax.rsqrt(variance + eps_norm)
    unit_rows = centred * inv_scale
    return (unit_rows * gain_row + shift_row, unit_rows, inv_scale)


def norm_backward(gradient, unit_rows, inv_scale, gain_row):
    scaled = gradient * gain_row
    grad_in = inv_scale * (
        scaled
        - jnp.mean(scaled, axis=-1, keepdims=True)
        - unit_rows * jnp.mean(scaled * unit_rows, axis=-1, keepdims=True)
    )
    return (grad_in, jnp.sum(gradient * unit_rows, axis=0), jnp.sum(gradient, axis=0))


def gelu_tanh(source):
    return jax.nn.gelu(source, approximate=True)


def adam_step(weight_now, gradient, first_old, second_old):
    first_new = beta_first * first_old + (1.0 - beta_first) * gradient
    second_new = beta_second * second_old + (1.0 - beta_second) * gradient * gradient
    first_hat = first_new / (1.0 - beta_first**STEP)
    second_hat = second_new / (1.0 - beta_second**STEP)
    update = -learn_rate * (
        first_hat / (jnp.sqrt(second_hat) + eps_adam)
        + weight_decay * weight_now.astype(jnp.float32)
    )
    return (first_new, second_new, update)


def round_up(count, unit):
    return -(-count // unit) * unit


def per_device(
    inputs, image_ids, token_mask, cotangent,
    w_qkv, w_out, w_up, w_down, norm_gains, bias_rows, up_bias,
    first_qkv, first_out, first_up, first_down, first_gains, first_bias, first_upbias,
    second_qkv, second_out, second_up, second_down, second_gains, second_bias, second_upbias,
):
    tok, width = inputs.shape
    layers, _, hidden_width = w_up.shape
    places = lax.axis_size("seq")
    place = lax.axis_index("seq")
    layout = Layout(lax.axis_size("dp"), places, width)
    group_tok = tok * places
    spare_count = group_tok - group_tok // IMG * IMG
    left = round_up(IMG - 1 + spare_count, 16)
    right = round_up(IMG - 1, 16)
    tile = tok // 2

    reach_left = [min(tok, left - first) for first in range(0, left, tok)]
    reach_right = [min(tok, right - first) for first in range(0, right, tok)]

    def window_of(array):
        parts = [shifted(array[tok - rows :], by + 1) for by, rows in enumerate(reach_left)][::-1]
        parts += [array]
        parts += [shifted(array[:rows], -by - 1) for by, rows in enumerate(reach_right)]
        return jnp.concatenate(parts)

    def owned_of(window):
        total = window[left : left + tok].astype(jnp.float32)
        for by, rows in enumerate(reach_left):
            first = left - by * tok - rows
            part = shifted(window[first : first + rows], -by - 1).astype(jnp.float32)
            total = total + jnp.pad(part, ((tok - rows, 0), (0, 0)))
        for by, rows in enumerate(reach_right):
            first = left + (by + 1) * tok
            part = shifted(window[first : first + rows], by + 1).astype(jnp.float32)
            total = total + jnp.pad(part, ((0, tok - rows), (0, 0)))
        return total.astype(jnp.bfloat16)

    half = hidden_width // 2
    half_pad = round_up(half + 8 * layers, 128)
    wide_columns = 2 * half_pad

    def spread(array):
        pad = [(0, 0)] * (array.ndim - 1) + [(0, half_pad - half)]
        return jnp.concatenate([jnp.pad(array[..., :half], pad), jnp.pad(array[..., half:], pad)], -1)

    def unspread(array):
        return jnp.concatenate(
            [array[..., :half], array[..., half_pad : half_pad + half]], axis=-1
        )

    def filled(array, rows, columns):
        return jnp.pad(array, ((0, rows - array.shape[0]), (0, columns - array.shape[1])))

    shared = (False, True, False)
    attn_columns = layout.columns(4 * width, False)
    up_columns = layout.columns(wide_columns, True)
    down_columns = layout.columns(wide_columns, False)
    rows_of = jnp.concatenate([norm_gains.reshape(-1, layout.rows), bias_rows.reshape(-1, layout.rows)])
    row_count = rows_of.shape[0]
    shards = []
    for layer in range(layers):
        attn_shard = jnp.concatenate([w_qkv[layer], w_out[layer]], axis=1)
        up_shard = spread(w_up[layer])
        if layer == 0:
            up_shard = up_shard.at[:, half : half + row_count].set(rows_of.T)
        down_shard = spread(w_down[layer].T)
        shards += [
            filled(attn_shard, layout.padded, attn_columns),
            filled(up_shard, layout.padded, up_columns),
            filled(down_shard, layout.padded, down_columns),
        ]
    gathered = gather_parameters(layout, shards, shared * layers)
    all_rows = gathered[1][:, half : half + row_count].T.astype(jnp.float32)
    gains = all_rows[: 2 * layers].reshape(layers, 2, width)
    shifts = all_rows[2 * layers :].reshape(layers, 6, width)
    up_shift = spread(up_bias.astype(jnp.float32))

    window_word = window_of(image_ids * 2 + (token_mask > 0).astype(jnp.int32))
    plan, own_code, span_code = attention_plan(
        tile, left, right, image_ids, token_mask, window_word // 2, window_word % 2, place, places
    )

    residual = inputs.astype(jnp.float32)
    kept_layers = []
    for layer in range(layers):
        attn_weight, up_weight, down_weight = gathered[3 * layer : 3 * layer + 3]
        down_weight = down_weight[:, :wide_columns]
        normed, unit_one, inv_one = norm_forward(residual, gains[layer, 0], shifts[layer, 0])
        normed_low = normed.astype(jnp.bfloat16)
        projected = dot_nn(normed_low, attn_weight[:, : 3 * width])
        queries = (projected[:, :width] + shifts[layer, 2]).astype(jnp.bfloat16)
        value_shift = jnp.concatenate([jnp.zeros_like(shifts[layer, 3]), shifts[layer, 3]])
        key_value = (projected[:, width:] + value_shift).astype(jnp.bfloat16)
        window = window_of(key_value)
        attended, lse = attention_forward(tile, left, plan, queries, window, own_code, span_code)
        middle = (
            residual
            + dot_nn(attended, attn_weight[:, 3 * width : 4 * width])
            + shifts[layer, 4]
        )
        hidden, unit_two, inv_two = norm_forward(middle, gains[layer, 1], shifts[layer, 1])
        hidden_low = hidden.astype(jnp.bfloat16)
        pre_act = dot_nn(hidden_low, up_weight[:, :wide_columns]) + up_shift[layer]
        active = gelu_tanh(pre_act).astype(jnp.bfloat16)
        residual = middle + dot_nt(active, down_weight) + shifts[layer, 5]
        kept_layers.append(
            (window, unit_one, inv_one, normed_low, queries, lse, attended,
             unit_two, inv_two, hidden_low, pre_act, active)
        )

    grad_res = cotangent.astype(jnp.float32)
    owned = [None] * layers
    upbias_grads = [None] * layers
    for layer in reversed(range(layers)):
        (window, unit_one, inv_one, normed_low, queries, lse, attended,
         unit_two, inv_two, hidden_low, pre_act, active) = kept_layers[layer]
        attn_weight, up_weight, down_weight = gathered[3 * layer : 3 * layer + 3]
        down_weight = down_weight[:, :wide_columns]
        grad_branch = grad_res.astype(jnp.bfloat16)
        grad_downw = dot_tn(grad_branch, active).astype(jnp.bfloat16)
        grad_active = dot_nn(grad_branch, down_weight)
        _, gelu_pull = jax.vjp(gelu_tanh, pre_act)
        grad_pre = gelu_pull(grad_active)[0].astype(jnp.bfloat16)
        grad_upw = dot_tn(hidden_low, grad_pre).astype(jnp.bfloat16)
        upbias_grads[layer] = lax.psum(unspread(column_sum(grad_pre)), ("dp", "seq"))
        grad_hidden = dot_nt(grad_pre, up_weight[:, :wide_columns])
        back_two, gain_two, shift_two = norm_backward(
            grad_hidden, unit_two, inv_two, gains[layer, 1]
        )
        grad_mid = grad_res + back_two
        grad_attn = grad_mid.astype(jnp.bfloat16)
        grad_outw = dot_tn(attended, grad_attn).astype(jnp.bfloat16)
        grad_attended = dot_nt(grad_attn, attn_weight[:, 3 * width : 4 * width]).astype(
            jnp.bfloat16
        )
        grad_query, grad_window = attention_backward(
            tile, left, plan, queries, window, grad_attended, lse, own_code, span_code
        )
        grad_key_value = owned_of(grad_window)
        grad_proj = jnp.concatenate([grad_query, grad_key_value], axis=1)
        grad_qkvw = dot_tn(normed_low, grad_proj).astype(jnp.bfloat16)
        grad_normed = dot_nt(grad_proj, attn_weight[:, : 3 * width])
        back_one, gain_one, shift_one = norm_backward(
            grad_normed, unit_one, inv_one, gains[layer, 0]
        )
        grad_res = grad_mid + back_one
        grad_rows = jnp.stack(
            [
                gain_one,
                gain_two,
                shift_one,
                shift_two,
                column_sum(grad_query),
                column_sum(grad_key_value[:, width:]),
                column_sum(grad_attn),
                column_sum(grad_branch),
            ]
        )
        grad_upw = grad_upw.at[:, half : half + 8].set(grad_rows.T.astype(jnp.bfloat16))
        owned[layer] = reduce_gradients(
            layout,
            [
                filled(jnp.concatenate([grad_qkvw, grad_outw], axis=1), width, attn_columns),
                filled(grad_upw, width, up_columns),
                filled(grad_downw, width, down_columns),
            ],
            shared,
        )

    def stacked(part):
        return jnp.stack([part(*owned[layer]) for layer in range(layers)])

    rows = layout.rows
    grads = (
        stacked(lambda attn, up, down: attn[:rows, : 3 * width]),
        stacked(lambda attn, up, down: attn[:rows, 3 * width : 4 * width]),
        stacked(lambda attn, up, down: unspread(up[:rows])),
        stacked(lambda attn, up, down: unspread(down[:rows]).T),
        stacked(lambda attn, up, down: up[:rows, half : half + 2].T),
        stacked(lambda attn, up, down: up[:rows, half + 2 : half + 8].T),
        jnp.stack(upbias_grads),
    )
    params = (w_qkv, w_out, w_up, w_down, norm_gains, bias_rows, up_bias)
    firsts = (first_qkv, first_out, first_up, first_down, first_gains, first_bias, first_upbias)
    seconds = (
        second_qkv, second_out, second_up, second_down, second_gains, second_bias, second_upbias,
    )
    results = [adam_step(*packed) for packed in zip(params, grads, firsts, seconds)]
    return (
        (residual, grad_res)
        + grads
        + tuple(result[0] for result in results)
        + tuple(result[1] for result in results)
        + tuple(result[2] for result in results)
    )


def solution(mesh):
    in_specs = (
        P(("dp", "seq"), None),
        P(("dp", "seq")),
        P(("dp", "seq")),
        P(("dp", "seq"), None),
        P(None, ("dp", "seq"), None),
        P(None, ("dp", "seq"), None),
        P(None, ("dp", "seq"), None),
        P(None, None, ("dp", "seq")),
        P(None, None, ("dp", "seq")),
        P(None, None, ("dp", "seq")),
        P(),
        P(None, ("dp", "seq"), None),
        P(None, ("dp", "seq"), None),
        P(None, ("dp", "seq"), None),
        P(None, None, ("dp", "seq")),
        P(None, None, ("dp", "seq")),
        P(None, None, ("dp", "seq")),
        P(),
        P(None, ("dp", "seq"), None),
        P(None, ("dp", "seq"), None),
        P(None, ("dp", "seq"), None),
        P(None, None, ("dp", "seq")),
        P(None, None, ("dp", "seq")),
        P(None, None, ("dp", "seq")),
        P(),
    )
    out_specs = (
        P(("dp", "seq"), None),
        P(("dp", "seq"), None),
        P(None, ("dp", "seq"), None),
        P(None, ("dp", "seq"), None),
        P(None, ("dp", "seq"), None),
        P(None, None, ("dp", "seq")),
        P(None, None, ("dp", "seq")),
        P(None, None, ("dp", "seq")),
        P(),
        P(None, ("dp", "seq"), None),
        P(None, ("dp", "seq"), None),
        P(None, ("dp", "seq"), None),
        P(None, None, ("dp", "seq")),
        P(None, None, ("dp", "seq")),
        P(None, None, ("dp", "seq")),
        P(),
        P(None, ("dp", "seq"), None),
        P(None, ("dp", "seq"), None),
        P(None, ("dp", "seq"), None),
        P(None, None, ("dp", "seq")),
        P(None, None, ("dp", "seq")),
        P(None, None, ("dp", "seq")),
        P(),
        P(None, ("dp", "seq"), None),
        P(None, ("dp", "seq"), None),
        P(None, ("dp", "seq"), None),
        P(None, None, ("dp", "seq")),
        P(None, None, ("dp", "seq")),
        P(None, None, ("dp", "seq")),
        P(),
    )
    return jax.shard_map(
        per_device, mesh=mesh, in_specs=in_specs, out_specs=out_specs, check_vma=False
    )
```

```python
import functools
import math

import jax
import jax.numpy as jnp
from jax import lax
from jax.experimental import pallas as pl
from jax.experimental.pallas import tpu as pltpu
from jax.sharding import PartitionSpec as P

HEADS = 16
IMG = 729
STEP = 8

eps_norm = 1e-06
beta_first = 0.9
beta_second = 0.95
learn_rate = 0.025
weight_decay = 0.1
eps_adam = 1e-08
span_len = 768
lane_pair = 256
masked_score = -1e30
mib = 2**20


def head_lanes(head, head_size, width):
    low = head * head_size
    first = jnp.minimum(low // 128 * 128, width - lane_pair)
    lanes = lax.broadcasted_iota(jnp.int32, (1, lane_pair), 1)
    inside = (lanes >= low - first) & (lanes < low - first + head_size)
    keys = pl.ds(pl.multiple_of(first, 128), lane_pair)
    values = pl.ds(pl.multiple_of(first + width, 128), lane_pair)
    return keys, values, inside


def dot_nn(left, right):
    return lax.dot_general(left, right, (((1,), (0,)), ((), ())), preferred_element_type=jnp.float32)


def dot_nt(left, right):
    return lax.dot_general(left, right, (((1,), (1,)), ((), ())), preferred_element_type=jnp.float32)


def dot_tn(left, right):
    return lax.dot_general(left, right, (((0,), (0,)), ((), ())), preferred_element_type=jnp.float32)


def attention_forward_kernel(
    tile, left, exp_scale, plan, query, window, own_code, span_code, out, lse_out, bias, mix
):
    tok, width = query.shape
    head_size = width // HEADS

    def one_span(tile_index, which):
        offset = pl.multiple_of(plan[4 * tile_index + which], 16)
        image = plan[4 * tile_index + 2 + which]
        rows = pl.ds(pl.multiple_of(tile_index * tile, 16), tile)
        own_rows = pl.ds(pl.multiple_of(left + tile_index * tile, 16), tile)
        span = pl.ds(offset, span_len)
        code = own_code[rows, :]
        row_image = jnp.maximum(code, -code)
        mine = row_image == image
        bias[...] = jnp.where(row_image == span_code[2 * tile_index + which], 0.0, masked_score)
        self_bias = jnp.where(code < 0, 0.0, masked_score)
        lse_lane = lax.broadcasted_iota(jnp.int32, (tile, lse_out.shape[1]), 1)

        def one_head(head, carry):
            lanes, value_lanes, inside = head_lanes(head, head_size, width)
            queries = jnp.where(inside, query[rows, lanes], 0)
            scores = dot_nt(queries, window[span, lanes]) * exp_scale + bias[...]
            own_key = window[own_rows, lanes].astype(jnp.float32)
            own_value = window[own_rows, value_lanes].astype(jnp.float32)
            self_score = (
                jnp.sum(queries.astype(jnp.float32) * own_key, axis=1, keepdims=True) * exp_scale
                + self_bias
            )
            top = jnp.maximum(jnp.max(scores, axis=1, keepdims=True), self_score)
            powers = jnp.exp2(scores - top)
            self_power = jnp.exp2(self_score - top)
            total = jnp.sum(powers, axis=1, keepdims=True) + self_power
            mixed = dot_nn(powers.astype(jnp.bfloat16), window[span, value_lanes])
            mixed = (mixed + self_power * own_value) / total
            mix[rows, lanes] = jnp.where(inside & mine, mixed, mix[rows, lanes])
            lse_out[rows, :] = jnp.where(
                (lse_lane == head) & mine, top + jnp.log2(total), lse_out[rows, :]
            )
            return carry

        lax.fori_loop(0, HEADS, one_head, 0, unroll=2)

    def one_tile(tile_index, carry):
        one_span(tile_index, 0)

        @pl.when(plan[4 * tile_index + 2] != plan[4 * tile_index + 3])
        def _():
            one_span(tile_index, 1)

        return carry

    lax.fori_loop(0, tok // tile, one_tile, 0)
    out[...] = mix[...].astype(out.dtype)


def attention_backward_kernel(
    tile, left, exp_scale, plan, query, window, grad, lse_in, own_code, span_code,
    grad_query, grad_window, bias, acc_query, acc_window,
):
    tok, width = query.shape
    head_size = width // HEADS
    scale = 1.0 / math.sqrt(head_size)
    acc_query[...] = jnp.zeros_like(acc_query)
    acc_window[...] = jnp.zeros_like(acc_window)

    def one_span(tile_index, which):
        offset = pl.multiple_of(plan[4 * tile_index + which], 16)
        image = plan[4 * tile_index + 2 + which]
        rows = pl.ds(pl.multiple_of(tile_index * tile, 16), tile)
        own_rows = pl.ds(pl.multiple_of(left + tile_index * tile, 16), tile)
        span = pl.ds(offset, span_len)
        code = own_code[rows, :]
        row_image = jnp.maximum(code, -code)
        mine = row_image == image
        bias[...] = jnp.where(
            mine & (span_code[2 * tile_index + which] == image), 0.0, masked_score
        )
        self_bias = jnp.where((code < 0) & mine, 0.0, masked_score)
        lse_lane = lax.broadcasted_iota(jnp.int32, (tile, lse_in.shape[1]), 1)

        def one_head(head, carry):
            lanes, value_lanes, inside = head_lanes(head, head_size, width)
            queries = jnp.where(inside, query[rows, lanes], 0)
            grads = jnp.where(inside, grad[rows, lanes], 0)
            lse = jnp.sum(jnp.where(lse_lane == head, lse_in[rows, :], 0.0), axis=1, keepdims=True)
            keys = window[span, lanes]
            own_key = window[own_rows, lanes].astype(jnp.float32)
            own_value = window[own_rows, value_lanes].astype(jnp.float32)
            queries_wide = queries.astype(jnp.float32)
            grads_wide = grads.astype(jnp.float32)
            prob = jnp.exp2(dot_nt(queries, keys) * exp_scale + bias[...] - lse)
            self_score = jnp.sum(queries_wide * own_key, axis=1, keepdims=True) * exp_scale
            self_prob = jnp.exp2(self_score + self_bias - lse)
            grad_prob = dot_nt(grads, window[span, value_lanes])
            self_grad = jnp.sum(grads_wide * own_value, axis=1, keepdims=True)
            inner = jnp.sum(prob * grad_prob, axis=1, keepdims=True) + self_prob * self_grad
            grad_scores = (prob * (grad_prob - inner)).astype(jnp.bfloat16)
            self_grad_score = self_prob * (self_grad - inner)
            part = dot_nn(grad_scores, keys) + self_grad_score * own_key
            acc_query[rows, lanes] += jnp.where(inside, part, 0.0)
            acc_window[span, lanes] += dot_tn(grad_scores, queries)
            acc_window[span, value_lanes] += dot_tn(prob.astype(jnp.bfloat16), grads)
            acc_window[own_rows, lanes] += self_grad_score * queries_wide
            acc_window[own_rows, value_lanes] += self_prob * grads_wide
            return carry

        lax.fori_loop(0, HEADS, one_head, 0, unroll=2)

    def one_tile(tile_index, carry):
        one_span(tile_index, 0)

        @pl.when(plan[4 * tile_index + 2] != plan[4 * tile_index + 3])
        def _():
            one_span(tile_index, 1)

        return carry

    lax.fori_loop(0, tok // tile, one_tile, 0)
    grad_query[...] = (acc_query[...] * scale).astype(grad_query.dtype)
    step = 16

    def narrow(index, carry):
        rows = pl.ds(pl.multiple_of(index * step, step), step)
        grad_window[rows, :width] = (acc_window[rows, :width] * scale).astype(grad_window.dtype)
        grad_window[rows, width:] = acc_window[rows, width:].astype(grad_window.dtype)
        return carry

    lax.fori_loop(0, acc_window.shape[0] // step, narrow, 0)


def in_vmem():
    return pl.BlockSpec(memory_space=pltpu.VMEM)


def attention_forward(tile, left, plan, query, window, own_code, span_code):
    tok, width = query.shape
    exp_scale = math.log2(math.e) / math.sqrt(width // HEADS)
    return pl.pallas_call(
        functools.partial(attention_forward_kernel, tile, left, exp_scale),
        name="attention_forward",
        out_shape=[
            jax.ShapeDtypeStruct((tok, width), jnp.bfloat16),
            jax.ShapeDtypeStruct((tok, 128), jnp.float32),
        ],
        in_specs=[pl.BlockSpec(memory_space=pltpu.SMEM)] + [in_vmem()] * 4,
        out_specs=[in_vmem()] * 2,
        scratch_shapes=[
            pltpu.VMEM((tile, span_len), jnp.float32),
            pltpu.VMEM((tok, width), jnp.float32),
        ],
        compiler_params=pltpu.CompilerParams(vmem_limit_bytes=60 * mib),
    )(plan, query, window, own_code, span_code)


def attention_backward(tile, left, plan, query, window, grad, lse, own_code, span_code):
    tok, width = query.shape
    exp_scale = math.log2(math.e) / math.sqrt(width // HEADS)
    return pl.pallas_call(
        functools.partial(attention_backward_kernel, tile, left, exp_scale),
        name="attention_backward",
        out_shape=[
            jax.ShapeDtypeStruct((tok, width), jnp.bfloat16),
            jax.ShapeDtypeStruct(window.shape, jnp.bfloat16),
        ],
        in_specs=[pl.BlockSpec(memory_space=pltpu.SMEM)] + [in_vmem()] * 6,
        out_specs=[in_vmem()] * 2,
        scratch_shapes=[
            pltpu.VMEM((tile, span_len), jnp.float32),
            pltpu.VMEM((tok, width), jnp.float32),
            pltpu.VMEM(window.shape, jnp.float32),
        ],
        compiler_params=pltpu.CompilerParams(vmem_limit_bytes=62 * mib),
    )(plan, query, window, grad, lse, own_code, span_code)


def attention_plan(tile, left, right, own_ids, own_mask, window_ids, window_mask, place, places):
    tok = own_ids.shape[0]
    window_len = left + tok + right
    room = jnp.minimum(window_len, left + (places - place) * tok) - span_len
    position = jnp.arange(window_len)
    present = (position >= left - place * tok) & (position < left + (places - place) * tok)
    floor_ids = jnp.where(position < left, -1, window_ids + 0)
    ids = jnp.where(present, window_ids, floor_ids)
    codes = jnp.where((window_mask > 0) & present, window_ids + 1, 0)
    plans, spans = [], []
    for index in range(tok // tile):
        images = (own_ids[index * tile], own_ids[(index + 1) * tile - 1])
        offsets = []
        for image in images:
            start = jnp.sum((ids < image) & (position < left + tok)).astype(jnp.int32)
            offset = jnp.minimum(start // 16 * 16, room)
            offsets.append(offset)
            spans.append(lax.dynamic_slice(codes, (offset,), (span_len,)))
        plans += offsets + [image + 1 for image in images]
    plan = jnp.stack(plans).astype(jnp.int32)
    own_code = jnp.where(own_mask > 0, own_ids + 1, -(own_ids + 1)).astype(jnp.int32)[:, None]
    return plan, own_code, jnp.stack(spans)[:, None, :].astype(jnp.int32)


class Layout:
    def __init__(self, groups, seats, model_width):
        self.rows = model_width // (groups * seats)
        self.members = 2
        while self.members * self.rows % 16:
            self.members *= 2
        self.sides = self.members // 2
        self.lines = seats // self.members
        self.slab = self.members * self.rows
        self.padded = -(-self.rows // 16) * 16
        self.near = model_width // groups
        self.model_width = model_width

    def blocks(self, one_block):
        return 2 if one_block else 2 * self.sides

    def columns(self, columns, one_block):
        unit = 128 * self.blocks(one_block)
        return -(-columns // unit) * unit


class Mail:
    def __init__(self, layout, send, recv, slots):
        self.layout, self.send_sems, self.recv_sems, self.slots = layout, send, recv, slots
        self.group = lax.axis_index("dp")
        seat = lax.axis_index("seq")
        self.line = seat // layout.members
        self.member = seat % layout.members
        self.side = self.member // 2
        self.core = self.member % 2
        self.started = {}

    def at(self, group=None, line=None, side=None, core=None):
        group = self.group if group is None else group
        line = self.line if line is None else line
        side = self.side if side is None else side
        core = self.core if core is None else core
        return (group, line * self.layout.members + side * 2 + core)

    def copy(self, slot, source, target, device, shift=0):
        index = self.slots[slot] + shift
        return pltpu.make_async_remote_copy(
            src_ref=source,
            dst_ref=target,
            send_sem=self.send_sems.at[index],
            recv_sem=self.recv_sems.at[index],
            device_id=device,
            device_id_type=pl.DeviceIdType.MESH,
        )

    def send(self, slot, source, target, device, when=None):
        copy = self.copy(slot, source, target, device)
        self.started[slot] = (copy, when)
        guarded(when, copy.start)

    def wait(self, slot, target, shift=0):
        self.copy(slot, target, target, self.at(core=1 - self.core), shift).wait_recv()

    def settle(self, slot):
        copy, when = self.started.pop(slot)
        guarded(when, copy.wait_send)

    def finish(self):
        for slot in list(self.started):
            self.settle(slot)


class Desk:
    def __init__(self, mail, index, local):
        self.mail, self.index, self.local_sems = mail, index, local
        self.group, self.line, self.member = mail.group, mail.line, mail.member
        self.side, self.core, self.at = mail.side, mail.core, mail.at

    def send(self, slot, source, target, device, when=None):
        self.mail.send((self.index, slot), source, target, device, when)

    def wait(self, slot, target, shift=0):
        self.mail.wait((self.index, slot), target, shift)

    def settle(self, slot):
        self.mail.settle((self.index, slot))

    def local(self, number, source, target):
        return pltpu.make_async_copy(source, target, self.local_sems.at[number])


class Work:
    def __init__(self, steps, ins, outs, scratch, slots, local):
        self.steps, self.ins, self.outs, self.scratch = steps, ins, outs, scratch
        self.slots, self.local = slots, local


def guarded(when, action):
    if when is None:
        action()
    else:
        pl.when(when)(action)


def all_of(*conditions):
    kept = [condition for condition in conditions if condition is not None]
    return functools.reduce(jnp.logical_and, kept) if kept else None


def run_steps(works, turns):
    queue = []
    for index, (work, first) in enumerate(zip(works, turns)):
        next(work)
        queue.append((first[0], index, 0))
    while queue:
        turn, index, done = min(queue)
        queue.remove((turn, index, done))
        try:
            next(works[index])
        except StopIteration:
            continue
        done += 1
        listed = turns[index]
        queue.append((listed[done] if done < len(listed) else turn + 1, index, done))


def anywhere():
    return pl.BlockSpec(memory_space=pl.ANY)


def exchange(name, layout, works, starts, megabytes, common=()):
    slots = [(index, slot) for index, work in enumerate(works) for slot in work.slots]
    numbers = {slot: index for index, slot in enumerate(slots)}
    ins = [entry for work in works for entry in work.ins]
    outs = [entry for work in works for entry in work.outs]
    scratch = [entry for work in works for entry in work.scratch]

    def kernel(*refs):
        refs = list(refs)

        def take(count):
            taken = refs[:count]
            del refs[:count]
            return taken

        in_refs = [take(len(work.ins)) for work in works]
        out_refs = [take(len(work.outs)) for work in works]
        scratch_refs = [take(len(work.scratch)) for work in works]
        common_refs = take(len(common))
        locals_of = [take(1)[0] for work in works]
        send, recv = refs
        mail = Mail(layout, send, recv, numbers)
        run_steps(
            [
                work.steps(
                    Desk(mail, index, locals_of[index]),
                    in_refs[index],
                    out_refs[index],
                    scratch_refs[index],
                    common_refs,
                )
                for index, work in enumerate(works)
            ],
            starts,
        )
        mail.finish()

    results = pl.pallas_call(
        kernel,
        name=name,
        out_shape=[shape for shape, _ in outs],
        in_specs=[spec for _, spec in ins],
        out_specs=[spec for _, spec in outs],
        scratch_shapes=scratch
        + list(common)
        + [pltpu.SemaphoreType.DMA((work.local,)) for work in works]
        + [pltpu.SemaphoreType.DMA((len(slots),))] * 2,
        compiler_params=pltpu.CompilerParams(
            has_side_effects=True, vmem_limit_bytes=megabytes * mib
        ),
    )(*[array for array, _ in ins])
    results = list(results)
    grouped = []
    for work in works:
        grouped.append(results[: len(work.outs)])
        del results[: len(work.outs)]
    return grouped


def gather_work(layout, shard, one_block):
    lines, members, sides = layout.lines, layout.members, layout.sides
    width = shard.shape[1] // layout.blocks(one_block)
    spots = [("own", 0)]
    for t in range(1, lines):
        spots += [(f"below{t}", -t), (f"above{t}", t)]
    slots = [("mix", j) for j in range(1, members)]
    slots += [(way, t) for way in ("up", "down") for t in range(lines)]
    slots += [("cross", source) for source, _ in spots]
    slots += [("core", j) for j in range(1 if one_block else sides)]
    if not one_block:
        slots += [
            ("side", half, source, j)
            for half in (0, 1)
            for source, _ in spots
            for j in range(1, sides)
        ]

    def steps(desk, ins, outs, scratch, common):
        (shard,), (out,), (landing, slab, wide) = ins, outs, scratch
        group, line, member, side, core = desk.group, desk.line, desk.member, desk.side, desk.core
        has_up, has_down = line < lines - 1, line > 0

        def columns(side_of, core_of):
            block = core_of if one_block else core_of * sides + side_of
            return pl.ds(pl.multiple_of(block * width, 128), width)

        own = columns(side, core)

        def place(group_of, line_of, lanes=own):
            first = (group_of * lines + line_of) * layout.slab
            return out.at[pl.ds(pl.multiple_of(first, 16), layout.slab), lanes]

        def present(step):
            return None if step == 0 else line >= -step if step < 0 else line < lines - step

        for j in range(1, members):
            other = (member + j) % members
            desk.send(
                ("mix", j),
                shard.at[:, columns(other // 2, other % 2)],
                landing.at[member],
                desk.at(side=other // 2, core=other % 2),
            )
        mine = desk.local(0, shard.at[:, own], landing.at[member])
        mine.start()
        yield
        for j in range(1, members):
            desk.wait(("mix", j), landing.at[(member + members - j) % members])
        mine.wait()
        for m in range(members):
            rows = slice(m * layout.rows, (m + 1) * layout.rows)
            wide[rows, :] = landing[m, : layout.rows, :].astype(jnp.float32)
        slab[...] = wide[...].astype(slab.dtype)
        keep = desk.local(1, slab, place(group, line))
        keep.start()

        def pass_on(source, what, half, where, when):
            if half == 0:
                desk.send(("cross", source), what, where, desk.at(group=1 - group), when)
            if not one_block:
                for j in range(1, sides):
                    slot = ("side", half, source, j)
                    desk.send(slot, what, where, desk.at(side=(side + j) % sides), when)

        home = place(group, line)
        desk.send(("up", 0), slab, home, desk.at(line=line + 1), has_up)
        desk.send(("down", 0), slab, home, desk.at(line=line - 1), has_down)
        pass_on("own", slab, 0, home, None)
        yield
        for t in range(1, lines):
            for way, name, step, further, to in (
                ("up", "below", -t, has_up, line + 1),
                ("down", "above", t, has_down, line - 1),
            ):
                when, where = present(step), place(group, line + step)
                guarded(when, functools.partial(desk.wait, (way, t - 1), where))
                desk.send((way, t), where, where, desk.at(line=to), all_of(when, further))
                pass_on(f"{name}{t}", where, 0, where, when)
            if t == 1:
                where = place(1 - group, line)
                desk.wait(("cross", "own"), where)
                pass_on("own", where, 1, where, None)
            yield
        for t in range(1, lines):
            for name, step in ((f"below{t}", -t), (f"above{t}", t)):
                when, where = present(step), place(1 - group, line + step)
                guarded(when, functools.partial(desk.wait, ("cross", name), where))
                pass_on(name, where, 1, where, when)
            yield
        keep.wait()
        partner = desk.at(core=1 - core)
        desk.send(("core", 0), out.at[:, own], out.at[:, own], partner)
        if not one_block:
            yield
            for j in range(1, sides):
                theirs = columns((side + sides - j) % sides, core)
                for half, group_of in ((0, group), (1, 1 - group)):
                    for source, step in spots:
                        where = place(group_of, line + step, theirs)
                        slot = ("side", half, source, j)
                        guarded(present(step), functools.partial(desk.wait, slot, where))
                desk.send(("core", j), out.at[:, theirs], out.at[:, theirs], partner)
        yield
        desk.wait(("core", 0), out.at[:, columns(side, 1 - core)])
        if not one_block:
            for j in range(1, sides):
                theirs = columns((side + sides - j) % sides, 1 - core)
                desk.wait(("core", j), out.at[:, theirs])

    low = jnp.bfloat16
    return Work(
        steps,
        [(shard, anywhere())],
        [(jax.ShapeDtypeStruct((layout.model_width, shard.shape[1]), low), anywhere())],
        [
            pltpu.VMEM((members, layout.padded, width), low),
            pltpu.VMEM((layout.slab, width), low),
            pltpu.VMEM((layout.slab, width), jnp.float32),
        ],
        slots,
        2,
    )


def add_rows(target, first, target_columns, source, source_columns, count, source_first=0):
    step = math.gcd(count, 48)

    def one(index, carry):
        rows = pl.ds(pl.multiple_of(first + index * step, 16), step)
        theirs = pl.ds(pl.multiple_of(source_first + index * step, 16), step)
        total = target[rows, target_columns].astype(jnp.float32)
        total += source[theirs, source_columns].astype(jnp.float32)
        target[rows, target_columns] = total.astype(target.dtype)
        return carry

    lax.fori_loop(0, count // step, one, 0)


def reduce_work(layout, lefts, right, one_block, switch=0, split=3):
    lines, members, sides = layout.lines, layout.members, layout.sides
    tok, columns = right.shape
    blocks = layout.blocks(one_block)
    width, half = columns // blocks, columns // 2
    near_rows, slab_rows, low = layout.near, layout.slab, jnp.bfloat16
    count, depth = min(split, width // 128), min(4, lines)
    parts = []
    for index in range(count):
        first = width // 128 * index // count * 128
        parts.append((first, width // 128 * (index + 1) // count * 128 - first))
    order = []
    for t in range(lines):
        goal = lines - 1 - t // 2 if t % 2 == 0 else t // 2
        order.append(goal)
    slots = [("left", k) for k in range(len(lefts))] + ["right"]
    slots += [("cross", part, t) for part in parts for t in range(lines)]
    slots += [
        (way, part, t) for way in ("up", "down") for part in parts for t in range(1, lines)
    ]
    slots += [("mix", j) for j in range(1, members)]
    if not one_block:
        slots += [
            ("side", part, tag, t, j)
            for part in parts
            for tag in (0, 1)
            for t in range(lines)
            for j in range(1, sides)
        ]

    def steps(desk, ins, outs, scratch, common):
        left_in, right_in = ins[: len(lefts)], ins[len(lefts)]
        out, left_land, right_land = outs[0], outs[1 : 1 + len(lefts)], outs[1 + len(lefts)]
        total, cross, up, down, piece, landing, wide = scratch[:7]
        from_side = None if one_block else scratch[7]
        left_all, right_all = common
        group, line, member, side, core = desk.group, desk.line, desk.member, desk.side, desk.core
        partner = desk.at(core=1 - core)
        own = pl.ds(0 if one_block else pl.multiple_of(side * width, 128), width)
        stay = pl.ds(pl.multiple_of(core * half, 128), half)
        away = pl.ds(pl.multiple_of((1 - core) * half, 128), half)

        def first_of(tag, goal):
            return pl.multiple_of((group if tag else 1 - group) * near_rows + goal * slab_rows, 16)

        for k, left in enumerate(left_in):
            desk.send(("left", k), left, left_land[k], partner)
        desk.send("right", right_in.at[:, away], right_land, partner)
        yield
        loads = []

        def load(source, target):
            copy = desk.local(len(loads), source, target)
            copy.start()
            loads.append(copy)

        for k, left in enumerate(left_in):
            load(left, left_all.at[k, 0])
        load(right_in.at[:, stay], right_all.at[0, :, pl.ds(0, half)])
        for k in range(len(left_in)):
            desk.wait(("left", k), left_land[k])
            load(left_land[k], left_all.at[k, 1])
        desk.wait("right", right_land)
        load(right_land, right_all.at[1, :, pl.ds(0, half)])
        for copy in loads:
            copy.wait()

        def multiply(tag):
            rows = pl.ds(first_of(tag, 0), near_rows)

            def piece_of(first, lanes, which):
                theirs = pl.ds(first, lanes)
                product = dot_nn(left_all[which, 0, rows, :], right_all[0, :, theirs])
                product += dot_nn(left_all[which, 1, rows, :], right_all[1, :, theirs])
                total[rows, theirs] = product.astype(low)

            lanes = 256 if len(lefts) == 1 else math.gcd(switch, 384)

            def one(index, carry):
                first = pl.multiple_of(index * lanes, 128)
                which = 0
                if len(lefts) > 1:
                    which = jnp.where(core * half + index * lanes >= switch, 1, 0)
                piece_of(first, lanes, which)
                return carry

            lax.fori_loop(0, half // lanes, one, 0)
            if half % lanes:
                piece_of(half // lanes * lanes, half % lanes, 0)

        own_first = 0 if one_block else side * width
        pieces = [
            (part, tag, goal)
            for part in parts
            for tag in ((0,) if one_block else (0, 1))
            for goal in order
        ]

        def lanes_of(part, first):
            return pl.ds(pl.multiple_of(first + part[0], 128), part[1])

        def post(number):
            if number >= len(pieces):
                return
            part, tag, goal = pieces[number]
            if one_block:
                if number >= depth:
                    before = pieces[number - depth]
                    desk.settle(("cross", before[0], before[2]))
                send_across(part, goal)
                return
            rows = pl.ds(first_of(tag, goal), slab_rows)
            for j in range(1, sides):
                if number >= depth:
                    desk.settle(("side", *pieces[number - depth], j))
                other = (side + j) % sides
                desk.send(
                    ("side", part, tag, goal, j),
                    total.at[rows, lanes_of(part, other * width)],
                    from_side.at[j - 1, rows, lanes_of(part, 0)],
                    desk.at(side=other),
                )

        def send_across(part, goal):
            rows = pl.ds(first_of(0, goal), slab_rows)
            desk.send(
                ("cross", part, goal),
                total.at[rows, lanes_of(part, own_first)],
                cross.at[goal, :, lanes_of(part, 0)],
                desk.at(group=1 - group),
            )

        def take_side(part, tag, goal):
            first = first_of(tag, goal)
            rows, lanes = pl.ds(first, slab_rows), lanes_of(part, 0)
            for j in range(1, sides):
                desk.wait(("side", part, tag, goal, j), from_side.at[j - 1, rows, lanes])
            post(pieces.index((part, tag, goal)) + depth)
            for j in range(1, sides):
                add_rows(
                    total, first, lanes_of(part, own_first), from_side.at[j - 1], lanes,
                    slab_rows, first,
                )

        ends = lines - 1 - line

        def part_steps(part):
            lanes, mine = lanes_of(part, 0), lanes_of(part, own_first)
            if not one_block:
                for goal in order:
                    take_side(part, 0, goal)
                    send_across(part, goal)
                    yield
            for goal in order:
                if not one_block:
                    take_side(part, 1, goal)
                desk.wait(("cross", part, goal), cross.at[goal, :, lanes])
                if one_block:
                    post(pieces.index((part, 0, goal)) + depth)
                add_rows(total, first_of(1, goal), mine, cross.at[goal], lanes, slab_rows)
                yield
            for t in range(1, lines):
                for way, buffer, going, fed, goal, to in (
                    ("up", up, line < t, line > 0, lines - t + line, line + 1),
                    ("down", down, ends < t, ends > 0, t - lines + line, line - 1),
                ):
                    first = first_of(1, goal)

                    @pl.when(all_of(going, fed))
                    def _():
                        if t > 1:
                            desk.wait((way, part, t - 1), buffer.at[t - 2, :, lanes])
                            add_rows(total, first, mine, buffer.at[t - 2], lanes, slab_rows)

                    desk.send(
                        (way, part, t),
                        total.at[pl.ds(first, slab_rows), mine],
                        buffer.at[t - 1, :, lanes],
                        desk.at(line=to),
                        going,
                    )
                yield

        multiply(0)
        for number in range(depth):
            post(number)
        yield
        multiply(1)
        yield
        running = [part_steps(part) for part in parts]
        turn, lag = 0, len(pieces) // len(parts)
        while running:
            for index, steps_of in enumerate(running):
                if steps_of is not None and turn >= lag * index:
                    try:
                        next(steps_of)
                    except StopIteration:
                        running[index] = None
            if not any(running):
                break
            turn += 1
            yield
        first = first_of(1, line)
        wide[...] = total[pl.ds(first, slab_rows), own].astype(jnp.float32)
        for way, buffer, fed in (("up", up, line > 0), ("down", down, ends > 0)):

            @pl.when(fed)
            def _():
                for part in parts:
                    where = buffer.at[lines - 2, :, lanes_of(part, 0)]
                    desk.wait((way, part, lines - 1), where)
                wide[...] += buffer[lines - 2].astype(jnp.float32)

        for m in range(members):
            rows = slice(m * layout.rows, (m + 1) * layout.rows)
            piece[m] = jnp.zeros(piece.shape[1:], piece.dtype)
            piece[m, : layout.rows, :] = wide[rows, :].astype(piece.dtype)
        seat = core * sides + side
        for j in range(1, members):
            other = (member + j) % members
            desk.send(
                ("mix", j),
                piece.at[other],
                landing.at[seat],
                desk.at(side=other // 2, core=other % 2),
            )
        landing[seat] = piece[member]
        yield
        for j in range(1, members):
            other = (member + members - j) % members
            desk.wait(("mix", j), landing.at[other % 2 * sides + other // 2])
        if one_block:
            for c in range(2):
                block = landing[c * sides].astype(jnp.float32)
                for s in range(1, sides):
                    block += landing[c * sides + s].astype(jnp.float32)
                out[:, c * width : (c + 1) * width] = block
        else:
            for b in range(blocks):
                out[:, b * width : (b + 1) * width] = landing[b].astype(jnp.float32)

    scratch = [
        pltpu.VMEM((layout.model_width, half), low),
        pltpu.VMEM((lines, slab_rows, width), low),
        pltpu.VMEM((lines - 1, slab_rows, width), low),
        pltpu.VMEM((lines - 1, slab_rows, width), low),
        pltpu.VMEM((members, layout.padded, width), low),
        pltpu.VMEM((members, layout.padded, width), low),
        pltpu.VMEM((slab_rows, width), jnp.float32),
    ]
    if not one_block:
        scratch.append(pltpu.VMEM((sides - 1, layout.model_width, width), low))
    ins = [(array, anywhere()) for array in [*lefts, right]]
    return Work(
        steps,
        ins,
        [(jax.ShapeDtypeStruct((layout.padded, columns), jnp.float32), in_vmem())]
        + [(jax.ShapeDtypeStruct(left.shape, low), anywhere()) for left in lefts]
        + [(jax.ShapeDtypeStruct((tok, half), low), anywhere())],
        scratch,
        slots,
        2 * len(lefts) + 2,
    )


class Reach:
    def __init__(self, tok, left, right):
        self.tok, self.left, self.right = tok, left, right
        self.window = left + tok + right
        self.deltas = [d for d in range(-8, 9) if d != 0 and self.rows(d) > 0]

    def first(self, delta):
        return max(0, self.tok * delta - self.left)

    def rows(self, delta):
        last = min(self.tok, self.tok * delta - self.left + self.window)
        return last - self.first(delta)

    def spot(self, delta):
        return self.first(delta) - self.tok * delta + self.left


def parts_of(count, step=80):
    return [(first, min(step, count - first)) for first in range(0, count, step)]


def window_work(layout, reach, key_value):
    tok, width = key_value.shape
    left, lines, places = reach.left, layout.lines, layout.lines * layout.members
    routed = layout.sides == 2
    pieces, depth = parts_of(tok), 2
    near_below, far_below = reach.spot(2), reach.spot(3)
    tail = (reach.first(3), max(reach.rows(3), 0))
    head = max(reach.rows(-2), 0)
    if routed:
        slots = ["pair", "tail", "share", "wide", "thin", "last"]
        slots += [(name, k) for name in ("right", "left", "climb", "drop") for k in range(len(pieces))]
        slots += [("fall", k) for k in range(len(parts_of(head)))]
    else:
        slots = [("reach", delta) for delta in reach.deltas]

    def direct(desk, own, window):
        seat = desk.line * layout.members + desk.member
        for delta in reach.deltas:
            count = reach.rows(delta)
            desk.send(
                ("reach", delta),
                own.at[pl.ds(reach.first(delta), count)],
                window.at[pl.ds(reach.spot(delta), count)],
                (desk.group, seat + delta),
                (seat + delta >= 0) & (seat + delta < places),
            )
        yield
        for delta in reach.deltas:
            where = window.at[pl.ds(reach.spot(delta), reach.rows(delta))]
            when = (seat - delta >= 0) & (seat - delta < places)
            guarded(when, functools.partial(desk.wait, ("reach", delta), where))

    def by_way(desk, own, window, transit):
        line, core = desk.line, desk.core
        first_side, last_side = desk.side == 0, desk.side == 1
        low_core, high_core = core == 0, core == 1
        has_up, has_down = line < lines - 1, line > 0
        has_before = last_side | has_down
        partner = desk.at(core=1 - core)

        def part(ref, first, count):
            return ref.at[pl.ds(first, count)]

        def post(k):
            if k >= len(pieces):
                return
            if k >= depth:
                desk.settle(("right", k - depth))
                desk.settle(("left", k - depth))
            first, count = pieces[k]
            desk.send(
                ("right", k), part(own, first, count), part(window, near_below + first, count),
                desk.at(side=1), first_side,
            )
            desk.send(
                ("left", k), part(own, first, count), part(transit, first, count),
                desk.at(side=0), last_side,
            )

        for k in range(depth):
            post(k)
        desk.send(
            "tail", part(own, *tail), part(window, far_below, tail[1]),
            desk.at(line=line + 1, core=0), high_core & has_up,
        )
        mirrored = pl.multiple_of(left + (2 * core - 1) * tok, 16)
        desk.send("pair", own, part(window, mirrored, tok), partner)
        yield
        for k, (first, count) in enumerate(pieces):
            ahead = part(transit, first, count)
            guarded(first_side, functools.partial(desk.wait, ("left", k), ahead))
            desk.send(
                ("climb", k), ahead, part(window, near_below + first, count),
                desk.at(line=line + 1), first_side & has_up,
            )
            behind = part(window, near_below + first, count)
            guarded(last_side, functools.partial(desk.wait, ("right", k), behind))
            post(k + depth)
            desk.send(
                ("drop", k), behind, part(window, left + tok + first, count),
                desk.at(line=line - 1, core=1), last_side & has_down & low_core,
            )
            if first < head:
                count = min(count, head - first)
                desk.send(
                    ("fall", k), part(window, near_below + first, count),
                    part(window, left + 2 * tok + first, count),
                    desk.at(line=line - 1), last_side & has_down & high_core,
                )
            yield
        stay = desk.local(1, part(transit, 0, head), part(window, left + 2 * tok, head))
        guarded(first_side, stay.start)
        desk.send(
            "share", transit, part(window, left + tok, tok), partner, first_side & low_core
        )

        def share_before(when):
            desk.send(
                "wide", part(window, near_below, tok), part(window, left - tok, tok), partner,
                when & high_core,
            )
            desk.send(
                "thin", part(window, near_below + tail[0], tail[1]),
                part(window, far_below, tail[1]), partner, when & low_core,
            )

        def climbed():
            for k, (first, count) in enumerate(pieces):
                desk.wait(("climb", k), part(window, near_below + first, count))

        guarded(first_side & has_down, climbed)
        share_before(has_before)
        yield

        def dropped():
            for k, (first, count) in enumerate(pieces):
                desk.wait(("drop", k), part(window, left + tok + first, count))
            for k, (first, count) in enumerate(parts_of(head)):
                desk.wait(("fall", k), part(window, left + 2 * tok + first, count))

        guarded(last_side & has_up & high_core, dropped)
        desk.send(
            "last", part(window, left + tok, head), part(window, left + 2 * tok, head), partner,
            last_side & has_up & high_core,
        )
        yield
        desk.wait("pair", part(window, pl.multiple_of(left + (1 - 2 * core) * tok, 16), tok))
        for when, slot, first, count in (
            (low_core & has_down, "tail", far_below, tail[1]),
            (first_side & high_core, "share", left + tok, tok),
            (has_before & low_core, "wide", left - tok, tok),
            (has_before & high_core, "thin", far_below, tail[1]),
            (last_side & has_up & low_core, "last", left + 2 * tok, head),
        ):
            guarded(when, functools.partial(desk.wait, slot, part(window, first, count)))
        guarded(first_side, stay.wait)

    def steps(desk, ins, outs, scratch, common):
        (own,), (window,) = ins, outs
        keep = desk.local(0, own, window.at[pl.ds(left, tok)])
        keep.start()
        yield from by_way(desk, own, window, *scratch) if routed else direct(desk, own, window)
        keep.wait()

    outs = [(jax.ShapeDtypeStruct((reach.window, width), key_value.dtype), anywhere())]
    scratch = [pltpu.VMEM((tok, width), key_value.dtype)] if routed else []
    return Work(steps, [(key_value, in_vmem())], outs, scratch, slots, 2)


def owned_work(layout, reach, grad_window):
    width = grad_window.shape[1]
    tok, left, lines = reach.tok, reach.left, layout.lines
    places = layout.lines * layout.members
    routed = layout.sides == 2
    pieces, depth = parts_of(tok), 2
    near_below, far_below = reach.spot(2), reach.spot(3)
    tail = (reach.first(3), max(reach.rows(3), 0))
    head = max(reach.rows(-2), 0)
    every = pl.ds(0, width)
    low = grad_window.dtype
    if routed:
        slots = ["pair", "tail", "share", "wide", "thin", "last", "rise"]
        slots += [(name, k) for name in ("right", "left", "fall", "lift") for k in range(len(pieces))]
    else:
        slots = [("reach", delta) for delta in reach.deltas]

    def direct(desk, grad, out, landing):
        seat = desk.line * layout.members + desk.member
        for delta in reach.deltas:
            count = reach.rows(delta)
            desk.send(
                ("reach", delta),
                grad.at[pl.ds(reach.spot(delta), count)],
                landing[delta],
                (desk.group, seat - delta),
                (seat - delta >= 0) & (seat - delta < places),
            )
        load = desk.local(0, grad.at[pl.ds(left, tok)], out)
        load.start()
        load.wait()
        yield
        for delta in reach.deltas:

            @pl.when((seat + delta >= 0) & (seat + delta < places))
            def _():
                desk.wait(("reach", delta), landing[delta])
                first, count = reach.first(delta), reach.rows(delta)
                add_rows(out, first, every, landing[delta], every, count)

    def by_way(desk, grad, out, scratch):
        near, middle, l_wide, l_far, l_climb, l_y, l_pair, l_tail = scratch
        line, core = desk.line, desk.core
        first_side, last_side = desk.side == 0, desk.side == 1
        low_core, high_core = core == 0, core == 1
        has_up, has_down = line < lines - 1, line > 0
        has_before = last_side | has_down
        gate = last_side & has_up & high_core
        partner = desk.at(core=1 - core)

        def part(ref, first, count):
            return ref.at[pl.ds(first, count)]

        def receive(when, slot, target, first, buffer, at, count):
            @pl.when(when)
            def _():
                desk.wait(slot, part(buffer, at, count))
                add_rows(target, first, every, buffer, every, count, at)

        desk.send(
            "last", part(grad, left + 2 * tok, head), part(l_climb, 0, head), partner,
            last_side & has_up & low_core,
        )
        desk.send(
            "wide", part(grad, left - tok, tok), l_wide, partner, has_before & low_core
        )
        desk.send(
            "thin", part(grad, far_below, tail[1]), part(l_wide, 0, tail[1]), partner,
            has_before & high_core,
        )
        desk.send(
            "share", part(grad, left + tok, tok), l_far, partner, first_side & high_core
        )
        desk.send(
            "tail", part(grad, far_below, tail[1]), l_tail,
            desk.at(line=line - 1, core=1), low_core & has_down,
        )
        desk.send("rise", part(grad, left + 2 * tok, head), part(l_far, 0, head),
            desk.at(line=line + 1), gate,
        )
        loads = [
            (desk.local(0, part(grad, near_below, tok), near), None),
            (desk.local(1, part(grad, left + tok, tok), middle), last_side),
            (desk.local(2, part(grad, left + 2 * tok, head), part(middle, 0, head)), first_side),
            (desk.local(3, part(grad, left, tok), out), None),
        ]
        for load, when in loads:
            guarded(when, load.start)

        @pl.when(first_side)
        def _():
            middle[head:, :] = jnp.zeros((tok - head, width), low)

        yield
        for load, when in loads:
            guarded(when, load.wait)
        receive(gate, "last", middle, 0, l_climb, 0, head)
        receive(has_before & high_core, "wide", near, 0, l_wide, 0, tok)
        receive(has_before & low_core, "thin", near, tail[0], l_wide, 0, tail[1])

        def post(k):
            if k >= len(pieces):
                return
            if k >= depth:
                desk.settle(("fall", k - depth))
                desk.settle(("lift", k - depth))
            first, count = pieces[k]
            desk.send(
                ("fall", k), part(middle, first, count), part(l_far, first, count),
                desk.at(line=line + 1, core=0), gate,
            )
            desk.send(
                ("lift", k), part(near, first, count), part(l_climb, first, count),
                desk.at(line=line - 1), first_side & has_down,
            )

        for k in range(depth):
            post(k)
        mirrored = pl.multiple_of(left + (1 - 2 * core) * tok, 16)
        desk.send("pair", part(grad, mirrored, tok), l_pair, partner)
        yield
        receive(first_side & low_core, "share", middle, 0, l_far, 0, tok)
        receive(last_side & has_down & high_core, "rise", near, 0, l_far, 0, head)
        for k, (first, count) in enumerate(pieces):
            receive(first_side & has_up, ("lift", k), middle, first, l_climb, first, count)
            desk.send(
                ("left", k), part(middle, first, count), part(l_y, first, count),
                desk.at(side=1), first_side,
            )
            receive(
                last_side & has_down & low_core, ("fall", k), near, first, l_far, first, count
            )
            desk.send(
                ("right", k), part(near, first, count), part(l_y, first, count),
                desk.at(side=0), last_side,
            )
            post(k + depth)
            yield
        receive(has_up & high_core, "tail", out, tail[0], l_tail, 0, tail[1])
        desk.wait("pair", l_pair)
        for k, (first, count) in enumerate(pieces):
            where = part(l_y, first, count)
            guarded(first_side, functools.partial(desk.wait, ("right", k), where))
            guarded(last_side, functools.partial(desk.wait, ("left", k), where))

            def one(index, carry):
                rows = pl.ds(pl.multiple_of(first + index * 16, 16), 16)
                total = out[rows, :].astype(jnp.float32) + l_pair[rows, :].astype(jnp.float32)
                out[rows, :] = (total + l_y[rows, :].astype(jnp.float32)).astype(out.dtype)
                return carry

            lax.fori_loop(0, count // 16, one, 0)
            yield

    def steps(desk, ins, outs, scratch, common):
        if routed:
            yield from by_way(desk, ins[0], outs[0], scratch)
        else:
            yield from direct(desk, ins[0], outs[0], dict(zip(reach.deltas, scratch)))

    if routed:
        counts = [tok] * 7 + [tail[1]]
    else:
        counts = [reach.rows(delta) for delta in reach.deltas]
    return Work(
        steps,
        [(grad_window, anywhere())],
        [(jax.ShapeDtypeStruct((tok, width), low), in_vmem())],
        [pltpu.VMEM((count, width), low) for count in counts],
        slots,
        4,
    )


def sum_work(layout, block):
    sizes = (2, layout.sides, layout.model_width // layout.near, layout.lines)
    slots = [(stage, j) for stage, size in enumerate(sizes) for j in range(1, size)]

    def steps(desk, ins, outs, scratch, common):
        (block,), (out,) = ins, outs
        yield
        out[...] = block[...]
        for stage, (landing, size) in enumerate(zip(scratch, sizes)):
            mine = (desk.core, desk.side, desk.group, desk.line)[stage]
            landing[mine] = out[...]
            for j in range(1, size):
                other = (mine + j) % size
                to = desk.at(**{("core", "side", "group", "line")[stage]: other})
                desk.send((stage, j), landing.at[mine], landing.at[mine], to)
            yield
            for j in range(1, size):
                desk.wait((stage, j), landing.at[(mine + size - j) % size])
            total = landing[0]
            for j in range(1, size):
                total = total + landing[j]
            out[...] = total

    return Work(
        steps,
        [(block, in_vmem())],
        [(jax.ShapeDtypeStruct(block.shape, block.dtype), in_vmem())],
        [pltpu.VMEM((size, *block.shape), block.dtype) for size in sizes],
        slots,
        1,
    )


def column_sum(source):
    return jnp.sum(source.astype(jnp.float32), axis=0)


def norm_forward(source, gain_row, shift_row):
    row_mean = jnp.mean(source, axis=-1, keepdims=True)
    centred = source - row_mean
    variance = jnp.mean(centred * centred, axis=-1, keepdims=True)
    inv_scale = lax.rsqrt(variance + eps_norm)
    unit_rows = centred * inv_scale
    return (unit_rows * gain_row + shift_row, unit_rows, inv_scale)


def norm_backward(gradient, unit_rows, inv_scale, gain_row):
    scaled = gradient * gain_row
    grad_in = inv_scale * (
        scaled
        - jnp.mean(scaled, axis=-1, keepdims=True)
        - unit_rows * jnp.mean(scaled * unit_rows, axis=-1, keepdims=True)
    )
    return (grad_in, jnp.sum(gradient * unit_rows, axis=0), jnp.sum(gradient, axis=0))


def gelu_tanh(source):
    return jax.nn.gelu(source, approximate=True)


def adam_step(weight_now, gradient, first_old, second_old):
    first_new = beta_first * first_old + (1.0 - beta_first) * gradient
    second_new = beta_second * second_old + (1.0 - beta_second) * gradient * gradient
    first_hat = first_new / (1.0 - beta_first**STEP)
    second_hat = second_new / (1.0 - beta_second**STEP)
    update = -learn_rate * (
        first_hat / (jnp.sqrt(second_hat) + eps_adam)
        + weight_decay * weight_now.astype(jnp.float32)
    )
    return (first_new, second_new, update)


def round_up(count, unit):
    return -(-count // unit) * unit


def per_device(
    inputs, image_ids, token_mask, cotangent,
    w_qkv, w_out, w_up, w_down, norm_gains, bias_rows, up_bias,
    first_qkv, first_out, first_up, first_down, first_gains, first_bias, first_upbias,
    second_qkv, second_out, second_up, second_down, second_gains, second_bias, second_upbias,
):
    tok, width = inputs.shape
    layers, _, hidden_width = w_up.shape
    places = lax.axis_size("seq")
    place = lax.axis_index("seq")
    layout = Layout(lax.axis_size("dp"), places, width)
    group_tok = tok * places
    spare_count = group_tok - group_tok // IMG * IMG
    left = round_up(IMG - 1 + spare_count, 16)
    right = round_up(IMG - 1, 16)
    tile = tok // 2

    reach = Reach(tok, left, right)

    half = hidden_width // 2
    half_pad = round_up(half + 8 * layers, 128)
    wide_columns = 2 * half_pad

    def spread(array):
        pad = [(0, 0)] * (array.ndim - 1) + [(0, half_pad - half)]
        return jnp.concatenate([jnp.pad(array[..., :half], pad), jnp.pad(array[..., half:], pad)], -1)

    def unspread(array):
        return jnp.concatenate(
            [array[..., :half], array[..., half_pad : half_pad + half]], axis=-1
        )

    def filled(array, rows, columns):
        return jnp.pad(array, ((0, rows - array.shape[0]), (0, columns - array.shape[1])))

    attn_columns = layout.columns(4 * width, False)
    up_columns = layout.columns(wide_columns, True)
    down_columns = layout.columns(wide_columns, False)
    rows_of = jnp.concatenate([norm_gains.reshape(-1, layout.rows), bias_rows.reshape(-1, layout.rows)])
    row_count = rows_of.shape[0]
    shards = []
    for layer in range(layers):
        attn_shard = jnp.concatenate([w_qkv[layer], w_out[layer]], axis=1)
        up_shard = spread(w_up[layer])
        if layer == 0:
            up_shard = up_shard.at[:, half : half + row_count].set(rows_of.T)
        down_shard = spread(w_down[layer].T)
        shards += [
            filled(attn_shard, layout.padded, attn_columns),
            filled(up_shard, layout.padded, up_columns),
            filled(down_shard, layout.padded, down_columns if layer else up_columns),
        ]
    word = image_ids * 2 + (token_mask > 0).astype(jnp.int32)
    word = jnp.broadcast_to(word[:, None], (tok, 128))
    def gather(layer, which):
        return gather_work(layout, shards[3 * layer + which], which == 1 or (which == 2 and layer == 0))

    gathered = [[None] * 3 for _ in range(layers)]
    begun = [(layer, which) for layer in range(layers) for which in range(3)]
    *results, (window_word, *_) = exchange(
        "gather_parameters",
        layout,
        [gather(*spot) for spot in begun] + [window_work(layout, reach, word)],
        [[index] for index in range(len(begun))] + [[1]],
        40,
    )
    for (layer, which), (matrix,) in zip(begun, results):
        gathered[layer][which] = matrix
    window_word = window_word[:, 0]
    all_rows = gathered[0][1][:, half : half + row_count].T.astype(jnp.float32)
    gains = all_rows[: 2 * layers].reshape(layers, 2, width)
    shifts = all_rows[2 * layers :].reshape(layers, 6, width)
    up_shift = spread(up_bias.astype(jnp.float32))

    plan, own_code, span_code = attention_plan(
        tile, left, right, image_ids, token_mask, window_word // 2, window_word % 2, place, places
    )

    residual = inputs.astype(jnp.float32)
    kept_layers = []
    for layer in range(layers):
        attn_weight, up_weight, down_weight = gathered[layer]
        down_weight = down_weight[:, :wide_columns]
        normed, unit_one, inv_one = norm_forward(residual, gains[layer, 0], shifts[layer, 0])
        normed_low = normed.astype(jnp.bfloat16)
        projected = dot_nn(normed_low, attn_weight[:, : 3 * width])
        queries = (projected[:, :width] + shifts[layer, 2]).astype(jnp.bfloat16)
        value_shift = jnp.concatenate([jnp.zeros_like(shifts[layer, 3]), shifts[layer, 3]])
        key_value = (projected[:, width:] + value_shift).astype(jnp.bfloat16)
        ((window, *_),) = exchange(
            "fetch_window", layout, [window_work(layout, reach, key_value)], [[0]], 20
        )
        attended, lse = attention_forward(tile, left, plan, queries, window, own_code, span_code)
        middle = (
            residual
            + dot_nn(attended, attn_weight[:, 3 * width : 4 * width])
            + shifts[layer, 4]
        )
        hidden, unit_two, inv_two = norm_forward(middle, gains[layer, 1], shifts[layer, 1])
        hidden_low = hidden.astype(jnp.bfloat16)
        pre_act = dot_nn(hidden_low, up_weight[:, :wide_columns]) + up_shift[layer]
        active = gelu_tanh(pre_act).astype(jnp.bfloat16)
        residual = middle + dot_nt(active, down_weight) + shifts[layer, 5]
        active = filled(active, tok, down_columns)
        kept_layers.append(
            (window, unit_one, inv_one, normed_low, queries, lse, attended,
             unit_two, inv_two, hidden_low, pre_act, active)
        )

    def packed(rows):
        flat = jnp.concatenate([row.reshape(-1) for row in rows])
        return jnp.pad(flat, (0, -flat.size % 1024)).reshape(-1, 128)

    grad_res = cotangent.astype(jnp.float32)
    owned = [[None] * 3 for _ in range(layers)]
    row_grads = [None] * layers
    upbias_grads = [None] * layers
    for layer in reversed(range(layers)):
        (window, unit_one, inv_one, normed_low, queries, lse, attended,
         unit_two, inv_two, hidden_low, pre_act, active) = kept_layers[layer]
        attn_weight, up_weight, down_weight = gathered[layer]
        down_weight = down_weight[:, :wide_columns]
        grad_branch = grad_res.astype(jnp.bfloat16)
        grad_active = dot_nn(grad_branch, down_weight)
        _, gelu_pull = jax.vjp(gelu_tanh, pre_act)
        grad_pre = gelu_pull(grad_active)[0].astype(jnp.bfloat16)
        upbias_grads[layer] = unspread(column_sum(grad_pre))
        grad_hidden = dot_nt(grad_pre, up_weight[:, :wide_columns])
        back_two, gain_two, shift_two = norm_backward(
            grad_hidden, unit_two, inv_two, gains[layer, 1]
        )
        grad_mid = grad_res + back_two
        grad_attn = grad_mid.astype(jnp.bfloat16)
        grad_attended = dot_nt(grad_attn, attn_weight[:, 3 * width : 4 * width]).astype(
            jnp.bfloat16
        )
        grad_query, grad_window = attention_backward(
            tile, left, plan, queries, window, grad_attended, lse, own_code, span_code
        )
        works = [owned_work(layout, reach, grad_window)]
        if layer == 0:
            works.append(sum_work(layout, packed([*upbias_grads, *row_grads[1:]])))
        (grad_key_value,), *small_sum = exchange(
            "return_window", layout, works, [[0], [2, 4, 6, 7, 8]][: len(works)], 40
        )
        grad_proj = jnp.concatenate([grad_query, grad_key_value], axis=1)
        grad_normed = dot_nt(grad_proj, attn_weight[:, : 3 * width])
        back_one, gain_one, shift_one = norm_backward(
            grad_normed, unit_one, inv_one, gains[layer, 0]
        )
        grad_res = grad_mid + back_one
        row_grads[layer] = jnp.stack(
            [
                gain_one,
                gain_two,
                shift_one,
                shift_two,
                column_sum(grad_query),
                column_sum(grad_key_value[:, width:]),
                column_sum(grad_attn),
                column_sum(grad_branch),
            ]
        )
        grad_side = filled(jnp.concatenate([grad_proj, grad_attn], axis=1), tok, attn_columns)
        works = [
            reduce_work(layout, [normed_low.T, attended.T], grad_side, False, 3 * width),
            reduce_work(layout, [hidden_low.T], grad_pre, True),
            reduce_work(layout, [grad_branch.T], active, False),
        ]
        turns = [[0], [1], [2]]
        if layer == 0:
            works.append(sum_work(layout, packed(row_grads[:1])))
            turns.append([2, 4, 6, 8, 10])
        left_operands = pltpu.VMEM((2, 2, width, tok), jnp.bfloat16)
        right_operands = pltpu.VMEM((2, tok, max(attn_columns, down_columns) // 2), jnp.bfloat16)
        results = exchange(
            "reduce_gradients", layout, works, turns, 63, [left_operands, right_operands]
        )
        owned[layer], row_sum = [result[0] for result in results[:3]], results[3:]

    flat = small_sum[0][0].reshape(-1)
    upbias_grads = flat[: layers * hidden_width].reshape(layers, hidden_width)
    later = flat[layers * hidden_width :][: (layers - 1) * 8 * width].reshape(-1, 8, width)
    row_sums = jnp.concatenate([row_sum[0][0].reshape(-1)[: 8 * width].reshape(1, 8, width), later])
    seat = lax.axis_index("dp") * places + place
    row_sums = lax.dynamic_slice_in_dim(row_sums, seat * layout.rows, layout.rows, axis=2)

    def stacked(part):
        return jnp.stack([part(*owned[layer]) for layer in range(layers)])

    rows = layout.rows

    grads = (
        stacked(lambda attn, up, down: attn[:rows, : 3 * width]),
        stacked(lambda attn, up, down: attn[:rows, 3 * width : 4 * width]),
        stacked(lambda attn, up, down: unspread(up[:rows])),
        stacked(lambda attn, up, down: unspread(down[:rows]).T),
        row_sums[:, :2],
        row_sums[:, 2:],
        upbias_grads,
    )
    params = (w_qkv, w_out, w_up, w_down, norm_gains, bias_rows, up_bias)
    firsts = (first_qkv, first_out, first_up, first_down, first_gains, first_bias, first_upbias)
    seconds = (
        second_qkv, second_out, second_up, second_down, second_gains, second_bias, second_upbias,
    )
    results = [adam_step(*packed) for packed in zip(params, grads, firsts, seconds)]
    return (
        (residual, grad_res)
        + grads
        + tuple(result[0] for result in results)
        + tuple(result[1] for result in results)
        + tuple(result[2] for result in results)
    )


def solution(mesh):
    in_specs = (
        P(("dp", "seq"), None),
        P(("dp", "seq")),
        P(("dp", "seq")),
        P(("dp", "seq"), None),
        P(None, ("dp", "seq"), None),
        P(None, ("dp", "seq"), None),
        P(None, ("dp", "seq"), None),
        P(None, None, ("dp", "seq")),
        P(None, None, ("dp", "seq")),
        P(None, None, ("dp", "seq")),
        P(),
        P(None, ("dp", "seq"), None),
        P(None, ("dp", "seq"), None),
        P(None, ("dp", "seq"), None),
        P(None, None, ("dp", "seq")),
        P(None, None, ("dp", "seq")),
        P(None, None, ("dp", "seq")),
        P(),
        P(None, ("dp", "seq"), None),
        P(None, ("dp", "seq"), None),
        P(None, ("dp", "seq"), None),
        P(None, None, ("dp", "seq")),
        P(None, None, ("dp", "seq")),
        P(None, None, ("dp", "seq")),
        P(),
    )
    out_specs = (
        P(("dp", "seq"), None),
        P(("dp", "seq"), None),
        P(None, ("dp", "seq"), None),
        P(None, ("dp", "seq"), None),
        P(None, ("dp", "seq"), None),
        P(None, None, ("dp", "seq")),
        P(None, None, ("dp", "seq")),
        P(None, None, ("dp", "seq")),
        P(),
        P(None, ("dp", "seq"), None),
        P(None, ("dp", "seq"), None),
        P(None, ("dp", "seq"), None),
        P(None, None, ("dp", "seq")),
        P(None, None, ("dp", "seq")),
        P(None, None, ("dp", "seq")),
        P(),
        P(None, ("dp", "seq"), None),
        P(None, ("dp", "seq"), None),
        P(None, ("dp", "seq"), None),
        P(None, None, ("dp", "seq")),
        P(None, None, ("dp", "seq")),
        P(None, None, ("dp", "seq")),
        P(),
        P(None, ("dp", "seq"), None),
        P(None, ("dp", "seq"), None),
        P(None, ("dp", "seq"), None),
        P(None, None, ("dp", "seq")),
        P(None, None, ("dp", "seq")),
        P(None, None, ("dp", "seq")),
        P(),
    )
    return jax.shard_map(
        per_device, mesh=mesh, in_specs=in_specs, out_specs=out_specs, check_vma=False
    )
```

```python
import functools
import math

import jax
import jax.numpy as jnp
from jax import lax
from jax.experimental import pallas as pl
from jax.experimental.pallas import tpu as pltpu
from jax.sharding import PartitionSpec as P

HEADS = 16
IMG = 729
STEP = 8

eps_norm = 1e-06
beta_first = 0.9
beta_second = 0.95
learn_rate = 0.025
weight_decay = 0.1
eps_adam = 1e-08
gelu_rate = math.sqrt(2.0 / math.pi)
gelu_cube = 0.044715
span_len = 768
lane_pair = 256
masked_score = -1e30
mib = 2**20


def head_lanes(head, head_size, width):
    low = head * head_size
    first = jnp.minimum(low // 128 * 128, width - lane_pair)
    lanes = lax.broadcasted_iota(jnp.int32, (1, lane_pair), 1)
    inside = (lanes >= low - first) & (lanes < low - first + head_size)
    keys = pl.ds(pl.multiple_of(first, 128), lane_pair)
    values = pl.ds(pl.multiple_of(first + width, 128), lane_pair)
    return keys, values, inside


def valid_lanes(start):
    lanes = lax.broadcasted_iota(jnp.int32, (1, span_len), 1)
    return (lanes >= start) & (lanes < start + IMG)


def dot_nn(left, right):
    return lax.dot_general(left, right, (((1,), (0,)), ((), ())), preferred_element_type=jnp.float32)


def dot_nt(left, right):
    return lax.dot_general(left, right, (((1,), (1,)), ((), ())), preferred_element_type=jnp.float32)


def dot_tn(left, right):
    return lax.dot_general(left, right, (((0,), (0,)), ((), ())), preferred_element_type=jnp.float32)


def attention_forward_kernel(
    tile, left, exp_scale, plan, query, window, own_code, out, lse_out, bias, mix
):
    tok, width = query.shape
    head_size = width // HEADS

    def one_span(tile_index, which):
        spot = 2 * tile_index + which
        offset, image = pl.multiple_of(plan[0, spot], 16), plan[1, spot]
        valid = valid_lanes(plan[2, spot])
        rows = pl.ds(pl.multiple_of(tile_index * tile, 16), tile)
        own_rows = pl.ds(pl.multiple_of(left + tile_index * tile, 16), tile)
        span = pl.ds(offset, span_len)
        code = own_code[rows, :]
        row_image = jnp.maximum(code, -code)
        mine = row_image == image
        bias[...] = jnp.where(mine & valid, 0.0, masked_score)
        self_bias = jnp.where(code < 0, 0.0, masked_score)
        lse_lane = lax.broadcasted_iota(jnp.int32, (tile, lse_out.shape[1]), 1)

        def one_head(head, carry):
            lanes, value_lanes, inside = head_lanes(head, head_size, width)
            queries = jnp.where(inside, query[rows, lanes], 0)
            scores = dot_nt(queries, window[span, lanes]) * exp_scale + bias[...]
            own_key = window[own_rows, lanes].astype(jnp.float32)
            own_value = window[own_rows, value_lanes].astype(jnp.float32)
            self_score = (
                jnp.sum(queries.astype(jnp.float32) * own_key, axis=1, keepdims=True) * exp_scale
                + self_bias
            )
            top = jnp.maximum(jnp.max(scores, axis=1, keepdims=True), self_score)
            powers = jnp.exp2(scores - top)
            self_power = jnp.exp2(self_score - top)
            total = jnp.sum(powers, axis=1, keepdims=True) + self_power
            mixed = dot_nn(powers.astype(jnp.bfloat16), window[span, value_lanes])
            mixed = (mixed + self_power * own_value) / total
            mix[rows, lanes] = jnp.where(inside & mine, mixed, mix[rows, lanes])
            lse_out[rows, :] = jnp.where(
                (lse_lane == head) & mine, top + jnp.log2(total), lse_out[rows, :]
            )
            return carry

        lax.fori_loop(0, HEADS, one_head, 0, unroll=2)

    def one_tile(tile_index, carry):
        one_span(tile_index, 0)

        @pl.when(plan[1, 2 * tile_index] != plan[1, 2 * tile_index + 1])
        def _():
            one_span(tile_index, 1)

        return carry

    lax.fori_loop(0, tok // tile, one_tile, 0)
    out[...] = mix[...].astype(out.dtype)


def attention_backward_kernel(
    tile, left, exp_scale, plan, query, window, grad, lse_in, own_code,
    grad_query, grad_window, bias, acc_query, acc_window,
):
    tok, width = query.shape
    head_size = width // HEADS
    scale = 1.0 / math.sqrt(head_size)
    acc_query[...] = jnp.zeros_like(acc_query)
    acc_window[...] = jnp.zeros_like(acc_window)

    def one_span(tile_index, which):
        spot = 2 * tile_index + which
        offset, image = pl.multiple_of(plan[0, spot], 16), plan[1, spot]
        valid = valid_lanes(plan[2, spot])
        rows = pl.ds(pl.multiple_of(tile_index * tile, 16), tile)
        own_rows = pl.ds(pl.multiple_of(left + tile_index * tile, 16), tile)
        span = pl.ds(offset, span_len)
        code = own_code[rows, :]
        row_image = jnp.maximum(code, -code)
        mine = row_image == image
        bias[...] = jnp.where(mine & valid, 0.0, masked_score)
        self_bias = jnp.where((code < 0) & mine, 0.0, masked_score)
        lse_lane = lax.broadcasted_iota(jnp.int32, (tile, lse_in.shape[1]), 1)

        def one_head(head, carry):
            lanes, value_lanes, inside = head_lanes(head, head_size, width)
            queries = jnp.where(inside, query[rows, lanes], 0)
            grads = jnp.where(inside, grad[rows, lanes], 0)
            lse = jnp.sum(jnp.where(lse_lane == head, lse_in[rows, :], 0.0), axis=1, keepdims=True)
            keys = window[span, lanes]
            own_key = window[own_rows, lanes].astype(jnp.float32)
            own_value = window[own_rows, value_lanes].astype(jnp.float32)
            queries_wide = queries.astype(jnp.float32)
            grads_wide = grads.astype(jnp.float32)
            prob = jnp.exp2(dot_nt(queries, keys) * exp_scale + bias[...] - lse)
            self_score = jnp.sum(queries_wide * own_key, axis=1, keepdims=True) * exp_scale
            self_prob = jnp.exp2(self_score + self_bias - lse)
            grad_prob = dot_nt(grads, window[span, value_lanes])
            self_grad = jnp.sum(grads_wide * own_value, axis=1, keepdims=True)
            inner = jnp.sum(prob * grad_prob, axis=1, keepdims=True) + self_prob * self_grad
            grad_scores = (prob * (grad_prob - inner)).astype(jnp.bfloat16)
            self_grad_score = self_prob * (self_grad - inner)
            part = dot_nn(grad_scores, keys) + self_grad_score * own_key
            acc_query[rows, lanes] += jnp.where(inside, part, 0.0)
            acc_window[span, lanes] += dot_tn(grad_scores, queries)
            acc_window[span, value_lanes] += dot_tn(prob.astype(jnp.bfloat16), grads)
            acc_window[own_rows, lanes] += self_grad_score * queries_wide
            acc_window[own_rows, value_lanes] += self_prob * grads_wide
            return carry

        lax.fori_loop(0, HEADS, one_head, 0, unroll=2)

    def one_tile(tile_index, carry):
        one_span(tile_index, 0)

        @pl.when(plan[1, 2 * tile_index] != plan[1, 2 * tile_index + 1])
        def _():
            one_span(tile_index, 1)

        return carry

    lax.fori_loop(0, tok // tile, one_tile, 0)
    grad_query[...] = (acc_query[...] * scale).astype(grad_query.dtype)
    step = 16

    def narrow(index, carry):
        rows = pl.ds(pl.multiple_of(index * step, step), step)
        grad_window[rows, :width] = (acc_window[rows, :width] * scale).astype(grad_window.dtype)
        grad_window[rows, width:] = acc_window[rows, width:].astype(grad_window.dtype)
        return carry

    lax.fori_loop(0, acc_window.shape[0] // step, narrow, 0)


def in_vmem():
    return pl.BlockSpec(memory_space=pltpu.VMEM)


def attention_forward(tile, left, plan, query, window, own_code):
    tok, width = query.shape
    exp_scale = math.log2(math.e) / math.sqrt(width // HEADS)
    return pl.pallas_call(
        functools.partial(attention_forward_kernel, tile, left, exp_scale),
        name="attention_forward",
        out_shape=[
            jax.ShapeDtypeStruct((tok, width), jnp.bfloat16),
            jax.ShapeDtypeStruct((tok, 128), jnp.float32),
        ],
        in_specs=[pl.BlockSpec(memory_space=pltpu.SMEM)] + [in_vmem()] * 3,
        out_specs=[in_vmem()] * 2,
        scratch_shapes=[
            pltpu.VMEM((tile, span_len), jnp.float32),
            pltpu.VMEM((tok, width), jnp.float32),
        ],
        compiler_params=pltpu.CompilerParams(vmem_limit_bytes=60 * mib),
    )(plan, query, window, own_code)


def attention_backward(tile, left, plan, query, window, grad, lse, own_code):
    tok, width = query.shape
    exp_scale = math.log2(math.e) / math.sqrt(width // HEADS)
    return pl.pallas_call(
        functools.partial(attention_backward_kernel, tile, left, exp_scale),
        name="attention_backward",
        out_shape=[
            jax.ShapeDtypeStruct((tok, width), jnp.bfloat16),
            jax.ShapeDtypeStruct(window.shape, jnp.bfloat16),
        ],
        in_specs=[pl.BlockSpec(memory_space=pltpu.SMEM)] + [in_vmem()] * 5,
        out_specs=[in_vmem()] * 2,
        scratch_shapes=[
            pltpu.VMEM((tile, span_len), jnp.float32),
            pltpu.VMEM((tok, width), jnp.float32),
            pltpu.VMEM(window.shape, jnp.float32),
        ],
        compiler_params=pltpu.CompilerParams(vmem_limit_bytes=62 * mib),
    )(plan, query, window, grad, lse, own_code)


def attention_plan(tile, left, right, own_ids, own_mask, window_ids, place, places):
    tok = own_ids.shape[0]
    window_len = left + tok + right
    room = jnp.minimum(window_len, left + (places - place) * tok) - span_len
    position = jnp.arange(window_len)
    ids = jnp.where(position < left - place * tok, -1, window_ids)
    images = own_ids.reshape(tok // tile, tile)[:, :: tile - 1].reshape(-1)
    before = (ids[None, :] < images[:, None]) & (position < left + tok)[None, :]
    starts = jnp.sum(before.astype(jnp.int32), axis=1)
    offsets = jnp.minimum(starts // 16 * 16, room)
    plan = jnp.stack([offsets, images + 1, starts - offsets]).astype(jnp.int32)
    own_code = jnp.where(own_mask > 0, own_ids + 1, -(own_ids + 1)).astype(jnp.int32)[:, None]
    return plan, own_code


class Layout:
    def __init__(self, groups, seats, model_width):
        self.rows = model_width // (groups * seats)
        self.members = 2
        while self.members * self.rows % 16:
            self.members *= 2
        self.sides = self.members // 2
        self.lines = seats // self.members
        self.slab = self.members * self.rows
        self.padded = -(-self.rows // 16) * 16
        self.near = model_width // groups
        self.model_width = model_width

    def blocks(self, one_block):
        return 2 if one_block else 2 * self.sides

    def columns(self, columns, one_block):
        unit = 128 * self.blocks(one_block)
        return -(-columns // unit) * unit


class Mail:
    def __init__(self, layout, send, recv, slots):
        self.layout, self.send_sems, self.recv_sems, self.slots = layout, send, recv, slots
        self.group = lax.axis_index("dp")
        seat = lax.axis_index("seq")
        self.line = seat // layout.members
        self.member = seat % layout.members
        self.side = self.member // 2
        self.core = self.member % 2
        self.started = {}

    def at(self, group=None, line=None, side=None, core=None):
        group = self.group if group is None else group
        line = self.line if line is None else line
        side = self.side if side is None else side
        core = self.core if core is None else core
        return (group, line * self.layout.members + side * 2 + core)

    def copy(self, slot, source, target, device, shift=0):
        index = self.slots[slot] + shift
        return pltpu.make_async_remote_copy(
            src_ref=source,
            dst_ref=target,
            send_sem=self.send_sems.at[index],
            recv_sem=self.recv_sems.at[index],
            device_id=device,
            device_id_type=pl.DeviceIdType.MESH,
        )

    def send(self, slot, source, target, device, when=None):
        copy = self.copy(slot, source, target, device)
        self.started[slot] = (copy, when)
        guarded(when, copy.start)

    def wait(self, slot, target, shift=0):
        self.copy(slot, target, target, self.at(core=1 - self.core), shift).wait_recv()

    def settle(self, slot):
        copy, when = self.started.pop(slot)
        guarded(when, copy.wait_send)

    def finish(self):
        for slot in list(self.started):
            self.settle(slot)


class Desk:
    def __init__(self, mail, index, local):
        self.mail, self.index, self.local_sems = mail, index, local
        self.group, self.line, self.member = mail.group, mail.line, mail.member
        self.side, self.core, self.at = mail.side, mail.core, mail.at

    def send(self, slot, source, target, device, when=None):
        self.mail.send((self.index, slot), source, target, device, when)

    def wait(self, slot, target, shift=0):
        self.mail.wait((self.index, slot), target, shift)

    def settle(self, slot):
        self.mail.settle((self.index, slot))

    def local(self, number, source, target):
        return pltpu.make_async_copy(source, target, self.local_sems.at[number])


class Work:
    def __init__(self, steps, ins, outs, scratch, slots, local):
        self.steps, self.ins, self.outs, self.scratch = steps, ins, outs, scratch
        self.slots, self.local = slots, local


def guarded(when, action):
    if when is None:
        action()
    else:
        pl.when(when)(action)


def all_of(*conditions):
    kept = [condition for condition in conditions if condition is not None]
    return functools.reduce(jnp.logical_and, kept) if kept else None


def run_steps(works, turns):
    queue = []
    for index, (work, first) in enumerate(zip(works, turns)):
        next(work)
        queue.append((first[0], index, 0))
    while queue:
        turn, index, done = min(queue)
        queue.remove((turn, index, done))
        try:
            next(works[index])
        except StopIteration:
            continue
        done += 1
        listed = turns[index]
        queue.append((listed[done] if done < len(listed) else turn + 1, index, done))


def anywhere():
    return pl.BlockSpec(memory_space=pl.ANY)


def exchange(name, layout, works, starts, megabytes, common=()):
    slots = [(index, slot) for index, work in enumerate(works) for slot in work.slots]
    numbers = {slot: index for index, slot in enumerate(slots)}
    ins = [entry for work in works for entry in work.ins]
    outs = [entry for work in works for entry in work.outs]
    scratch = [entry for work in works for entry in work.scratch]

    def kernel(*refs):
        refs = list(refs)

        def take(count):
            taken = refs[:count]
            del refs[:count]
            return taken

        in_refs = [take(len(work.ins)) for work in works]
        out_refs = [take(len(work.outs)) for work in works]
        scratch_refs = [take(len(work.scratch)) for work in works]
        common_refs = take(len(common))
        locals_of = [take(1)[0] for work in works]
        send, recv = refs
        mail = Mail(layout, send, recv, numbers)
        run_steps(
            [
                work.steps(
                    Desk(mail, index, locals_of[index]),
                    in_refs[index],
                    out_refs[index],
                    scratch_refs[index],
                    common_refs,
                )
                for index, work in enumerate(works)
            ],
            starts,
        )
        mail.finish()

    results = pl.pallas_call(
        kernel,
        name=name,
        out_shape=[shape for shape, _ in outs],
        in_specs=[spec for _, spec in ins],
        out_specs=[spec for _, spec in outs],
        scratch_shapes=scratch
        + list(common)
        + [pltpu.SemaphoreType.DMA((work.local,)) for work in works]
        + [pltpu.SemaphoreType.DMA((len(slots),))] * 2,
        compiler_params=pltpu.CompilerParams(
            has_side_effects=True, vmem_limit_bytes=megabytes * mib
        ),
    )(*[array for array, _ in ins])
    results = list(results)
    grouped = []
    for work in works:
        grouped.append(results[: len(work.outs)])
        del results[: len(work.outs)]
    return grouped


def gather_work(layout, shard, one_block):
    lines, members, sides = layout.lines, layout.members, layout.sides
    width = shard.shape[1] // layout.blocks(one_block)
    spots = [("own", 0)]
    for t in range(1, lines):
        spots += [(f"below{t}", -t), (f"above{t}", t)]
    slots = [("mix", j) for j in range(1, members)]
    slots += [(way, t) for way in ("up", "down") for t in range(lines)]
    slots += [("cross", source) for source, _ in spots]
    slots += [("core", j) for j in range(1 if one_block else sides)]
    if not one_block:
        slots += [
            ("side", half, source, j)
            for half in (0, 1)
            for source, _ in spots
            for j in range(1, sides)
        ]

    def steps(desk, ins, outs, scratch, common):
        (shard,), (out,), (landing, slab, wide) = ins, outs, scratch
        group, line, member, side, core = desk.group, desk.line, desk.member, desk.side, desk.core
        has_up, has_down = line < lines - 1, line > 0

        def columns(side_of, core_of):
            block = core_of if one_block else core_of * sides + side_of
            return pl.ds(pl.multiple_of(block * width, 128), width)

        own = columns(side, core)

        def place(group_of, line_of, lanes=own):
            first = (group_of * lines + line_of) * layout.slab
            return out.at[pl.ds(pl.multiple_of(first, 16), layout.slab), lanes]

        def present(step):
            return None if step == 0 else line >= -step if step < 0 else line < lines - step

        for j in range(1, members):
            other = (member + j) % members
            desk.send(
                ("mix", j),
                shard.at[:, columns(other // 2, other % 2)],
                landing.at[member],
                desk.at(side=other // 2, core=other % 2),
            )
        mine = desk.local(0, shard.at[:, own], landing.at[member])
        mine.start()
        yield
        for j in range(1, members):
            desk.wait(("mix", j), landing.at[(member + members - j) % members])
        mine.wait()
        for m in range(members):
            rows = slice(m * layout.rows, (m + 1) * layout.rows)
            wide[rows, :] = landing[m, : layout.rows, :].astype(jnp.float32)
        slab[...] = wide[...].astype(slab.dtype)
        keep = desk.local(1, slab, place(group, line))
        keep.start()

        def pass_on(source, what, half, where, when):
            if half == 0:
                desk.send(("cross", source), what, where, desk.at(group=1 - group), when)
            if not one_block:
                for j in range(1, sides):
                    slot = ("side", half, source, j)
                    desk.send(slot, what, where, desk.at(side=(side + j) % sides), when)

        home = place(group, line)
        desk.send(("up", 0), slab, home, desk.at(line=line + 1), has_up)
        desk.send(("down", 0), slab, home, desk.at(line=line - 1), has_down)
        pass_on("own", slab, 0, home, None)
        yield
        for t in range(1, lines):
            for way, name, step, further, to in (
                ("up", "below", -t, has_up, line + 1),
                ("down", "above", t, has_down, line - 1),
            ):
                when, where = present(step), place(group, line + step)
                guarded(when, functools.partial(desk.wait, (way, t - 1), where))
                desk.send((way, t), where, where, desk.at(line=to), all_of(when, further))
                pass_on(f"{name}{t}", where, 0, where, when)
            if t == 1:
                where = place(1 - group, line)
                desk.wait(("cross", "own"), where)
                pass_on("own", where, 1, where, None)
            yield
        for t in range(1, lines):
            for name, step in ((f"below{t}", -t), (f"above{t}", t)):
                when, where = present(step), place(1 - group, line + step)
                guarded(when, functools.partial(desk.wait, ("cross", name), where))
                pass_on(name, where, 1, where, when)
            yield
        keep.wait()
        partner = desk.at(core=1 - core)
        desk.send(("core", 0), out.at[:, own], out.at[:, own], partner)
        if not one_block:
            yield
            for j in range(1, sides):
                theirs = columns((side + sides - j) % sides, core)
                for half, group_of in ((0, group), (1, 1 - group)):
                    for source, step in spots:
                        where = place(group_of, line + step, theirs)
                        slot = ("side", half, source, j)
                        guarded(present(step), functools.partial(desk.wait, slot, where))
                desk.send(("core", j), out.at[:, theirs], out.at[:, theirs], partner)
        yield
        desk.wait(("core", 0), out.at[:, columns(side, 1 - core)])
        if not one_block:
            for j in range(1, sides):
                theirs = columns((side + sides - j) % sides, 1 - core)
                desk.wait(("core", j), out.at[:, theirs])

    low = jnp.bfloat16
    return Work(
        steps,
        [(shard, anywhere())],
        [(jax.ShapeDtypeStruct((layout.model_width, shard.shape[1]), low), anywhere())],
        [
            pltpu.VMEM((members, layout.padded, width), low),
            pltpu.VMEM((layout.slab, width), low),
            pltpu.VMEM((layout.slab, width), jnp.float32),
        ],
        slots,
        2,
    )


def add_rows(target, first, target_columns, source, source_columns, count, source_first=0):
    step = math.gcd(count, 48)

    def one(index, carry):
        rows = pl.ds(pl.multiple_of(first + index * step, 16), step)
        theirs = pl.ds(pl.multiple_of(source_first + index * step, 16), step)
        total = target[rows, target_columns].astype(jnp.float32)
        total += source[theirs, source_columns].astype(jnp.float32)
        target[rows, target_columns] = total.astype(target.dtype)
        return carry

    lax.fori_loop(0, count // step, one, 0)


def reduce_work(layout, lefts, right, one_block, switch=0, split=3):
    lines, members, sides = layout.lines, layout.members, layout.sides
    tok, columns = right.shape
    blocks = layout.blocks(one_block)
    width, half = columns // blocks, columns // 2
    near_rows, slab_rows, low = layout.near, layout.slab, jnp.bfloat16
    count, depth = min(split, width // 128), min(4, lines)
    parts = []
    for index in range(count):
        first = width // 128 * index // count * 128
        parts.append((first, width // 128 * (index + 1) // count * 128 - first))
    order = []
    for t in range(lines):
        goal = lines - 1 - t // 2 if t % 2 == 0 else t // 2
        order.append(goal)
    slots = [("left", k) for k in range(len(lefts))] + ["right"]
    slots += [("cross", part, t) for part in parts for t in range(lines)]
    slots += [
        (way, part, t) for way in ("up", "down") for part in parts for t in range(1, lines)
    ]
    slots += [("mix", j) for j in range(1, members)]
    if not one_block:
        slots += [
            ("side", part, tag, t, j)
            for part in parts
            for tag in (0, 1)
            for t in range(lines)
            for j in range(1, sides)
        ]

    def steps(desk, ins, outs, scratch, common):
        left_in, right_in = ins[: len(lefts)], ins[len(lefts)]
        out, left_land, right_land = outs[0], outs[1 : 1 + len(lefts)], outs[1 + len(lefts)]
        total, cross, up, down, piece, landing, wide = scratch[:7]
        from_side = None if one_block else scratch[7]
        left_all, right_all = common
        group, line, member, side, core = desk.group, desk.line, desk.member, desk.side, desk.core
        partner = desk.at(core=1 - core)
        own = pl.ds(0 if one_block else pl.multiple_of(side * width, 128), width)
        stay = pl.ds(pl.multiple_of(core * half, 128), half)
        away = pl.ds(pl.multiple_of((1 - core) * half, 128), half)

        def first_of(tag, goal):
            return pl.multiple_of((group if tag else 1 - group) * near_rows + goal * slab_rows, 16)

        for k, left in enumerate(left_in):
            desk.send(("left", k), left, left_land[k], partner)
        desk.send("right", right_in.at[:, away], right_land, partner)
        yield
        loads = []

        def load(source, target):
            copy = desk.local(len(loads), source, target)
            copy.start()
            loads.append(copy)

        for k, left in enumerate(left_in):
            load(left, left_all.at[k, 0])
        load(right_in.at[:, stay], right_all.at[0, :, pl.ds(0, half)])
        for k in range(len(left_in)):
            desk.wait(("left", k), left_land[k])
            load(left_land[k], left_all.at[k, 1])
        desk.wait("right", right_land)
        load(right_land, right_all.at[1, :, pl.ds(0, half)])
        for copy in loads:
            copy.wait()

        def multiply(tag):
            rows = pl.ds(first_of(tag, 0), near_rows)

            def piece_of(first, lanes, which):
                theirs = pl.ds(first, lanes)
                product = dot_nn(left_all[which, 0, rows, :], right_all[0, :, theirs])
                product += dot_nn(left_all[which, 1, rows, :], right_all[1, :, theirs])
                total[rows, theirs] = product.astype(low)

            lanes = 256 if len(lefts) == 1 else math.gcd(switch, 384)

            def one(index, carry):
                first = pl.multiple_of(index * lanes, 128)
                which = 0
                if len(lefts) > 1:
                    which = jnp.where(core * half + index * lanes >= switch, 1, 0)
                piece_of(first, lanes, which)
                return carry

            lax.fori_loop(0, half // lanes, one, 0)
            if half % lanes:
                piece_of(half // lanes * lanes, half % lanes, 0)

        own_first = 0 if one_block else side * width
        pieces = [
            (part, tag, goal)
            for part in parts
            for tag in ((0,) if one_block else (0, 1))
            for goal in order
        ]

        def lanes_of(part, first):
            return pl.ds(pl.multiple_of(first + part[0], 128), part[1])

        def post(number):
            if number >= len(pieces):
                return
            part, tag, goal = pieces[number]
            if one_block:
                if number >= depth:
                    before = pieces[number - depth]
                    desk.settle(("cross", before[0], before[2]))
                send_across(part, goal)
                return
            rows = pl.ds(first_of(tag, goal), slab_rows)
            for j in range(1, sides):
                if number >= depth:
                    desk.settle(("side", *pieces[number - depth], j))
                other = (side + j) % sides
                desk.send(
                    ("side", part, tag, goal, j),
                    total.at[rows, lanes_of(part, other * width)],
                    from_side.at[j - 1, rows, lanes_of(part, 0)],
                    desk.at(side=other),
                )

        def send_across(part, goal):
            rows = pl.ds(first_of(0, goal), slab_rows)
            desk.send(
                ("cross", part, goal),
                total.at[rows, lanes_of(part, own_first)],
                cross.at[goal, :, lanes_of(part, 0)],
                desk.at(group=1 - group),
            )

        def take_side(part, tag, goal):
            first = first_of(tag, goal)
            rows, lanes = pl.ds(first, slab_rows), lanes_of(part, 0)
            for j in range(1, sides):
                desk.wait(("side", part, tag, goal, j), from_side.at[j - 1, rows, lanes])
            post(pieces.index((part, tag, goal)) + depth)
            for j in range(1, sides):
                add_rows(
                    total, first, lanes_of(part, own_first), from_side.at[j - 1], lanes,
                    slab_rows, first,
                )

        ends = lines - 1 - line

        def part_steps(part):
            lanes, mine = lanes_of(part, 0), lanes_of(part, own_first)
            if not one_block:
                for goal in order:
                    take_side(part, 0, goal)
                    send_across(part, goal)
                    yield
            for goal in order:
                if not one_block:
                    take_side(part, 1, goal)
                desk.wait(("cross", part, goal), cross.at[goal, :, lanes])
                if one_block:
                    post(pieces.index((part, 0, goal)) + depth)
                add_rows(total, first_of(1, goal), mine, cross.at[goal], lanes, slab_rows)
                yield
            for t in range(1, lines):
                for way, buffer, going, fed, goal, to in (
                    ("up", up, line < t, line > 0, lines - t + line, line + 1),
                    ("down", down, ends < t, ends > 0, t - lines + line, line - 1),
                ):
                    first = first_of(1, goal)

                    @pl.when(all_of(going, fed))
                    def _():
                        if t > 1:
                            desk.wait((way, part, t - 1), buffer.at[t - 2, :, lanes])
                            add_rows(total, first, mine, buffer.at[t - 2], lanes, slab_rows)

                    desk.send(
                        (way, part, t),
                        total.at[pl.ds(first, slab_rows), mine],
                        buffer.at[t - 1, :, lanes],
                        desk.at(line=to),
                        going,
                    )
                yield

        multiply(0)
        for number in range(depth):
            post(number)
        yield
        multiply(1)
        yield
        running = [part_steps(part) for part in parts]
        turn, lag = 0, len(pieces) // len(parts)
        while running:
            for index, steps_of in enumerate(running):
                if steps_of is not None and turn >= lag * index:
                    try:
                        next(steps_of)
                    except StopIteration:
                        running[index] = None
            if not any(running):
                break
            turn += 1
            yield
        first = first_of(1, line)
        wide[...] = total[pl.ds(first, slab_rows), own].astype(jnp.float32)
        for way, buffer, fed in (("up", up, line > 0), ("down", down, ends > 0)):

            @pl.when(fed)
            def _():
                for part in parts:
                    where = buffer.at[lines - 2, :, lanes_of(part, 0)]
                    desk.wait((way, part, lines - 1), where)
                wide[...] += buffer[lines - 2].astype(jnp.float32)

        for m in range(members):
            rows = slice(m * layout.rows, (m + 1) * layout.rows)
            piece[m] = jnp.zeros(piece.shape[1:], piece.dtype)
            piece[m, : layout.rows, :] = wide[rows, :].astype(piece.dtype)
        seat = core * sides + side
        for j in range(1, members):
            other = (member + j) % members
            desk.send(
                ("mix", j),
                piece.at[other],
                landing.at[seat],
                desk.at(side=other // 2, core=other % 2),
            )
        landing[seat] = piece[member]
        yield
        for j in range(1, members):
            other = (member + members - j) % members
            desk.wait(("mix", j), landing.at[other % 2 * sides + other // 2])
        if one_block:
            for c in range(2):
                block = landing[c * sides].astype(jnp.float32)
                for s in range(1, sides):
                    block += landing[c * sides + s].astype(jnp.float32)
                out[:, c * width : (c + 1) * width] = block
        else:
            for b in range(blocks):
                out[:, b * width : (b + 1) * width] = landing[b].astype(jnp.float32)

    scratch = [
        pltpu.VMEM((layout.model_width, half), low),
        pltpu.VMEM((lines, slab_rows, width), low),
        pltpu.VMEM((lines - 1, slab_rows, width), low),
        pltpu.VMEM((lines - 1, slab_rows, width), low),
        pltpu.VMEM((members, layout.padded, width), low),
        pltpu.VMEM((members, layout.padded, width), low),
        pltpu.VMEM((slab_rows, width), jnp.float32),
    ]
    if not one_block:
        scratch.append(pltpu.VMEM((sides - 1, layout.model_width, width), low))
    ins = [(array, anywhere()) for array in [*lefts, right]]
    return Work(
        steps,
        ins,
        [(jax.ShapeDtypeStruct((layout.padded, columns), jnp.float32), in_vmem())]
        + [(jax.ShapeDtypeStruct(left.shape, low), anywhere()) for left in lefts]
        + [(jax.ShapeDtypeStruct((tok, half), low), anywhere())],
        scratch,
        slots,
        2 * len(lefts) + 2,
    )


class Reach:
    def __init__(self, tok, left, right):
        self.tok, self.left, self.right = tok, left, right
        self.window = left + tok + right
        self.deltas = [d for d in range(-8, 9) if d != 0 and self.rows(d) > 0]

    def first(self, delta):
        return max(0, self.tok * delta - self.left)

    def rows(self, delta):
        last = min(self.tok, self.tok * delta - self.left + self.window)
        return last - self.first(delta)

    def spot(self, delta):
        return self.first(delta) - self.tok * delta + self.left


def parts_of(count, step=80):
    return [(first, min(step, count - first)) for first in range(0, count, step)]


def window_work(layout, reach, key_value):
    tok, width = key_value.shape
    left, lines, places = reach.left, layout.lines, layout.lines * layout.members
    routed = layout.sides == 2
    pieces, depth = parts_of(tok), 2
    near_below, far_below = reach.spot(2), reach.spot(3)
    tail = (reach.first(3), max(reach.rows(3), 0))
    head = max(reach.rows(-2), 0)
    if routed:
        slots = ["pair", "tail", "share", "wide", "thin", "last"]
        slots += [(name, k) for name in ("right", "left", "climb", "drop") for k in range(len(pieces))]
        slots += [("fall", k) for k in range(len(parts_of(head)))]
    else:
        slots = [("reach", delta) for delta in reach.deltas]

    def direct(desk, own, window):
        seat = desk.line * layout.members + desk.member
        for delta in reach.deltas:
            count = reach.rows(delta)
            desk.send(
                ("reach", delta),
                own.at[pl.ds(reach.first(delta), count)],
                window.at[pl.ds(reach.spot(delta), count)],
                (desk.group, seat + delta),
                (seat + delta >= 0) & (seat + delta < places),
            )
        yield
        for delta in reach.deltas:
            where = window.at[pl.ds(reach.spot(delta), reach.rows(delta))]
            when = (seat - delta >= 0) & (seat - delta < places)
            guarded(when, functools.partial(desk.wait, ("reach", delta), where))

    def by_way(desk, own, window, transit):
        line, core = desk.line, desk.core
        first_side, last_side = desk.side == 0, desk.side == 1
        low_core, high_core = core == 0, core == 1
        has_up, has_down = line < lines - 1, line > 0
        has_before = last_side | has_down
        partner = desk.at(core=1 - core)

        def part(ref, first, count):
            return ref.at[pl.ds(first, count)]

        def post(k):
            if k >= len(pieces):
                return
            if k >= depth:
                desk.settle(("right", k - depth))
                desk.settle(("left", k - depth))
            first, count = pieces[k]
            desk.send(
                ("right", k), part(own, first, count), part(window, near_below + first, count),
                desk.at(side=1), first_side,
            )
            desk.send(
                ("left", k), part(own, first, count), part(transit, first, count),
                desk.at(side=0), last_side,
            )

        for k in range(depth):
            post(k)
        desk.send(
            "tail", part(own, *tail), part(window, far_below, tail[1]),
            desk.at(line=line + 1, core=0), high_core & has_up,
        )
        mirrored = pl.multiple_of(left + (2 * core - 1) * tok, 16)
        desk.send("pair", own, part(window, mirrored, tok), partner)
        yield
        for k, (first, count) in enumerate(pieces):
            ahead = part(transit, first, count)
            guarded(first_side, functools.partial(desk.wait, ("left", k), ahead))
            desk.send(
                ("climb", k), ahead, part(window, near_below + first, count),
                desk.at(line=line + 1), first_side & has_up,
            )
            behind = part(window, near_below + first, count)
            guarded(last_side, functools.partial(desk.wait, ("right", k), behind))
            post(k + depth)
            desk.send(
                ("drop", k), behind, part(window, left + tok + first, count),
                desk.at(line=line - 1, core=1), last_side & has_down & low_core,
            )
            if first < head:
                count = min(count, head - first)
                desk.send(
                    ("fall", k), part(window, near_below + first, count),
                    part(window, left + 2 * tok + first, count),
                    desk.at(line=line - 1), last_side & has_down & high_core,
                )
            yield
        stay = desk.local(1, part(transit, 0, head), part(window, left + 2 * tok, head))
        guarded(first_side, stay.start)
        desk.send(
            "share", transit, part(window, left + tok, tok), partner, first_side & low_core
        )

        def share_before(when):
            desk.send(
                "wide", part(window, near_below, tok), part(window, left - tok, tok), partner,
                when & high_core,
            )
            desk.send(
                "thin", part(window, near_below + tail[0], tail[1]),
                part(window, far_below, tail[1]), partner, when & low_core,
            )

        def climbed():
            for k, (first, count) in enumerate(pieces):
                desk.wait(("climb", k), part(window, near_below + first, count))

        guarded(first_side & has_down, climbed)
        share_before(has_before)
        yield

        def dropped():
            for k, (first, count) in enumerate(pieces):
                desk.wait(("drop", k), part(window, left + tok + first, count))
            for k, (first, count) in enumerate(parts_of(head)):
                desk.wait(("fall", k), part(window, left + 2 * tok + first, count))

        guarded(last_side & has_up & high_core, dropped)
        desk.send(
            "last", part(window, left + tok, head), part(window, left + 2 * tok, head), partner,
            last_side & has_up & high_core,
        )
        yield
        desk.wait("pair", part(window, pl.multiple_of(left + (1 - 2 * core) * tok, 16), tok))
        for when, slot, first, count in (
            (low_core & has_down, "tail", far_below, tail[1]),
            (first_side & high_core, "share", left + tok, tok),
            (has_before & low_core, "wide", left - tok, tok),
            (has_before & high_core, "thin", far_below, tail[1]),
            (last_side & has_up & low_core, "last", left + 2 * tok, head),
        ):
            guarded(when, functools.partial(desk.wait, slot, part(window, first, count)))
        guarded(first_side, stay.wait)

    def steps(desk, ins, outs, scratch, common):
        (own,), (window,) = ins, outs
        keep = desk.local(0, own, window.at[pl.ds(left, tok)])
        keep.start()
        yield from by_way(desk, own, window, *scratch) if routed else direct(desk, own, window)
        keep.wait()

    outs = [(jax.ShapeDtypeStruct((reach.window, width), key_value.dtype), anywhere())]
    scratch = [pltpu.VMEM((tok, width), key_value.dtype)] if routed else []
    return Work(steps, [(key_value, in_vmem())], outs, scratch, slots, 2)


def owned_work(layout, reach, grad_window):
    width = grad_window.shape[1]
    tok, left, lines = reach.tok, reach.left, layout.lines
    places = layout.lines * layout.members
    routed = layout.sides == 2
    pieces, depth = parts_of(tok), 2
    near_below, far_below = reach.spot(2), reach.spot(3)
    tail = (reach.first(3), max(reach.rows(3), 0))
    head = max(reach.rows(-2), 0)
    every = pl.ds(0, width)
    low = grad_window.dtype
    if routed:
        slots = ["pair", "tail", "share", "wide", "thin", "last", "rise"]
        slots += [(name, k) for name in ("right", "left", "fall", "lift") for k in range(len(pieces))]
    else:
        slots = [("reach", delta) for delta in reach.deltas]

    def direct(desk, grad, out, landing):
        seat = desk.line * layout.members + desk.member
        for delta in reach.deltas:
            count = reach.rows(delta)
            desk.send(
                ("reach", delta),
                grad.at[pl.ds(reach.spot(delta), count)],
                landing[delta],
                (desk.group, seat - delta),
                (seat - delta >= 0) & (seat - delta < places),
            )
        load = desk.local(0, grad.at[pl.ds(left, tok)], out)
        load.start()
        load.wait()
        yield
        for delta in reach.deltas:

            @pl.when((seat + delta >= 0) & (seat + delta < places))
            def _():
                desk.wait(("reach", delta), landing[delta])
                first, count = reach.first(delta), reach.rows(delta)
                add_rows(out, first, every, landing[delta], every, count)

    def by_way(desk, grad, out, scratch):
        near, middle, l_wide, l_far, l_climb, l_y, l_pair, l_tail = scratch
        line, core = desk.line, desk.core
        first_side, last_side = desk.side == 0, desk.side == 1
        low_core, high_core = core == 0, core == 1
        has_up, has_down = line < lines - 1, line > 0
        has_before = last_side | has_down
        gate = last_side & has_up & high_core
        partner = desk.at(core=1 - core)

        def part(ref, first, count):
            return ref.at[pl.ds(first, count)]

        def receive(when, slot, target, first, buffer, at, count):
            @pl.when(when)
            def _():
                desk.wait(slot, part(buffer, at, count))
                add_rows(target, first, every, buffer, every, count, at)

        desk.send(
            "last", part(grad, left + 2 * tok, head), part(l_climb, 0, head), partner,
            last_side & has_up & low_core,
        )
        desk.send(
            "wide", part(grad, left - tok, tok), l_wide, partner, has_before & low_core
        )
        desk.send(
            "thin", part(grad, far_below, tail[1]), part(l_wide, 0, tail[1]), partner,
            has_before & high_core,
        )
        desk.send(
            "share", part(grad, left + tok, tok), l_far, partner, first_side & high_core
        )
        desk.send(
            "tail", part(grad, far_below, tail[1]), l_tail,
            desk.at(line=line - 1, core=1), low_core & has_down,
        )
        desk.send("rise", part(grad, left + 2 * tok, head), part(l_far, 0, head),
            desk.at(line=line + 1), gate,
        )
        loads = [
            (desk.local(0, part(grad, near_below, tok), near), None),
            (desk.local(1, part(grad, left + tok, tok), middle), last_side),
            (desk.local(2, part(grad, left + 2 * tok, head), part(middle, 0, head)), first_side),
            (desk.local(3, part(grad, left, tok), out), None),
        ]
        for load, when in loads:
            guarded(when, load.start)

        @pl.when(first_side)
        def _():
            middle[head:, :] = jnp.zeros((tok - head, width), low)

        yield
        for load, when in loads:
            guarded(when, load.wait)
        receive(gate, "last", middle, 0, l_climb, 0, head)
        receive(has_before & high_core, "wide", near, 0, l_wide, 0, tok)
        receive(has_before & low_core, "thin", near, tail[0], l_wide, 0, tail[1])

        def post(k):
            if k >= len(pieces):
                return
            if k >= depth:
                desk.settle(("fall", k - depth))
                desk.settle(("lift", k - depth))
            first, count = pieces[k]
            desk.send(
                ("fall", k), part(middle, first, count), part(l_far, first, count),
                desk.at(line=line + 1, core=0), gate,
            )
            desk.send(
                ("lift", k), part(near, first, count), part(l_climb, first, count),
                desk.at(line=line - 1), first_side & has_down,
            )

        for k in range(depth):
            post(k)
        mirrored = pl.multiple_of(left + (1 - 2 * core) * tok, 16)
        desk.send("pair", part(grad, mirrored, tok), l_pair, partner)
        yield
        receive(first_side & low_core, "share", middle, 0, l_far, 0, tok)
        receive(last_side & has_down & high_core, "rise", near, 0, l_far, 0, head)
        for k, (first, count) in enumerate(pieces):
            receive(first_side & has_up, ("lift", k), middle, first, l_climb, first, count)
            desk.send(
                ("left", k), part(middle, first, count), part(l_y, first, count),
                desk.at(side=1), first_side,
            )
            receive(
                last_side & has_down & low_core, ("fall", k), near, first, l_far, first, count
            )
            desk.send(
                ("right", k), part(near, first, count), part(l_y, first, count),
                desk.at(side=0), last_side,
            )
            post(k + depth)
            yield
        receive(has_up & high_core, "tail", out, tail[0], l_tail, 0, tail[1])
        desk.wait("pair", l_pair)
        for k, (first, count) in enumerate(pieces):
            where = part(l_y, first, count)
            guarded(first_side, functools.partial(desk.wait, ("right", k), where))
            guarded(last_side, functools.partial(desk.wait, ("left", k), where))

            def one(index, carry):
                rows = pl.ds(pl.multiple_of(first + index * 16, 16), 16)
                total = out[rows, :].astype(jnp.float32) + l_pair[rows, :].astype(jnp.float32)
                out[rows, :] = (total + l_y[rows, :].astype(jnp.float32)).astype(out.dtype)
                return carry

            lax.fori_loop(0, count // 16, one, 0)
            yield

    def steps(desk, ins, outs, scratch, common):
        if routed:
            yield from by_way(desk, ins[0], outs[0], scratch)
        else:
            yield from direct(desk, ins[0], outs[0], dict(zip(reach.deltas, scratch)))

    if routed:
        counts = [tok] * 7 + [tail[1]]
    else:
        counts = [reach.rows(delta) for delta in reach.deltas]
    return Work(
        steps,
        [(grad_window, anywhere())],
        [(jax.ShapeDtypeStruct((tok, width), low), in_vmem())],
        [pltpu.VMEM((count, width), low) for count in counts],
        slots,
        4,
    )


def sum_work(layout, block):
    sizes = (2, layout.sides, layout.model_width // layout.near, layout.lines)
    slots = [(stage, j) for stage, size in enumerate(sizes) for j in range(1, size)]

    def steps(desk, ins, outs, scratch, common):
        (block,), (out,) = ins, outs
        yield
        out[...] = block[...]
        for stage, (landing, size) in enumerate(zip(scratch, sizes)):
            mine = (desk.core, desk.side, desk.group, desk.line)[stage]
            landing[mine] = out[...]
            for j in range(1, size):
                other = (mine + j) % size
                to = desk.at(**{("core", "side", "group", "line")[stage]: other})
                desk.send((stage, j), landing.at[mine], landing.at[mine], to)
            yield
            for j in range(1, size):
                desk.wait((stage, j), landing.at[(mine + size - j) % size])
            total = landing[0]
            for j in range(1, size):
                total = total + landing[j]
            out[...] = total

    return Work(
        steps,
        [(block, in_vmem())],
        [(jax.ShapeDtypeStruct(block.shape, block.dtype), in_vmem())],
        [pltpu.VMEM((size, *block.shape), block.dtype) for size in sizes],
        slots,
        1,
    )


def lane_mean(source):
    return jnp.mean(source, axis=1, keepdims=True)


def unit_of(source):
    centred = source - lane_mean(source)
    inv_scale = lax.rsqrt(lane_mean(centred * centred) + eps_norm)
    return centred * inv_scale, inv_scale


def norm_input_gradient(gradient, unit_rows, inv_scale, gain_row):
    scaled = gradient * gain_row
    return inv_scale * (scaled - lane_mean(scaled) - unit_rows * lane_mean(scaled * unit_rows))


def rows_sum(source):
    return jnp.sum(source.astype(jnp.float32), axis=0, keepdims=True)


def gelu_and_slope(source):
    square = source * source
    curve = jnp.tanh(gelu_rate * source * (1.0 + gelu_cube * square))
    rise = gelu_rate * (1.0 + 3.0 * gelu_cube * square)
    half_sum = 0.5 * (1.0 + curve)
    return source * half_sum, half_sum + 0.5 * source * (1.0 - curve * curve) * rise


def chunks_of(columns, lanes=768):
    return [(first, min(lanes, columns - first)) for first in range(0, columns, lanes)]


def moves(sources, targets, sems):
    return [
        pltpu.make_async_copy(source, target, sems.at[index])
        for index, (source, target) in enumerate(zip(sources, targets))
    ]


def projection_forward_kernel(
    residual, rows, weight, normed_out, inv_out, query_out, pair_out, unit_out, held, sems
):
    width = rows.shape[1]
    sources = [weight.at[:, pl.ds(j * width, width)] for j in range(3)]
    loads = moves(sources, [held.at[j] for j in range(3)], sems)
    for load in loads:
        load.start()
    unit_rows, inv_scale = unit_of(residual[...].astype(jnp.float32))
    unit_out[...] = unit_rows
    inv_out[...] = jnp.broadcast_to(inv_scale, inv_out.shape)
    normed = (unit_rows * rows[0:1, :] + rows[1:2, :]).astype(normed_out.dtype)
    normed_out[...] = normed
    loads[0].wait()
    query_out[...] = (dot_nn(normed_out[...], held[0]) + rows[2:3, :]).astype(query_out.dtype)
    loads[1].wait()
    pair_out[:, :width] = dot_nn(normed_out[...], held[1]).astype(pair_out.dtype)
    loads[2].wait()
    values = dot_nn(normed_out[...], held[2]) + rows[3:4, :]
    pair_out[:, width:] = values.astype(pair_out.dtype)


def dense_call(kernel, name, ins, outs, scratch, *arrays):
    return pl.pallas_call(
        kernel,
        name=name,
        in_specs=ins,
        out_specs=[spec for _, spec in outs],
        out_shape=[shape for shape, _ in outs],
        scratch_shapes=scratch,
        compiler_params=pltpu.CompilerParams(vmem_limit_bytes=60 * mib),
    )(*arrays)


def kept(shape, kind=jnp.bfloat16):
    return (jax.ShapeDtypeStruct(shape, kind), in_vmem())


def projection_forward(residual, rows, attn_weight):
    tok, width = residual.shape
    return dense_call(
        projection_forward_kernel,
        "projection_forward",
        [in_vmem(), in_vmem(), anywhere()],
        [
            kept((tok, width)),
            kept((tok, 128), jnp.float32),
            kept((tok, width)),
            kept((tok, 2 * width)),
            kept((tok, width), jnp.float32),
        ],
        [pltpu.VMEM((3, width, width), jnp.bfloat16), pltpu.SemaphoreType.DMA((3,))],
        residual,
        rows,
        attn_weight,
    )


def whole(shape):
    return pl.BlockSpec(shape, lambda step: (0,) * len(shape))


def projection_backward_kernel(
    grad_query, grad_pair, weight, unit, inv, rows, grad_mid, grad_res, sums, acc
):
    step = pl.program_id(0)
    width = grad_query.shape[1]

    @pl.when(step == 0)
    def _():
        acc[...] = dot_nt(grad_query[...], weight[...])

    @pl.when(step == 1)
    def _():
        acc[...] += dot_nt(grad_pair[:, :width], weight[...])

    @pl.when(step == 2)
    def _():
        gradient = acc[...] + dot_nt(grad_pair[:, width:], weight[...])
        unit_rows = unit[...]
        grad_res[...] = grad_mid[...] + norm_input_gradient(
            gradient, unit_rows, inv[:, 0:1], rows[0:1, :]
        )
        sums[...] = jnp.zeros_like(sums)
        sums[0:1, :] = rows_sum(gradient * unit_rows)
        sums[1:2, :] = rows_sum(gradient)
        sums[2:3, :] = rows_sum(grad_query[...])
        sums[3:4, :] = rows_sum(grad_pair[:, width:])


def projection_backward(grad_query, grad_pair, attn_weight, unit, inv, rows, grad_mid):
    tok, width = grad_query.shape
    return pl.pallas_call(
        projection_backward_kernel,
        name="projection_backward",
        grid=(3,),
        in_specs=[
            whole((tok, width)),
            whole((tok, 2 * width)),
            pl.BlockSpec((width, width), lambda step: (0, step)),
            whole((tok, width)),
            whole((tok, 128)),
            whole(rows.shape),
            whole((tok, width)),
        ],
        out_specs=[whole((tok, width)), whole((8, width))],
        out_shape=[
            jax.ShapeDtypeStruct((tok, width), jnp.float32),
            jax.ShapeDtypeStruct((8, width), jnp.float32),
        ],
        scratch_shapes=[pltpu.VMEM((tok, width), jnp.float32)],
        compiler_params=pltpu.CompilerParams(vmem_limit_bytes=58 * mib),
    )(grad_query, grad_pair, attn_weight, unit, inv, rows, grad_mid)


class Stream:
    def __init__(self, source, held, sems, chunks):
        self.held, self.chunks = held, chunks
        self.copies = [
            pltpu.make_async_copy(
                source.at[:, pl.ds(first, count)], held.at[k % 2, :, pl.ds(0, count)], sems.at[k]
            )
            for k, (first, count) in enumerate(chunks)
        ]

    def start(self, k):
        if k < len(self.chunks):
            self.copies[k].start()

    def take(self, k):
        self.copies[k].wait()
        return self.held[k % 2, :, : self.chunks[k][1]]


def mlp_forward_kernel(
    chunks, attended, residual, attn_weight, rows, up_weight, up_shift, down_weight,
    residual_out, hidden_out, inv_out, unit_out, active_out, slope_out,
    out_held, up_held, down_held, active_held, slope_held, sems,
):
    width, count = rows.shape[1], len(chunks)
    load = pltpu.make_async_copy(attn_weight.at[:, pl.ds(3 * width, width)], out_held, sems.at[4, 0])
    load.start()
    up = Stream(up_weight, up_held, sems.at[0], chunks)
    down = Stream(down_weight, down_held, sems.at[1], chunks)
    up.start(0)
    down.start(0)
    up.start(1)
    load.wait()
    middle = residual[...].astype(jnp.float32) + rows[4:5, :] + dot_nn(attended[...], out_held[...])
    residual_out[...] = middle + rows[5:6, :]
    unit_rows, inv_scale = unit_of(middle)
    unit_out[...] = unit_rows
    inv_out[...] = jnp.broadcast_to(inv_scale, inv_out.shape)
    hidden_out[...] = (unit_rows * rows[6:7, :] + rows[7:8, :]).astype(hidden_out.dtype)
    ahead = dot_nn(hidden_out[...], up.take(0))
    stores = []
    for k, (first, lanes) in enumerate(chunks):
        now = ahead
        columns = pl.ds(first, lanes)
        up.start(k + 2)
        down.start(k + 1)
        if k + 1 < count:
            ahead = dot_nn(hidden_out[...], up.take(k + 1))
        value, slope = gelu_and_slope(now + up_shift[:, columns])
        active_held[:, columns] = value.astype(active_held.dtype)
        slope_held[:, columns] = slope.astype(slope_held.dtype)
        for row, held, target in ((2, active_held, active_out), (3, slope_held, slope_out)):
            store = pltpu.make_async_copy(
                held.at[:, columns], target.at[:, columns], sems.at[row, k]
            )
            store.start()
            stores.append(store)
        residual_out[...] += dot_nt(active_held[:, columns], down.take(k))
    for store in stores:
        store.wait()


def mlp_forward(attended, residual, attn_weight, rows, up_weight, up_shift, down_weight):
    tok, width = attended.shape
    columns = up_shift.shape[1]
    chunks = chunks_of(columns)
    hidden = (jax.ShapeDtypeStruct((tok, columns), jnp.bfloat16), anywhere())
    weight_chunk = pltpu.VMEM((2, width, chunks[0][1]), jnp.bfloat16)
    hidden_held = pltpu.VMEM((tok, columns), jnp.bfloat16)
    return dense_call(
        functools.partial(mlp_forward_kernel, chunks),
        "mlp_forward",
        [in_vmem(), in_vmem(), anywhere(), in_vmem(), anywhere(), in_vmem(), anywhere()],
        [
            kept((tok, width), jnp.float32),
            kept((tok, width)),
            kept((tok, 128), jnp.float32),
            kept((tok, width), jnp.float32),
            hidden,
            hidden,
        ],
        [pltpu.VMEM((width, width), jnp.bfloat16)]
        + [weight_chunk] * 2
        + [hidden_held] * 2
        + [pltpu.SemaphoreType.DMA((5, len(chunks)))],
        attended,
        residual,
        attn_weight,
        rows,
        up_weight,
        up_shift,
        down_weight,
    )


def mlp_backward_kernel(
    chunks, grad_res, down_weight, slope, up_weight, unit, inv, rows, attn_weight,
    grad_pre, up_sum, grad_branch, grad_mid, grad_attn, grad_attended, sums,
    out_held, up_held, down_held, pre_held, acc, sems,
):
    width, count = rows.shape[1], len(chunks)
    down = Stream(down_weight, down_held, sems.at[1], chunks)
    up = Stream(up_weight, up_held, sems.at[0], chunks)
    down.start(0)
    up.start(0)
    down.start(1)
    load = pltpu.make_async_copy(attn_weight.at[:, pl.ds(3 * width, width)], out_held, sems.at[3, 0])
    load.start()
    grad_branch[...] = grad_res[...].astype(grad_branch.dtype)
    acc[...] = jnp.zeros_like(acc)
    ahead = dot_nn(grad_branch[...], down.take(0))
    stores = []
    for k, (first, lanes) in enumerate(chunks):
        now = ahead
        columns = pl.ds(first, lanes)
        down.start(k + 2)
        up.start(k + 1)
        if k + 1 < count:
            ahead = dot_nn(grad_branch[...], down.take(k + 1))
        low = (now * slope[:, columns].astype(jnp.float32)).astype(jnp.bfloat16)
        pre_held[:, columns] = low
        up_sum[:, columns] = rows_sum(low)
        store = pltpu.make_async_copy(
            pre_held.at[:, columns], grad_pre.at[:, columns], sems.at[2, k]
        )
        store.start()
        stores.append(store)
        acc[...] += dot_nt(pre_held[:, columns], up.take(k))
    gradient = acc[...]
    unit_rows = unit[...]
    middle = grad_res[...].astype(jnp.float32) + norm_input_gradient(
        gradient, unit_rows, inv[:, 0:1], rows[6:7, :]
    )
    grad_mid[...] = middle
    grad_attn[...] = middle.astype(grad_attn.dtype)
    load.wait()
    grad_attended[...] = dot_nt(grad_attn[...], out_held[...]).astype(grad_attended.dtype)
    sums[...] = jnp.zeros_like(sums)
    sums[0:1, :] = rows_sum(gradient * unit_rows)
    sums[1:2, :] = rows_sum(gradient)
    sums[2:3, :] = rows_sum(grad_attn[...])
    sums[3:4, :] = rows_sum(grad_branch[...])
    for store in stores:
        store.wait()


def mlp_backward(grad_res, down_weight, slope, up_weight, unit, inv, rows, attn_weight):
    tok, width = grad_res.shape
    columns = slope.shape[1]
    chunks = chunks_of(columns)
    weight_chunk = pltpu.VMEM((2, width, chunks[0][1]), jnp.bfloat16)
    return dense_call(
        functools.partial(mlp_backward_kernel, chunks),
        "mlp_backward",
        [in_vmem(), anywhere(), in_vmem(), anywhere(), in_vmem(), in_vmem(), in_vmem(), anywhere()],
        [
            (jax.ShapeDtypeStruct((tok, columns), jnp.bfloat16), anywhere()),
            kept((1, columns), jnp.float32),
            kept((tok, width)),
            kept((tok, width), jnp.float32),
            kept((tok, width)),
            kept((tok, width)),
            kept((8, width), jnp.float32),
        ],
        [pltpu.VMEM((width, width), jnp.bfloat16)]
        + [weight_chunk] * 2
        + [
            pltpu.VMEM((tok, columns), jnp.bfloat16),
            pltpu.VMEM((tok, width), jnp.float32),
            pltpu.SemaphoreType.DMA((4, len(chunks))),
        ],
        grad_res,
        down_weight,
        slope,
        up_weight,
        unit,
        inv,
        rows,
        attn_weight,
    )


def adam_step(weight_now, gradient, first_old, second_old):
    first_new = beta_first * first_old + (1.0 - beta_first) * gradient
    second_new = beta_second * second_old + (1.0 - beta_second) * gradient * gradient
    first_hat = first_new / (1.0 - beta_first**STEP)
    second_hat = second_new / (1.0 - beta_second**STEP)
    update = -learn_rate * (
        first_hat / (jnp.sqrt(second_hat) + eps_adam)
        + weight_decay * weight_now.astype(jnp.float32)
    )
    return (first_new, second_new, update)


def round_up(count, unit):
    return -(-count // unit) * unit


def per_device(
    inputs, image_ids, token_mask, cotangent,
    w_qkv, w_out, w_up, w_down, norm_gains, bias_rows, up_bias,
    first_qkv, first_out, first_up, first_down, first_gains, first_bias, first_upbias,
    second_qkv, second_out, second_up, second_down, second_gains, second_bias, second_upbias,
):
    tok, width = inputs.shape
    layers, _, hidden_width = w_up.shape
    places = lax.axis_size("seq")
    place = lax.axis_index("seq")
    layout = Layout(lax.axis_size("dp"), places, width)
    group_tok = tok * places
    spare_count = group_tok - group_tok // IMG * IMG
    left = round_up(IMG - 1 + spare_count, 16)
    right = round_up(IMG - 1, 16)
    tile = tok // 2

    reach = Reach(tok, left, right)

    half = hidden_width // 2
    half_pad = round_up(half + 8 * layers, 128)
    wide_columns = 2 * half_pad

    def spread(array):
        pad = [(0, 0)] * (array.ndim - 1) + [(0, half_pad - half)]
        return jnp.concatenate([jnp.pad(array[..., :half], pad), jnp.pad(array[..., half:], pad)], -1)

    def unspread(array):
        return jnp.concatenate(
            [array[..., :half], array[..., half_pad : half_pad + half]], axis=-1
        )

    def filled(array, rows, columns):
        return jnp.pad(array, ((0, rows - array.shape[0]), (0, columns - array.shape[1])))

    attn_columns = layout.columns(4 * width, False)
    up_columns = layout.columns(wide_columns, True)
    down_columns = layout.columns(wide_columns, False)
    rows_of = jnp.concatenate([norm_gains.reshape(-1, layout.rows), bias_rows.reshape(-1, layout.rows)])
    row_count = rows_of.shape[0]
    shards = []
    for layer in range(layers):
        attn_shard = jnp.concatenate([w_qkv[layer], w_out[layer]], axis=1)
        up_shard = spread(w_up[layer])
        if layer == 0:
            up_shard = up_shard.at[:, half : half + row_count].set(rows_of.T)
        down_shard = spread(w_down[layer].T)
        shards += [
            filled(attn_shard, layout.padded, attn_columns),
            filled(up_shard, layout.padded, up_columns),
            filled(down_shard, layout.padded, down_columns if layer else up_columns),
        ]
    word = jnp.broadcast_to(image_ids[:, None], (tok, 128))
    def gather(layer, which):
        return gather_work(layout, shards[3 * layer + which], which == 1 or (which == 2 and layer == 0))

    gathered = [[None] * 3 for _ in range(layers)]
    begun = [(layer, which) for layer in range(layers) for which in range(3)]
    *results, (window_word, *_) = exchange(
        "gather_parameters",
        layout,
        [gather(*spot) for spot in begun] + [window_work(layout, reach, word)],
        [[index] for index in range(len(begun))] + [[1]],
        40,
    )
    for (layer, which), (matrix,) in zip(begun, results):
        gathered[layer][which] = matrix
    window_word = window_word[:, 0]
    all_rows = gathered[0][1][:, half : half + row_count].T.astype(jnp.float32)
    gains = all_rows[: 2 * layers].reshape(layers, 2, width)
    shifts = all_rows[2 * layers :].reshape(layers, 6, width)
    vectors = jnp.concatenate(
        [gains[:, :1], shifts[:, :1], shifts[:, 2:], gains[:, 1:], shifts[:, 1:2]], axis=1
    )
    up_shift = spread(up_bias.astype(jnp.float32))[:, None, :]

    plan, own_code = attention_plan(
        tile, left, right, image_ids, token_mask, window_word, place, places
    )

    residual = inputs
    kept_layers = []
    for layer in range(layers):
        attn_weight, up_weight, down_weight = gathered[layer]
        rows = vectors[layer]
        normed_low, inv_one, queries, key_value, unit_one = projection_forward(
            residual, rows, attn_weight
        )
        ((window, *_),) = exchange(
            "fetch_window", layout, [window_work(layout, reach, key_value)], [[0]], 20
        )
        attended, lse = attention_forward(tile, left, plan, queries, window, own_code)
        residual, hidden_low, inv_two, unit_two, active, slope = mlp_forward(
            attended, residual, attn_weight, rows, up_weight, up_shift[layer], down_weight
        )
        kept_layers.append(
            (window, unit_one, inv_one, normed_low, queries, lse, attended,
             unit_two, inv_two, hidden_low, slope, active)
        )

    def reduce(works, turns):
        left_operands = pltpu.VMEM((2, 2, width, tok), jnp.bfloat16)
        right_operands = pltpu.VMEM((2, tok, max(attn_columns, up_columns) // 2), jnp.bfloat16)
        operands = [left_operands, right_operands]
        results = exchange("reduce_gradients", layout, works, turns, 63, operands)
        return [result[0] for result in results]

    def packed(rows):
        flat = jnp.concatenate([row.reshape(-1) for row in rows])
        return jnp.pad(flat, (0, -flat.size % 1024)).reshape(-1, 128)

    grad_res = cotangent
    owned = [[None] * 3 for _ in range(layers)]
    row_grads = [None] * layers
    upbias_grads = [None] * layers
    for layer in reversed(range(layers)):
        (window, unit_one, inv_one, normed_low, queries, lse, attended,
         unit_two, inv_two, hidden_low, slope, active) = kept_layers[layer]
        attn_weight, up_weight, down_weight = gathered[layer]
        rows = vectors[layer]
        grad_pre, up_sum, grad_branch, grad_mid, grad_attn, grad_attended, second_sums = (
            mlp_backward(
                grad_res, down_weight, slope, up_weight, unit_two, inv_two, rows, attn_weight
            )
        )
        upbias_grads[layer] = unspread(up_sum[0])
        grad_query, grad_window = attention_backward(
            tile, left, plan, queries, window, grad_attended, lse, own_code
        )
        works = [owned_work(layout, reach, grad_window)]
        reduce_up = reduce_work(layout, [hidden_low.T], grad_pre, True)
        reduce_down = reduce_work(layout, [grad_branch.T], active, True)
        if layer > 0:
            works += [reduce_up, reduce_down]
            results = reduce(works, [[0], [0], [1]])
            grad_key_value, owned[layer][1], owned[layer][2] = results
        else:
            small = packed([*upbias_grads, *row_grads[1:]])
            works += [waiting, reduce_up, sum_work(layout, small)]
            results = reduce(works, [[0], [0], [1], [3, 5, 7, 8, 9]])
            grad_key_value, owned[1][0], owned[0][1], small_sum = results
        grad_res, first_sums = projection_backward(
            grad_query, grad_key_value, attn_weight, unit_one, inv_one, rows, grad_mid
        )
        row_grads[layer] = jnp.stack(
            [
                first_sums[0], second_sums[0], first_sums[1], second_sums[1],
                first_sums[2], first_sums[3], second_sums[2], second_sums[3],
            ]
        )
        grad_proj = jnp.concatenate([grad_query, grad_key_value], axis=1)
        grad_side = filled(jnp.concatenate([grad_proj, grad_attn], axis=1), tok, attn_columns)
        waiting = reduce_work(
            layout, [normed_low.T, attended.T], grad_side, False, 3 * width
        )
        if layer == 0:
            works = [reduce_down, waiting, sum_work(layout, packed(row_grads[:1]))]
            owned[0][2], owned[0][0], row_sum = reduce(works, [[0], [1], [2, 4, 6, 8, 10]])

    flat = small_sum.reshape(-1)
    upbias_grads = flat[: layers * hidden_width].reshape(layers, hidden_width)
    later = flat[layers * hidden_width :][: (layers - 1) * 8 * width].reshape(-1, 8, width)
    row_sums = jnp.concatenate([row_sum.reshape(-1)[: 8 * width].reshape(1, 8, width), later])
    seat = lax.axis_index("dp") * places + place
    row_sums = lax.dynamic_slice_in_dim(row_sums, seat * layout.rows, layout.rows, axis=2)

    def stacked(part):
        return jnp.stack([part(*owned[layer]) for layer in range(layers)], axis=1)

    rows = layout.rows
    grads = (
        stacked(lambda attn, up, down: attn[:rows, : 3 * width]),
        stacked(lambda attn, up, down: attn[:rows, 3 * width : 4 * width]),
        stacked(lambda attn, up, down: unspread(up[:rows])),
        stacked(lambda attn, up, down: unspread(down[:rows])),
        row_sums[:, :2],
        row_sums[:, 2:],
        upbias_grads,
    )
    there = ((1, 0, 2), (1, 0, 2), (1, 0, 2), (2, 0, 1)) + ((0, 1, 2),) * 2 + ((0, 1),)
    back = ((1, 0, 2), (1, 0, 2), (1, 0, 2), (1, 2, 0)) + ((0, 1, 2),) * 2 + ((0, 1),)

    def turned(arrays, orders):
        return tuple(jnp.transpose(array, order) for array, order in zip(arrays, orders))

    params = (w_qkv, w_out, w_up, w_down, norm_gains, bias_rows, up_bias)
    firsts = (first_qkv, first_out, first_up, first_down, first_gains, first_bias, first_upbias)
    seconds = (
        second_qkv, second_out, second_up, second_down, second_gains, second_bias, second_upbias,
    )
    states = [turned(arrays, there) for arrays in (params, firsts, seconds)]
    results = [
        adam_step(param, gradient, first, second)
        for param, gradient, first, second in zip(states[0], grads, states[1], states[2])
    ]
    grads = turned(grads, back)
    return (
        (residual, grad_res)
        + grads
        + turned([result[0] for result in results], back)
        + turned([result[1] for result in results], back)
        + turned([result[2] for result in results], back)
    )


def solution(mesh):
    in_specs = (
        P(("dp", "seq"), None),
        P(("dp", "seq")),
        P(("dp", "seq")),
        P(("dp", "seq"), None),
        P(None, ("dp", "seq"), None),
        P(None, ("dp", "seq"), None),
        P(None, ("dp", "seq"), None),
        P(None, None, ("dp", "seq")),
        P(None, None, ("dp", "seq")),
        P(None, None, ("dp", "seq")),
        P(),
        P(None, ("dp", "seq"), None),
        P(None, ("dp", "seq"), None),
        P(None, ("dp", "seq"), None),
        P(None, None, ("dp", "seq")),
        P(None, None, ("dp", "seq")),
        P(None, None, ("dp", "seq")),
        P(),
        P(None, ("dp", "seq"), None),
        P(None, ("dp", "seq"), None),
        P(None, ("dp", "seq"), None),
        P(None, None, ("dp", "seq")),
        P(None, None, ("dp", "seq")),
        P(None, None, ("dp", "seq")),
        P(),
    )
    out_specs = (
        P(("dp", "seq"), None),
        P(("dp", "seq"), None),
        P(None, ("dp", "seq"), None),
        P(None, ("dp", "seq"), None),
        P(None, ("dp", "seq"), None),
        P(None, None, ("dp", "seq")),
        P(None, None, ("dp", "seq")),
        P(None, None, ("dp", "seq")),
        P(),
        P(None, ("dp", "seq"), None),
        P(None, ("dp", "seq"), None),
        P(None, ("dp", "seq"), None),
        P(None, None, ("dp", "seq")),
        P(None, None, ("dp", "seq")),
        P(None, None, ("dp", "seq")),
        P(),
        P(None, ("dp", "seq"), None),
        P(None, ("dp", "seq"), None),
        P(None, ("dp", "seq"), None),
        P(None, None, ("dp", "seq")),
        P(None, None, ("dp", "seq")),
        P(None, None, ("dp", "seq")),
        P(),
        P(None, ("dp", "seq"), None),
        P(None, ("dp", "seq"), None),
        P(None, ("dp", "seq"), None),
        P(None, None, ("dp", "seq")),
        P(None, None, ("dp", "seq")),
        P(None, None, ("dp", "seq")),
        P(),
    )
    return jax.shard_map(
        per_device, mesh=mesh, in_specs=in_specs, out_specs=out_specs, check_vma=False
    )
```

```python
import functools
import math

import jax
import jax.numpy as jnp
from jax import lax
from jax.experimental import layout as array_layout
from jax.experimental import pallas as pl
from jax.experimental.pallas import tpu as pltpu
from jax.sharding import PartitionSpec as P

HEADS = 16
IMG = 729
STEP = 8

eps_norm = 1e-06
beta_first = 0.9
beta_second = 0.95
learn_rate = 0.025
weight_decay = 0.1
eps_adam = 1e-08
gelu_rate = math.sqrt(2.0 / math.pi)
gelu_cube = 0.044715
span_len = 768
lane_pair = 256
masked_score = -1e30
mib = 2**20


def head_lanes(head, head_size, width):
    low = head * head_size
    first = jnp.minimum(low // 128 * 128, width - lane_pair)
    lanes = lax.broadcasted_iota(jnp.int32, (1, lane_pair), 1)
    inside = (lanes >= low - first) & (lanes < low - first + head_size)
    keys = pl.ds(pl.multiple_of(first, 128), lane_pair)
    values = pl.ds(pl.multiple_of(first + width, 128), lane_pair)
    return keys, values, inside


def valid_lanes(start):
    lanes = lax.broadcasted_iota(jnp.int32, (1, span_len), 1)
    return (lanes >= start) & (lanes < start + IMG)


def dot_nn(left, right):
    return lax.dot_general(left, right, (((1,), (0,)), ((), ())), preferred_element_type=jnp.float32)


def dot_nt(left, right):
    return lax.dot_general(left, right, (((1,), (1,)), ((), ())), preferred_element_type=jnp.float32)


def dot_tn(left, right):
    return lax.dot_general(left, right, (((0,), (0,)), ((), ())), preferred_element_type=jnp.float32)


def attention_forward_kernel(
    tile, left, exp_scale, plan, query, window, own_code, out, lse_out, bias, mix
):
    tok, width = query.shape
    head_size = width // HEADS

    def one_span(tile_index, which):
        spot = 2 * tile_index + which
        offset, image = pl.multiple_of(plan[0, spot], 16), plan[1, spot]
        valid = valid_lanes(plan[2, spot])
        rows = pl.ds(pl.multiple_of(tile_index * tile, 16), tile)
        own_rows = pl.ds(pl.multiple_of(left + tile_index * tile, 16), tile)
        span = pl.ds(offset, span_len)
        code = own_code[rows, :]
        row_image = jnp.maximum(code, -code)
        mine = row_image == image
        bias[...] = jnp.where(mine & valid, 0.0, masked_score)
        self_bias = jnp.where(code < 0, 0.0, masked_score)
        lse_lane = lax.broadcasted_iota(jnp.int32, (tile, lse_out.shape[1]), 1)

        def one_head(head, carry):
            lanes, value_lanes, inside = head_lanes(head, head_size, width)
            queries = jnp.where(inside, query[rows, lanes], 0)
            scores = dot_nt(queries, window[span, lanes]) * exp_scale + bias[...]
            own_key = window[own_rows, lanes].astype(jnp.float32)
            own_value = window[own_rows, value_lanes].astype(jnp.float32)
            self_score = (
                jnp.sum(queries.astype(jnp.float32) * own_key, axis=1, keepdims=True) * exp_scale
                + self_bias
            )
            top = jnp.maximum(jnp.max(scores, axis=1, keepdims=True), self_score)
            powers = jnp.exp2(scores - top)
            self_power = jnp.exp2(self_score - top)
            total = jnp.sum(powers, axis=1, keepdims=True) + self_power
            mixed = dot_nn(powers.astype(jnp.bfloat16), window[span, value_lanes])
            mixed = (mixed + self_power * own_value) / total
            mix[rows, lanes] = jnp.where(inside & mine, mixed, mix[rows, lanes])
            lse_out[rows, :] = jnp.where(
                (lse_lane == head) & mine, top + jnp.log2(total), lse_out[rows, :]
            )
            return carry

        lax.fori_loop(0, HEADS, one_head, 0, unroll=8)

    def one_tile(tile_index, carry):
        one_span(tile_index, 0)

        @pl.when(plan[1, 2 * tile_index] != plan[1, 2 * tile_index + 1])
        def _():
            one_span(tile_index, 1)

        return carry

    lax.fori_loop(0, tok // tile, one_tile, 0)
    out[...] = mix[...].astype(out.dtype)


def dot_fine(left, right, contract):
    high = left.astype(jnp.bfloat16)
    low = (left - high.astype(jnp.float32)).astype(jnp.bfloat16)
    numbers = (contract, ((), ()))
    product = lax.dot_general(high, right, numbers, preferred_element_type=jnp.float32)
    return product + lax.dot_general(low, right, numbers, preferred_element_type=jnp.float32)


def attention_backward_kernel(
    tile, left, exp_scale, plan, query, window, grad, lse_in, own_code, row_code,
    grad_query, grad_window, bias, acc_query, acc_window, self_rows, lse_rows, inner_rows, square,
):
    tok, width = query.shape
    head_size = width // HEADS
    scale = 1.0 / math.sqrt(head_size)
    acc_query[...] = jnp.zeros_like(acc_query)
    acc_window[...] = jnp.zeros_like(acc_window)
    square[...] = jnp.zeros_like(square)
    head_of = lax.broadcasted_iota(jnp.int32, (128, width), 1) // head_size
    spread = (head_of == lax.broadcasted_iota(jnp.int32, (128, width), 0)).astype(jnp.bfloat16)

    def turned(columns):
        square[:tile, :] = columns
        return square[...].T[:, :tile]

    def one_span(tile_index, which):
        spot = 2 * tile_index + which
        offset, image = pl.multiple_of(plan[0, spot], 16), plan[1, spot]
        rows = pl.ds(pl.multiple_of(tile_index * tile, 16), tile)
        span = pl.ds(offset, span_len)
        code = row_code[tile_index]
        mine = jnp.maximum(code, -code) == image
        place = lax.broadcasted_iota(jnp.int32, (span_len, 1), 0)
        valid = (place >= plan[2, spot]) & (place < plan[2, spot] + IMG)
        bias[...] = jnp.where(mine & valid, 0.0, masked_score)

        def one_head(head, carry):
            lanes, value_lanes, inside = head_lanes(head, head_size, width)
            queries = jnp.where(inside, query[rows, lanes], 0)
            grads = jnp.where(inside, grad[rows, lanes], 0)
            keys = window[span, lanes]
            this = pl.ds(head, 1)
            scores = dot_nt(keys, queries) * exp_scale + bias[...]
            prob = jnp.exp2(scores - lse_rows[this, :])
            grad_prob = dot_nt(window[span, value_lanes], grads)
            inner = jnp.sum(prob * grad_prob, axis=0, keepdims=True) + self_rows[this, :]
            inner_rows[this, :] = jnp.where(mine, inner, inner_rows[this, :])
            grad_scores = (prob * (grad_prob - inner)).astype(jnp.bfloat16)
            acc_window[span, lanes] += dot_nn(grad_scores, queries)
            acc_window[span, value_lanes] += dot_nn(prob.astype(jnp.bfloat16), grads)
            part = dot_tn(grad_scores, keys)
            acc_query[rows, lanes] += jnp.where(inside, part, 0.0)
            return carry

        lax.fori_loop(0, HEADS, one_head, 0, unroll=8)

    def one_tile(tile_index, carry):
        rows = pl.ds(pl.multiple_of(tile_index * tile, 16), tile)
        own_rows = pl.ds(pl.multiple_of(left + tile_index * tile, 16), tile)
        queries, grads = query[rows, :].astype(jnp.float32), grad[rows, :].astype(jnp.float32)
        own_key = window[own_rows, :width].astype(jnp.float32)
        own_value = window[own_rows, width:].astype(jnp.float32)
        self_score = dot_fine(queries * own_key, spread, ((1,), (1,))) * exp_scale
        self_grad = dot_fine(grads * own_value, spread, ((1,), (1,)))
        lse = lse_in[rows, :]
        self_prob = jnp.where(own_code[rows, :] < 0, jnp.exp2(self_score - lse), 0.0)
        self_rows[...] = turned(self_prob * self_grad)
        lse_rows[...] = turned(lse)
        one_span(tile_index, 0)

        @pl.when(plan[1, 2 * tile_index] != plan[1, 2 * tile_index + 1])
        def _():
            one_span(tile_index, 1)

        inner = inner_rows[...].T
        self_change = self_prob * (self_grad - inner[:tile, :])
        change = dot_fine(self_change, spread, ((1,), (0,)))
        acc_query[rows, :] += change * own_key
        acc_window[own_rows, :width] += change * queries
        acc_window[own_rows, width:] += dot_fine(self_prob, spread, ((1,), (0,))) * grads
        return carry

    inner_rows[...] = jnp.zeros_like(inner_rows)
    lax.fori_loop(0, tok // tile, one_tile, 0)
    grad_query[...] = (acc_query[...] * scale).astype(grad_query.dtype)
    step = 16

    def narrow(index, carry):
        rows = pl.ds(pl.multiple_of(index * step, step), step)
        grad_window[rows, :width] = (acc_window[rows, :width] * scale).astype(grad_window.dtype)
        grad_window[rows, width:] = acc_window[rows, width:].astype(grad_window.dtype)
        return carry

    lax.fori_loop(0, acc_window.shape[0] // step, narrow, 0)


def in_vmem():
    return pl.BlockSpec(memory_space=pltpu.VMEM)


def attention_forward(tile, left, plan, query, window, own_code):
    tok, width = query.shape
    exp_scale = math.log2(math.e) / math.sqrt(width // HEADS)
    return pl.pallas_call(
        functools.partial(attention_forward_kernel, tile, left, exp_scale),
        name="attention_forward",
        out_shape=[
            jax.ShapeDtypeStruct((tok, width), jnp.bfloat16),
            jax.ShapeDtypeStruct((tok, 128), jnp.float32),
        ],
        in_specs=[pl.BlockSpec(memory_space=pltpu.SMEM)] + [in_vmem()] * 3,
        out_specs=[in_vmem()] * 2,
        scratch_shapes=[
            pltpu.VMEM((tile, span_len), jnp.float32),
            pltpu.VMEM((tok, width), jnp.float32),
        ],
        compiler_params=pltpu.CompilerParams(vmem_limit_bytes=60 * mib),
    )(plan, query, window, own_code)


def attention_backward(tile, left, plan, query, window, grad, lse, own_code):
    tok, width = query.shape
    exp_scale = math.log2(math.e) / math.sqrt(width // HEADS)
    return pl.pallas_call(
        functools.partial(attention_backward_kernel, tile, left, exp_scale),
        name="attention_backward",
        out_shape=[
            jax.ShapeDtypeStruct((tok, width), jnp.bfloat16),
            jax.ShapeDtypeStruct(window.shape, jnp.bfloat16),
        ],
        in_specs=[pl.BlockSpec(memory_space=pltpu.SMEM)] + [in_vmem()] * 6,
        out_specs=[in_vmem()] * 2,
        scratch_shapes=[
            pltpu.VMEM((span_len, tile), jnp.float32),
            pltpu.VMEM((tok, width), jnp.float32),
            pltpu.VMEM(window.shape, jnp.float32),
            pltpu.VMEM((128, tile), jnp.float32),
            pltpu.VMEM((128, tile), jnp.float32),
            pltpu.VMEM((128, tile), jnp.float32),
            pltpu.VMEM((-(-tile // 128) * 128, 128), jnp.float32),
        ],
        compiler_params=pltpu.CompilerParams(vmem_limit_bytes=62 * mib),
    )(plan, query, window, grad, lse, own_code, own_code.reshape(tok // tile, 1, tile))


def attention_plan(tile, left, right, own_ids, own_mask, window_ids, place, places):
    tok = own_ids.shape[0]
    window_len = left + tok + right
    room = jnp.minimum(window_len, left + (places - place) * tok) - span_len
    position = jnp.arange(window_len)
    ids = jnp.where(position < left - place * tok, -1, window_ids)
    images = own_ids.reshape(tok // tile, tile)[:, :: tile - 1].reshape(-1)
    before = (ids[None, :] < images[:, None]) & (position < left + tok)[None, :]
    starts = jnp.sum(before.astype(jnp.int32), axis=1)
    offsets = jnp.minimum(starts // 16 * 16, room)
    plan = jnp.stack([offsets, images + 1, starts - offsets]).astype(jnp.int32)
    own_code = jnp.where(own_mask > 0, own_ids + 1, -(own_ids + 1)).astype(jnp.int32)[:, None]
    return plan, own_code


class Layout:
    def __init__(self, groups, seats, model_width):
        self.rows = model_width // (groups * seats)
        self.members = 2
        while self.members * self.rows % 16:
            self.members *= 2
        self.sides = self.members // 2
        self.lines = seats // self.members
        self.slab = self.members * self.rows
        self.padded = -(-self.rows // 16) * 16
        self.near = model_width // groups
        self.model_width = model_width

    def blocks(self, one_block):
        return 2 if one_block else 2 * self.sides

    def columns(self, columns, one_block):
        unit = 128 * self.blocks(one_block)
        return -(-columns // unit) * unit


class Mail:
    def __init__(self, layout, send, recv, slots):
        self.layout, self.send_sems, self.recv_sems, self.slots = layout, send, recv, slots
        self.group = lax.axis_index("dp")
        seat = lax.axis_index("seq")
        self.line = seat // layout.members
        self.member = seat % layout.members
        self.side = self.member // 2
        self.core = self.member % 2
        self.started = {}

    def at(self, group=None, line=None, side=None, core=None):
        group = self.group if group is None else group
        line = self.line if line is None else line
        side = self.side if side is None else side
        core = self.core if core is None else core
        return (group, line * self.layout.members + side * 2 + core)

    def copy(self, slot, source, target, device, shift=0):
        index = self.slots[slot] + shift
        return pltpu.make_async_remote_copy(
            src_ref=source,
            dst_ref=target,
            send_sem=self.send_sems.at[index],
            recv_sem=self.recv_sems.at[index],
            device_id=device,
            device_id_type=pl.DeviceIdType.MESH,
        )

    def send(self, slot, source, target, device, when=None):
        copy = self.copy(slot, source, target, device)
        self.started[slot] = (copy, when)
        guarded(when, copy.start)

    def wait(self, slot, target, shift=0):
        self.copy(slot, target, target, self.at(core=1 - self.core), shift).wait_recv()

    def settle(self, slot):
        copy, when = self.started.pop(slot)
        guarded(when, copy.wait_send)

    def finish(self):
        for slot in list(self.started):
            self.settle(slot)


class Desk:
    def __init__(self, mail, index, local):
        self.mail, self.index, self.local_sems = mail, index, local
        self.group, self.line, self.member = mail.group, mail.line, mail.member
        self.side, self.core, self.at = mail.side, mail.core, mail.at

    def send(self, slot, source, target, device, when=None):
        self.mail.send((self.index, slot), source, target, device, when)

    def wait(self, slot, target, shift=0):
        self.mail.wait((self.index, slot), target, shift)

    def settle(self, slot):
        self.mail.settle((self.index, slot))

    def local(self, number, source, target):
        return pltpu.make_async_copy(source, target, self.local_sems.at[number])


class Work:
    def __init__(self, steps, ins, outs, scratch, slots, local):
        self.steps, self.ins, self.outs, self.scratch = steps, ins, outs, scratch
        self.slots, self.local = slots, local


def guarded(when, action):
    if when is None:
        action()
    else:
        pl.when(when)(action)


def all_of(*conditions):
    kept = [condition for condition in conditions if condition is not None]
    return functools.reduce(jnp.logical_and, kept) if kept else None


def run_steps(works, turns):
    queue = []
    for index, (work, first) in enumerate(zip(works, turns)):
        next(work)
        queue.append((first[0], index, 0))
    while queue:
        turn, index, done = min(queue)
        queue.remove((turn, index, done))
        try:
            next(works[index])
        except StopIteration:
            continue
        done += 1
        listed = turns[index]
        queue.append((listed[done] if done < len(listed) else turn + 1, index, done))


def anywhere():
    return pl.BlockSpec(memory_space=pl.ANY)


def exchange(name, layout, works, starts, megabytes, common=()):
    slots = [(index, slot) for index, work in enumerate(works) for slot in work.slots]
    numbers = {slot: index for index, slot in enumerate(slots)}
    ins = [entry for work in works for entry in work.ins]
    outs = [entry for work in works for entry in work.outs]
    scratch = [entry for work in works for entry in work.scratch]

    def kernel(*refs):
        refs = list(refs)

        def take(count):
            taken = refs[:count]
            del refs[:count]
            return taken

        in_refs = [take(len(work.ins)) for work in works]
        out_refs = [take(len(work.outs)) for work in works]
        scratch_refs = [take(len(work.scratch)) for work in works]
        common_refs = take(len(common))
        locals_of = [take(1)[0] for work in works]
        send, recv = refs
        mail = Mail(layout, send, recv, numbers)
        run_steps(
            [
                work.steps(
                    Desk(mail, index, locals_of[index]),
                    in_refs[index],
                    out_refs[index],
                    scratch_refs[index],
                    common_refs,
                )
                for index, work in enumerate(works)
            ],
            starts,
        )
        mail.finish()

    results = pl.pallas_call(
        kernel,
        name=name,
        out_shape=[shape for shape, _ in outs],
        in_specs=[spec for _, spec in ins],
        out_specs=[spec for _, spec in outs],
        scratch_shapes=scratch
        + list(common)
        + [pltpu.SemaphoreType.DMA((work.local,)) for work in works]
        + [pltpu.SemaphoreType.DMA((len(slots),))] * 2,
        compiler_params=pltpu.CompilerParams(
            has_side_effects=True, vmem_limit_bytes=megabytes * mib
        ),
    )(*[array for array, _ in ins])
    results = list(results)
    grouped = []
    for work in works:
        grouped.append(results[: len(work.outs)])
        del results[: len(work.outs)]
    return grouped


def gather_work(layout, shard, one_block, line_last=False):
    lines, members, sides = layout.lines, layout.members, layout.sides
    width = shard.shape[1] // layout.blocks(one_block)
    spots = [("own", 0)]
    for t in range(1, lines):
        spots += [(f"below{t}", -t), (f"above{t}", t)]
    slots = [("mix", j) for j in range(1, members)]
    halves = (0, 1) if line_last else (0,)
    slots += [(way, half, t) for way in ("up", "down") for half in halves for t in range(lines)]
    slots += [("cross", source) for source, _ in (spots[:1] if line_last else spots)]
    slots += [("core", j) for j in range(1 if one_block else sides)]
    if not one_block:
        slots += [
            ("side", half, source, j)
            for half in (0, 1)
            for source, _ in spots
            for j in range(1, sides)
        ]

    def steps(desk, ins, outs, scratch, common):
        (shard,), (out,), (landing, slab, wide) = ins, outs, scratch
        group, line, member, side, core = desk.group, desk.line, desk.member, desk.side, desk.core
        has_up, has_down = line < lines - 1, line > 0

        def columns(side_of, core_of):
            block = core_of if one_block else core_of * sides + side_of
            return pl.ds(pl.multiple_of(block * width, 128), width)

        own = columns(side, core)

        def place(group_of, line_of, lanes=own):
            first = (group_of * lines + line_of) * layout.slab
            return out.at[pl.ds(pl.multiple_of(first, 16), layout.slab), lanes]

        def present(step):
            return None if step == 0 else line >= -step if step < 0 else line < lines - step

        yield
        for j in range(1, members):
            other = (member + j) % members
            desk.send(
                ("mix", j),
                shard.at[:, columns(other // 2, other % 2)],
                landing.at[member],
                desk.at(side=other // 2, core=other % 2),
            )
        mine = desk.local(0, shard.at[:, own], landing.at[member])
        mine.start()
        yield
        for j in range(1, members):
            desk.wait(("mix", j), landing.at[(member + members - j) % members])
        mine.wait()
        for m in range(members):
            rows = slice(m * layout.rows, (m + 1) * layout.rows)
            wide[rows, :] = landing[m, : layout.rows, :].astype(jnp.float32)
        slab[...] = wide[...].astype(slab.dtype)
        keep = desk.local(1, slab, place(group, line))
        keep.start()

        def pass_on(source, what, half, where, when):
            if half == 0 and (source == "own" or not line_last):
                desk.send(("cross", source), what, where, desk.at(group=1 - group), when)
            if not one_block:
                for j in range(1, sides):
                    slot = ("side", half, source, j)
                    desk.send(slot, what, where, desk.at(side=(side + j) % sides), when)

        def along(half, t, what, where, when):
            for way, further, to in (("up", has_up, line + 1), ("down", has_down, line - 1)):
                desk.send((way, half, t), what, where, desk.at(line=to), all_of(when, further))

        home = place(group, line)
        along(0, 0, slab, home, None)
        pass_on("own", slab, 0, home, None)
        yield

        def crossed():
            where = place(1 - group, line)
            desk.wait(("cross", "own"), where)
            pass_on("own", where, 1, where, None)
            if line_last:
                along(1, 0, where, where, None)

        if line_last:
            crossed()
            yield
        for t in range(1, lines):
            for half in halves:
                for way, name, step, further, to in (
                    ("up", "below", -t, has_up, line + 1),
                    ("down", "above", t, has_down, line - 1),
                ):
                    when, where = present(step), place(1 - group if half else group, line + step)
                    guarded(when, functools.partial(desk.wait, (way, half, t - 1), where))
                    desk.send(
                        (way, half, t), where, where, desk.at(line=to), all_of(when, further)
                    )
                    pass_on(f"{name}{t}", where, half, where, when)
            if t == 1 and not line_last:
                crossed()
            yield
        for t in range(1, 1 if line_last else lines):
            for name, step in ((f"below{t}", -t), (f"above{t}", t)):
                when, where = present(step), place(1 - group, line + step)
                guarded(when, functools.partial(desk.wait, ("cross", name), where))
                pass_on(name, where, 1, where, when)
            yield
        keep.wait()
        partner = desk.at(core=1 - core)
        desk.send(("core", 0), out.at[:, own], out.at[:, own], partner)
        if not one_block:
            yield
            for j in range(1, sides):
                theirs = columns((side + sides - j) % sides, core)
                for half, group_of in ((0, group), (1, 1 - group)):
                    for source, step in spots:
                        where = place(group_of, line + step, theirs)
                        slot = ("side", half, source, j)
                        guarded(present(step), functools.partial(desk.wait, slot, where))
                desk.send(("core", j), out.at[:, theirs], out.at[:, theirs], partner)
        yield
        desk.wait(("core", 0), out.at[:, columns(side, 1 - core)])
        if not one_block:
            for j in range(1, sides):
                theirs = columns((side + sides - j) % sides, 1 - core)
                desk.wait(("core", j), out.at[:, theirs])

    low = jnp.bfloat16
    return Work(
        steps,
        [(shard, anywhere())],
        [(jax.ShapeDtypeStruct((layout.model_width, shard.shape[1]), low), anywhere())],
        [
            pltpu.VMEM((members, layout.padded, width), low),
            pltpu.VMEM((layout.slab, width), low),
            pltpu.VMEM((layout.slab, width), jnp.float32),
        ],
        slots,
        2,
    )


def add_rows(target, first, target_columns, source, source_columns, count, source_first=0):
    step = math.gcd(count, 48)

    def one(index, carry):
        rows = pl.ds(pl.multiple_of(first + index * step, 16), step)
        theirs = pl.ds(pl.multiple_of(source_first + index * step, 16), step)
        total = target[rows, target_columns].astype(jnp.float32)
        total += source[theirs, source_columns].astype(jnp.float32)
        target[rows, target_columns] = total.astype(target.dtype)
        return carry

    lax.fori_loop(0, count // step, one, 0)


def reduce_work(layout, lefts, right, one_block, switch=0, split=3):
    lines, members, sides = layout.lines, layout.members, layout.sides
    tok, columns = right.shape
    blocks = layout.blocks(one_block)
    width, half = columns // blocks, columns // 2
    near_rows, slab_rows, low = layout.near, layout.slab, jnp.bfloat16
    count, depth = min(split, width // 128), min(4, lines)
    parts = []
    for index in range(count):
        first = width // 128 * index // count * 128
        parts.append((first, width // 128 * (index + 1) // count * 128 - first))
    order = []
    for t in range(lines):
        goal = lines - 1 - t // 2 if t % 2 == 0 else t // 2
        order.append(goal)
    slots = [("left", k) for k in range(len(lefts))] + ["right"]
    slots += [("cross", part, t) for part in parts for t in range(lines)]
    slots += [
        (way, part, t) for way in ("up", "down") for part in parts for t in range(1, lines)
    ]
    slots += [("mix", j) for j in range(1, members)]
    if not one_block:
        slots += [
            ("side", part, tag, t, j)
            for part in parts
            for tag in (0, 1)
            for t in range(lines)
            for j in range(1, sides)
        ]

    def steps(desk, ins, outs, scratch, common):
        left_in, right_in = ins[: len(lefts)], ins[len(lefts)]
        out, left_land, right_land = outs[0], outs[1 : 1 + len(lefts)], outs[1 + len(lefts)]
        total, cross, up, down, piece, landing, wide = scratch[:7]
        from_side = None if one_block else scratch[7]
        left_all, right_all = common
        group, line, member, side, core = desk.group, desk.line, desk.member, desk.side, desk.core
        partner = desk.at(core=1 - core)
        own = pl.ds(0 if one_block else pl.multiple_of(side * width, 128), width)
        stay = pl.ds(pl.multiple_of(core * half, 128), half)
        away = pl.ds(pl.multiple_of((1 - core) * half, 128), half)

        def first_of(tag, goal):
            return pl.multiple_of((group if tag else 1 - group) * near_rows + goal * slab_rows, 16)

        yield
        for k, left in enumerate(left_in):
            desk.send(("left", k), left, left_land[k], partner)
        desk.send("right", right_in.at[:, away], right_land, partner)
        yield
        loads = []

        def load(source, target):
            copy = desk.local(len(loads), source, target)
            copy.start()
            loads.append(copy)

        for k, left in enumerate(left_in):
            load(left, left_all.at[k, 0])
        load(right_in.at[:, stay], right_all.at[0, :, pl.ds(0, half)])
        for k in range(len(left_in)):
            desk.wait(("left", k), left_land[k])
            load(left_land[k], left_all.at[k, 1])
        desk.wait("right", right_land)
        load(right_land, right_all.at[1, :, pl.ds(0, half)])
        for copy in loads:
            copy.wait()

        def multiply(tag):
            rows = pl.ds(first_of(tag, 0), near_rows)

            def piece_of(first, lanes, which):
                theirs = pl.ds(first, lanes)
                product = dot_nn(left_all[which, 0, rows, :], right_all[0, :, theirs])
                product += dot_nn(left_all[which, 1, rows, :], right_all[1, :, theirs])
                total[rows, theirs] = product.astype(low)

            lanes = 256 if len(lefts) == 1 else math.gcd(switch, 384)

            def one(index, carry):
                first = pl.multiple_of(index * lanes, 128)
                which = 0
                if len(lefts) > 1:
                    which = jnp.where(core * half + index * lanes >= switch, 1, 0)
                piece_of(first, lanes, which)
                return carry

            lax.fori_loop(0, half // lanes, one, 0)
            if half % lanes:
                piece_of(half // lanes * lanes, half % lanes, 0)

        own_first = 0 if one_block else side * width
        pieces = [
            (part, tag, goal)
            for part in parts
            for tag in ((0,) if one_block else (0, 1))
            for goal in order
        ]

        def lanes_of(part, first):
            return pl.ds(pl.multiple_of(first + part[0], 128), part[1])

        def post(number):
            if number >= len(pieces):
                return
            part, tag, goal = pieces[number]
            if one_block:
                if number >= depth:
                    before = pieces[number - depth]
                    desk.settle(("cross", before[0], before[2]))
                send_across(part, goal)
                return
            rows = pl.ds(first_of(tag, goal), slab_rows)
            for j in range(1, sides):
                if number >= depth:
                    desk.settle(("side", *pieces[number - depth], j))
                other = (side + j) % sides
                desk.send(
                    ("side", part, tag, goal, j),
                    total.at[rows, lanes_of(part, other * width)],
                    from_side.at[j - 1, rows, lanes_of(part, 0)],
                    desk.at(side=other),
                )

        def send_across(part, goal):
            rows = pl.ds(first_of(0, goal), slab_rows)
            desk.send(
                ("cross", part, goal),
                total.at[rows, lanes_of(part, own_first)],
                cross.at[goal, :, lanes_of(part, 0)],
                desk.at(group=1 - group),
            )

        def take_side(part, tag, goal):
            first = first_of(tag, goal)
            rows, lanes = pl.ds(first, slab_rows), lanes_of(part, 0)
            for j in range(1, sides):
                desk.wait(("side", part, tag, goal, j), from_side.at[j - 1, rows, lanes])
            post(pieces.index((part, tag, goal)) + depth)
            for j in range(1, sides):
                add_rows(
                    total, first, lanes_of(part, own_first), from_side.at[j - 1], lanes,
                    slab_rows, first,
                )

        ends = lines - 1 - line

        def part_steps(part):
            lanes, mine = lanes_of(part, 0), lanes_of(part, own_first)
            if not one_block:
                for goal in order:
                    take_side(part, 0, goal)
                    send_across(part, goal)
                    yield
            for goal in order:
                if not one_block:
                    take_side(part, 1, goal)
                desk.wait(("cross", part, goal), cross.at[goal, :, lanes])
                if one_block:
                    post(pieces.index((part, 0, goal)) + depth)
                add_rows(total, first_of(1, goal), mine, cross.at[goal], lanes, slab_rows)
                yield
            for t in range(1, lines):
                for way, buffer, going, fed, goal, to in (
                    ("up", up, line < t, line > 0, lines - t + line, line + 1),
                    ("down", down, ends < t, ends > 0, t - lines + line, line - 1),
                ):
                    first = first_of(1, goal)

                    @pl.when(all_of(going, fed))
                    def _():
                        if t > 1:
                            desk.wait((way, part, t - 1), buffer.at[t - 2, :, lanes])
                            add_rows(total, first, mine, buffer.at[t - 2], lanes, slab_rows)

                    desk.send(
                        (way, part, t),
                        total.at[pl.ds(first, slab_rows), mine],
                        buffer.at[t - 1, :, lanes],
                        desk.at(line=to),
                        going,
                    )
                yield

        multiply(0)
        for number in range(depth):
            post(number)
        yield
        multiply(1)
        yield
        running = [part_steps(part) for part in parts]
        turn, lag = 0, len(pieces) // len(parts)
        while running:
            for index, steps_of in enumerate(running):
                if steps_of is not None and turn >= lag * index:
                    try:
                        next(steps_of)
                    except StopIteration:
                        running[index] = None
            if not any(running):
                break
            turn += 1
            yield
        first = first_of(1, line)
        wide[...] = total[pl.ds(first, slab_rows), own].astype(jnp.float32)
        for way, buffer, fed in (("up", up, line > 0), ("down", down, ends > 0)):

            @pl.when(fed)
            def _():
                for part in parts:
                    where = buffer.at[lines - 2, :, lanes_of(part, 0)]
                    desk.wait((way, part, lines - 1), where)
                wide[...] += buffer[lines - 2].astype(jnp.float32)

        for m in range(members):
            rows = slice(m * layout.rows, (m + 1) * layout.rows)
            piece[m] = jnp.zeros(piece.shape[1:], piece.dtype)
            piece[m, : layout.rows, :] = wide[rows, :].astype(piece.dtype)
        seat = core * sides + side
        for j in range(1, members):
            other = (member + j) % members
            desk.send(
                ("mix", j),
                piece.at[other],
                landing.at[seat],
                desk.at(side=other // 2, core=other % 2),
            )
        landing[seat] = piece[member]
        yield
        for j in range(1, members):
            other = (member + members - j) % members
            desk.wait(("mix", j), landing.at[other % 2 * sides + other // 2])
        if one_block:
            for c in range(2):
                block = landing[c * sides].astype(jnp.float32)
                for s in range(1, sides):
                    block += landing[c * sides + s].astype(jnp.float32)
                out[:, c * width : (c + 1) * width] = block
        else:
            for b in range(blocks):
                out[:, b * width : (b + 1) * width] = landing[b].astype(jnp.float32)

    scratch = [
        pltpu.VMEM((layout.model_width, half), low),
        pltpu.VMEM((lines, slab_rows, width), low),
        pltpu.VMEM((lines - 1, slab_rows, width), low),
        pltpu.VMEM((lines - 1, slab_rows, width), low),
        pltpu.VMEM((members, layout.padded, width), low),
        pltpu.VMEM((members, layout.padded, width), low),
        pltpu.VMEM((slab_rows, width), jnp.float32),
    ]
    if not one_block:
        scratch.append(pltpu.VMEM((sides - 1, layout.model_width, width), low))
    ins = [(array, anywhere()) for array in [*lefts, right]]
    return Work(
        steps,
        ins,
        [(jax.ShapeDtypeStruct((layout.padded, columns), jnp.float32), in_vmem())]
        + [(jax.ShapeDtypeStruct(left.shape, low), anywhere()) for left in lefts]
        + [(jax.ShapeDtypeStruct((tok, half), low), anywhere())],
        scratch,
        slots,
        2 * len(lefts) + 2,
    )


class Reach:
    def __init__(self, tok, left, right):
        self.tok, self.left, self.right = tok, left, right
        self.window = left + tok + right
        self.deltas = [d for d in range(-8, 9) if d != 0 and self.rows(d) > 0]

    def first(self, delta):
        return max(0, self.tok * delta - self.left)

    def rows(self, delta):
        last = min(self.tok, self.tok * delta - self.left + self.window)
        return last - self.first(delta)

    def spot(self, delta):
        return self.first(delta) - self.tok * delta + self.left


def parts_of(count, step=80):
    return [(first, min(step, count - first)) for first in range(0, count, step)]


def window_work(layout, reach, key_value):
    tok, width = key_value.shape
    left, lines, places = reach.left, layout.lines, layout.lines * layout.members
    routed = layout.sides == 2
    pieces, depth = parts_of(tok), 2
    near_below, far_below = reach.spot(2), reach.spot(3)
    tail = (reach.first(3), max(reach.rows(3), 0))
    head = max(reach.rows(-2), 0)
    if routed:
        slots = ["pair", "tail", "share", "wide", "thin", "last"]
        slots += [(name, k) for name in ("right", "left", "climb", "drop") for k in range(len(pieces))]
        slots += [("fall", k) for k in range(len(parts_of(head)))]
    else:
        slots = [("reach", delta) for delta in reach.deltas]

    def direct(desk, own, window):
        seat = desk.line * layout.members + desk.member
        for delta in reach.deltas:
            count = reach.rows(delta)
            desk.send(
                ("reach", delta),
                own.at[pl.ds(reach.first(delta), count)],
                window.at[pl.ds(reach.spot(delta), count)],
                (desk.group, seat + delta),
                (seat + delta >= 0) & (seat + delta < places),
            )
        yield
        for delta in reach.deltas:
            where = window.at[pl.ds(reach.spot(delta), reach.rows(delta))]
            when = (seat - delta >= 0) & (seat - delta < places)
            guarded(when, functools.partial(desk.wait, ("reach", delta), where))

    def by_way(desk, own, window, transit):
        line, core = desk.line, desk.core
        first_side, last_side = desk.side == 0, desk.side == 1
        low_core, high_core = core == 0, core == 1
        has_up, has_down = line < lines - 1, line > 0
        has_before = last_side | has_down
        partner = desk.at(core=1 - core)

        def part(ref, first, count):
            return ref.at[pl.ds(first, count)]

        def post(k):
            if k >= len(pieces):
                return
            if k >= depth:
                desk.settle(("right", k - depth))
                desk.settle(("left", k - depth))
            first, count = pieces[k]
            desk.send(
                ("right", k), part(own, first, count), part(window, near_below + first, count),
                desk.at(side=1), first_side,
            )
            desk.send(
                ("left", k), part(own, first, count), part(transit, first, count),
                desk.at(side=0), last_side,
            )

        for k in range(depth):
            post(k)
        desk.send(
            "tail", part(own, *tail), part(window, far_below, tail[1]),
            desk.at(line=line + 1, core=0), high_core & has_up,
        )
        mirrored = pl.multiple_of(left + (2 * core - 1) * tok, 16)
        desk.send("pair", own, part(window, mirrored, tok), partner)
        yield
        for k, (first, count) in enumerate(pieces):
            ahead = part(transit, first, count)
            guarded(first_side, functools.partial(desk.wait, ("left", k), ahead))
            desk.send(
                ("climb", k), ahead, part(window, near_below + first, count),
                desk.at(line=line + 1), first_side & has_up,
            )
            behind = part(window, near_below + first, count)
            guarded(last_side, functools.partial(desk.wait, ("right", k), behind))
            post(k + depth)
            desk.send(
                ("drop", k), behind, part(window, left + tok + first, count),
                desk.at(line=line - 1, core=1), last_side & has_down & low_core,
            )
            if first < head:
                count = min(count, head - first)
                desk.send(
                    ("fall", k), part(window, near_below + first, count),
                    part(window, left + 2 * tok + first, count),
                    desk.at(line=line - 1), last_side & has_down & high_core,
                )
            yield
        stay = desk.local(1, part(transit, 0, head), part(window, left + 2 * tok, head))
        guarded(first_side, stay.start)
        desk.send(
            "share", transit, part(window, left + tok, tok), partner, first_side & low_core
        )

        def share_before(when):
            desk.send(
                "wide", part(window, near_below, tok), part(window, left - tok, tok), partner,
                when & high_core,
            )
            desk.send(
                "thin", part(window, near_below + tail[0], tail[1]),
                part(window, far_below, tail[1]), partner, when & low_core,
            )

        def climbed():
            for k, (first, count) in enumerate(pieces):
                desk.wait(("climb", k), part(window, near_below + first, count))

        guarded(first_side & has_down, climbed)
        share_before(has_before)
        yield

        def dropped():
            for k, (first, count) in enumerate(pieces):
                desk.wait(("drop", k), part(window, left + tok + first, count))
            for k, (first, count) in enumerate(parts_of(head)):
                desk.wait(("fall", k), part(window, left + 2 * tok + first, count))

        guarded(last_side & has_up & high_core, dropped)
        desk.send(
            "last", part(window, left + tok, head), part(window, left + 2 * tok, head), partner,
            last_side & has_up & high_core,
        )
        yield
        desk.wait("pair", part(window, pl.multiple_of(left + (1 - 2 * core) * tok, 16), tok))
        for when, slot, first, count in (
            (low_core & has_down, "tail", far_below, tail[1]),
            (first_side & high_core, "share", left + tok, tok),
            (has_before & low_core, "wide", left - tok, tok),
            (has_before & high_core, "thin", far_below, tail[1]),
            (last_side & has_up & low_core, "last", left + 2 * tok, head),
        ):
            guarded(when, functools.partial(desk.wait, slot, part(window, first, count)))
        guarded(first_side, stay.wait)

    def steps(desk, ins, outs, scratch, common):
        (own,), (window,) = ins, outs
        keep = desk.local(0, own, window.at[pl.ds(left, tok)])
        keep.start()
        yield from by_way(desk, own, window, *scratch) if routed else direct(desk, own, window)
        keep.wait()

    outs = [(jax.ShapeDtypeStruct((reach.window, width), key_value.dtype), anywhere())]
    scratch = [pltpu.VMEM((tok, width), key_value.dtype)] if routed else []
    return Work(steps, [(key_value, in_vmem())], outs, scratch, slots, 2)


def owned_work(layout, reach, grad_window):
    width = grad_window.shape[1]
    tok, left, lines = reach.tok, reach.left, layout.lines
    places = layout.lines * layout.members
    routed = layout.sides == 2
    pieces, depth = parts_of(tok), 2
    near_below, far_below = reach.spot(2), reach.spot(3)
    tail = (reach.first(3), max(reach.rows(3), 0))
    head = max(reach.rows(-2), 0)
    every = pl.ds(0, width)
    low = grad_window.dtype
    if routed:
        slots = ["pair", "tail", "share", "wide", "thin", "last", "rise"]
        slots += [(name, k) for name in ("right", "left", "fall", "lift") for k in range(len(pieces))]
    else:
        slots = [("reach", delta) for delta in reach.deltas]

    def direct(desk, grad, out, landing):
        seat = desk.line * layout.members + desk.member
        for delta in reach.deltas:
            count = reach.rows(delta)
            desk.send(
                ("reach", delta),
                grad.at[pl.ds(reach.spot(delta), count)],
                landing[delta],
                (desk.group, seat - delta),
                (seat - delta >= 0) & (seat - delta < places),
            )
        load = desk.local(0, grad.at[pl.ds(left, tok)], out)
        load.start()
        load.wait()
        yield
        for delta in reach.deltas:

            @pl.when((seat + delta >= 0) & (seat + delta < places))
            def _():
                desk.wait(("reach", delta), landing[delta])
                first, count = reach.first(delta), reach.rows(delta)
                add_rows(out, first, every, landing[delta], every, count)

    def by_way(desk, grad, out, scratch):
        near, middle, l_wide, l_far, l_climb, l_y, l_pair, l_tail = scratch
        line, core = desk.line, desk.core
        first_side, last_side = desk.side == 0, desk.side == 1
        low_core, high_core = core == 0, core == 1
        has_up, has_down = line < lines - 1, line > 0
        has_before = last_side | has_down
        gate = last_side & has_up & high_core
        partner = desk.at(core=1 - core)

        def part(ref, first, count):
            return ref.at[pl.ds(first, count)]

        def receive(when, slot, target, first, buffer, at, count):
            @pl.when(when)
            def _():
                desk.wait(slot, part(buffer, at, count))
                add_rows(target, first, every, buffer, every, count, at)

        desk.send(
            "last", part(grad, left + 2 * tok, head), part(l_climb, 0, head), partner,
            last_side & has_up & low_core,
        )
        desk.send(
            "wide", part(grad, left - tok, tok), l_wide, partner, has_before & low_core
        )
        desk.send(
            "thin", part(grad, far_below, tail[1]), part(l_wide, 0, tail[1]), partner,
            has_before & high_core,
        )
        desk.send(
            "share", part(grad, left + tok, tok), l_far, partner, first_side & high_core
        )
        desk.send(
            "tail", part(grad, far_below, tail[1]), l_tail,
            desk.at(line=line - 1, core=1), low_core & has_down,
        )
        desk.send("rise", part(grad, left + 2 * tok, head), part(l_far, 0, head),
            desk.at(line=line + 1), gate,
        )
        loads = [
            (desk.local(0, part(grad, near_below, tok), near), None),
            (desk.local(1, part(grad, left + tok, tok), middle), last_side),
            (desk.local(2, part(grad, left + 2 * tok, head), part(middle, 0, head)), first_side),
            (desk.local(3, part(grad, left, tok), out), None),
        ]
        for load, when in loads:
            guarded(when, load.start)

        @pl.when(first_side)
        def _():
            middle[head:, :] = jnp.zeros((tok - head, width), low)

        yield
        for load, when in loads:
            guarded(when, load.wait)
        receive(gate, "last", middle, 0, l_climb, 0, head)
        receive(has_before & high_core, "wide", near, 0, l_wide, 0, tok)
        receive(has_before & low_core, "thin", near, tail[0], l_wide, 0, tail[1])

        def post(k):
            if k >= len(pieces):
                return
            if k >= depth:
                desk.settle(("fall", k - depth))
                desk.settle(("lift", k - depth))
            first, count = pieces[k]
            desk.send(
                ("fall", k), part(middle, first, count), part(l_far, first, count),
                desk.at(line=line + 1, core=0), gate,
            )
            desk.send(
                ("lift", k), part(near, first, count), part(l_climb, first, count),
                desk.at(line=line - 1), first_side & has_down,
            )

        for k in range(depth):
            post(k)
        mirrored = pl.multiple_of(left + (1 - 2 * core) * tok, 16)
        desk.send("pair", part(grad, mirrored, tok), l_pair, partner)
        yield
        receive(first_side & low_core, "share", middle, 0, l_far, 0, tok)
        receive(last_side & has_down & high_core, "rise", near, 0, l_far, 0, head)
        for k, (first, count) in enumerate(pieces):
            receive(first_side & has_up, ("lift", k), middle, first, l_climb, first, count)
            desk.send(
                ("left", k), part(middle, first, count), part(l_y, first, count),
                desk.at(side=1), first_side,
            )
            receive(
                last_side & has_down & low_core, ("fall", k), near, first, l_far, first, count
            )
            desk.send(
                ("right", k), part(near, first, count), part(l_y, first, count),
                desk.at(side=0), last_side,
            )
            post(k + depth)
            yield
        receive(has_up & high_core, "tail", out, tail[0], l_tail, 0, tail[1])
        desk.wait("pair", l_pair)
        for k, (first, count) in enumerate(pieces):
            where = part(l_y, first, count)
            guarded(first_side, functools.partial(desk.wait, ("right", k), where))
            guarded(last_side, functools.partial(desk.wait, ("left", k), where))

            def one(index, carry):
                rows = pl.ds(pl.multiple_of(first + index * 16, 16), 16)
                total = out[rows, :].astype(jnp.float32) + l_pair[rows, :].astype(jnp.float32)
                out[rows, :] = (total + l_y[rows, :].astype(jnp.float32)).astype(out.dtype)
                return carry

            lax.fori_loop(0, count // 16, one, 0)
            yield

    def steps(desk, ins, outs, scratch, common):
        if routed:
            yield from by_way(desk, ins[0], outs[0], scratch)
        else:
            yield from direct(desk, ins[0], outs[0], dict(zip(reach.deltas, scratch)))

    if routed:
        counts = [tok] * 7 + [tail[1]]
    else:
        counts = [reach.rows(delta) for delta in reach.deltas]
    return Work(
        steps,
        [(grad_window, anywhere())],
        [(jax.ShapeDtypeStruct((tok, width), low), in_vmem())],
        [pltpu.VMEM((count, width), low) for count in counts],
        slots,
        4,
    )


def sum_work(layout, block):
    sizes = (2, layout.sides, layout.model_width // layout.near, layout.lines)
    slots = [(stage, j) for stage, size in enumerate(sizes) for j in range(1, size)]

    def steps(desk, ins, outs, scratch, common):
        (block,), (out,) = ins, outs
        yield
        out[...] = block[...]
        for stage, (landing, size) in enumerate(zip(scratch, sizes)):
            mine = (desk.core, desk.side, desk.group, desk.line)[stage]
            landing[mine] = out[...]
            for j in range(1, size):
                other = (mine + j) % size
                to = desk.at(**{("core", "side", "group", "line")[stage]: other})
                desk.send((stage, j), landing.at[mine], landing.at[mine], to)
            yield
            for j in range(1, size):
                desk.wait((stage, j), landing.at[(mine + size - j) % size])
            total = landing[0]
            for j in range(1, size):
                total = total + landing[j]
            out[...] = total

    return Work(
        steps,
        [(block, in_vmem())],
        [(jax.ShapeDtypeStruct(block.shape, block.dtype), in_vmem())],
        [pltpu.VMEM((size, *block.shape), block.dtype) for size in sizes],
        slots,
        1,
    )


def lane_mean(source):
    return jnp.mean(source, axis=1, keepdims=True)


def unit_of(source):
    centred = source - lane_mean(source)
    inv_scale = lax.rsqrt(lane_mean(centred * centred) + eps_norm)
    return centred * inv_scale, inv_scale


def norm_input_gradient(gradient, unit_rows, inv_scale, gain_row):
    scaled = gradient * gain_row
    return inv_scale * (scaled - lane_mean(scaled) - unit_rows * lane_mean(scaled * unit_rows))


def rows_sum(source):
    return jnp.sum(source.astype(jnp.float32), axis=0, keepdims=True)


def gelu_and_slope(source):
    square = source * source
    curve = jnp.tanh(gelu_rate * source * (1.0 + gelu_cube * square))
    rise = gelu_rate * (1.0 + 3.0 * gelu_cube * square)
    half_sum = 0.5 * (1.0 + curve)
    return source * half_sum, half_sum + 0.5 * source * (1.0 - curve * curve) * rise


def chunks_of(columns, lanes=768):
    return [(first, min(lanes, columns - first)) for first in range(0, columns, lanes)]


def moves(sources, targets, sems):
    return [
        pltpu.make_async_copy(source, target, sems.at[index])
        for index, (source, target) in enumerate(zip(sources, targets))
    ]


def projection_forward_kernel(
    residual, rows, weight, normed_out, inv_out, query_out, pair_out, unit_out, held, sems
):
    width = rows.shape[1]
    sources = [weight.at[:, pl.ds(j * width, width)] for j in range(3)]
    loads = moves(sources, [held.at[j] for j in range(3)], sems)
    for load in loads:
        load.start()
    unit_rows, inv_scale = unit_of(residual[...].astype(jnp.float32))
    unit_out[...] = unit_rows
    inv_out[...] = jnp.broadcast_to(inv_scale, inv_out.shape)
    normed = (unit_rows * rows[0:1, :] + rows[1:2, :]).astype(normed_out.dtype)
    normed_out[...] = normed
    loads[0].wait()
    query_out[...] = (dot_nn(normed_out[...], held[0]) + rows[2:3, :]).astype(query_out.dtype)
    loads[1].wait()
    pair_out[:, :width] = dot_nn(normed_out[...], held[1]).astype(pair_out.dtype)
    loads[2].wait()
    values = dot_nn(normed_out[...], held[2]) + rows[3:4, :]
    pair_out[:, width:] = values.astype(pair_out.dtype)


def dense_call(kernel, name, ins, outs, scratch, *arrays):
    return pl.pallas_call(
        kernel,
        name=name,
        in_specs=ins,
        out_specs=[spec for _, spec in outs],
        out_shape=[shape for shape, _ in outs],
        scratch_shapes=scratch,
        compiler_params=pltpu.CompilerParams(vmem_limit_bytes=60 * mib),
    )(*arrays)


def kept(shape, kind=jnp.bfloat16):
    return (jax.ShapeDtypeStruct(shape, kind), in_vmem())


def projection_forward(residual, rows, attn_weight):
    tok, width = residual.shape
    return dense_call(
        projection_forward_kernel,
        "projection_forward",
        [in_vmem(), in_vmem(), anywhere()],
        [
            kept((tok, width)),
            kept((tok, 128), jnp.float32),
            kept((tok, width)),
            kept((tok, 2 * width)),
            kept((tok, width), jnp.float32),
        ],
        [pltpu.VMEM((3, width, width), jnp.bfloat16), pltpu.SemaphoreType.DMA((3,))],
        residual,
        rows,
        attn_weight,
    )


def whole(shape):
    return pl.BlockSpec(shape, lambda step: (0,) * len(shape))


def projection_backward_kernel(
    grad_query, grad_pair, weight, unit, inv, rows, grad_mid, grad_res, sums, acc
):
    step = pl.program_id(0)
    width = grad_query.shape[1]

    @pl.when(step == 0)
    def _():
        acc[...] = dot_nt(grad_query[...], weight[...])

    @pl.when(step == 1)
    def _():
        acc[...] += dot_nt(grad_pair[:, :width], weight[...])

    @pl.when(step == 2)
    def _():
        gradient = acc[...] + dot_nt(grad_pair[:, width:], weight[...])
        unit_rows = unit[...]
        grad_res[...] = grad_mid[...] + norm_input_gradient(
            gradient, unit_rows, inv[:, 0:1], rows[0:1, :]
        )
        sums[...] = jnp.zeros_like(sums)
        sums[0:1, :] = rows_sum(gradient * unit_rows)
        sums[1:2, :] = rows_sum(gradient)
        sums[2:3, :] = rows_sum(grad_query[...])
        sums[3:4, :] = rows_sum(grad_pair[:, width:])


def projection_backward(grad_query, grad_pair, attn_weight, unit, inv, rows, grad_mid):
    tok, width = grad_query.shape
    return pl.pallas_call(
        projection_backward_kernel,
        name="projection_backward",
        grid=(3,),
        in_specs=[
            whole((tok, width)),
            whole((tok, 2 * width)),
            pl.BlockSpec((width, width), lambda step: (0, step)),
            whole((tok, width)),
            whole((tok, 128)),
            whole(rows.shape),
            whole((tok, width)),
        ],
        out_specs=[whole((tok, width)), whole((8, width))],
        out_shape=[
            jax.ShapeDtypeStruct((tok, width), jnp.float32),
            jax.ShapeDtypeStruct((8, width), jnp.float32),
        ],
        scratch_shapes=[pltpu.VMEM((tok, width), jnp.float32)],
        compiler_params=pltpu.CompilerParams(vmem_limit_bytes=58 * mib),
    )(grad_query, grad_pair, attn_weight, unit, inv, rows, grad_mid)


class Stream:
    def __init__(self, source, held, sems, chunks):
        self.held, self.chunks = held, chunks
        self.copies = [
            pltpu.make_async_copy(
                source.at[:, pl.ds(first, count)], held.at[k % 2, :, pl.ds(0, count)], sems.at[k]
            )
            for k, (first, count) in enumerate(chunks)
        ]

    def start(self, k):
        if k < len(self.chunks):
            self.copies[k].start()

    def take(self, k):
        self.copies[k].wait()
        return self.held[k % 2, :, : self.chunks[k][1]]


def mlp_forward_kernel(
    chunks, attended, residual, attn_weight, rows, up_weight, up_shift, down_weight,
    residual_out, hidden_out, inv_out, unit_out, active_out, slope_out,
    out_held, up_held, down_held, active_held, slope_held, sems,
):
    width, count = rows.shape[1], len(chunks)
    load = pltpu.make_async_copy(attn_weight.at[:, pl.ds(3 * width, width)], out_held, sems.at[4, 0])
    load.start()
    up = Stream(up_weight, up_held, sems.at[0], chunks)
    down = Stream(down_weight, down_held, sems.at[1], chunks)
    up.start(0)
    down.start(0)
    up.start(1)
    load.wait()
    middle = residual[...].astype(jnp.float32) + rows[4:5, :] + dot_nn(attended[...], out_held[...])
    residual_out[...] = middle + rows[5:6, :]
    unit_rows, inv_scale = unit_of(middle)
    unit_out[...] = unit_rows
    inv_out[...] = jnp.broadcast_to(inv_scale, inv_out.shape)
    hidden_out[...] = (unit_rows * rows[6:7, :] + rows[7:8, :]).astype(hidden_out.dtype)
    ahead = dot_nn(hidden_out[...], up.take(0))
    stores = []
    for k, (first, lanes) in enumerate(chunks):
        now = ahead
        columns = pl.ds(first, lanes)
        up.start(k + 2)
        down.start(k + 1)
        if k + 1 < count:
            ahead = dot_nn(hidden_out[...], up.take(k + 1))
        value, slope = gelu_and_slope(now + up_shift[:, columns])
        active_held[:, columns] = value.astype(active_held.dtype)
        slope_held[:, columns] = slope.astype(slope_held.dtype)
        for row, held, target in ((2, active_held, active_out), (3, slope_held, slope_out)):
            store = pltpu.make_async_copy(
                held.at[:, columns], target.at[:, columns], sems.at[row, k]
            )
            store.start()
            stores.append(store)
        residual_out[...] += dot_nt(active_held[:, columns], down.take(k))
    for store in stores:
        store.wait()


def mlp_forward(attended, residual, attn_weight, rows, up_weight, up_shift, down_weight):
    tok, width = attended.shape
    columns = up_shift.shape[1]
    chunks = chunks_of(columns)
    hidden = (jax.ShapeDtypeStruct((tok, columns), jnp.bfloat16), anywhere())
    weight_chunk = pltpu.VMEM((2, width, chunks[0][1]), jnp.bfloat16)
    hidden_held = pltpu.VMEM((tok, columns), jnp.bfloat16)
    return dense_call(
        functools.partial(mlp_forward_kernel, chunks),
        "mlp_forward",
        [in_vmem(), in_vmem(), anywhere(), in_vmem(), anywhere(), in_vmem(), anywhere()],
        [
            kept((tok, width), jnp.float32),
            kept((tok, width)),
            kept((tok, 128), jnp.float32),
            kept((tok, width), jnp.float32),
            hidden,
            hidden,
        ],
        [pltpu.VMEM((width, width), jnp.bfloat16)]
        + [weight_chunk] * 2
        + [hidden_held] * 2
        + [pltpu.SemaphoreType.DMA((5, len(chunks)))],
        attended,
        residual,
        attn_weight,
        rows,
        up_weight,
        up_shift,
        down_weight,
    )


def mlp_backward_kernel(
    chunks, grad_res, down_weight, slope, up_weight, unit, inv, rows, attn_weight,
    grad_pre, up_sum, grad_branch, grad_mid, grad_attn, grad_attended, sums,
    out_held, up_held, down_held, pre_held, acc, sems,
):
    width, count = rows.shape[1], len(chunks)
    down = Stream(down_weight, down_held, sems.at[1], chunks)
    up = Stream(up_weight, up_held, sems.at[0], chunks)
    down.start(0)
    up.start(0)
    down.start(1)
    load = pltpu.make_async_copy(attn_weight.at[:, pl.ds(3 * width, width)], out_held, sems.at[3, 0])
    load.start()
    grad_branch[...] = grad_res[...].astype(grad_branch.dtype)
    acc[...] = jnp.zeros_like(acc)
    ahead = dot_nn(grad_branch[...], down.take(0))
    stores = []
    for k, (first, lanes) in enumerate(chunks):
        now = ahead
        columns = pl.ds(first, lanes)
        down.start(k + 2)
        up.start(k + 1)
        if k + 1 < count:
            ahead = dot_nn(grad_branch[...], down.take(k + 1))
        low = (now * slope[:, columns].astype(jnp.float32)).astype(jnp.bfloat16)
        pre_held[:, columns] = low
        up_sum[:, columns] = rows_sum(low)
        store = pltpu.make_async_copy(
            pre_held.at[:, columns], grad_pre.at[:, columns], sems.at[2, k]
        )
        store.start()
        stores.append(store)
        acc[...] += dot_nt(pre_held[:, columns], up.take(k))
    gradient = acc[...]
    unit_rows = unit[...]
    middle = grad_res[...].astype(jnp.float32) + norm_input_gradient(
        gradient, unit_rows, inv[:, 0:1], rows[6:7, :]
    )
    grad_mid[...] = middle
    grad_attn[...] = middle.astype(grad_attn.dtype)
    load.wait()
    grad_attended[...] = dot_nt(grad_attn[...], out_held[...]).astype(grad_attended.dtype)
    sums[...] = jnp.zeros_like(sums)
    sums[0:1, :] = rows_sum(gradient * unit_rows)
    sums[1:2, :] = rows_sum(gradient)
    sums[2:3, :] = rows_sum(grad_attn[...])
    sums[3:4, :] = rows_sum(grad_branch[...])
    for store in stores:
        store.wait()


def mlp_backward(grad_res, down_weight, slope, up_weight, unit, inv, rows, attn_weight):
    tok, width = grad_res.shape
    columns = slope.shape[1]
    chunks = chunks_of(columns)
    weight_chunk = pltpu.VMEM((2, width, chunks[0][1]), jnp.bfloat16)
    return dense_call(
        functools.partial(mlp_backward_kernel, chunks),
        "mlp_backward",
        [in_vmem(), anywhere(), in_vmem(), anywhere(), in_vmem(), in_vmem(), in_vmem(), anywhere()],
        [
            (jax.ShapeDtypeStruct((tok, columns), jnp.bfloat16), anywhere()),
            kept((1, columns), jnp.float32),
            kept((tok, width)),
            kept((tok, width), jnp.float32),
            kept((tok, width)),
            kept((tok, width)),
            kept((8, width), jnp.float32),
        ],
        [pltpu.VMEM((width, width), jnp.bfloat16)]
        + [weight_chunk] * 2
        + [
            pltpu.VMEM((tok, columns), jnp.bfloat16),
            pltpu.VMEM((tok, width), jnp.float32),
            pltpu.SemaphoreType.DMA((4, len(chunks))),
        ],
        grad_res,
        down_weight,
        slope,
        up_weight,
        unit,
        inv,
        rows,
        attn_weight,
    )


def adam_step(weight_now, gradient, first_old, second_old):
    first_new = beta_first * first_old + (1.0 - beta_first) * gradient
    second_new = beta_second * second_old + (1.0 - beta_second) * gradient * gradient
    first_hat = first_new / (1.0 - beta_first**STEP)
    second_hat = second_new / (1.0 - beta_second**STEP)
    update = -learn_rate * (
        first_hat / (jnp.sqrt(second_hat) + eps_adam)
        + weight_decay * weight_now.astype(jnp.float32)
    )
    return (first_new, second_new, update)


def round_up(count, unit):
    return -(-count // unit) * unit


def per_device(
    inputs, image_ids, token_mask, cotangent,
    w_qkv, w_out, w_up, w_down, norm_gains, bias_rows, up_bias,
    first_qkv, first_out, first_up, first_down, first_gains, first_bias, first_upbias,
    second_qkv, second_out, second_up, second_down, second_gains, second_bias, second_upbias,
):
    tok, width = inputs.shape
    layers, _, hidden_width = w_up.shape
    places = lax.axis_size("seq")
    place = lax.axis_index("seq")
    layout = Layout(lax.axis_size("dp"), places, width)
    group_tok = tok * places
    spare_count = group_tok - group_tok // IMG * IMG
    left = round_up(IMG - 1 + spare_count, 16)
    right = round_up(IMG - 1, 16)
    tile = tok // 2

    reach = Reach(tok, left, right)

    half = hidden_width // 2
    half_pad = round_up(half + 8 * layers, 128)
    wide_columns = 2 * half_pad

    def spread(array):
        pad = [(0, 0)] * (array.ndim - 1) + [(0, half_pad - half)]
        return jnp.concatenate([jnp.pad(array[..., :half], pad), jnp.pad(array[..., half:], pad)], -1)

    def unspread(array):
        return jnp.concatenate(
            [array[..., :half], array[..., half_pad : half_pad + half]], axis=-1
        )

    def filled(array, rows, columns):
        return jnp.pad(array, ((0, rows - array.shape[0]), (0, columns - array.shape[1])))

    attn_columns = layout.columns(4 * width, False)
    up_columns = layout.columns(wide_columns, True)
    down_columns = layout.columns(wide_columns, False)
    rows_of = jnp.concatenate([norm_gains.reshape(-1, layout.rows), bias_rows.reshape(-1, layout.rows)])
    row_count = rows_of.shape[0]
    shards = []
    for layer in range(layers):
        attn_shard = jnp.concatenate([w_qkv[layer], w_out[layer]], axis=1)
        up_shard = spread(w_up[layer])
        if layer == 0:
            up_shard = up_shard.at[:, half : half + row_count].set(rows_of.T)
        down_shard = spread(w_down[layer].T)
        shards += [
            filled(attn_shard, layout.padded, attn_columns),
            filled(up_shard, layout.padded, up_columns),
            filled(down_shard, layout.padded, down_columns if layer else up_columns),
        ]
    word = jnp.broadcast_to(image_ids[:, None], (tok, 128))
    def gather(layer, which):
        return gather_work(layout, shards[3 * layer + which], which == 1 or (which == 2 and layer == 0))

    gathered = [[None] * 3 for _ in range(layers)]
    begun = [(0, 1), (0, 0), (0, 2)]
    for layer in range(1, layers):
        begun += [(layer, 0), (layer, 2), (layer, 1)]
    *results, (window_word, *_) = exchange(
        "gather_parameters",
        layout,
        [gather(*spot) for spot in begun] + [window_work(layout, reach, word)],
        [[index] for index in range(len(begun))] + [[1]],
        40,
    )
    for (layer, which), (matrix,) in zip(begun, results):
        gathered[layer][which] = matrix
    window_word = window_word[:, 0]
    all_rows = gathered[0][1][:, half : half + row_count].T.astype(jnp.float32)
    gains = all_rows[: 2 * layers].reshape(layers, 2, width)
    shifts = all_rows[2 * layers :].reshape(layers, 6, width)
    vectors = jnp.concatenate(
        [gains[:, :1], shifts[:, :1], shifts[:, 2:], gains[:, 1:], shifts[:, 1:2]], axis=1
    )
    up_shift = spread(up_bias.astype(jnp.float32))[:, None, :]

    plan, own_code = attention_plan(
        tile, left, right, image_ids, token_mask, window_word, place, places
    )

    residual = inputs
    kept_layers = []
    for layer in range(layers):
        attn_weight, up_weight, down_weight = gathered[layer]
        rows = vectors[layer]
        normed_low, inv_one, queries, key_value, unit_one = projection_forward(
            residual, rows, attn_weight
        )
        ((window, *_),) = exchange(
            "fetch_window", layout, [window_work(layout, reach, key_value)], [[0]], 20
        )
        attended, lse = attention_forward(tile, left, plan, queries, window, own_code)
        residual, hidden_low, inv_two, unit_two, active, slope = mlp_forward(
            attended, residual, attn_weight, rows, up_weight, up_shift[layer], down_weight
        )
        kept_layers.append(
            (window, unit_one, inv_one, normed_low, queries, lse, attended,
             unit_two, inv_two, hidden_low, slope, active)
        )

    def reduce(works, turns):
        left_operands = pltpu.VMEM((2, 2, width, tok), jnp.bfloat16)
        right_operands = pltpu.VMEM((2, tok, max(attn_columns, up_columns) // 2), jnp.bfloat16)
        operands = [left_operands, right_operands]
        results = exchange("reduce_gradients", layout, works, turns, 63, operands)
        return [result[0] for result in results]

    def packed(rows):
        flat = jnp.concatenate([row.reshape(-1) for row in rows])
        return jnp.pad(flat, (0, -flat.size % 1024)).reshape(-1, 128)

    grad_res = cotangent
    owned = [[None] * 3 for _ in range(layers)]
    row_grads = [None] * layers
    upbias_grads = [None] * layers
    for layer in reversed(range(layers)):
        (window, unit_one, inv_one, normed_low, queries, lse, attended,
         unit_two, inv_two, hidden_low, slope, active) = kept_layers[layer]
        attn_weight, up_weight, down_weight = gathered[layer]
        rows = vectors[layer]
        grad_pre, up_sum, grad_branch, grad_mid, grad_attn, grad_attended, second_sums = (
            mlp_backward(
                grad_res, down_weight, slope, up_weight, unit_two, inv_two, rows, attn_weight
            )
        )
        upbias_grads[layer] = unspread(up_sum[0])
        grad_query, grad_window = attention_backward(
            tile, left, plan, queries, window, grad_attended, lse, own_code
        )
        works = [owned_work(layout, reach, grad_window)]
        reduce_up = reduce_work(layout, [hidden_low.T], grad_pre, True)
        reduce_down = reduce_work(layout, [grad_branch.T], active, True)
        if layer > 0:
            works += [reduce_up, reduce_down]
            results = reduce(works, [[0], [0], [1]])
            grad_key_value, owned[layer][1], owned[layer][2] = results
        else:
            small = packed([*upbias_grads, *row_grads[1:]])
            works += [waiting, reduce_up, sum_work(layout, small)]
            results = reduce(works, [[0], [0], [1], [3, 5, 7, 8, 9]])
            grad_key_value, owned[1][0], owned[0][1], small_sum = results
        grad_res, first_sums = projection_backward(
            grad_query, grad_key_value, attn_weight, unit_one, inv_one, rows, grad_mid
        )
        row_grads[layer] = jnp.stack(
            [
                first_sums[0], second_sums[0], first_sums[1], second_sums[1],
                first_sums[2], first_sums[3], second_sums[2], second_sums[3],
            ]
        )
        grad_proj = jnp.concatenate([grad_query, grad_key_value], axis=1)
        grad_side = filled(jnp.concatenate([grad_proj, grad_attn], axis=1), tok, attn_columns)
        waiting = reduce_work(
            layout, [normed_low.T, attended.T], grad_side, False, 3 * width
        )
        if layer == 0:
            works = [reduce_down, waiting, sum_work(layout, packed(row_grads[:1]))]
            owned[0][2], owned[0][0], row_sum = reduce(works, [[0], [1], [2, 4, 6, 8, 10]])

    flat = small_sum.reshape(-1)
    upbias_grads = flat[: layers * hidden_width].reshape(layers, hidden_width)
    later = flat[layers * hidden_width :][: (layers - 1) * 8 * width].reshape(-1, 8, width)
    row_sums = jnp.concatenate([row_sum.reshape(-1)[: 8 * width].reshape(1, 8, width), later])
    seat = lax.axis_index("dp") * places + place
    row_sums = lax.dynamic_slice_in_dim(row_sums, seat * layout.rows, layout.rows, axis=2)

    def stacked(part):
        return jnp.stack([part(*owned[layer]) for layer in range(layers)], axis=1)

    rows = layout.rows
    grads = (
        stacked(lambda attn, up, down: attn[:rows, : 3 * width]),
        stacked(lambda attn, up, down: attn[:rows, 3 * width : 4 * width]),
        stacked(lambda attn, up, down: unspread(up[:rows])),
        stacked(lambda attn, up, down: unspread(down[:rows])),
        row_sums[:, :2],
        row_sums[:, 2:],
        upbias_grads,
    )
    there = ((1, 0, 2), (1, 0, 2), (1, 0, 2), (2, 0, 1)) + ((0, 1, 2),) * 2 + ((0, 1),)
    back = ((1, 0, 2), (1, 0, 2), (1, 0, 2), (1, 2, 0)) + ((0, 1, 2),) * 2 + ((0, 1),)

    def turned(arrays, orders):
        return tuple(jnp.transpose(array, order) for array, order in zip(arrays, orders))

    def handed_out(arrays):
        orders = ((1, 0, 2),) * 3 + ((2, 0, 1),)
        large = [
            array_layout.with_layout_constraint(
                array, array_layout.Layout(major_to_minor=order)
            )
            for array, order in zip(arrays, orders)
        ]
        return tuple(large) + tuple(arrays[len(orders) :])

    params = (w_qkv, w_out, w_up, w_down, norm_gains, bias_rows, up_bias)
    firsts = (first_qkv, first_out, first_up, first_down, first_gains, first_bias, first_upbias)
    seconds = (
        second_qkv, second_out, second_up, second_down, second_gains, second_bias, second_upbias,
    )
    states = [turned(arrays, there) for arrays in (params, firsts, seconds)]
    results = [
        adam_step(param, gradient, first, second)
        for param, gradient, first, second in zip(states[0], grads, states[1], states[2])
    ]
    grads = handed_out(turned(grads, back))
    return (
        (residual, grad_res)
        + grads
        + handed_out(turned([result[0] for result in results], back))
        + handed_out(turned([result[1] for result in results], back))
        + handed_out(turned([result[2] for result in results], back))
    )


def solution(mesh):
    in_specs = (
        P(("dp", "seq"), None),
        P(("dp", "seq")),
        P(("dp", "seq")),
        P(("dp", "seq"), None),
        P(None, ("dp", "seq"), None),
        P(None, ("dp", "seq"), None),
        P(None, ("dp", "seq"), None),
        P(None, None, ("dp", "seq")),
        P(None, None, ("dp", "seq")),
        P(None, None, ("dp", "seq")),
        P(),
        P(None, ("dp", "seq"), None),
        P(None, ("dp", "seq"), None),
        P(None, ("dp", "seq"), None),
        P(None, None, ("dp", "seq")),
        P(None, None, ("dp", "seq")),
        P(None, None, ("dp", "seq")),
        P(),
        P(None, ("dp", "seq"), None),
        P(None, ("dp", "seq"), None),
        P(None, ("dp", "seq"), None),
        P(None, None, ("dp", "seq")),
        P(None, None, ("dp", "seq")),
        P(None, None, ("dp", "seq")),
        P(),
    )
    out_specs = (
        P(("dp", "seq"), None),
        P(("dp", "seq"), None),
        P(None, ("dp", "seq"), None),
        P(None, ("dp", "seq"), None),
        P(None, ("dp", "seq"), None),
        P(None, None, ("dp", "seq")),
        P(None, None, ("dp", "seq")),
        P(None, None, ("dp", "seq")),
        P(),
        P(None, ("dp", "seq"), None),
        P(None, ("dp", "seq"), None),
        P(None, ("dp", "seq"), None),
        P(None, None, ("dp", "seq")),
        P(None, None, ("dp", "seq")),
        P(None, None, ("dp", "seq")),
        P(),
        P(None, ("dp", "seq"), None),
        P(None, ("dp", "seq"), None),
        P(None, ("dp", "seq"), None),
        P(None, None, ("dp", "seq")),
        P(None, None, ("dp", "seq")),
        P(None, None, ("dp", "seq")),
        P(),
        P(None, ("dp", "seq"), None),
        P(None, ("dp", "seq"), None),
        P(None, ("dp", "seq"), None),
        P(None, None, ("dp", "seq")),
        P(None, None, ("dp", "seq")),
        P(None, None, ("dp", "seq")),
        P(),
    )
    return jax.shard_map(
        per_device, mesh=mesh, in_specs=in_specs, out_specs=out_specs, check_vma=False
    )
```

```python
import functools
import math

import jax
import jax.numpy as jnp
from jax import lax
from jax.experimental import layout as array_layout
from jax.experimental import pallas as pl
from jax.experimental.pallas import tpu as pltpu
from jax.sharding import PartitionSpec as P

HEADS = 16
IMG = 729
STEP = 8

eps_norm = 1e-06
beta_first = 0.9
beta_second = 0.95
learn_rate = 0.025
weight_decay = 0.1
eps_adam = 1e-08
gelu_rate = math.sqrt(2.0 / math.pi)
gelu_cube = 0.044715
span_len = 768
lane_pair = 256
masked_score = -1e30
mib = 2**20


def head_lanes(head, head_size, width):
    low = head * head_size
    first = jnp.minimum(low // 128 * 128, width - lane_pair)
    lanes = lax.broadcasted_iota(jnp.int32, (1, lane_pair), 1)
    inside = (lanes >= low - first) & (lanes < low - first + head_size)
    keys = pl.ds(pl.multiple_of(first, 128), lane_pair)
    values = pl.ds(pl.multiple_of(first + width, 128), lane_pair)
    return keys, values, inside


def valid_lanes(start):
    lanes = lax.broadcasted_iota(jnp.int32, (1, span_len), 1)
    return (lanes >= start) & (lanes < start + IMG)


def dot_nn(left, right):
    return lax.dot_general(left, right, (((1,), (0,)), ((), ())), preferred_element_type=jnp.float32)


def dot_nt(left, right):
    return lax.dot_general(left, right, (((1,), (1,)), ((), ())), preferred_element_type=jnp.float32)


def dot_tn(left, right):
    return lax.dot_general(left, right, (((0,), (0,)), ((), ())), preferred_element_type=jnp.float32)


def attention_forward_kernel(
    tile, left, exp_scale, plan, query, source, own_code, out, lse_out, bias, mix, window, sems
):
    tok, width = query.shape
    head_size = width // HEADS
    cut = min((HEADS // 2 - 1) * head_size // 128 * 128, width - lane_pair) + lane_pair
    loads = []
    for first, lanes in ((0, cut), (cut, width - cut)):
        for shift in (0, width):
            columns = pl.ds(first + shift, lanes)
            load = pltpu.make_async_copy(
                source.at[:, columns], window.at[:, columns], sems.at[len(loads)]
            )
            load.start()
            loads.append(load)

    def one_span(tile_index, which):
        spot = 2 * tile_index + which
        offset, image = pl.multiple_of(plan[0, spot], 16), plan[1, spot]
        valid = valid_lanes(plan[2, spot])
        rows = pl.ds(pl.multiple_of(tile_index * tile, 16), tile)
        own_rows = pl.ds(pl.multiple_of(left + tile_index * tile, 16), tile)
        span = pl.ds(offset, span_len)
        code = own_code[rows, :]
        row_image = jnp.maximum(code, -code)
        mine = row_image == image
        bias[...] = jnp.where(mine & valid, 0.0, masked_score)
        self_bias = jnp.where(code < 0, 0.0, masked_score)
        lse_lane = lax.broadcasted_iota(jnp.int32, (tile, lse_out.shape[1]), 1)

        def one_head(head, carry):
            lanes, value_lanes, inside = head_lanes(head, head_size, width)
            queries = jnp.where(inside, query[rows, lanes], 0)
            scores = dot_nt(queries, window[span, lanes]) * exp_scale + bias[...]
            own_key = window[own_rows, lanes].astype(jnp.float32)
            own_value = window[own_rows, value_lanes].astype(jnp.float32)
            self_score = (
                jnp.sum(queries.astype(jnp.float32) * own_key, axis=1, keepdims=True) * exp_scale
                + self_bias
            )
            top = jnp.maximum(jnp.max(scores, axis=1, keepdims=True), self_score)
            powers = jnp.exp2(scores - top)
            self_power = jnp.exp2(self_score - top)
            total = jnp.sum(powers, axis=1, keepdims=True) + self_power
            mixed = dot_nn(powers.astype(jnp.bfloat16), window[span, value_lanes])
            mixed = (mixed + self_power * own_value) / total
            mix[rows, lanes] = jnp.where(inside & mine, mixed, mix[rows, lanes])
            lse_out[rows, :] = jnp.where(
                (lse_lane == head) & mine, top + jnp.log2(total), lse_out[rows, :]
            )
            return carry

        def one_half(half, carry):
            for number in (0, 1):

                @pl.when((tile_index == 0) & (which == 0) & (half == number))
                def _():
                    for load in loads[2 * number : 2 * number + 2]:
                        load.wait()

            for index in range(HEADS // 2):
                one_head(half * (HEADS // 2) + index, 0)
            return carry

        lax.fori_loop(0, 2, one_half, 0)

    def one_tile(tile_index, carry):
        one_span(tile_index, 0)

        @pl.when(plan[1, 2 * tile_index] != plan[1, 2 * tile_index + 1])
        def _():
            one_span(tile_index, 1)

        return carry

    lax.fori_loop(0, tok // tile, one_tile, 0)
    out[...] = mix[...].astype(out.dtype)


def dot_fine(left, right, contract):
    high = left.astype(jnp.bfloat16)
    low = (left - high.astype(jnp.float32)).astype(jnp.bfloat16)
    numbers = (contract, ((), ()))
    product = lax.dot_general(high, right, numbers, preferred_element_type=jnp.float32)
    return product + lax.dot_general(low, right, numbers, preferred_element_type=jnp.float32)


def attention_backward_kernel(
    tile, left, exp_scale, plan, query, source, grad, lse_in, own_code, row_code,
    grad_query, target, bias, acc_query, acc_window, self_rows, lse_rows, inner_rows, square,
    window, grad_window, sems,
):
    tok, width = query.shape
    head_size = width // HEADS
    scale = 1.0 / math.sqrt(head_size)
    load = pltpu.make_async_copy(source, window, sems.at[0])
    load.start()
    acc_query[...] = jnp.zeros_like(acc_query)
    acc_window[...] = jnp.zeros_like(acc_window)
    square[...] = jnp.zeros_like(square)
    head_of = lax.broadcasted_iota(jnp.int32, (128, width), 1) // head_size
    spread = (head_of == lax.broadcasted_iota(jnp.int32, (128, width), 0)).astype(jnp.bfloat16)

    def turned(columns):
        square[:tile, :] = columns
        return square[...].T[:, :tile]

    def one_span(tile_index, which):
        spot = 2 * tile_index + which
        offset, image = pl.multiple_of(plan[0, spot], 16), plan[1, spot]
        rows = pl.ds(pl.multiple_of(tile_index * tile, 16), tile)
        span = pl.ds(offset, span_len)
        code = row_code[tile_index]
        mine = jnp.maximum(code, -code) == image
        place = lax.broadcasted_iota(jnp.int32, (span_len, 1), 0)
        valid = (place >= plan[2, spot]) & (place < plan[2, spot] + IMG)
        bias[...] = jnp.where(mine & valid, 0.0, masked_score)

        def one_head(head, carry):
            lanes, value_lanes, inside = head_lanes(head, head_size, width)
            queries = jnp.where(inside, query[rows, lanes], 0)
            grads = jnp.where(inside, grad[rows, lanes], 0)
            keys = window[span, lanes]
            this = pl.ds(head, 1)
            scores = dot_nt(keys, queries) * exp_scale + bias[...]
            prob = jnp.exp2(scores - lse_rows[this, :])
            grad_prob = dot_nt(window[span, value_lanes], grads)
            inner = jnp.sum(prob * grad_prob, axis=0, keepdims=True) + self_rows[this, :]
            inner_rows[this, :] = jnp.where(mine, inner, inner_rows[this, :])
            grad_scores = (prob * (grad_prob - inner)).astype(jnp.bfloat16)
            acc_window[span, lanes] += dot_nn(grad_scores, queries)
            acc_window[span, value_lanes] += dot_nn(prob.astype(jnp.bfloat16), grads)
            part = dot_tn(grad_scores, keys)
            acc_query[rows, lanes] += jnp.where(inside, part, 0.0)
            return carry

        lax.fori_loop(0, HEADS, one_head, 0, unroll=8)

    def one_tile(tile_index, carry):
        rows = pl.ds(pl.multiple_of(tile_index * tile, 16), tile)
        own_rows = pl.ds(pl.multiple_of(left + tile_index * tile, 16), tile)
        queries, grads = query[rows, :].astype(jnp.float32), grad[rows, :].astype(jnp.float32)
        own_key = window[own_rows, :width].astype(jnp.float32)
        own_value = window[own_rows, width:].astype(jnp.float32)
        self_score = dot_fine(queries * own_key, spread, ((1,), (1,))) * exp_scale
        self_grad = dot_fine(grads * own_value, spread, ((1,), (1,)))
        lse = lse_in[rows, :]
        self_prob = jnp.where(own_code[rows, :] < 0, jnp.exp2(self_score - lse), 0.0)
        self_rows[...] = turned(self_prob * self_grad)
        lse_rows[...] = turned(lse)
        one_span(tile_index, 0)

        @pl.when(plan[1, 2 * tile_index] != plan[1, 2 * tile_index + 1])
        def _():
            one_span(tile_index, 1)

        inner = inner_rows[...].T
        self_change = self_prob * (self_grad - inner[:tile, :])
        change = dot_fine(self_change, spread, ((1,), (0,)))
        acc_query[rows, :] += change * own_key
        acc_window[own_rows, :width] += change * queries
        acc_window[own_rows, width:] += dot_fine(self_prob, spread, ((1,), (0,))) * grads
        return carry

    inner_rows[...] = jnp.zeros_like(inner_rows)
    load.wait()
    lax.fori_loop(0, tok // tile, one_tile, 0)
    grad_query[...] = (acc_query[...] * scale).astype(grad_query.dtype)
    step = 16

    def narrow(index, carry):
        rows = pl.ds(pl.multiple_of(index * step, step), step)
        grad_window[rows, :width] = (acc_window[rows, :width] * scale).astype(grad_window.dtype)
        grad_window[rows, width:] = acc_window[rows, width:].astype(grad_window.dtype)
        return carry

    blocks, stores = acc_window.shape[0] // step, []
    for part in range(4):
        first, last = blocks * part // 4, blocks * (part + 1) // 4
        lax.fori_loop(first, last, narrow, 0)
        rows = pl.ds(first * step, (last - first) * step)
        store = pltpu.make_async_copy(grad_window.at[rows], target.at[rows], sems.at[1 + part])
        store.start()
        stores.append(store)
    for store in stores:
        store.wait()


def in_vmem():
    return pl.BlockSpec(memory_space=pltpu.VMEM)


def attention_forward(tile, left, plan, query, window, own_code):
    tok, width = query.shape
    exp_scale = math.log2(math.e) / math.sqrt(width // HEADS)
    return pl.pallas_call(
        functools.partial(attention_forward_kernel, tile, left, exp_scale),
        name="attention_forward",
        out_shape=[
            jax.ShapeDtypeStruct((tok, width), jnp.bfloat16),
            jax.ShapeDtypeStruct((tok, 128), jnp.float32),
        ],
        in_specs=[pl.BlockSpec(memory_space=pltpu.SMEM), in_vmem(), anywhere(), in_vmem()],
        out_specs=[in_vmem()] * 2,
        scratch_shapes=[
            pltpu.VMEM((tile, span_len), jnp.float32),
            pltpu.VMEM((tok, width), jnp.float32),
            pltpu.VMEM(window.shape, window.dtype),
            pltpu.SemaphoreType.DMA((4,)),
        ],
        compiler_params=pltpu.CompilerParams(vmem_limit_bytes=60 * mib),
    )(plan, query, window, own_code)


def attention_backward(tile, left, plan, query, window, grad, lse, own_code):
    tok, width = query.shape
    exp_scale = math.log2(math.e) / math.sqrt(width // HEADS)
    return pl.pallas_call(
        functools.partial(attention_backward_kernel, tile, left, exp_scale),
        name="attention_backward",
        out_shape=[
            jax.ShapeDtypeStruct((tok, width), jnp.bfloat16),
            jax.ShapeDtypeStruct(window.shape, jnp.bfloat16),
        ],
        in_specs=[pl.BlockSpec(memory_space=pltpu.SMEM), in_vmem(), anywhere()] + [in_vmem()] * 4,
        out_specs=[in_vmem(), anywhere()],
        scratch_shapes=[
            pltpu.VMEM((span_len, tile), jnp.float32),
            pltpu.VMEM((tok, width), jnp.float32),
            pltpu.VMEM(window.shape, jnp.float32),
            pltpu.VMEM((128, tile), jnp.float32),
            pltpu.VMEM((128, tile), jnp.float32),
            pltpu.VMEM((128, tile), jnp.float32),
            pltpu.VMEM((-(-tile // 128) * 128, 128), jnp.float32),
            pltpu.VMEM(window.shape, jnp.bfloat16),
            pltpu.VMEM(window.shape, jnp.bfloat16),
            pltpu.SemaphoreType.DMA((5,)),
        ],
        compiler_params=pltpu.CompilerParams(vmem_limit_bytes=62 * mib),
    )(plan, query, window, grad, lse, own_code, own_code.reshape(tok // tile, 1, tile))


def attention_plan(tile, left, right, own_ids, own_mask, window_ids, place, places):
    tok = own_ids.shape[0]
    window_len = left + tok + right
    room = jnp.minimum(window_len, left + (places - place) * tok) - span_len
    position = jnp.arange(window_len)
    ids = jnp.where(position < left - place * tok, -1, window_ids)
    images = own_ids.reshape(tok // tile, tile)[:, :: tile - 1].reshape(-1)
    before = (ids[None, :] < images[:, None]) & (position < left + tok)[None, :]
    starts = jnp.sum(before.astype(jnp.int32), axis=1)
    offsets = jnp.minimum(starts // 16 * 16, room)
    plan = jnp.stack([offsets, images + 1, starts - offsets]).astype(jnp.int32)
    own_code = jnp.where(own_mask > 0, own_ids + 1, -(own_ids + 1)).astype(jnp.int32)[:, None]
    return plan, own_code


class Layout:
    def __init__(self, groups, seats, model_width):
        self.rows = model_width // (groups * seats)
        self.members = 2
        while self.members * self.rows % 16:
            self.members *= 2
        self.sides = self.members // 2
        self.lines = seats // self.members
        self.slab = self.members * self.rows
        self.padded = -(-self.rows // 16) * 16
        self.near = model_width // groups
        self.model_width = model_width

    def blocks(self, one_block):
        return 2 if one_block else 2 * self.sides

    def columns(self, columns, one_block):
        unit = 128 * self.blocks(one_block)
        return -(-columns // unit) * unit


class Mail:
    def __init__(self, layout, send, recv, slots):
        self.layout, self.send_sems, self.recv_sems, self.slots = layout, send, recv, slots
        self.group = lax.axis_index("dp")
        seat = lax.axis_index("seq")
        self.line = seat // layout.members
        self.member = seat % layout.members
        self.side = self.member // 2
        self.core = self.member % 2
        self.started = {}

    def at(self, group=None, line=None, side=None, core=None):
        group = self.group if group is None else group
        line = self.line if line is None else line
        side = self.side if side is None else side
        core = self.core if core is None else core
        return (group, line * self.layout.members + side * 2 + core)

    def copy(self, slot, source, target, device, shift=0):
        index = self.slots[slot] + shift
        return pltpu.make_async_remote_copy(
            src_ref=source,
            dst_ref=target,
            send_sem=self.send_sems.at[index],
            recv_sem=self.recv_sems.at[index],
            device_id=device,
            device_id_type=pl.DeviceIdType.MESH,
        )

    def send(self, slot, source, target, device, when=None):
        copy = self.copy(slot, source, target, device)
        self.started[slot] = (copy, when)
        guarded(when, copy.start)

    def wait(self, slot, target, shift=0):
        self.copy(slot, target, target, self.at(core=1 - self.core), shift).wait_recv()

    def settle(self, slot):
        copy, when = self.started.pop(slot)
        guarded(when, copy.wait_send)

    def finish(self):
        for slot in list(self.started):
            self.settle(slot)


class Desk:
    def __init__(self, mail, index, local):
        self.mail, self.index, self.local_sems = mail, index, local
        self.group, self.line, self.member = mail.group, mail.line, mail.member
        self.side, self.core, self.at = mail.side, mail.core, mail.at

    def send(self, slot, source, target, device, when=None):
        self.mail.send((self.index, slot), source, target, device, when)

    def wait(self, slot, target, shift=0):
        self.mail.wait((self.index, slot), target, shift)

    def settle(self, slot):
        self.mail.settle((self.index, slot))

    def local(self, number, source, target):
        return pltpu.make_async_copy(source, target, self.local_sems.at[number])


class Work:
    def __init__(self, steps, ins, outs, scratch, slots, local):
        self.steps, self.ins, self.outs, self.scratch = steps, ins, outs, scratch
        self.slots, self.local = slots, local


def guarded(when, action):
    if when is None:
        action()
    else:
        pl.when(when)(action)


def all_of(*conditions):
    kept = [condition for condition in conditions if condition is not None]
    return functools.reduce(jnp.logical_and, kept) if kept else None


def run_steps(works, turns):
    queue = []
    for index, (work, first) in enumerate(zip(works, turns)):
        next(work)
        queue.append((first[0], index, 0))
    while queue:
        turn, index, done = min(queue)
        queue.remove((turn, index, done))
        try:
            next(works[index])
        except StopIteration:
            continue
        done += 1
        listed = turns[index]
        queue.append((listed[done] if done < len(listed) else turn + 1, index, done))


def anywhere():
    return pl.BlockSpec(memory_space=pl.ANY)


def exchange(name, layout, works, starts, megabytes, common=()):
    slots = [(index, slot) for index, work in enumerate(works) for slot in work.slots]
    numbers = {slot: index for index, slot in enumerate(slots)}
    ins = [entry for work in works for entry in work.ins]
    outs = [entry for work in works for entry in work.outs]
    scratch = [entry for work in works for entry in work.scratch]

    def kernel(*refs):
        refs = list(refs)

        def take(count):
            taken = refs[:count]
            del refs[:count]
            return taken

        in_refs = [take(len(work.ins)) for work in works]
        out_refs = [take(len(work.outs)) for work in works]
        scratch_refs = [take(len(work.scratch)) for work in works]
        common_refs = take(len(common))
        locals_of = [take(1)[0] for work in works]
        send, recv = refs
        mail = Mail(layout, send, recv, numbers)
        run_steps(
            [
                work.steps(
                    Desk(mail, index, locals_of[index]),
                    in_refs[index],
                    out_refs[index],
                    scratch_refs[index],
                    common_refs,
                )
                for index, work in enumerate(works)
            ],
            starts,
        )
        mail.finish()

    results = pl.pallas_call(
        kernel,
        name=name,
        out_shape=[shape for shape, _ in outs],
        in_specs=[spec for _, spec in ins],
        out_specs=[spec for _, spec in outs],
        scratch_shapes=scratch
        + list(common)
        + [pltpu.SemaphoreType.DMA((work.local,)) for work in works]
        + [pltpu.SemaphoreType.DMA((len(slots),))] * 2,
        compiler_params=pltpu.CompilerParams(
            has_side_effects=True, vmem_limit_bytes=megabytes * mib
        ),
    )(*[array for array, _ in ins])
    results = list(results)
    grouped = []
    for work in works:
        grouped.append(results[: len(work.outs)])
        del results[: len(work.outs)]
    return grouped


def gather_work(layout, shard, one_block, line_last=False):
    lines, members, sides = layout.lines, layout.members, layout.sides
    width = shard.shape[1] // layout.blocks(one_block)
    spots = [("own", 0)]
    for t in range(1, lines):
        spots += [(f"below{t}", -t), (f"above{t}", t)]
    slots = [("mix", j) for j in range(1, members)]
    halves = (0, 1) if line_last else (0,)
    slots += [(way, half, t) for way in ("up", "down") for half in halves for t in range(lines)]
    slots += [("cross", source) for source, _ in (spots[:1] if line_last else spots)]
    slots += [("core", j) for j in range(1 if one_block else sides)]
    if not one_block:
        slots += [
            ("side", half, source, j)
            for half in (0, 1)
            for source, _ in spots
            for j in range(1, sides)
        ]

    def steps(desk, ins, outs, scratch, common):
        (shard,), (out,), (landing, slab, wide) = ins, outs, scratch
        group, line, member, side, core = desk.group, desk.line, desk.member, desk.side, desk.core
        has_up, has_down = line < lines - 1, line > 0

        def columns(side_of, core_of):
            block = core_of if one_block else core_of * sides + side_of
            return pl.ds(pl.multiple_of(block * width, 128), width)

        own = columns(side, core)

        def place(group_of, line_of, lanes=own):
            first = (group_of * lines + line_of) * layout.slab
            return out.at[pl.ds(pl.multiple_of(first, 16), layout.slab), lanes]

        def present(step):
            return None if step == 0 else line >= -step if step < 0 else line < lines - step

        yield
        for j in range(1, members):
            other = (member + j) % members
            desk.send(
                ("mix", j),
                shard.at[:, columns(other // 2, other % 2)],
                landing.at[member],
                desk.at(side=other // 2, core=other % 2),
            )
        mine = desk.local(0, shard.at[:, own], landing.at[member])
        mine.start()
        yield
        for j in range(1, members):
            desk.wait(("mix", j), landing.at[(member + members - j) % members])
        mine.wait()
        for m in range(members):
            rows = slice(m * layout.rows, (m + 1) * layout.rows)
            wide[rows, :] = landing[m, : layout.rows, :].astype(jnp.float32)
        slab[...] = wide[...].astype(slab.dtype)
        keep = desk.local(1, slab, place(group, line))
        keep.start()

        def pass_on(source, what, half, where, when):
            if half == 0 and (source == "own" or not line_last):
                desk.send(("cross", source), what, where, desk.at(group=1 - group), when)
            if not one_block:
                for j in range(1, sides):
                    slot = ("side", half, source, j)
                    desk.send(slot, what, where, desk.at(side=(side + j) % sides), when)

        def along(half, t, what, where, when):
            for way, further, to in (("up", has_up, line + 1), ("down", has_down, line - 1)):
                desk.send((way, half, t), what, where, desk.at(line=to), all_of(when, further))

        home = place(group, line)
        along(0, 0, slab, home, None)
        pass_on("own", slab, 0, home, None)
        yield

        def crossed():
            where = place(1 - group, line)
            desk.wait(("cross", "own"), where)
            pass_on("own", where, 1, where, None)
            if line_last:
                along(1, 0, where, where, None)

        if line_last:
            crossed()
            yield
        for t in range(1, lines):
            for half in halves:
                for way, name, step, further, to in (
                    ("up", "below", -t, has_up, line + 1),
                    ("down", "above", t, has_down, line - 1),
                ):
                    when, where = present(step), place(1 - group if half else group, line + step)
                    guarded(when, functools.partial(desk.wait, (way, half, t - 1), where))
                    desk.send(
                        (way, half, t), where, where, desk.at(line=to), all_of(when, further)
                    )
                    pass_on(f"{name}{t}", where, half, where, when)
            if t == 1 and not line_last:
                crossed()
            yield
        for t in range(1, 1 if line_last else lines):
            for name, step in ((f"below{t}", -t), (f"above{t}", t)):
                when, where = present(step), place(1 - group, line + step)
                guarded(when, functools.partial(desk.wait, ("cross", name), where))
                pass_on(name, where, 1, where, when)
            yield
        keep.wait()
        partner = desk.at(core=1 - core)
        desk.send(("core", 0), out.at[:, own], out.at[:, own], partner)
        if not one_block:
            yield
            for j in range(1, sides):
                theirs = columns((side + sides - j) % sides, core)
                for half, group_of in ((0, group), (1, 1 - group)):
                    for source, step in spots:
                        where = place(group_of, line + step, theirs)
                        slot = ("side", half, source, j)
                        guarded(present(step), functools.partial(desk.wait, slot, where))
                desk.send(("core", j), out.at[:, theirs], out.at[:, theirs], partner)
        yield
        desk.wait(("core", 0), out.at[:, columns(side, 1 - core)])
        if not one_block:
            for j in range(1, sides):
                theirs = columns((side + sides - j) % sides, 1 - core)
                desk.wait(("core", j), out.at[:, theirs])

    low = jnp.bfloat16
    return Work(
        steps,
        [(shard, anywhere())],
        [(jax.ShapeDtypeStruct((layout.model_width, shard.shape[1]), low), anywhere())],
        [
            pltpu.VMEM((members, layout.padded, width), low),
            pltpu.VMEM((layout.slab, width), low),
            pltpu.VMEM((layout.slab, width), jnp.float32),
        ],
        slots,
        2,
    )


def add_rows(target, first, target_columns, source, source_columns, count, source_first=0):
    step = math.gcd(count, 48)

    def one(index, carry):
        rows = pl.ds(pl.multiple_of(first + index * step, 16), step)
        theirs = pl.ds(pl.multiple_of(source_first + index * step, 16), step)
        total = target[rows, target_columns].astype(jnp.float32)
        total += source[theirs, source_columns].astype(jnp.float32)
        target[rows, target_columns] = total.astype(target.dtype)
        return carry

    lax.fori_loop(0, count // step, one, 0)


def reduce_work(layout, lefts, right, one_block, switch=0, split=3):
    lines, members, sides = layout.lines, layout.members, layout.sides
    tok, columns = right.shape
    blocks = layout.blocks(one_block)
    width, half = columns // blocks, columns // 2
    near_rows, slab_rows, low = layout.near, layout.slab, jnp.bfloat16
    count, depth = min(split, width // 128), min(4, lines)
    parts = []
    for index in range(count):
        first = width // 128 * index // count * 128
        parts.append((first, width // 128 * (index + 1) // count * 128 - first))
    order = []
    for t in range(lines):
        goal = lines - 1 - t // 2 if t % 2 == 0 else t // 2
        order.append(goal)
    slots = [("left", k) for k in range(len(lefts))] + ["right"]
    slots += [("cross", part, t) for part in parts for t in range(lines)]
    slots += [
        (way, part, t) for way in ("up", "down") for part in parts for t in range(1, lines)
    ]
    slots += [("mix", j) for j in range(1, members)]
    if not one_block:
        slots += [
            ("side", part, tag, t, j)
            for part in parts
            for tag in (0, 1)
            for t in range(lines)
            for j in range(1, sides)
        ]

    def steps(desk, ins, outs, scratch, common):
        left_in, right_in = ins[: len(lefts)], ins[len(lefts)]
        out, left_land, right_land = outs[0], outs[1 : 1 + len(lefts)], outs[1 + len(lefts)]
        total, cross, up, down, piece, landing, wide = scratch[:7]
        from_side = None if one_block else scratch[7]
        left_all, right_all = common
        group, line, member, side, core = desk.group, desk.line, desk.member, desk.side, desk.core
        partner = desk.at(core=1 - core)
        own = pl.ds(0 if one_block else pl.multiple_of(side * width, 128), width)
        stay = pl.ds(pl.multiple_of(core * half, 128), half)
        away = pl.ds(pl.multiple_of((1 - core) * half, 128), half)

        def first_of(tag, goal):
            return pl.multiple_of((group if tag else 1 - group) * near_rows + goal * slab_rows, 16)

        yield
        for k, left in enumerate(left_in):
            desk.send(("left", k), left, left_land[k], partner)
        desk.send("right", right_in.at[:, away], right_land, partner)
        yield
        loads = []

        def load(source, target):
            copy = desk.local(len(loads), source, target)
            copy.start()
            loads.append(copy)

        for k, left in enumerate(left_in):
            load(left, left_all.at[k, 0])
        load(right_in.at[:, stay], right_all.at[0, :, pl.ds(0, half)])
        for k in range(len(left_in)):
            desk.wait(("left", k), left_land[k])
            load(left_land[k], left_all.at[k, 1])
        desk.wait("right", right_land)
        load(right_land, right_all.at[1, :, pl.ds(0, half)])
        for copy in loads:
            copy.wait()

        def multiply(tag):
            rows = pl.ds(first_of(tag, 0), near_rows)

            def piece_of(first, lanes, which):
                theirs = pl.ds(first, lanes)
                product = dot_nn(left_all[which, 0, rows, :], right_all[0, :, theirs])
                product += dot_nn(left_all[which, 1, rows, :], right_all[1, :, theirs])
                total[rows, theirs] = product.astype(low)

            lanes = 256 if len(lefts) == 1 else math.gcd(switch, 384)

            def one(index, carry):
                first = pl.multiple_of(index * lanes, 128)
                which = 0
                if len(lefts) > 1:
                    which = jnp.where(core * half + index * lanes >= switch, 1, 0)
                piece_of(first, lanes, which)
                return carry

            lax.fori_loop(0, half // lanes, one, 0)
            if half % lanes:
                piece_of(half // lanes * lanes, half % lanes, 0)

        own_first = 0 if one_block else side * width
        pieces = [
            (part, tag, goal)
            for part in parts
            for tag in ((0,) if one_block else (0, 1))
            for goal in order
        ]

        def lanes_of(part, first):
            return pl.ds(pl.multiple_of(first + part[0], 128), part[1])

        def post(number):
            if number >= len(pieces):
                return
            part, tag, goal = pieces[number]
            if one_block:
                if number >= depth:
                    before = pieces[number - depth]
                    desk.settle(("cross", before[0], before[2]))
                send_across(part, goal)
                return
            rows = pl.ds(first_of(tag, goal), slab_rows)
            for j in range(1, sides):
                if number >= depth:
                    desk.settle(("side", *pieces[number - depth], j))
                other = (side + j) % sides
                desk.send(
                    ("side", part, tag, goal, j),
                    total.at[rows, lanes_of(part, other * width)],
                    from_side.at[j - 1, rows, lanes_of(part, 0)],
                    desk.at(side=other),
                )

        def send_across(part, goal):
            rows = pl.ds(first_of(0, goal), slab_rows)
            desk.send(
                ("cross", part, goal),
                total.at[rows, lanes_of(part, own_first)],
                cross.at[goal, :, lanes_of(part, 0)],
                desk.at(group=1 - group),
            )

        def take_side(part, tag, goal):
            first = first_of(tag, goal)
            rows, lanes = pl.ds(first, slab_rows), lanes_of(part, 0)
            for j in range(1, sides):
                desk.wait(("side", part, tag, goal, j), from_side.at[j - 1, rows, lanes])
            post(pieces.index((part, tag, goal)) + depth)
            for j in range(1, sides):
                add_rows(
                    total, first, lanes_of(part, own_first), from_side.at[j - 1], lanes,
                    slab_rows, first,
                )

        ends = lines - 1 - line

        def part_steps(part):
            lanes, mine = lanes_of(part, 0), lanes_of(part, own_first)
            if not one_block:
                for goal in order:
                    take_side(part, 0, goal)
                    send_across(part, goal)
                    yield
            for goal in order:
                if not one_block:
                    take_side(part, 1, goal)
                desk.wait(("cross", part, goal), cross.at[goal, :, lanes])
                if one_block:
                    post(pieces.index((part, 0, goal)) + depth)
                add_rows(total, first_of(1, goal), mine, cross.at[goal], lanes, slab_rows)
                yield
            for t in range(1, lines):
                for way, buffer, going, fed, goal, to in (
                    ("up", up, line < t, line > 0, lines - t + line, line + 1),
                    ("down", down, ends < t, ends > 0, t - lines + line, line - 1),
                ):
                    first = first_of(1, goal)

                    @pl.when(all_of(going, fed))
                    def _():
                        if t > 1:
                            desk.wait((way, part, t - 1), buffer.at[t - 2, :, lanes])
                            add_rows(total, first, mine, buffer.at[t - 2], lanes, slab_rows)

                    desk.send(
                        (way, part, t),
                        total.at[pl.ds(first, slab_rows), mine],
                        buffer.at[t - 1, :, lanes],
                        desk.at(line=to),
                        going,
                    )
                yield

        multiply(0)
        for number in range(depth):
            post(number)
        yield
        multiply(1)
        yield
        running = [part_steps(part) for part in parts]
        turn, lag = 0, len(pieces) // len(parts)
        while running:
            for index, steps_of in enumerate(running):
                if steps_of is not None and turn >= lag * index:
                    try:
                        next(steps_of)
                    except StopIteration:
                        running[index] = None
            if not any(running):
                break
            turn += 1
            yield
        first = first_of(1, line)
        wide[...] = total[pl.ds(first, slab_rows), own].astype(jnp.float32)
        for way, buffer, fed in (("up", up, line > 0), ("down", down, ends > 0)):

            @pl.when(fed)
            def _():
                for part in parts:
                    where = buffer.at[lines - 2, :, lanes_of(part, 0)]
                    desk.wait((way, part, lines - 1), where)
                wide[...] += buffer[lines - 2].astype(jnp.float32)

        for m in range(members):
            rows = slice(m * layout.rows, (m + 1) * layout.rows)
            piece[m] = jnp.zeros(piece.shape[1:], piece.dtype)
            piece[m, : layout.rows, :] = wide[rows, :].astype(piece.dtype)
        seat = core * sides + side
        for j in range(1, members):
            other = (member + j) % members
            desk.send(
                ("mix", j),
                piece.at[other],
                landing.at[seat],
                desk.at(side=other // 2, core=other % 2),
            )
        landing[seat] = piece[member]
        yield
        for j in range(1, members):
            other = (member + members - j) % members
            desk.wait(("mix", j), landing.at[other % 2 * sides + other // 2])
        if one_block:
            for c in range(2):
                block = landing[c * sides].astype(jnp.float32)
                for s in range(1, sides):
                    block += landing[c * sides + s].astype(jnp.float32)
                out[:, c * width : (c + 1) * width] = block
        else:
            for b in range(blocks):
                out[:, b * width : (b + 1) * width] = landing[b].astype(jnp.float32)

    scratch = [
        pltpu.VMEM((layout.model_width, half), low),
        pltpu.VMEM((lines, slab_rows, width), low),
        pltpu.VMEM((lines - 1, slab_rows, width), low),
        pltpu.VMEM((lines - 1, slab_rows, width), low),
        pltpu.VMEM((members, layout.padded, width), low),
        pltpu.VMEM((members, layout.padded, width), low),
        pltpu.VMEM((slab_rows, width), jnp.float32),
    ]
    if not one_block:
        scratch.append(pltpu.VMEM((sides - 1, layout.model_width, width), low))
    ins = [(array, anywhere()) for array in [*lefts, right]]
    return Work(
        steps,
        ins,
        [(jax.ShapeDtypeStruct((layout.padded, columns), jnp.float32), in_vmem())]
        + [(jax.ShapeDtypeStruct(left.shape, low), anywhere()) for left in lefts]
        + [(jax.ShapeDtypeStruct((tok, half), low), anywhere())],
        scratch,
        slots,
        2 * len(lefts) + 2,
    )


class Reach:
    def __init__(self, tok, left, right):
        self.tok, self.left, self.right = tok, left, right
        self.window = left + tok + right
        self.deltas = [d for d in range(-8, 9) if d != 0 and self.rows(d) > 0]

    def first(self, delta):
        return max(0, self.tok * delta - self.left)

    def rows(self, delta):
        last = min(self.tok, self.tok * delta - self.left + self.window)
        return last - self.first(delta)

    def spot(self, delta):
        return self.first(delta) - self.tok * delta + self.left


def parts_of(count, step=80):
    return [(first, min(step, count - first)) for first in range(0, count, step)]


def window_work(layout, reach, key_value):
    tok, width = key_value.shape
    left, lines, places = reach.left, layout.lines, layout.lines * layout.members
    routed = layout.sides == 2
    pieces, depth = parts_of(tok), 2
    near_below, far_below = reach.spot(2), reach.spot(3)
    tail = (reach.first(3), max(reach.rows(3), 0))
    head = max(reach.rows(-2), 0)
    if routed:
        slots = ["pair", "tail", "share", "wide", "thin", "last"]
        slots += [(name, k) for name in ("right", "left", "climb", "drop") for k in range(len(pieces))]
        slots += [("fall", k) for k in range(len(parts_of(head)))]
    else:
        slots = [("reach", delta) for delta in reach.deltas]

    def direct(desk, own, window):
        seat = desk.line * layout.members + desk.member
        for delta in reach.deltas:
            count = reach.rows(delta)
            desk.send(
                ("reach", delta),
                own.at[pl.ds(reach.first(delta), count)],
                window.at[pl.ds(reach.spot(delta), count)],
                (desk.group, seat + delta),
                (seat + delta >= 0) & (seat + delta < places),
            )
        yield
        for delta in reach.deltas:
            where = window.at[pl.ds(reach.spot(delta), reach.rows(delta))]
            when = (seat - delta >= 0) & (seat - delta < places)
            guarded(when, functools.partial(desk.wait, ("reach", delta), where))

    def by_way(desk, own, window, transit):
        line, core = desk.line, desk.core
        first_side, last_side = desk.side == 0, desk.side == 1
        low_core, high_core = core == 0, core == 1
        has_up, has_down = line < lines - 1, line > 0
        has_before = last_side | has_down
        partner = desk.at(core=1 - core)

        def part(ref, first, count):
            return ref.at[pl.ds(first, count)]

        def post(k):
            if k >= len(pieces):
                return
            if k >= depth:
                desk.settle(("right", k - depth))
                desk.settle(("left", k - depth))
            first, count = pieces[k]
            desk.send(
                ("right", k), part(own, first, count), part(window, near_below + first, count),
                desk.at(side=1), first_side,
            )
            desk.send(
                ("left", k), part(own, first, count), part(transit, first, count),
                desk.at(side=0), last_side,
            )

        for k in range(depth):
            post(k)
        desk.send(
            "tail", part(own, *tail), part(window, far_below, tail[1]),
            desk.at(line=line + 1, core=0), high_core & has_up,
        )
        mirrored = pl.multiple_of(left + (2 * core - 1) * tok, 16)
        desk.send("pair", own, part(window, mirrored, tok), partner)
        yield
        for k, (first, count) in enumerate(pieces):
            ahead = part(transit, first, count)
            guarded(first_side, functools.partial(desk.wait, ("left", k), ahead))
            desk.send(
                ("climb", k), ahead, part(window, near_below + first, count),
                desk.at(line=line + 1), first_side & has_up,
            )
            behind = part(window, near_below + first, count)
            guarded(last_side, functools.partial(desk.wait, ("right", k), behind))
            post(k + depth)
            desk.send(
                ("drop", k), behind, part(window, left + tok + first, count),
                desk.at(line=line - 1, core=1), last_side & has_down & low_core,
            )
            if first < head:
                count = min(count, head - first)
                desk.send(
                    ("fall", k), part(window, near_below + first, count),
                    part(window, left + 2 * tok + first, count),
                    desk.at(line=line - 1), last_side & has_down & high_core,
                )
            yield
        stay = desk.local(1, part(transit, 0, head), part(window, left + 2 * tok, head))
        guarded(first_side, stay.start)
        desk.send(
            "share", transit, part(window, left + tok, tok), partner, first_side & low_core
        )

        def share_before(when):
            desk.send(
                "wide", part(window, near_below, tok), part(window, left - tok, tok), partner,
                when & high_core,
            )
            desk.send(
                "thin", part(window, near_below + tail[0], tail[1]),
                part(window, far_below, tail[1]), partner, when & low_core,
            )

        def climbed():
            for k, (first, count) in enumerate(pieces):
                desk.wait(("climb", k), part(window, near_below + first, count))

        guarded(first_side & has_down, climbed)
        share_before(has_before)
        yield

        def dropped():
            for k, (first, count) in enumerate(pieces):
                desk.wait(("drop", k), part(window, left + tok + first, count))
            for k, (first, count) in enumerate(parts_of(head)):
                desk.wait(("fall", k), part(window, left + 2 * tok + first, count))

        guarded(last_side & has_up & high_core, dropped)
        desk.send(
            "last", part(window, left + tok, head), part(window, left + 2 * tok, head), partner,
            last_side & has_up & high_core,
        )
        yield
        desk.wait("pair", part(window, pl.multiple_of(left + (1 - 2 * core) * tok, 16), tok))
        for when, slot, first, count in (
            (low_core & has_down, "tail", far_below, tail[1]),
            (first_side & high_core, "share", left + tok, tok),
            (has_before & low_core, "wide", left - tok, tok),
            (has_before & high_core, "thin", far_below, tail[1]),
            (last_side & has_up & low_core, "last", left + 2 * tok, head),
        ):
            guarded(when, functools.partial(desk.wait, slot, part(window, first, count)))
        guarded(first_side, stay.wait)

    def steps(desk, ins, outs, scratch, common):
        (own,), (window,) = ins, outs
        keep = desk.local(0, own, window.at[pl.ds(left, tok)])
        keep.start()
        yield from by_way(desk, own, window, *scratch) if routed else direct(desk, own, window)
        keep.wait()

    outs = [(jax.ShapeDtypeStruct((reach.window, width), key_value.dtype), anywhere())]
    scratch = [pltpu.VMEM((tok, width), key_value.dtype)] if routed else []
    return Work(steps, [(key_value, in_vmem())], outs, scratch, slots, 2)


def owned_work(layout, reach, grad_window):
    width = grad_window.shape[1]
    tok, left, lines = reach.tok, reach.left, layout.lines
    places = layout.lines * layout.members
    routed = layout.sides == 2
    pieces, depth = parts_of(tok), 2
    near_below, far_below = reach.spot(2), reach.spot(3)
    tail = (reach.first(3), max(reach.rows(3), 0))
    head = max(reach.rows(-2), 0)
    every = pl.ds(0, width)
    low = grad_window.dtype
    if routed:
        slots = ["pair", "tail", "share", "wide", "thin", "last", "rise"]
        slots += [(name, k) for name in ("right", "left", "fall", "lift") for k in range(len(pieces))]
    else:
        slots = [("reach", delta) for delta in reach.deltas]

    def direct(desk, grad, out, landing):
        seat = desk.line * layout.members + desk.member
        for delta in reach.deltas:
            count = reach.rows(delta)
            desk.send(
                ("reach", delta),
                grad.at[pl.ds(reach.spot(delta), count)],
                landing[delta],
                (desk.group, seat - delta),
                (seat - delta >= 0) & (seat - delta < places),
            )
        load = desk.local(0, grad.at[pl.ds(left, tok)], out)
        load.start()
        load.wait()
        yield
        for delta in reach.deltas:

            @pl.when((seat + delta >= 0) & (seat + delta < places))
            def _():
                desk.wait(("reach", delta), landing[delta])
                first, count = reach.first(delta), reach.rows(delta)
                add_rows(out, first, every, landing[delta], every, count)

    def by_way(desk, grad, out, scratch):
        near, middle, l_wide, l_far, l_climb, l_y, l_pair, l_tail = scratch
        line, core = desk.line, desk.core
        first_side, last_side = desk.side == 0, desk.side == 1
        low_core, high_core = core == 0, core == 1
        has_up, has_down = line < lines - 1, line > 0
        has_before = last_side | has_down
        gate = last_side & has_up & high_core
        partner = desk.at(core=1 - core)

        def part(ref, first, count):
            return ref.at[pl.ds(first, count)]

        def receive(when, slot, target, first, buffer, at, count):
            @pl.when(when)
            def _():
                desk.wait(slot, part(buffer, at, count))
                add_rows(target, first, every, buffer, every, count, at)

        desk.send(
            "last", part(grad, left + 2 * tok, head), part(l_climb, 0, head), partner,
            last_side & has_up & low_core,
        )
        desk.send(
            "wide", part(grad, left - tok, tok), l_wide, partner, has_before & low_core
        )
        desk.send(
            "thin", part(grad, far_below, tail[1]), part(l_wide, 0, tail[1]), partner,
            has_before & high_core,
        )
        desk.send(
            "share", part(grad, left + tok, tok), l_far, partner, first_side & high_core
        )
        desk.send(
            "tail", part(grad, far_below, tail[1]), l_tail,
            desk.at(line=line - 1, core=1), low_core & has_down,
        )
        desk.send("rise", part(grad, left + 2 * tok, head), part(l_far, 0, head),
            desk.at(line=line + 1), gate,
        )
        loads = [
            (desk.local(0, part(grad, near_below, tok), near), None),
            (desk.local(1, part(grad, left + tok, tok), middle), last_side),
            (desk.local(2, part(grad, left + 2 * tok, head), part(middle, 0, head)), first_side),
            (desk.local(3, part(grad, left, tok), out), None),
        ]
        for load, when in loads:
            guarded(when, load.start)

        @pl.when(first_side)
        def _():
            middle[head:, :] = jnp.zeros((tok - head, width), low)

        yield
        for load, when in loads:
            guarded(when, load.wait)
        receive(gate, "last", middle, 0, l_climb, 0, head)
        receive(has_before & high_core, "wide", near, 0, l_wide, 0, tok)
        receive(has_before & low_core, "thin", near, tail[0], l_wide, 0, tail[1])

        def post(k):
            if k >= len(pieces):
                return
            if k >= depth:
                desk.settle(("fall", k - depth))
                desk.settle(("lift", k - depth))
            first, count = pieces[k]
            desk.send(
                ("fall", k), part(middle, first, count), part(l_far, first, count),
                desk.at(line=line + 1, core=0), gate,
            )
            desk.send(
                ("lift", k), part(near, first, count), part(l_climb, first, count),
                desk.at(line=line - 1), first_side & has_down,
            )

        for k in range(depth):
            post(k)
        mirrored = pl.multiple_of(left + (1 - 2 * core) * tok, 16)
        desk.send("pair", part(grad, mirrored, tok), l_pair, partner)
        yield
        receive(first_side & low_core, "share", middle, 0, l_far, 0, tok)
        receive(last_side & has_down & high_core, "rise", near, 0, l_far, 0, head)
        for k, (first, count) in enumerate(pieces):
            receive(first_side & has_up, ("lift", k), middle, first, l_climb, first, count)
            desk.send(
                ("left", k), part(middle, first, count), part(l_y, first, count),
                desk.at(side=1), first_side,
            )
            receive(
                last_side & has_down & low_core, ("fall", k), near, first, l_far, first, count
            )
            desk.send(
                ("right", k), part(near, first, count), part(l_y, first, count),
                desk.at(side=0), last_side,
            )
            post(k + depth)
            yield
        receive(has_up & high_core, "tail", out, tail[0], l_tail, 0, tail[1])
        desk.wait("pair", l_pair)
        for k, (first, count) in enumerate(pieces):
            where = part(l_y, first, count)
            guarded(first_side, functools.partial(desk.wait, ("right", k), where))
            guarded(last_side, functools.partial(desk.wait, ("left", k), where))

            def one(index, carry):
                rows = pl.ds(pl.multiple_of(first + index * 16, 16), 16)
                total = out[rows, :].astype(jnp.float32) + l_pair[rows, :].astype(jnp.float32)
                out[rows, :] = (total + l_y[rows, :].astype(jnp.float32)).astype(out.dtype)
                return carry

            lax.fori_loop(0, count // 16, one, 0)
            yield

    def steps(desk, ins, outs, scratch, common):
        if routed:
            yield from by_way(desk, ins[0], outs[0], scratch)
        else:
            yield from direct(desk, ins[0], outs[0], dict(zip(reach.deltas, scratch)))

    if routed:
        counts = [tok] * 7 + [tail[1]]
    else:
        counts = [reach.rows(delta) for delta in reach.deltas]
    return Work(
        steps,
        [(grad_window, anywhere())],
        [(jax.ShapeDtypeStruct((tok, width), low), in_vmem())],
        [pltpu.VMEM((count, width), low) for count in counts],
        slots,
        4,
    )


def sum_work(layout, block):
    sizes = (2, layout.sides, layout.model_width // layout.near, layout.lines)
    slots = [(stage, j) for stage, size in enumerate(sizes) for j in range(1, size)]

    def steps(desk, ins, outs, scratch, common):
        (block,), (out,) = ins, outs
        yield
        out[...] = block[...]
        for stage, (landing, size) in enumerate(zip(scratch, sizes)):
            mine = (desk.core, desk.side, desk.group, desk.line)[stage]
            landing[mine] = out[...]
            for j in range(1, size):
                other = (mine + j) % size
                to = desk.at(**{("core", "side", "group", "line")[stage]: other})
                desk.send((stage, j), landing.at[mine], landing.at[mine], to)
            yield
            for j in range(1, size):
                desk.wait((stage, j), landing.at[(mine + size - j) % size])
            total = landing[0]
            for j in range(1, size):
                total = total + landing[j]
            out[...] = total

    return Work(
        steps,
        [(block, in_vmem())],
        [(jax.ShapeDtypeStruct(block.shape, block.dtype), in_vmem())],
        [pltpu.VMEM((size, *block.shape), block.dtype) for size in sizes],
        slots,
        1,
    )


def lane_mean(source):
    return jnp.mean(source, axis=1, keepdims=True)


def unit_of(source):
    centred = source - lane_mean(source)
    inv_scale = lax.rsqrt(lane_mean(centred * centred) + eps_norm)
    return centred * inv_scale, inv_scale


def norm_input_gradient(gradient, unit_rows, inv_scale, gain_row):
    scaled = gradient * gain_row
    return inv_scale * (scaled - lane_mean(scaled) - unit_rows * lane_mean(scaled * unit_rows))


def rows_sum(source):
    return jnp.sum(source.astype(jnp.float32), axis=0, keepdims=True)


def gelu_and_slope(source):
    square = source * source
    curve = jnp.tanh(gelu_rate * source * (1.0 + gelu_cube * square))
    rise = gelu_rate * (1.0 + 3.0 * gelu_cube * square)
    half_sum = 0.5 * (1.0 + curve)
    return source * half_sum, half_sum + 0.5 * source * (1.0 - curve * curve) * rise


def chunks_of(columns, lanes=768):
    return [(first, min(lanes, columns - first)) for first in range(0, columns, lanes)]


def moves(sources, targets, sems):
    return [
        pltpu.make_async_copy(source, target, sems.at[index])
        for index, (source, target) in enumerate(zip(sources, targets))
    ]


def projection_forward_kernel(
    residual, rows, weight, normed_out, inv_out, query_out, pair_out, unit_out, held, sems
):
    width = rows.shape[1]
    sources = [weight.at[:, pl.ds(j * width, width)] for j in range(3)]
    loads = moves(sources, [held.at[j] for j in range(3)], sems)
    for load in loads:
        load.start()
    unit_rows, inv_scale = unit_of(residual[...].astype(jnp.float32))
    unit_out[...] = unit_rows
    inv_out[...] = jnp.broadcast_to(inv_scale, inv_out.shape)
    normed = (unit_rows * rows[0:1, :] + rows[1:2, :]).astype(normed_out.dtype)
    normed_out[...] = normed
    loads[0].wait()
    query_out[...] = (dot_nn(normed_out[...], held[0]) + rows[2:3, :]).astype(query_out.dtype)
    loads[1].wait()
    pair_out[:, :width] = dot_nn(normed_out[...], held[1]).astype(pair_out.dtype)
    loads[2].wait()
    values = dot_nn(normed_out[...], held[2]) + rows[3:4, :]
    pair_out[:, width:] = values.astype(pair_out.dtype)


def dense_call(kernel, name, ins, outs, scratch, *arrays):
    return pl.pallas_call(
        kernel,
        name=name,
        in_specs=ins,
        out_specs=[spec for _, spec in outs],
        out_shape=[shape for shape, _ in outs],
        scratch_shapes=scratch,
        compiler_params=pltpu.CompilerParams(vmem_limit_bytes=60 * mib),
    )(*arrays)


def kept(shape, kind=jnp.bfloat16):
    return (jax.ShapeDtypeStruct(shape, kind), in_vmem())


def projection_forward(residual, rows, attn_weight):
    tok, width = residual.shape
    return dense_call(
        projection_forward_kernel,
        "projection_forward",
        [in_vmem(), in_vmem(), anywhere()],
        [
            kept((tok, width)),
            kept((tok, 128), jnp.float32),
            kept((tok, width)),
            kept((tok, 2 * width)),
            kept((tok, width), jnp.float32),
        ],
        [pltpu.VMEM((3, width, width), jnp.bfloat16), pltpu.SemaphoreType.DMA((3,))],
        residual,
        rows,
        attn_weight,
    )


def whole(shape):
    return pl.BlockSpec(shape, lambda step: (0,) * len(shape))


def projection_backward_kernel(
    grad_query, grad_pair, weight, unit, inv, rows, grad_mid, grad_res, sums, acc
):
    step = pl.program_id(0)
    width = grad_query.shape[1]

    @pl.when(step == 0)
    def _():
        acc[...] = dot_nt(grad_query[...], weight[...])

    @pl.when(step == 1)
    def _():
        acc[...] += dot_nt(grad_pair[:, :width], weight[...])

    @pl.when(step == 2)
    def _():
        gradient = acc[...] + dot_nt(grad_pair[:, width:], weight[...])
        unit_rows = unit[...]
        grad_res[...] = grad_mid[...] + norm_input_gradient(
            gradient, unit_rows, inv[:, 0:1], rows[0:1, :]
        )
        sums[...] = jnp.zeros_like(sums)
        sums[0:1, :] = rows_sum(gradient * unit_rows)
        sums[1:2, :] = rows_sum(gradient)
        sums[2:3, :] = rows_sum(grad_query[...])
        sums[3:4, :] = rows_sum(grad_pair[:, width:])


def projection_backward(grad_query, grad_pair, attn_weight, unit, inv, rows, grad_mid):
    tok, width = grad_query.shape
    return pl.pallas_call(
        projection_backward_kernel,
        name="projection_backward",
        grid=(3,),
        in_specs=[
            whole((tok, width)),
            whole((tok, 2 * width)),
            pl.BlockSpec((width, width), lambda step: (0, step)),
            whole((tok, width)),
            whole((tok, 128)),
            whole(rows.shape),
            whole((tok, width)),
        ],
        out_specs=[whole((tok, width)), whole((8, width))],
        out_shape=[
            jax.ShapeDtypeStruct((tok, width), jnp.float32),
            jax.ShapeDtypeStruct((8, width), jnp.float32),
        ],
        scratch_shapes=[pltpu.VMEM((tok, width), jnp.float32)],
        compiler_params=pltpu.CompilerParams(vmem_limit_bytes=58 * mib),
    )(grad_query, grad_pair, attn_weight, unit, inv, rows, grad_mid)


class Stream:
    def __init__(self, source, held, sems, chunks):
        self.held, self.chunks = held, chunks
        self.copies = [
            pltpu.make_async_copy(
                source.at[:, pl.ds(first, count)], held.at[k % 2, :, pl.ds(0, count)], sems.at[k]
            )
            for k, (first, count) in enumerate(chunks)
        ]

    def start(self, k):
        if k < len(self.chunks):
            self.copies[k].start()

    def take(self, k):
        self.copies[k].wait()
        return self.held[k % 2, :, : self.chunks[k][1]]


def mlp_forward_kernel(
    chunks, attended, residual, attn_weight, rows, up_weight, up_shift, down_weight,
    residual_out, hidden_out, inv_out, unit_out, active_out, slope_out,
    out_held, up_held, down_held, active_held, slope_held, sems,
):
    width, count = rows.shape[1], len(chunks)
    load = pltpu.make_async_copy(attn_weight.at[:, pl.ds(3 * width, width)], out_held, sems.at[4, 0])
    load.start()
    up = Stream(up_weight, up_held, sems.at[0], chunks)
    down = Stream(down_weight, down_held, sems.at[1], chunks)
    up.start(0)
    down.start(0)
    up.start(1)
    load.wait()
    middle = residual[...].astype(jnp.float32) + rows[4:5, :] + dot_nn(attended[...], out_held[...])
    residual_out[...] = middle + rows[5:6, :]
    unit_rows, inv_scale = unit_of(middle)
    unit_out[...] = unit_rows
    inv_out[...] = jnp.broadcast_to(inv_scale, inv_out.shape)
    hidden_out[...] = (unit_rows * rows[6:7, :] + rows[7:8, :]).astype(hidden_out.dtype)
    ahead = dot_nn(hidden_out[...], up.take(0))
    stores = []
    for k, (first, lanes) in enumerate(chunks):
        now = ahead
        columns = pl.ds(first, lanes)
        up.start(k + 2)
        down.start(k + 1)
        if k + 1 < count:
            ahead = dot_nn(hidden_out[...], up.take(k + 1))
        value, slope = gelu_and_slope(now + up_shift[:, columns])
        active_held[:, columns] = value.astype(active_held.dtype)
        slope_held[:, columns] = slope.astype(slope_held.dtype)
        for row, held, target in ((2, active_held, active_out), (3, slope_held, slope_out)):
            store = pltpu.make_async_copy(
                held.at[:, columns], target.at[:, columns], sems.at[row, k]
            )
            store.start()
            stores.append(store)
        residual_out[...] += dot_nt(active_held[:, columns], down.take(k))
    for store in stores:
        store.wait()


def mlp_forward(attended, residual, attn_weight, rows, up_weight, up_shift, down_weight):
    tok, width = attended.shape
    columns = up_shift.shape[1]
    chunks = chunks_of(columns)
    hidden = (jax.ShapeDtypeStruct((tok, columns), jnp.bfloat16), anywhere())
    weight_chunk = pltpu.VMEM((2, width, chunks[0][1]), jnp.bfloat16)
    hidden_held = pltpu.VMEM((tok, columns), jnp.bfloat16)
    return dense_call(
        functools.partial(mlp_forward_kernel, chunks),
        "mlp_forward",
        [in_vmem(), in_vmem(), anywhere(), in_vmem(), anywhere(), in_vmem(), anywhere()],
        [
            kept((tok, width), jnp.float32),
            kept((tok, width)),
            kept((tok, 128), jnp.float32),
            kept((tok, width), jnp.float32),
            hidden,
            hidden,
        ],
        [pltpu.VMEM((width, width), jnp.bfloat16)]
        + [weight_chunk] * 2
        + [hidden_held] * 2
        + [pltpu.SemaphoreType.DMA((5, len(chunks)))],
        attended,
        residual,
        attn_weight,
        rows,
        up_weight,
        up_shift,
        down_weight,
    )


def mlp_backward_kernel(
    chunks, grad_res, down_weight, slope, up_weight, unit, inv, rows, attn_weight,
    grad_pre, up_sum, grad_branch, grad_mid, grad_attn, grad_attended, sums,
    out_held, up_held, down_held, pre_held, acc, sems,
):
    width, count = rows.shape[1], len(chunks)
    down = Stream(down_weight, down_held, sems.at[1], chunks)
    up = Stream(up_weight, up_held, sems.at[0], chunks)
    down.start(0)
    up.start(0)
    down.start(1)
    load = pltpu.make_async_copy(attn_weight.at[:, pl.ds(3 * width, width)], out_held, sems.at[3, 0])
    load.start()
    grad_branch[...] = grad_res[...].astype(grad_branch.dtype)
    acc[...] = jnp.zeros_like(acc)
    ahead = dot_nn(grad_branch[...], down.take(0))
    stores = []
    for k, (first, lanes) in enumerate(chunks):
        now = ahead
        columns = pl.ds(first, lanes)
        down.start(k + 2)
        up.start(k + 1)
        if k + 1 < count:
            ahead = dot_nn(grad_branch[...], down.take(k + 1))
        low = (now * slope[:, columns].astype(jnp.float32)).astype(jnp.bfloat16)
        pre_held[:, columns] = low
        up_sum[:, columns] = rows_sum(low)
        store = pltpu.make_async_copy(
            pre_held.at[:, columns], grad_pre.at[:, columns], sems.at[2, k]
        )
        store.start()
        stores.append(store)
        acc[...] += dot_nt(pre_held[:, columns], up.take(k))
    gradient = acc[...]
    unit_rows = unit[...]
    middle = grad_res[...].astype(jnp.float32) + norm_input_gradient(
        gradient, unit_rows, inv[:, 0:1], rows[6:7, :]
    )
    grad_mid[...] = middle
    grad_attn[...] = middle.astype(grad_attn.dtype)
    load.wait()
    grad_attended[...] = dot_nt(grad_attn[...], out_held[...]).astype(grad_attended.dtype)
    sums[...] = jnp.zeros_like(sums)
    sums[0:1, :] = rows_sum(gradient * unit_rows)
    sums[1:2, :] = rows_sum(gradient)
    sums[2:3, :] = rows_sum(grad_attn[...])
    sums[3:4, :] = rows_sum(grad_branch[...])
    for store in stores:
        store.wait()


def mlp_backward(grad_res, down_weight, slope, up_weight, unit, inv, rows, attn_weight):
    tok, width = grad_res.shape
    columns = slope.shape[1]
    chunks = chunks_of(columns)
    weight_chunk = pltpu.VMEM((2, width, chunks[0][1]), jnp.bfloat16)
    return dense_call(
        functools.partial(mlp_backward_kernel, chunks),
        "mlp_backward",
        [in_vmem(), anywhere(), in_vmem(), anywhere(), in_vmem(), in_vmem(), in_vmem(), anywhere()],
        [
            (jax.ShapeDtypeStruct((tok, columns), jnp.bfloat16), anywhere()),
            kept((1, columns), jnp.float32),
            kept((tok, width)),
            kept((tok, width), jnp.float32),
            kept((tok, width)),
            kept((tok, width)),
            kept((8, width), jnp.float32),
        ],
        [pltpu.VMEM((width, width), jnp.bfloat16)]
        + [weight_chunk] * 2
        + [
            pltpu.VMEM((tok, columns), jnp.bfloat16),
            pltpu.VMEM((tok, width), jnp.float32),
            pltpu.SemaphoreType.DMA((4, len(chunks))),
        ],
        grad_res,
        down_weight,
        slope,
        up_weight,
        unit,
        inv,
        rows,
        attn_weight,
    )


def adam_step(weight_now, gradient, first_old, second_old):
    first_new = beta_first * first_old + (1.0 - beta_first) * gradient
    second_new = beta_second * second_old + (1.0 - beta_second) * gradient * gradient
    first_hat = first_new / (1.0 - beta_first**STEP)
    second_hat = second_new / (1.0 - beta_second**STEP)
    update = -learn_rate * (
        first_hat / (jnp.sqrt(second_hat) + eps_adam)
        + weight_decay * weight_now.astype(jnp.float32)
    )
    return (first_new, second_new, update)


def round_up(count, unit):
    return -(-count // unit) * unit


def per_device(
    inputs, image_ids, token_mask, cotangent,
    w_qkv, w_out, w_up, w_down, norm_gains, bias_rows, up_bias,
    first_qkv, first_out, first_up, first_down, first_gains, first_bias, first_upbias,
    second_qkv, second_out, second_up, second_down, second_gains, second_bias, second_upbias,
):
    tok, width = inputs.shape
    layers, _, hidden_width = w_up.shape
    places = lax.axis_size("seq")
    place = lax.axis_index("seq")
    layout = Layout(lax.axis_size("dp"), places, width)
    group_tok = tok * places
    spare_count = group_tok - group_tok // IMG * IMG
    left = round_up(IMG - 1 + spare_count, 16)
    right = round_up(IMG - 1, 16)
    tile = tok // 2

    reach = Reach(tok, left, right)

    half = hidden_width // 2
    half_pad = round_up(half + 8 * layers, 128)
    wide_columns = 2 * half_pad

    def spread(array):
        pad = [(0, 0)] * (array.ndim - 1) + [(0, half_pad - half)]
        return jnp.concatenate([jnp.pad(array[..., :half], pad), jnp.pad(array[..., half:], pad)], -1)

    def unspread(array):
        return jnp.concatenate(
            [array[..., :half], array[..., half_pad : half_pad + half]], axis=-1
        )

    def filled(array, rows, columns):
        return jnp.pad(array, ((0, rows - array.shape[0]), (0, columns - array.shape[1])))

    attn_columns = layout.columns(4 * width, False)
    up_columns = layout.columns(wide_columns, True)
    down_columns = layout.columns(wide_columns, False)
    rows_of = jnp.concatenate([norm_gains.reshape(-1, layout.rows), bias_rows.reshape(-1, layout.rows)])
    row_count = rows_of.shape[0]
    shards = []
    for layer in range(layers):
        attn_shard = jnp.concatenate([w_qkv[layer], w_out[layer]], axis=1)
        up_shard = spread(w_up[layer])
        if layer == 0:
            up_shard = up_shard.at[:, half : half + row_count].set(rows_of.T)
        down_shard = spread(w_down[layer].T)
        shards += [
            filled(attn_shard, layout.padded, attn_columns),
            filled(up_shard, layout.padded, up_columns),
            filled(down_shard, layout.padded, down_columns if layer else up_columns),
        ]
    word = jnp.broadcast_to(image_ids[:, None], (tok, 128))
    def gather(layer, which):
        return gather_work(layout, shards[3 * layer + which], which == 1 or (which == 2 and layer == 0))

    gathered = [[None] * 3 for _ in range(layers)]
    begun = [(0, 1), (0, 0), (0, 2)]
    for layer in range(1, layers):
        begun += [(layer, 0), (layer, 2), (layer, 1)]
    *results, (window_word, *_) = exchange(
        "gather_parameters",
        layout,
        [gather(*spot) for spot in begun] + [window_work(layout, reach, word)],
        [[index] for index in range(len(begun))] + [[1]],
        40,
    )
    for (layer, which), (matrix,) in zip(begun, results):
        gathered[layer][which] = matrix
    window_word = window_word[:, 0]
    all_rows = gathered[0][1][:, half : half + row_count].T.astype(jnp.float32)
    gains = all_rows[: 2 * layers].reshape(layers, 2, width)
    shifts = all_rows[2 * layers :].reshape(layers, 6, width)
    vectors = jnp.concatenate(
        [gains[:, :1], shifts[:, :1], shifts[:, 2:], gains[:, 1:], shifts[:, 1:2]], axis=1
    )
    up_shift = spread(up_bias.astype(jnp.float32))[:, None, :]

    plan, own_code = attention_plan(
        tile, left, right, image_ids, token_mask, window_word, place, places
    )

    residual = inputs
    kept_layers = []
    for layer in range(layers):
        attn_weight, up_weight, down_weight = gathered[layer]
        rows = vectors[layer]
        normed_low, inv_one, queries, key_value, unit_one = projection_forward(
            residual, rows, attn_weight
        )
        ((window, *_),) = exchange(
            "fetch_window", layout, [window_work(layout, reach, key_value)], [[0]], 20
        )
        attended, lse = attention_forward(tile, left, plan, queries, window, own_code)
        residual, hidden_low, inv_two, unit_two, active, slope = mlp_forward(
            attended, residual, attn_weight, rows, up_weight, up_shift[layer], down_weight
        )
        kept_layers.append(
            (window, unit_one, inv_one, normed_low, queries, lse, attended,
             unit_two, inv_two, hidden_low, slope, active)
        )

    def reduce(works, turns):
        left_operands = pltpu.VMEM((2, 2, width, tok), jnp.bfloat16)
        right_operands = pltpu.VMEM((2, tok, max(attn_columns, up_columns) // 2), jnp.bfloat16)
        operands = [left_operands, right_operands]
        results = exchange("reduce_gradients", layout, works, turns, 63, operands)
        return [result[0] for result in results]

    def packed(rows):
        flat = jnp.concatenate([row.reshape(-1) for row in rows])
        return jnp.pad(flat, (0, -flat.size % 1024)).reshape(-1, 128)

    grad_res = cotangent
    owned = [[None] * 3 for _ in range(layers)]
    row_grads = [None] * layers
    upbias_grads = [None] * layers
    for layer in reversed(range(layers)):
        (window, unit_one, inv_one, normed_low, queries, lse, attended,
         unit_two, inv_two, hidden_low, slope, active) = kept_layers[layer]
        attn_weight, up_weight, down_weight = gathered[layer]
        rows = vectors[layer]
        grad_pre, up_sum, grad_branch, grad_mid, grad_attn, grad_attended, second_sums = (
            mlp_backward(
                grad_res, down_weight, slope, up_weight, unit_two, inv_two, rows, attn_weight
            )
        )
        upbias_grads[layer] = unspread(up_sum[0])
        grad_query, grad_window = attention_backward(
            tile, left, plan, queries, window, grad_attended, lse, own_code
        )
        works = [owned_work(layout, reach, grad_window)]
        reduce_up = reduce_work(layout, [hidden_low.T], grad_pre, True)
        split = 3 if layer else 6
        reduce_down = reduce_work(layout, [grad_branch.T], active, True, split=split)
        if layer > 0:
            works += [reduce_up, reduce_down]
            results = reduce(works, [[0], [0], [1]])
            grad_key_value, owned[layer][1], owned[layer][2] = results
        else:
            small = packed([*upbias_grads, *row_grads[1:]])
            works += [waiting, reduce_up, sum_work(layout, small)]
            results = reduce(works, [[0], [0], [1], [3, 5, 7, 8, 9]])
            grad_key_value, owned[1][0], owned[0][1], small_sum = results
        grad_res, first_sums = projection_backward(
            grad_query, grad_key_value, attn_weight, unit_one, inv_one, rows, grad_mid
        )
        row_grads[layer] = jnp.stack(
            [
                first_sums[0], second_sums[0], first_sums[1], second_sums[1],
                first_sums[2], first_sums[3], second_sums[2], second_sums[3],
            ]
        )
        grad_proj = jnp.concatenate([grad_query, grad_key_value], axis=1)
        grad_side = filled(jnp.concatenate([grad_proj, grad_attn], axis=1), tok, attn_columns)
        waiting = reduce_work(
            layout, [normed_low.T, attended.T], grad_side, False, 3 * width
        )
        if layer == 0:
            works = [reduce_down, waiting, sum_work(layout, packed(row_grads[:1]))]
            owned[0][2], owned[0][0], row_sum = reduce(works, [[0], [1], [2, 4, 6, 8, 10]])

    flat = small_sum.reshape(-1)
    upbias_grads = flat[: layers * hidden_width].reshape(layers, hidden_width)
    later = flat[layers * hidden_width :][: (layers - 1) * 8 * width].reshape(-1, 8, width)
    row_sums = jnp.concatenate([row_sum.reshape(-1)[: 8 * width].reshape(1, 8, width), later])
    seat = lax.axis_index("dp") * places + place
    row_sums = lax.dynamic_slice_in_dim(row_sums, seat * layout.rows, layout.rows, axis=2)

    def stacked(part):
        return jnp.stack([part(*owned[layer]) for layer in range(layers)], axis=1)

    rows = layout.rows
    grads = (
        stacked(lambda attn, up, down: attn[:rows, : 3 * width]),
        stacked(lambda attn, up, down: attn[:rows, 3 * width : 4 * width]),
        stacked(lambda attn, up, down: unspread(up[:rows])),
        stacked(lambda attn, up, down: unspread(down[:rows])),
        row_sums[:, :2],
        row_sums[:, 2:],
        upbias_grads,
    )
    there = ((1, 0, 2), (1, 0, 2), (1, 0, 2), (2, 0, 1)) + ((0, 1, 2),) * 2 + ((0, 1),)
    back = ((1, 0, 2), (1, 0, 2), (1, 0, 2), (1, 2, 0)) + ((0, 1, 2),) * 2 + ((0, 1),)

    def turned(arrays, orders):
        return tuple(jnp.transpose(array, order) for array, order in zip(arrays, orders))

    def handed_out(arrays):
        orders = ((1, 0, 2),) * 3 + ((2, 0, 1),)
        large = [
            array_layout.with_layout_constraint(
                array, array_layout.Layout(major_to_minor=order)
            )
            for array, order in zip(arrays, orders)
        ]
        return tuple(large) + tuple(arrays[len(orders) :])

    params = (w_qkv, w_out, w_up, w_down, norm_gains, bias_rows, up_bias)
    firsts = (first_qkv, first_out, first_up, first_down, first_gains, first_bias, first_upbias)
    seconds = (
        second_qkv, second_out, second_up, second_down, second_gains, second_bias, second_upbias,
    )
    states = [turned(arrays, there) for arrays in (params, firsts, seconds)]
    results = [
        adam_step(param, gradient, first, second)
        for param, gradient, first, second in zip(states[0], grads, states[1], states[2])
    ]
    grads = handed_out(turned(grads, back))
    return (
        (residual, grad_res)
        + grads
        + handed_out(turned([result[0] for result in results], back))
        + handed_out(turned([result[1] for result in results], back))
        + handed_out(turned([result[2] for result in results], back))
    )


def solution(mesh):
    in_specs = (
        P(("dp", "seq"), None),
        P(("dp", "seq")),
        P(("dp", "seq")),
        P(("dp", "seq"), None),
        P(None, ("dp", "seq"), None),
        P(None, ("dp", "seq"), None),
        P(None, ("dp", "seq"), None),
        P(None, None, ("dp", "seq")),
        P(None, None, ("dp", "seq")),
        P(None, None, ("dp", "seq")),
        P(),
        P(None, ("dp", "seq"), None),
        P(None, ("dp", "seq"), None),
        P(None, ("dp", "seq"), None),
        P(None, None, ("dp", "seq")),
        P(None, None, ("dp", "seq")),
        P(None, None, ("dp", "seq")),
        P(),
        P(None, ("dp", "seq"), None),
        P(None, ("dp", "seq"), None),
        P(None, ("dp", "seq"), None),
        P(None, None, ("dp", "seq")),
        P(None, None, ("dp", "seq")),
        P(None, None, ("dp", "seq")),
        P(),
    )
    out_specs = (
        P(("dp", "seq"), None),
        P(("dp", "seq"), None),
        P(None, ("dp", "seq"), None),
        P(None, ("dp", "seq"), None),
        P(None, ("dp", "seq"), None),
        P(None, None, ("dp", "seq")),
        P(None, None, ("dp", "seq")),
        P(None, None, ("dp", "seq")),
        P(),
        P(None, ("dp", "seq"), None),
        P(None, ("dp", "seq"), None),
        P(None, ("dp", "seq"), None),
        P(None, None, ("dp", "seq")),
        P(None, None, ("dp", "seq")),
        P(None, None, ("dp", "seq")),
        P(),
        P(None, ("dp", "seq"), None),
        P(None, ("dp", "seq"), None),
        P(None, ("dp", "seq"), None),
        P(None, None, ("dp", "seq")),
        P(None, None, ("dp", "seq")),
        P(None, None, ("dp", "seq")),
        P(),
        P(None, ("dp", "seq"), None),
        P(None, ("dp", "seq"), None),
        P(None, ("dp", "seq"), None),
        P(None, None, ("dp", "seq")),
        P(None, None, ("dp", "seq")),
        P(None, None, ("dp", "seq")),
        P(),
    )
    return jax.shard_map(
        per_device, mesh=mesh, in_specs=in_specs, out_specs=out_specs, check_vma=False
    )
```

```python
import functools
import math

import jax
import jax.numpy as jnp
from jax import lax
from jax.experimental import layout as array_layout
from jax.experimental import pallas as pl
from jax.experimental.pallas import tpu as pltpu
from jax.sharding import PartitionSpec as P

HEADS = 16
IMG = 729
STEP = 8

eps_norm = 1e-06
beta_first = 0.9
beta_second = 0.95
learn_rate = 0.025
weight_decay = 0.1
eps_adam = 1e-08
gelu_rate = math.sqrt(2.0 / math.pi)
gelu_cube = 0.044715
span_len = 768
lane_pair = 256
masked_score = -1e30
mib = 2**20


def head_lanes(head, head_size, width):
    low = head * head_size
    first = jnp.minimum(low // 128 * 128, width - lane_pair)
    lanes = lax.broadcasted_iota(jnp.int32, (1, lane_pair), 1)
    inside = (lanes >= low - first) & (lanes < low - first + head_size)
    keys = pl.ds(pl.multiple_of(first, 128), lane_pair)
    values = pl.ds(pl.multiple_of(first + width, 128), lane_pair)
    return keys, values, inside


def valid_lanes(start):
    lanes = lax.broadcasted_iota(jnp.int32, (1, span_len), 1)
    return (lanes >= start) & (lanes < start + IMG)


def dot_nn(left, right):
    return lax.dot_general(left, right, (((1,), (0,)), ((), ())), preferred_element_type=jnp.float32)


def dot_nt(left, right):
    return lax.dot_general(left, right, (((1,), (1,)), ((), ())), preferred_element_type=jnp.float32)


def dot_tn(left, right):
    return lax.dot_general(left, right, (((0,), (0,)), ((), ())), preferred_element_type=jnp.float32)


def attention_forward_kernel(
    tile, left, exp_scale, plan, query, source, own_code, out, lse_out, bias, mix, window, sems
):
    tok, width = query.shape
    head_size = width // HEADS
    cut = min((HEADS // 2 - 1) * head_size // 128 * 128, width - lane_pair) + lane_pair
    loads = []
    for first, lanes in ((0, cut), (cut, width - cut)):
        for shift in (0, width):
            columns = pl.ds(first + shift, lanes)
            load = pltpu.make_async_copy(
                source.at[:, columns], window.at[:, columns], sems.at[len(loads)]
            )
            load.start()
            loads.append(load)

    def one_span(tile_index, which):
        spot = 2 * tile_index + which
        offset, image = pl.multiple_of(plan[0, spot], 16), plan[1, spot]
        valid = valid_lanes(plan[2, spot])
        rows = pl.ds(pl.multiple_of(tile_index * tile, 16), tile)
        own_rows = pl.ds(pl.multiple_of(left + tile_index * tile, 16), tile)
        span = pl.ds(offset, span_len)
        code = own_code[rows, :]
        row_image = jnp.maximum(code, -code)
        mine = row_image == image
        bias[...] = jnp.where(mine & valid, 0.0, masked_score)
        self_bias = jnp.where(code < 0, 0.0, masked_score)
        lse_lane = lax.broadcasted_iota(jnp.int32, (tile, lse_out.shape[1]), 1)

        def one_head(head, carry):
            lanes, value_lanes, inside = head_lanes(head, head_size, width)
            queries = jnp.where(inside, query[rows, lanes], 0)
            scores = dot_nt(queries, window[span, lanes]) * exp_scale + bias[...]
            own_key = window[own_rows, lanes].astype(jnp.float32)
            own_value = window[own_rows, value_lanes].astype(jnp.float32)
            self_score = (
                jnp.sum(queries.astype(jnp.float32) * own_key, axis=1, keepdims=True) * exp_scale
                + self_bias
            )
            top = jnp.maximum(jnp.max(scores, axis=1, keepdims=True), self_score)
            powers = jnp.exp2(scores - top)
            self_power = jnp.exp2(self_score - top)
            total = jnp.sum(powers, axis=1, keepdims=True) + self_power
            mixed = dot_nn(powers.astype(jnp.bfloat16), window[span, value_lanes])
            mixed = (mixed + self_power * own_value) / total
            mix[rows, lanes] = jnp.where(inside & mine, mixed, mix[rows, lanes])
            lse_out[rows, :] = jnp.where(
                (lse_lane == head) & mine, top + jnp.log2(total), lse_out[rows, :]
            )
            return carry

        def one_half(half, carry):
            for number in (0, 1):

                @pl.when((tile_index == 0) & (which == 0) & (half == number))
                def _():
                    for load in loads[2 * number : 2 * number + 2]:
                        load.wait()

            for index in range(HEADS // 2):
                one_head(half * (HEADS // 2) + index, 0)
            return carry

        lax.fori_loop(0, 2, one_half, 0)

    def one_tile(tile_index, carry):
        one_span(tile_index, 0)

        @pl.when(plan[1, 2 * tile_index] != plan[1, 2 * tile_index + 1])
        def _():
            one_span(tile_index, 1)

        return carry

    lax.fori_loop(0, tok // tile, one_tile, 0)
    out[...] = mix[...].astype(out.dtype)


def dot_fine(left, right, contract):
    high = left.astype(jnp.bfloat16)
    low = (left - high.astype(jnp.float32)).astype(jnp.bfloat16)
    numbers = (contract, ((), ()))
    product = lax.dot_general(high, right, numbers, preferred_element_type=jnp.float32)
    return product + lax.dot_general(low, right, numbers, preferred_element_type=jnp.float32)


def attention_backward_kernel(
    tile, left, exp_scale, plan, query, source, grad, lse_in, own_code, row_code,
    grad_query, target, bias, acc_query, acc_window, self_rows, lse_rows, inner_rows, square,
    window, grad_window, sems,
):
    tok, width = query.shape
    head_size = width // HEADS
    scale = 1.0 / math.sqrt(head_size)
    load = pltpu.make_async_copy(source, window, sems.at[0])
    load.start()
    acc_query[...] = jnp.zeros_like(acc_query)
    acc_window[...] = jnp.zeros_like(acc_window)
    square[...] = jnp.zeros_like(square)
    head_of = lax.broadcasted_iota(jnp.int32, (128, width), 1) // head_size
    spread = (head_of == lax.broadcasted_iota(jnp.int32, (128, width), 0)).astype(jnp.bfloat16)

    def turned(columns):
        square[:tile, :] = columns
        return square[...].T[:, :tile]

    def one_span(tile_index, which):
        spot = 2 * tile_index + which
        offset, image = pl.multiple_of(plan[0, spot], 16), plan[1, spot]
        rows = pl.ds(pl.multiple_of(tile_index * tile, 16), tile)
        span = pl.ds(offset, span_len)
        code = row_code[tile_index]
        mine = jnp.maximum(code, -code) == image
        place = lax.broadcasted_iota(jnp.int32, (span_len, 1), 0)
        valid = (place >= plan[2, spot]) & (place < plan[2, spot] + IMG)
        bias[...] = jnp.where(mine & valid, 0.0, masked_score)

        def one_head(head, carry):
            lanes, value_lanes, inside = head_lanes(head, head_size, width)
            queries = jnp.where(inside, query[rows, lanes], 0)
            grads = jnp.where(inside, grad[rows, lanes], 0)
            keys = window[span, lanes]
            this = pl.ds(head, 1)
            scores = dot_nt(keys, queries) * exp_scale + bias[...]
            prob = jnp.exp2(scores - lse_rows[this, :])
            grad_prob = dot_nt(window[span, value_lanes], grads)
            inner = jnp.sum(prob * grad_prob, axis=0, keepdims=True) + self_rows[this, :]
            inner_rows[this, :] = jnp.where(mine, inner, inner_rows[this, :])
            grad_scores = (prob * (grad_prob - inner)).astype(jnp.bfloat16)
            acc_window[span, lanes] += dot_nn(grad_scores, queries)
            acc_window[span, value_lanes] += dot_nn(prob.astype(jnp.bfloat16), grads)
            part = dot_tn(grad_scores, keys)
            acc_query[rows, lanes] += jnp.where(inside, part, 0.0)
            return carry

        lax.fori_loop(0, HEADS, one_head, 0, unroll=8)

    def one_tile(tile_index, carry):
        rows = pl.ds(pl.multiple_of(tile_index * tile, 16), tile)
        own_rows = pl.ds(pl.multiple_of(left + tile_index * tile, 16), tile)
        queries, grads = query[rows, :].astype(jnp.float32), grad[rows, :].astype(jnp.float32)
        own_key = window[own_rows, :width].astype(jnp.float32)
        own_value = window[own_rows, width:].astype(jnp.float32)
        self_score = dot_fine(queries * own_key, spread, ((1,), (1,))) * exp_scale
        self_grad = dot_fine(grads * own_value, spread, ((1,), (1,)))
        lse = lse_in[rows, :]
        self_prob = jnp.where(own_code[rows, :] < 0, jnp.exp2(self_score - lse), 0.0)
        self_rows[...] = turned(self_prob * self_grad)
        lse_rows[...] = turned(lse)
        one_span(tile_index, 0)

        @pl.when(plan[1, 2 * tile_index] != plan[1, 2 * tile_index + 1])
        def _():
            one_span(tile_index, 1)

        inner = inner_rows[...].T
        self_change = self_prob * (self_grad - inner[:tile, :])
        change = dot_fine(self_change, spread, ((1,), (0,)))
        acc_query[rows, :] += change * own_key
        acc_window[own_rows, :width] += change * queries
        acc_window[own_rows, width:] += dot_fine(self_prob, spread, ((1,), (0,))) * grads
        return carry

    inner_rows[...] = jnp.zeros_like(inner_rows)
    load.wait()
    lax.fori_loop(0, tok // tile, one_tile, 0)
    grad_query[...] = (acc_query[...] * scale).astype(grad_query.dtype)
    step = 16

    def narrow(index, carry):
        rows = pl.ds(pl.multiple_of(index * step, step), step)
        grad_window[rows, :width] = (acc_window[rows, :width] * scale).astype(grad_window.dtype)
        grad_window[rows, width:] = acc_window[rows, width:].astype(grad_window.dtype)
        return carry

    blocks, stores = acc_window.shape[0] // step, []
    for part in range(4):
        first, last = blocks * part // 4, blocks * (part + 1) // 4
        lax.fori_loop(first, last, narrow, 0)
        rows = pl.ds(first * step, (last - first) * step)
        store = pltpu.make_async_copy(grad_window.at[rows], target.at[rows], sems.at[1 + part])
        store.start()
        stores.append(store)
    for store in stores:
        store.wait()


def in_vmem():
    return pl.BlockSpec(memory_space=pltpu.VMEM)


def attention_forward(tile, left, plan, query, window, own_code):
    tok, width = query.shape
    exp_scale = math.log2(math.e) / math.sqrt(width // HEADS)
    return pl.pallas_call(
        functools.partial(attention_forward_kernel, tile, left, exp_scale),
        name="attention_forward",
        out_shape=[
            jax.ShapeDtypeStruct((tok, width), jnp.bfloat16),
            jax.ShapeDtypeStruct((tok, 128), jnp.float32),
        ],
        in_specs=[pl.BlockSpec(memory_space=pltpu.SMEM), in_vmem(), anywhere(), in_vmem()],
        out_specs=[in_vmem()] * 2,
        scratch_shapes=[
            pltpu.VMEM((tile, span_len), jnp.float32),
            pltpu.VMEM((tok, width), jnp.float32),
            pltpu.VMEM(window.shape, window.dtype),
            pltpu.SemaphoreType.DMA((4,)),
        ],
        compiler_params=pltpu.CompilerParams(vmem_limit_bytes=60 * mib),
    )(plan, query, window, own_code)


def attention_backward(tile, left, plan, query, window, grad, lse, own_code):
    tok, width = query.shape
    exp_scale = math.log2(math.e) / math.sqrt(width // HEADS)
    return pl.pallas_call(
        functools.partial(attention_backward_kernel, tile, left, exp_scale),
        name="attention_backward",
        out_shape=[
            jax.ShapeDtypeStruct((tok, width), jnp.bfloat16),
            jax.ShapeDtypeStruct(window.shape, jnp.bfloat16),
        ],
        in_specs=[pl.BlockSpec(memory_space=pltpu.SMEM), in_vmem(), anywhere()] + [in_vmem()] * 4,
        out_specs=[in_vmem(), anywhere()],
        scratch_shapes=[
            pltpu.VMEM((span_len, tile), jnp.float32),
            pltpu.VMEM((tok, width), jnp.float32),
            pltpu.VMEM(window.shape, jnp.float32),
            pltpu.VMEM((128, tile), jnp.float32),
            pltpu.VMEM((128, tile), jnp.float32),
            pltpu.VMEM((128, tile), jnp.float32),
            pltpu.VMEM((-(-tile // 128) * 128, 128), jnp.float32),
            pltpu.VMEM(window.shape, jnp.bfloat16),
            pltpu.VMEM(window.shape, jnp.bfloat16),
            pltpu.SemaphoreType.DMA((5,)),
        ],
        compiler_params=pltpu.CompilerParams(vmem_limit_bytes=62 * mib),
    )(plan, query, window, grad, lse, own_code, own_code.reshape(tok // tile, 1, tile))


def attention_plan(tile, left, right, own_ids, own_mask, window_ids, place, places):
    tok = own_ids.shape[0]
    window_len = left + tok + right
    room = jnp.minimum(window_len, left + (places - place) * tok) - span_len
    position = jnp.arange(window_len)
    ids = jnp.where(position < left - place * tok, -1, window_ids)
    images = own_ids.reshape(tok // tile, tile)[:, :: tile - 1].reshape(-1)
    before = (ids[None, :] < images[:, None]) & (position < left + tok)[None, :]
    starts = jnp.sum(before.astype(jnp.int32), axis=1)
    offsets = jnp.minimum(starts // 16 * 16, room)
    plan = jnp.stack([offsets, images + 1, starts - offsets]).astype(jnp.int32)
    own_code = jnp.where(own_mask > 0, own_ids + 1, -(own_ids + 1)).astype(jnp.int32)[:, None]
    return plan, own_code


class Layout:
    def __init__(self, groups, seats, model_width):
        self.rows = model_width // (groups * seats)
        self.members = 2
        while self.members * self.rows % 16:
            self.members *= 2
        self.sides = self.members // 2
        self.lines = seats // self.members
        self.slab = self.members * self.rows
        self.padded = -(-self.rows // 16) * 16
        self.near = model_width // groups
        self.model_width = model_width

    def blocks(self, one_block):
        return 2 if one_block else 2 * self.sides

    def columns(self, columns, one_block):
        unit = 128 * self.blocks(one_block)
        return -(-columns // unit) * unit


class Mail:
    def __init__(self, layout, send, recv, slots):
        self.layout, self.send_sems, self.recv_sems, self.slots = layout, send, recv, slots
        self.group = lax.axis_index("dp")
        seat = lax.axis_index("seq")
        self.line = seat // layout.members
        self.member = seat % layout.members
        self.side = self.member // 2
        self.core = self.member % 2
        self.started = {}

    def at(self, group=None, line=None, side=None, core=None):
        group = self.group if group is None else group
        line = self.line if line is None else line
        side = self.side if side is None else side
        core = self.core if core is None else core
        return (group, line * self.layout.members + side * 2 + core)

    def copy(self, slot, source, target, device, shift=0):
        index = self.slots[slot] + shift
        return pltpu.make_async_remote_copy(
            src_ref=source,
            dst_ref=target,
            send_sem=self.send_sems.at[index],
            recv_sem=self.recv_sems.at[index],
            device_id=device,
            device_id_type=pl.DeviceIdType.MESH,
        )

    def send(self, slot, source, target, device, when=None):
        copy = self.copy(slot, source, target, device)
        self.started[slot] = (copy, when)
        guarded(when, copy.start)

    def wait(self, slot, target, shift=0):
        self.copy(slot, target, target, self.at(core=1 - self.core), shift).wait_recv()

    def settle(self, slot):
        copy, when = self.started.pop(slot)
        guarded(when, copy.wait_send)

    def finish(self):
        for slot in list(self.started):
            self.settle(slot)


class Desk:
    def __init__(self, mail, index, local):
        self.mail, self.index, self.local_sems = mail, index, local
        self.group, self.line, self.member = mail.group, mail.line, mail.member
        self.side, self.core, self.at = mail.side, mail.core, mail.at

    def send(self, slot, source, target, device, when=None):
        self.mail.send((self.index, slot), source, target, device, when)

    def wait(self, slot, target, shift=0):
        self.mail.wait((self.index, slot), target, shift)

    def settle(self, slot):
        self.mail.settle((self.index, slot))

    def local(self, number, source, target):
        return pltpu.make_async_copy(source, target, self.local_sems.at[number])


class Work:
    def __init__(self, steps, ins, outs, scratch, slots, local):
        self.steps, self.ins, self.outs, self.scratch = steps, ins, outs, scratch
        self.slots, self.local = slots, local


def guarded(when, action):
    if when is None:
        action()
    else:
        pl.when(when)(action)


def all_of(*conditions):
    kept = [condition for condition in conditions if condition is not None]
    return functools.reduce(jnp.logical_and, kept) if kept else None


def run_steps(works, turns):
    queue = []
    for index, (work, first) in enumerate(zip(works, turns)):
        next(work)
        queue.append((first[0], index, 0))
    while queue:
        turn, index, done = min(queue)
        queue.remove((turn, index, done))
        try:
            next(works[index])
        except StopIteration:
            continue
        done += 1
        listed = turns[index]
        queue.append((listed[done] if done < len(listed) else turn + 1, index, done))


def anywhere():
    return pl.BlockSpec(memory_space=pl.ANY)


def exchange(name, layout, works, starts, megabytes, common=()):
    slots = [(index, slot) for index, work in enumerate(works) for slot in work.slots]
    numbers = {slot: index for index, slot in enumerate(slots)}
    ins = [entry for work in works for entry in work.ins]
    outs = [entry for work in works for entry in work.outs]
    scratch = [entry for work in works for entry in work.scratch]

    def kernel(*refs):
        refs = list(refs)

        def take(count):
            taken = refs[:count]
            del refs[:count]
            return taken

        in_refs = [take(len(work.ins)) for work in works]
        out_refs = [take(len(work.outs)) for work in works]
        scratch_refs = [take(len(work.scratch)) for work in works]
        common_refs = take(len(common))
        locals_of = [take(1)[0] for work in works]
        send, recv = refs
        mail = Mail(layout, send, recv, numbers)
        run_steps(
            [
                work.steps(
                    Desk(mail, index, locals_of[index]),
                    in_refs[index],
                    out_refs[index],
                    scratch_refs[index],
                    common_refs,
                )
                for index, work in enumerate(works)
            ],
            starts,
        )
        mail.finish()

    results = pl.pallas_call(
        kernel,
        name=name,
        out_shape=[shape for shape, _ in outs],
        in_specs=[spec for _, spec in ins],
        out_specs=[spec for _, spec in outs],
        scratch_shapes=scratch
        + list(common)
        + [pltpu.SemaphoreType.DMA((work.local,)) for work in works]
        + [pltpu.SemaphoreType.DMA((len(slots),))] * 2,
        compiler_params=pltpu.CompilerParams(
            has_side_effects=True, vmem_limit_bytes=megabytes * mib
        ),
    )(*[array for array, _ in ins])
    results = list(results)
    grouped = []
    for work in works:
        grouped.append(results[: len(work.outs)])
        del results[: len(work.outs)]
    return grouped


def gather_work(layout, shard, one_block, line_last=False):
    lines, members, sides = layout.lines, layout.members, layout.sides
    width = shard.shape[1] // layout.blocks(one_block)
    spots = [("own", 0)]
    for t in range(1, lines):
        spots += [(f"below{t}", -t), (f"above{t}", t)]
    slots = [("mix", j) for j in range(1, members)]
    halves = (0, 1) if line_last else (0,)
    slots += [(way, half, t) for way in ("up", "down") for half in halves for t in range(lines)]
    slots += [("cross", source) for source, _ in (spots[:1] if line_last else spots)]
    slots += [("core", j) for j in range(1 if one_block else sides)]
    if not one_block:
        slots += [
            ("side", half, source, j)
            for half in (0, 1)
            for source, _ in spots
            for j in range(1, sides)
        ]

    def steps(desk, ins, outs, scratch, common):
        (shard,), (out,), (landing, slab, wide) = ins, outs, scratch
        group, line, member, side, core = desk.group, desk.line, desk.member, desk.side, desk.core
        has_up, has_down = line < lines - 1, line > 0

        def columns(side_of, core_of):
            block = core_of if one_block else core_of * sides + side_of
            return pl.ds(pl.multiple_of(block * width, 128), width)

        own = columns(side, core)

        def place(group_of, line_of, lanes=own):
            first = (group_of * lines + line_of) * layout.slab
            return out.at[pl.ds(pl.multiple_of(first, 16), layout.slab), lanes]

        def present(step):
            return None if step == 0 else line >= -step if step < 0 else line < lines - step

        yield
        for j in range(1, members):
            other = (member + j) % members
            desk.send(
                ("mix", j),
                shard.at[:, columns(other // 2, other % 2)],
                landing.at[member],
                desk.at(side=other // 2, core=other % 2),
            )
        mine = desk.local(0, shard.at[:, own], landing.at[member])
        mine.start()
        yield
        for j in range(1, members):
            desk.wait(("mix", j), landing.at[(member + members - j) % members])
        mine.wait()
        for m in range(members):
            rows = slice(m * layout.rows, (m + 1) * layout.rows)
            wide[rows, :] = landing[m, : layout.rows, :].astype(jnp.float32)
        slab[...] = wide[...].astype(slab.dtype)
        keep = desk.local(1, slab, place(group, line))
        keep.start()

        def pass_on(source, what, half, where, when):
            if half == 0 and (source == "own" or not line_last):
                desk.send(("cross", source), what, where, desk.at(group=1 - group), when)
            if not one_block:
                for j in range(1, sides):
                    slot = ("side", half, source, j)
                    desk.send(slot, what, where, desk.at(side=(side + j) % sides), when)

        def along(half, t, what, where, when):
            for way, further, to in (("up", has_up, line + 1), ("down", has_down, line - 1)):
                desk.send((way, half, t), what, where, desk.at(line=to), all_of(when, further))

        home = place(group, line)
        along(0, 0, slab, home, None)
        pass_on("own", slab, 0, home, None)
        yield

        def crossed():
            where = place(1 - group, line)
            desk.wait(("cross", "own"), where)
            pass_on("own", where, 1, where, None)
            if line_last:
                along(1, 0, where, where, None)

        if line_last:
            crossed()
            yield
        for t in range(1, lines):
            for half in halves:
                for way, name, step, further, to in (
                    ("up", "below", -t, has_up, line + 1),
                    ("down", "above", t, has_down, line - 1),
                ):
                    when, where = present(step), place(1 - group if half else group, line + step)
                    guarded(when, functools.partial(desk.wait, (way, half, t - 1), where))
                    desk.send(
                        (way, half, t), where, where, desk.at(line=to), all_of(when, further)
                    )
                    pass_on(f"{name}{t}", where, half, where, when)
            if t == 1 and not line_last:
                crossed()
            yield
        for t in range(1, 1 if line_last else lines):
            for name, step in ((f"below{t}", -t), (f"above{t}", t)):
                when, where = present(step), place(1 - group, line + step)
                guarded(when, functools.partial(desk.wait, ("cross", name), where))
                pass_on(name, where, 1, where, when)
            yield
        keep.wait()
        partner = desk.at(core=1 - core)
        desk.send(("core", 0), out.at[:, own], out.at[:, own], partner)
        if not one_block:
            yield
            for j in range(1, sides):
                theirs = columns((side + sides - j) % sides, core)
                for half, group_of in ((0, group), (1, 1 - group)):
                    for source, step in spots:
                        where = place(group_of, line + step, theirs)
                        slot = ("side", half, source, j)
                        guarded(present(step), functools.partial(desk.wait, slot, where))
                desk.send(("core", j), out.at[:, theirs], out.at[:, theirs], partner)
        yield
        desk.wait(("core", 0), out.at[:, columns(side, 1 - core)])
        if not one_block:
            for j in range(1, sides):
                theirs = columns((side + sides - j) % sides, 1 - core)
                desk.wait(("core", j), out.at[:, theirs])

    low = jnp.bfloat16
    return Work(
        steps,
        [(shard, anywhere())],
        [(jax.ShapeDtypeStruct((layout.model_width, shard.shape[1]), low), anywhere())],
        [
            pltpu.VMEM((members, layout.padded, width), low),
            pltpu.VMEM((layout.slab, width), low),
            pltpu.VMEM((layout.slab, width), jnp.float32),
        ],
        slots,
        2,
    )


def add_rows(target, first, target_columns, source, source_columns, count, source_first=0):
    step = math.gcd(count, 48)

    def one(index, carry):
        rows = pl.ds(pl.multiple_of(first + index * step, 16), step)
        theirs = pl.ds(pl.multiple_of(source_first + index * step, 16), step)
        total = target[rows, target_columns].astype(jnp.float32)
        total += source[theirs, source_columns].astype(jnp.float32)
        target[rows, target_columns] = total.astype(target.dtype)
        return carry

    lax.fori_loop(0, count // step, one, 0)


def reduce_work(layout, lefts, right, one_block, switch=0, split=3):
    lines, members, sides = layout.lines, layout.members, layout.sides
    tok, columns = right.shape
    blocks = layout.blocks(one_block)
    width, half = columns // blocks, columns // 2
    near_rows, slab_rows, low = layout.near, layout.slab, jnp.bfloat16
    count, depth = min(split, width // 128), min(4, lines)
    parts = []
    for index in range(count):
        first = width // 128 * index // count * 128
        parts.append((first, width // 128 * (index + 1) // count * 128 - first))
    order = []
    for t in range(lines):
        goal = lines - 1 - t // 2 if t % 2 == 0 else t // 2
        order.append(goal)
    slots = [("left", k) for k in range(len(lefts))] + ["right"]
    slots += [("cross", part, t) for part in parts for t in range(lines)]
    slots += [
        (way, part, t) for way in ("up", "down") for part in parts for t in range(1, lines)
    ]
    slots += [("mix", j) for j in range(1, members)]
    if not one_block:
        slots += [
            ("side", part, tag, t, j)
            for part in parts
            for tag in (0, 1)
            for t in range(lines)
            for j in range(1, sides)
        ]

    def steps(desk, ins, outs, scratch, common):
        left_in, right_in = ins[: len(lefts)], ins[len(lefts)]
        out, left_land, right_land = outs[0], outs[1 : 1 + len(lefts)], outs[1 + len(lefts)]
        total, cross, up, down, piece, landing, wide = scratch[:7]
        from_side = None if one_block else scratch[7]
        left_all, right_all = common
        group, line, member, side, core = desk.group, desk.line, desk.member, desk.side, desk.core
        partner = desk.at(core=1 - core)
        own = pl.ds(0 if one_block else pl.multiple_of(side * width, 128), width)
        stay = pl.ds(pl.multiple_of(core * half, 128), half)
        away = pl.ds(pl.multiple_of((1 - core) * half, 128), half)

        def first_of(tag, goal):
            return pl.multiple_of((group if tag else 1 - group) * near_rows + goal * slab_rows, 16)

        yield
        for k, left in enumerate(left_in):
            desk.send(("left", k), left, left_land[k], partner)
        desk.send("right", right_in.at[:, away], right_land, partner)
        yield
        loads = []

        def load(source, target):
            copy = desk.local(len(loads), source, target)
            copy.start()
            loads.append(copy)

        for k, left in enumerate(left_in):
            load(left, left_all.at[k, 0])
        load(right_in.at[:, stay], right_all.at[0, :, pl.ds(0, half)])
        for k in range(len(left_in)):
            desk.wait(("left", k), left_land[k])
            load(left_land[k], left_all.at[k, 1])
        desk.wait("right", right_land)
        load(right_land, right_all.at[1, :, pl.ds(0, half)])
        for copy in loads:
            copy.wait()

        def multiply(tag):
            rows = pl.ds(first_of(tag, 0), near_rows)

            def piece_of(first, lanes, which):
                theirs = pl.ds(first, lanes)
                product = dot_nn(left_all[which, 0, rows, :], right_all[0, :, theirs])
                product += dot_nn(left_all[which, 1, rows, :], right_all[1, :, theirs])
                total[rows, theirs] = product.astype(low)

            lanes = 256 if len(lefts) == 1 else math.gcd(switch, 384)

            def one(index, carry):
                first = pl.multiple_of(index * lanes, 128)
                which = 0
                if len(lefts) > 1:
                    which = jnp.where(core * half + index * lanes >= switch, 1, 0)
                piece_of(first, lanes, which)
                return carry

            lax.fori_loop(0, half // lanes, one, 0)
            if half % lanes:
                piece_of(half // lanes * lanes, half % lanes, 0)

        own_first = 0 if one_block else side * width
        pieces = [
            (part, tag, goal)
            for part in parts
            for tag in ((0,) if one_block else (0, 1))
            for goal in order
        ]

        def lanes_of(part, first):
            return pl.ds(pl.multiple_of(first + part[0], 128), part[1])

        def post(number):
            if number >= len(pieces):
                return
            part, tag, goal = pieces[number]
            if one_block:
                if number >= depth:
                    before = pieces[number - depth]
                    desk.settle(("cross", before[0], before[2]))
                send_across(part, goal)
                return
            rows = pl.ds(first_of(tag, goal), slab_rows)
            for j in range(1, sides):
                if number >= depth:
                    desk.settle(("side", *pieces[number - depth], j))
                other = (side + j) % sides
                desk.send(
                    ("side", part, tag, goal, j),
                    total.at[rows, lanes_of(part, other * width)],
                    from_side.at[j - 1, rows, lanes_of(part, 0)],
                    desk.at(side=other),
                )

        def send_across(part, goal):
            rows = pl.ds(first_of(0, goal), slab_rows)
            desk.send(
                ("cross", part, goal),
                total.at[rows, lanes_of(part, own_first)],
                cross.at[goal, :, lanes_of(part, 0)],
                desk.at(group=1 - group),
            )

        def take_side(part, tag, goal):
            first = first_of(tag, goal)
            rows, lanes = pl.ds(first, slab_rows), lanes_of(part, 0)
            for j in range(1, sides):
                desk.wait(("side", part, tag, goal, j), from_side.at[j - 1, rows, lanes])
            post(pieces.index((part, tag, goal)) + depth)
            for j in range(1, sides):
                add_rows(
                    total, first, lanes_of(part, own_first), from_side.at[j - 1], lanes,
                    slab_rows, first,
                )

        ends = lines - 1 - line

        def part_steps(part):
            lanes, mine = lanes_of(part, 0), lanes_of(part, own_first)
            if not one_block:
                for goal in order:
                    take_side(part, 0, goal)
                    send_across(part, goal)
                    yield
            for goal in order:
                if not one_block:
                    take_side(part, 1, goal)
                desk.wait(("cross", part, goal), cross.at[goal, :, lanes])
                if one_block:
                    post(pieces.index((part, 0, goal)) + depth)
                add_rows(total, first_of(1, goal), mine, cross.at[goal], lanes, slab_rows)
                yield
            for t in range(1, lines):
                for way, buffer, going, fed, goal, to in (
                    ("up", up, line < t, line > 0, lines - t + line, line + 1),
                    ("down", down, ends < t, ends > 0, t - lines + line, line - 1),
                ):
                    first = first_of(1, goal)

                    @pl.when(all_of(going, fed))
                    def _():
                        if t > 1:
                            desk.wait((way, part, t - 1), buffer.at[t - 2, :, lanes])
                            add_rows(total, first, mine, buffer.at[t - 2], lanes, slab_rows)

                    desk.send(
                        (way, part, t),
                        total.at[pl.ds(first, slab_rows), mine],
                        buffer.at[t - 1, :, lanes],
                        desk.at(line=to),
                        going,
                    )
                yield

        multiply(0)
        for number in range(depth):
            post(number)
        yield
        multiply(1)
        yield
        running = [part_steps(part) for part in parts]
        turn, lag = 0, len(pieces) // len(parts)
        while running:
            for index, steps_of in enumerate(running):
                if steps_of is not None and turn >= lag * index:
                    try:
                        next(steps_of)
                    except StopIteration:
                        running[index] = None
            if not any(running):
                break
            turn += 1
            yield
        first = first_of(1, line)
        wide[...] = total[pl.ds(first, slab_rows), own].astype(jnp.float32)
        for way, buffer, fed in (("up", up, line > 0), ("down", down, ends > 0)):

            @pl.when(fed)
            def _():
                for part in parts:
                    where = buffer.at[lines - 2, :, lanes_of(part, 0)]
                    desk.wait((way, part, lines - 1), where)
                wide[...] += buffer[lines - 2].astype(jnp.float32)

        for m in range(members):
            rows = slice(m * layout.rows, (m + 1) * layout.rows)
            piece[m] = jnp.zeros(piece.shape[1:], piece.dtype)
            piece[m, : layout.rows, :] = wide[rows, :].astype(piece.dtype)
        seat = core * sides + side
        for j in range(1, members):
            other = (member + j) % members
            desk.send(
                ("mix", j),
                piece.at[other],
                landing.at[seat],
                desk.at(side=other // 2, core=other % 2),
            )
        landing[seat] = piece[member]
        yield
        for j in range(1, members):
            other = (member + members - j) % members
            desk.wait(("mix", j), landing.at[other % 2 * sides + other // 2])
        if one_block:
            for c in range(2):
                block = landing[c * sides].astype(jnp.float32)
                for s in range(1, sides):
                    block += landing[c * sides + s].astype(jnp.float32)
                out[:, c * width : (c + 1) * width] = block
        else:
            for b in range(blocks):
                out[:, b * width : (b + 1) * width] = landing[b].astype(jnp.float32)

    scratch = [
        pltpu.VMEM((layout.model_width, half), low),
        pltpu.VMEM((lines, slab_rows, width), low),
        pltpu.VMEM((lines - 1, slab_rows, width), low),
        pltpu.VMEM((lines - 1, slab_rows, width), low),
        pltpu.VMEM((members, layout.padded, width), low),
        pltpu.VMEM((members, layout.padded, width), low),
        pltpu.VMEM((slab_rows, width), jnp.float32),
    ]
    if not one_block:
        scratch.append(pltpu.VMEM((sides - 1, layout.model_width, width), low))
    ins = [(array, anywhere()) for array in [*lefts, right]]
    return Work(
        steps,
        ins,
        [(jax.ShapeDtypeStruct((layout.padded, columns), jnp.float32), in_vmem())]
        + [(jax.ShapeDtypeStruct(left.shape, low), anywhere()) for left in lefts]
        + [(jax.ShapeDtypeStruct((tok, half), low), anywhere())],
        scratch,
        slots,
        2 * len(lefts) + 2,
    )


class Reach:
    def __init__(self, tok, left, right):
        self.tok, self.left, self.right = tok, left, right
        self.window = left + tok + right
        self.deltas = [d for d in range(-8, 9) if d != 0 and self.rows(d) > 0]

    def first(self, delta):
        return max(0, self.tok * delta - self.left)

    def rows(self, delta):
        last = min(self.tok, self.tok * delta - self.left + self.window)
        return last - self.first(delta)

    def spot(self, delta):
        return self.first(delta) - self.tok * delta + self.left


def parts_of(count, step=48):
    return [(first, min(step, count - first)) for first in range(0, count, step)]


def window_work(layout, reach, key_value):
    tok, width = key_value.shape
    left, lines, places = reach.left, layout.lines, layout.lines * layout.members
    routed = layout.sides == 2
    pieces, depth = parts_of(tok), 2
    near_below, far_below = reach.spot(2), reach.spot(3)
    tail = (reach.first(3), max(reach.rows(3), 0))
    head = max(reach.rows(-2), 0)
    if routed:
        slots = ["pair", "tail", "share", "wide", "thin", "last"]
        slots += [(name, k) for name in ("right", "left", "climb", "drop") for k in range(len(pieces))]
        slots += [("fall", k) for k in range(len(parts_of(head)))]
    else:
        slots = [("reach", delta) for delta in reach.deltas]

    def direct(desk, own, window):
        seat = desk.line * layout.members + desk.member
        for delta in reach.deltas:
            count = reach.rows(delta)
            desk.send(
                ("reach", delta),
                own.at[pl.ds(reach.first(delta), count)],
                window.at[pl.ds(reach.spot(delta), count)],
                (desk.group, seat + delta),
                (seat + delta >= 0) & (seat + delta < places),
            )
        yield
        for delta in reach.deltas:
            where = window.at[pl.ds(reach.spot(delta), reach.rows(delta))]
            when = (seat - delta >= 0) & (seat - delta < places)
            guarded(when, functools.partial(desk.wait, ("reach", delta), where))

    def by_way(desk, own, window, transit):
        line, core = desk.line, desk.core
        first_side, last_side = desk.side == 0, desk.side == 1
        low_core, high_core = core == 0, core == 1
        has_up, has_down = line < lines - 1, line > 0
        has_before = last_side | has_down
        partner = desk.at(core=1 - core)

        def part(ref, first, count):
            return ref.at[pl.ds(first, count)]

        def post(k):
            if k >= len(pieces):
                return
            if k >= depth:
                desk.settle(("right", k - depth))
                desk.settle(("left", k - depth))
            first, count = pieces[k]
            desk.send(
                ("right", k), part(own, first, count), part(window, near_below + first, count),
                desk.at(side=1), first_side,
            )
            desk.send(
                ("left", k), part(own, first, count), part(transit, first, count),
                desk.at(side=0), last_side,
            )

        for k in range(depth):
            post(k)
        desk.send(
            "tail", part(own, *tail), part(window, far_below, tail[1]),
            desk.at(line=line + 1, core=0), high_core & has_up,
        )
        mirrored = pl.multiple_of(left + (2 * core - 1) * tok, 16)
        desk.send("pair", own, part(window, mirrored, tok), partner)
        yield
        for k, (first, count) in enumerate(pieces):
            ahead = part(transit, first, count)
            guarded(first_side, functools.partial(desk.wait, ("left", k), ahead))
            desk.send(
                ("climb", k), ahead, part(window, near_below + first, count),
                desk.at(line=line + 1), first_side & has_up,
            )
            behind = part(window, near_below + first, count)
            guarded(last_side, functools.partial(desk.wait, ("right", k), behind))
            post(k + depth)
            desk.send(
                ("drop", k), behind, part(window, left + tok + first, count),
                desk.at(line=line - 1, core=1), last_side & has_down & low_core,
            )
            if first < head:
                count = min(count, head - first)
                desk.send(
                    ("fall", k), part(window, near_below + first, count),
                    part(window, left + 2 * tok + first, count),
                    desk.at(line=line - 1), last_side & has_down & high_core,
                )
            yield
        stay = desk.local(1, part(transit, 0, head), part(window, left + 2 * tok, head))
        guarded(first_side, stay.start)
        desk.send(
            "share", transit, part(window, left + tok, tok), partner, first_side & low_core
        )

        def share_before(when):
            desk.send(
                "wide", part(window, near_below, tok), part(window, left - tok, tok), partner,
                when & high_core,
            )
            desk.send(
                "thin", part(window, near_below + tail[0], tail[1]),
                part(window, far_below, tail[1]), partner, when & low_core,
            )

        def climbed():
            for k, (first, count) in enumerate(pieces):
                desk.wait(("climb", k), part(window, near_below + first, count))

        guarded(first_side & has_down, climbed)
        share_before(has_before)
        yield

        def dropped():
            for k, (first, count) in enumerate(pieces):
                desk.wait(("drop", k), part(window, left + tok + first, count))
            for k, (first, count) in enumerate(parts_of(head)):
                desk.wait(("fall", k), part(window, left + 2 * tok + first, count))

        guarded(last_side & has_up & high_core, dropped)
        desk.send(
            "last", part(window, left + tok, head), part(window, left + 2 * tok, head), partner,
            last_side & has_up & high_core,
        )
        yield
        desk.wait("pair", part(window, pl.multiple_of(left + (1 - 2 * core) * tok, 16), tok))
        for when, slot, first, count in (
            (low_core & has_down, "tail", far_below, tail[1]),
            (first_side & high_core, "share", left + tok, tok),
            (has_before & low_core, "wide", left - tok, tok),
            (has_before & high_core, "thin", far_below, tail[1]),
            (last_side & has_up & low_core, "last", left + 2 * tok, head),
        ):
            guarded(when, functools.partial(desk.wait, slot, part(window, first, count)))
        guarded(first_side, stay.wait)

    def steps(desk, ins, outs, scratch, common):
        (own,), (window,) = ins, outs
        keep = desk.local(0, own, window.at[pl.ds(left, tok)])
        keep.start()
        yield from by_way(desk, own, window, *scratch) if routed else direct(desk, own, window)
        keep.wait()

    outs = [(jax.ShapeDtypeStruct((reach.window, width), key_value.dtype), anywhere())]
    scratch = [pltpu.VMEM((tok, width), key_value.dtype)] if routed else []
    return Work(steps, [(key_value, in_vmem())], outs, scratch, slots, 2)


def owned_work(layout, reach, grad_window):
    width = grad_window.shape[1]
    tok, left, lines = reach.tok, reach.left, layout.lines
    places = layout.lines * layout.members
    routed = layout.sides == 2
    pieces, depth = parts_of(tok), 2
    near_below, far_below = reach.spot(2), reach.spot(3)
    tail = (reach.first(3), max(reach.rows(3), 0))
    head = max(reach.rows(-2), 0)
    every = pl.ds(0, width)
    low = grad_window.dtype
    if routed:
        slots = ["pair", "tail", "share", "wide", "thin", "last", "rise"]
        slots += [(name, k) for name in ("right", "left", "fall", "lift") for k in range(len(pieces))]
    else:
        slots = [("reach", delta) for delta in reach.deltas]

    def direct(desk, grad, out, landing):
        seat = desk.line * layout.members + desk.member
        for delta in reach.deltas:
            count = reach.rows(delta)
            desk.send(
                ("reach", delta),
                grad.at[pl.ds(reach.spot(delta), count)],
                landing[delta],
                (desk.group, seat - delta),
                (seat - delta >= 0) & (seat - delta < places),
            )
        load = desk.local(0, grad.at[pl.ds(left, tok)], out)
        load.start()
        load.wait()
        yield
        for delta in reach.deltas:

            @pl.when((seat + delta >= 0) & (seat + delta < places))
            def _():
                desk.wait(("reach", delta), landing[delta])
                first, count = reach.first(delta), reach.rows(delta)
                add_rows(out, first, every, landing[delta], every, count)

    def by_way(desk, grad, out, scratch):
        near, middle, l_wide, l_far, l_climb, l_y, l_pair, l_tail = scratch
        line, core = desk.line, desk.core
        first_side, last_side = desk.side == 0, desk.side == 1
        low_core, high_core = core == 0, core == 1
        has_up, has_down = line < lines - 1, line > 0
        has_before = last_side | has_down
        gate = last_side & has_up & high_core
        partner = desk.at(core=1 - core)

        def part(ref, first, count):
            return ref.at[pl.ds(first, count)]

        def receive(when, slot, target, first, buffer, at, count):
            @pl.when(when)
            def _():
                desk.wait(slot, part(buffer, at, count))
                add_rows(target, first, every, buffer, every, count, at)

        desk.send(
            "last", part(grad, left + 2 * tok, head), part(l_climb, 0, head), partner,
            last_side & has_up & low_core,
        )
        desk.send(
            "wide", part(grad, left - tok, tok), l_wide, partner, has_before & low_core
        )
        desk.send(
            "thin", part(grad, far_below, tail[1]), part(l_wide, 0, tail[1]), partner,
            has_before & high_core,
        )
        desk.send(
            "share", part(grad, left + tok, tok), l_far, partner, first_side & high_core
        )
        desk.send(
            "tail", part(grad, far_below, tail[1]), l_tail,
            desk.at(line=line - 1, core=1), low_core & has_down,
        )
        desk.send("rise", part(grad, left + 2 * tok, head), part(l_far, 0, head),
            desk.at(line=line + 1), gate,
        )
        loads = [
            (desk.local(0, part(grad, near_below, tok), near), None),
            (desk.local(1, part(grad, left + tok, tok), middle), last_side),
            (desk.local(2, part(grad, left + 2 * tok, head), part(middle, 0, head)), first_side),
            (desk.local(3, part(grad, left, tok), out), None),
        ]
        for load, when in loads:
            guarded(when, load.start)

        @pl.when(first_side)
        def _():
            middle[head:, :] = jnp.zeros((tok - head, width), low)

        yield
        for load, when in loads:
            guarded(when, load.wait)
        receive(gate, "last", middle, 0, l_climb, 0, head)
        receive(has_before & high_core, "wide", near, 0, l_wide, 0, tok)
        receive(has_before & low_core, "thin", near, tail[0], l_wide, 0, tail[1])

        def post(k):
            if k >= len(pieces):
                return
            if k >= depth:
                desk.settle(("fall", k - depth))
                desk.settle(("lift", k - depth))
            first, count = pieces[k]
            desk.send(
                ("fall", k), part(middle, first, count), part(l_far, first, count),
                desk.at(line=line + 1, core=0), gate,
            )
            desk.send(
                ("lift", k), part(near, first, count), part(l_climb, first, count),
                desk.at(line=line - 1), first_side & has_down,
            )

        for k in range(depth):
            post(k)
        mirrored = pl.multiple_of(left + (1 - 2 * core) * tok, 16)
        desk.send("pair", part(grad, mirrored, tok), l_pair, partner)
        yield
        receive(first_side & low_core, "share", middle, 0, l_far, 0, tok)
        receive(last_side & has_down & high_core, "rise", near, 0, l_far, 0, head)
        for k, (first, count) in enumerate(pieces):
            receive(first_side & has_up, ("lift", k), middle, first, l_climb, first, count)
            desk.send(
                ("left", k), part(middle, first, count), part(l_y, first, count),
                desk.at(side=1), first_side,
            )
            receive(
                last_side & has_down & low_core, ("fall", k), near, first, l_far, first, count
            )
            desk.send(
                ("right", k), part(near, first, count), part(l_y, first, count),
                desk.at(side=0), last_side,
            )
            post(k + depth)
            yield
        receive(has_up & high_core, "tail", out, tail[0], l_tail, 0, tail[1])
        desk.wait("pair", l_pair)
        for k, (first, count) in enumerate(pieces):
            where = part(l_y, first, count)
            guarded(first_side, functools.partial(desk.wait, ("right", k), where))
            guarded(last_side, functools.partial(desk.wait, ("left", k), where))

            def one(index, carry):
                rows = pl.ds(pl.multiple_of(first + index * 16, 16), 16)
                total = out[rows, :].astype(jnp.float32) + l_pair[rows, :].astype(jnp.float32)
                out[rows, :] = (total + l_y[rows, :].astype(jnp.float32)).astype(out.dtype)
                return carry

            lax.fori_loop(0, count // 16, one, 0)
            yield

    def steps(desk, ins, outs, scratch, common):
        if routed:
            yield from by_way(desk, ins[0], outs[0], scratch)
        else:
            yield from direct(desk, ins[0], outs[0], dict(zip(reach.deltas, scratch)))

    if routed:
        counts = [tok] * 7 + [tail[1]]
    else:
        counts = [reach.rows(delta) for delta in reach.deltas]
    return Work(
        steps,
        [(grad_window, anywhere())],
        [(jax.ShapeDtypeStruct((tok, width), low), in_vmem())],
        [pltpu.VMEM((count, width), low) for count in counts],
        slots,
        4,
    )


def sum_work(layout, block):
    sizes = (2, layout.sides, layout.model_width // layout.near, layout.lines)
    slots = [(stage, j) for stage, size in enumerate(sizes) for j in range(1, size)]

    def steps(desk, ins, outs, scratch, common):
        (block,), (out,) = ins, outs
        yield
        out[...] = block[...]
        for stage, (landing, size) in enumerate(zip(scratch, sizes)):
            mine = (desk.core, desk.side, desk.group, desk.line)[stage]
            landing[mine] = out[...]
            for j in range(1, size):
                other = (mine + j) % size
                to = desk.at(**{("core", "side", "group", "line")[stage]: other})
                desk.send((stage, j), landing.at[mine], landing.at[mine], to)
            yield
            for j in range(1, size):
                desk.wait((stage, j), landing.at[(mine + size - j) % size])
            total = landing[0]
            for j in range(1, size):
                total = total + landing[j]
            out[...] = total

    return Work(
        steps,
        [(block, in_vmem())],
        [(jax.ShapeDtypeStruct(block.shape, block.dtype), in_vmem())],
        [pltpu.VMEM((size, *block.shape), block.dtype) for size in sizes],
        slots,
        1,
    )


def lane_mean(source):
    return jnp.mean(source, axis=1, keepdims=True)


def unit_of(source):
    centred = source - lane_mean(source)
    inv_scale = lax.rsqrt(lane_mean(centred * centred) + eps_norm)
    return centred * inv_scale, inv_scale


def norm_input_gradient(gradient, unit_rows, inv_scale, gain_row):
    scaled = gradient * gain_row
    return inv_scale * (scaled - lane_mean(scaled) - unit_rows * lane_mean(scaled * unit_rows))


def rows_sum(source):
    return jnp.sum(source.astype(jnp.float32), axis=0, keepdims=True)


def gelu_and_slope(source):
    square = source * source
    curve = jnp.tanh(gelu_rate * source * (1.0 + gelu_cube * square))
    rise = gelu_rate * (1.0 + 3.0 * gelu_cube * square)
    half_sum = 0.5 * (1.0 + curve)
    return source * half_sum, half_sum + 0.5 * source * (1.0 - curve * curve) * rise


def chunks_of(columns, lanes=768):
    return [(first, min(lanes, columns - first)) for first in range(0, columns, lanes)]


def moves(sources, targets, sems):
    return [
        pltpu.make_async_copy(source, target, sems.at[index])
        for index, (source, target) in enumerate(zip(sources, targets))
    ]


def projection_forward_kernel(
    residual, rows, weight, normed_out, inv_out, query_out, pair_out, unit_out, held, sems
):
    width = rows.shape[1]
    sources = [weight.at[:, pl.ds(j * width, width)] for j in range(3)]
    loads = moves(sources, [held.at[j] for j in range(3)], sems)
    for load in loads:
        load.start()
    unit_rows, inv_scale = unit_of(residual[...].astype(jnp.float32))
    unit_out[...] = unit_rows
    inv_out[...] = jnp.broadcast_to(inv_scale, inv_out.shape)
    normed = (unit_rows * rows[0:1, :] + rows[1:2, :]).astype(normed_out.dtype)
    normed_out[...] = normed
    loads[0].wait()
    query_out[...] = (dot_nn(normed_out[...], held[0]) + rows[2:3, :]).astype(query_out.dtype)
    loads[1].wait()
    pair_out[:, :width] = dot_nn(normed_out[...], held[1]).astype(pair_out.dtype)
    loads[2].wait()
    values = dot_nn(normed_out[...], held[2]) + rows[3:4, :]
    pair_out[:, width:] = values.astype(pair_out.dtype)


def dense_call(kernel, name, ins, outs, scratch, *arrays):
    return pl.pallas_call(
        kernel,
        name=name,
        in_specs=ins,
        out_specs=[spec for _, spec in outs],
        out_shape=[shape for shape, _ in outs],
        scratch_shapes=scratch,
        compiler_params=pltpu.CompilerParams(vmem_limit_bytes=60 * mib),
    )(*arrays)


def kept(shape, kind=jnp.bfloat16):
    return (jax.ShapeDtypeStruct(shape, kind), in_vmem())


def projection_forward(residual, rows, attn_weight):
    tok, width = residual.shape
    return dense_call(
        projection_forward_kernel,
        "projection_forward",
        [in_vmem(), in_vmem(), anywhere()],
        [
            kept((tok, width)),
            kept((tok, 128), jnp.float32),
            kept((tok, width)),
            kept((tok, 2 * width)),
            kept((tok, width), jnp.float32),
        ],
        [pltpu.VMEM((3, width, width), jnp.bfloat16), pltpu.SemaphoreType.DMA((3,))],
        residual,
        rows,
        attn_weight,
    )


def whole(shape):
    return pl.BlockSpec(shape, lambda step: (0,) * len(shape))


def projection_backward_kernel(
    grad_query, grad_pair, weight, unit, inv, rows, grad_mid, grad_res, sums, acc
):
    step = pl.program_id(0)
    width = grad_query.shape[1]

    @pl.when(step == 0)
    def _():
        acc[...] = dot_nt(grad_query[...], weight[...])

    @pl.when(step == 1)
    def _():
        acc[...] += dot_nt(grad_pair[:, :width], weight[...])

    @pl.when(step == 2)
    def _():
        gradient = acc[...] + dot_nt(grad_pair[:, width:], weight[...])
        unit_rows = unit[...]
        grad_res[...] = grad_mid[...] + norm_input_gradient(
            gradient, unit_rows, inv[:, 0:1], rows[0:1, :]
        )
        sums[...] = jnp.zeros_like(sums)
        sums[0:1, :] = rows_sum(gradient * unit_rows)
        sums[1:2, :] = rows_sum(gradient)
        sums[2:3, :] = rows_sum(grad_query[...])
        sums[3:4, :] = rows_sum(grad_pair[:, width:])


def projection_backward(grad_query, grad_pair, attn_weight, unit, inv, rows, grad_mid):
    tok, width = grad_query.shape
    return pl.pallas_call(
        projection_backward_kernel,
        name="projection_backward",
        grid=(3,),
        in_specs=[
            whole((tok, width)),
            whole((tok, 2 * width)),
            pl.BlockSpec((width, width), lambda step: (0, step)),
            whole((tok, width)),
            whole((tok, 128)),
            whole(rows.shape),
            whole((tok, width)),
        ],
        out_specs=[whole((tok, width)), whole((8, width))],
        out_shape=[
            jax.ShapeDtypeStruct((tok, width), jnp.float32),
            jax.ShapeDtypeStruct((8, width), jnp.float32),
        ],
        scratch_shapes=[pltpu.VMEM((tok, width), jnp.float32)],
        compiler_params=pltpu.CompilerParams(vmem_limit_bytes=58 * mib),
    )(grad_query, grad_pair, attn_weight, unit, inv, rows, grad_mid)


class Stream:
    def __init__(self, source, held, sems, chunks):
        self.held, self.chunks = held, chunks
        self.copies = [
            pltpu.make_async_copy(
                source.at[:, pl.ds(first, count)], held.at[k % 2, :, pl.ds(0, count)], sems.at[k]
            )
            for k, (first, count) in enumerate(chunks)
        ]

    def start(self, k):
        if k < len(self.chunks):
            self.copies[k].start()

    def take(self, k):
        self.copies[k].wait()
        return self.held[k % 2, :, : self.chunks[k][1]]


def mlp_forward_kernel(
    chunks, attended, residual, attn_weight, rows, up_weight, up_shift, down_weight,
    residual_out, hidden_out, inv_out, unit_out, active_out, slope_out,
    out_held, up_held, down_held, active_held, slope_held, sems,
):
    width, count = rows.shape[1], len(chunks)
    load = pltpu.make_async_copy(attn_weight.at[:, pl.ds(3 * width, width)], out_held, sems.at[4, 0])
    load.start()
    up = Stream(up_weight, up_held, sems.at[0], chunks)
    down = Stream(down_weight, down_held, sems.at[1], chunks)
    up.start(0)
    down.start(0)
    up.start(1)
    load.wait()
    middle = residual[...].astype(jnp.float32) + rows[4:5, :] + dot_nn(attended[...], out_held[...])
    residual_out[...] = middle + rows[5:6, :]
    unit_rows, inv_scale = unit_of(middle)
    unit_out[...] = unit_rows
    inv_out[...] = jnp.broadcast_to(inv_scale, inv_out.shape)
    hidden_out[...] = (unit_rows * rows[6:7, :] + rows[7:8, :]).astype(hidden_out.dtype)
    ahead = dot_nn(hidden_out[...], up.take(0))
    stores = []
    for k, (first, lanes) in enumerate(chunks):
        now = ahead
        columns = pl.ds(first, lanes)
        up.start(k + 2)
        down.start(k + 1)
        if k + 1 < count:
            ahead = dot_nn(hidden_out[...], up.take(k + 1))
        value, slope = gelu_and_slope(now + up_shift[:, columns])
        active_held[:, columns] = value.astype(active_held.dtype)
        slope_held[:, columns] = slope.astype(slope_held.dtype)
        for row, held, target in ((2, active_held, active_out), (3, slope_held, slope_out)):
            store = pltpu.make_async_copy(
                held.at[:, columns], target.at[:, columns], sems.at[row, k]
            )
            store.start()
            stores.append(store)
        residual_out[...] += dot_nt(active_held[:, columns], down.take(k))
    for store in stores:
        store.wait()


def mlp_forward(attended, residual, attn_weight, rows, up_weight, up_shift, down_weight):
    tok, width = attended.shape
    columns = up_shift.shape[1]
    chunks = chunks_of(columns)
    hidden = (jax.ShapeDtypeStruct((tok, columns), jnp.bfloat16), anywhere())
    weight_chunk = pltpu.VMEM((2, width, chunks[0][1]), jnp.bfloat16)
    hidden_held = pltpu.VMEM((tok, columns), jnp.bfloat16)
    return dense_call(
        functools.partial(mlp_forward_kernel, chunks),
        "mlp_forward",
        [in_vmem(), in_vmem(), anywhere(), in_vmem(), anywhere(), in_vmem(), anywhere()],
        [
            kept((tok, width), jnp.float32),
            kept((tok, width)),
            kept((tok, 128), jnp.float32),
            kept((tok, width), jnp.float32),
            hidden,
            hidden,
        ],
        [pltpu.VMEM((width, width), jnp.bfloat16)]
        + [weight_chunk] * 2
        + [hidden_held] * 2
        + [pltpu.SemaphoreType.DMA((5, len(chunks)))],
        attended,
        residual,
        attn_weight,
        rows,
        up_weight,
        up_shift,
        down_weight,
    )


def mlp_backward_kernel(
    chunks, grad_res, down_weight, slope, up_weight, unit, inv, rows, attn_weight,
    grad_pre, up_sum, grad_branch, grad_mid, grad_attn, grad_attended, sums,
    out_held, up_held, down_held, pre_held, acc, sems,
):
    width, count = rows.shape[1], len(chunks)
    down = Stream(down_weight, down_held, sems.at[1], chunks)
    up = Stream(up_weight, up_held, sems.at[0], chunks)
    down.start(0)
    up.start(0)
    down.start(1)
    load = pltpu.make_async_copy(attn_weight.at[:, pl.ds(3 * width, width)], out_held, sems.at[3, 0])
    load.start()
    grad_branch[...] = grad_res[...].astype(grad_branch.dtype)
    acc[...] = jnp.zeros_like(acc)
    ahead = dot_nn(grad_branch[...], down.take(0))
    stores = []
    for k, (first, lanes) in enumerate(chunks):
        now = ahead
        columns = pl.ds(first, lanes)
        down.start(k + 2)
        up.start(k + 1)
        if k + 1 < count:
            ahead = dot_nn(grad_branch[...], down.take(k + 1))
        low = (now * slope[:, columns].astype(jnp.float32)).astype(jnp.bfloat16)
        pre_held[:, columns] = low
        up_sum[:, columns] = rows_sum(low)
        store = pltpu.make_async_copy(
            pre_held.at[:, columns], grad_pre.at[:, columns], sems.at[2, k]
        )
        store.start()
        stores.append(store)
        acc[...] += dot_nt(pre_held[:, columns], up.take(k))
    gradient = acc[...]
    unit_rows = unit[...]
    middle = grad_res[...].astype(jnp.float32) + norm_input_gradient(
        gradient, unit_rows, inv[:, 0:1], rows[6:7, :]
    )
    grad_mid[...] = middle
    grad_attn[...] = middle.astype(grad_attn.dtype)
    load.wait()
    grad_attended[...] = dot_nt(grad_attn[...], out_held[...]).astype(grad_attended.dtype)
    sums[...] = jnp.zeros_like(sums)
    sums[0:1, :] = rows_sum(gradient * unit_rows)
    sums[1:2, :] = rows_sum(gradient)
    sums[2:3, :] = rows_sum(grad_attn[...])
    sums[3:4, :] = rows_sum(grad_branch[...])
    for store in stores:
        store.wait()


def mlp_backward(grad_res, down_weight, slope, up_weight, unit, inv, rows, attn_weight):
    tok, width = grad_res.shape
    columns = slope.shape[1]
    chunks = chunks_of(columns)
    weight_chunk = pltpu.VMEM((2, width, chunks[0][1]), jnp.bfloat16)
    return dense_call(
        functools.partial(mlp_backward_kernel, chunks),
        "mlp_backward",
        [in_vmem(), anywhere(), in_vmem(), anywhere(), in_vmem(), in_vmem(), in_vmem(), anywhere()],
        [
            (jax.ShapeDtypeStruct((tok, columns), jnp.bfloat16), anywhere()),
            kept((1, columns), jnp.float32),
            kept((tok, width)),
            kept((tok, width), jnp.float32),
            kept((tok, width)),
            kept((tok, width)),
            kept((8, width), jnp.float32),
        ],
        [pltpu.VMEM((width, width), jnp.bfloat16)]
        + [weight_chunk] * 2
        + [
            pltpu.VMEM((tok, columns), jnp.bfloat16),
            pltpu.VMEM((tok, width), jnp.float32),
            pltpu.SemaphoreType.DMA((4, len(chunks))),
        ],
        grad_res,
        down_weight,
        slope,
        up_weight,
        unit,
        inv,
        rows,
        attn_weight,
    )


def adam_step(weight_now, gradient, first_old, second_old):
    first_new = beta_first * first_old + (1.0 - beta_first) * gradient
    second_new = beta_second * second_old + (1.0 - beta_second) * gradient * gradient
    first_hat = first_new / (1.0 - beta_first**STEP)
    second_hat = second_new / (1.0 - beta_second**STEP)
    update = -learn_rate * (
        first_hat / (jnp.sqrt(second_hat) + eps_adam)
        + weight_decay * weight_now.astype(jnp.float32)
    )
    return (first_new, second_new, update)


def round_up(count, unit):
    return -(-count // unit) * unit


def per_device(
    inputs, image_ids, token_mask, cotangent,
    w_qkv, w_out, w_up, w_down, norm_gains, bias_rows, up_bias,
    first_qkv, first_out, first_up, first_down, first_gains, first_bias, first_upbias,
    second_qkv, second_out, second_up, second_down, second_gains, second_bias, second_upbias,
):
    tok, width = inputs.shape
    layers, _, hidden_width = w_up.shape
    places = lax.axis_size("seq")
    place = lax.axis_index("seq")
    layout = Layout(lax.axis_size("dp"), places, width)
    group_tok = tok * places
    spare_count = group_tok - group_tok // IMG * IMG
    left = round_up(IMG - 1 + spare_count, 16)
    right = round_up(IMG - 1, 16)
    tile = tok // 2

    reach = Reach(tok, left, right)

    half = hidden_width // 2
    half_pad = round_up(half + 8 * layers, 128)
    wide_columns = 2 * half_pad

    def spread(array):
        pad = [(0, 0)] * (array.ndim - 1) + [(0, half_pad - half)]
        return jnp.concatenate([jnp.pad(array[..., :half], pad), jnp.pad(array[..., half:], pad)], -1)

    def unspread(array):
        return jnp.concatenate(
            [array[..., :half], array[..., half_pad : half_pad + half]], axis=-1
        )

    def filled(array, rows, columns):
        return jnp.pad(array, ((0, rows - array.shape[0]), (0, columns - array.shape[1])))

    attn_columns = layout.columns(4 * width, False)
    up_columns = layout.columns(wide_columns, True)
    down_columns = layout.columns(wide_columns, False)
    rows_of = jnp.concatenate([norm_gains.reshape(-1, layout.rows), bias_rows.reshape(-1, layout.rows)])
    row_count = rows_of.shape[0]
    shards = []
    for layer in range(layers):
        attn_shard = jnp.concatenate([w_qkv[layer], w_out[layer]], axis=1)
        up_shard = spread(w_up[layer])
        if layer == 0:
            up_shard = up_shard.at[:, half : half + row_count].set(rows_of.T)
        down_shard = spread(w_down[layer].T)
        shards += [
            filled(attn_shard, layout.padded, attn_columns),
            filled(up_shard, layout.padded, up_columns),
            filled(down_shard, layout.padded, down_columns if layer else up_columns),
        ]
    word = jnp.broadcast_to(image_ids[:, None], (tok, 128))
    def gather(layer, which):
        return gather_work(layout, shards[3 * layer + which], which == 1 or (which == 2 and layer == 0))

    gathered = [[None] * 3 for _ in range(layers)]
    begun = [(0, 1), (0, 0), (0, 2)]
    for layer in range(1, layers):
        begun += [(layer, 0), (layer, 2), (layer, 1)]
    *results, (window_word, *_) = exchange(
        "gather_parameters",
        layout,
        [gather(*spot) for spot in begun] + [window_work(layout, reach, word)],
        [[index] for index in range(len(begun))] + [[1]],
        40,
    )
    for (layer, which), (matrix,) in zip(begun, results):
        gathered[layer][which] = matrix
    window_word = window_word[:, 0]
    all_rows = gathered[0][1][:, half : half + row_count].T.astype(jnp.float32)
    gains = all_rows[: 2 * layers].reshape(layers, 2, width)
    shifts = all_rows[2 * layers :].reshape(layers, 6, width)
    vectors = jnp.concatenate(
        [gains[:, :1], shifts[:, :1], shifts[:, 2:], gains[:, 1:], shifts[:, 1:2]], axis=1
    )
    up_shift = spread(up_bias.astype(jnp.float32))[:, None, :]

    plan, own_code = attention_plan(
        tile, left, right, image_ids, token_mask, window_word, place, places
    )

    residual = inputs
    kept_layers = []
    for layer in range(layers):
        attn_weight, up_weight, down_weight = gathered[layer]
        rows = vectors[layer]
        normed_low, inv_one, queries, key_value, unit_one = projection_forward(
            residual, rows, attn_weight
        )
        ((window, *_),) = exchange(
            "fetch_window", layout, [window_work(layout, reach, key_value)], [[0]], 20
        )
        attended, lse = attention_forward(tile, left, plan, queries, window, own_code)
        residual, hidden_low, inv_two, unit_two, active, slope = mlp_forward(
            attended, residual, attn_weight, rows, up_weight, up_shift[layer], down_weight
        )
        kept_layers.append(
            (window, unit_one, inv_one, normed_low, queries, lse, attended,
             unit_two, inv_two, hidden_low, slope, active)
        )

    def reduce(works, turns):
        left_operands = pltpu.VMEM((2, 2, width, tok), jnp.bfloat16)
        right_operands = pltpu.VMEM((2, tok, max(attn_columns, up_columns) // 2), jnp.bfloat16)
        operands = [left_operands, right_operands]
        results = exchange("reduce_gradients", layout, works, turns, 63, operands)
        return [result[0] for result in results]

    def packed(rows):
        flat = jnp.concatenate([row.reshape(-1) for row in rows])
        return jnp.pad(flat, (0, -flat.size % 1024)).reshape(-1, 128)

    grad_res = cotangent
    owned = [[None] * 3 for _ in range(layers)]
    row_grads = [None] * layers
    upbias_grads = [None] * layers
    for layer in reversed(range(layers)):
        (window, unit_one, inv_one, normed_low, queries, lse, attended,
         unit_two, inv_two, hidden_low, slope, active) = kept_layers[layer]
        attn_weight, up_weight, down_weight = gathered[layer]
        rows = vectors[layer]
        grad_pre, up_sum, grad_branch, grad_mid, grad_attn, grad_attended, second_sums = (
            mlp_backward(
                grad_res, down_weight, slope, up_weight, unit_two, inv_two, rows, attn_weight
            )
        )
        upbias_grads[layer] = unspread(up_sum[0])
        grad_query, grad_window = attention_backward(
            tile, left, plan, queries, window, grad_attended, lse, own_code
        )
        works = [owned_work(layout, reach, grad_window)]
        reduce_up = reduce_work(layout, [hidden_low.T], grad_pre, True)
        split = 3 if layer else 6
        reduce_down = reduce_work(layout, [grad_branch.T], active, True, split=split)
        if layer > 0:
            works += [reduce_up, reduce_down]
            results = reduce(works, [[0], [0], [1]])
            grad_key_value, owned[layer][1], owned[layer][2] = results
        else:
            small = packed([*upbias_grads, *row_grads[1:]])
            works += [waiting, reduce_up, sum_work(layout, small)]
            results = reduce(works, [[0], [0], [1], [3, 5, 7, 8, 9]])
            grad_key_value, owned[1][0], owned[0][1], small_sum = results
        grad_res, first_sums = projection_backward(
            grad_query, grad_key_value, attn_weight, unit_one, inv_one, rows, grad_mid
        )
        row_grads[layer] = jnp.stack(
            [
                first_sums[0], second_sums[0], first_sums[1], second_sums[1],
                first_sums[2], first_sums[3], second_sums[2], second_sums[3],
            ]
        )
        grad_proj = jnp.concatenate([grad_query, grad_key_value], axis=1)
        grad_side = filled(jnp.concatenate([grad_proj, grad_attn], axis=1), tok, attn_columns)
        waiting = reduce_work(
            layout, [normed_low.T, attended.T], grad_side, False, 3 * width
        )
        if layer == 0:
            works = [reduce_down, waiting, sum_work(layout, packed(row_grads[:1]))]
            owned[0][2], owned[0][0], row_sum = reduce(works, [[0], [1], [2, 4, 6, 8, 10]])

    flat = small_sum.reshape(-1)
    upbias_grads = flat[: layers * hidden_width].reshape(layers, hidden_width)
    later = flat[layers * hidden_width :][: (layers - 1) * 8 * width].reshape(-1, 8, width)
    row_sums = jnp.concatenate([row_sum.reshape(-1)[: 8 * width].reshape(1, 8, width), later])
    seat = lax.axis_index("dp") * places + place
    row_sums = lax.dynamic_slice_in_dim(row_sums, seat * layout.rows, layout.rows, axis=2)

    def stacked(part):
        return jnp.stack([part(*owned[layer]) for layer in range(layers)], axis=1)

    rows = layout.rows
    grads = (
        stacked(lambda attn, up, down: attn[:rows, : 3 * width]),
        stacked(lambda attn, up, down: attn[:rows, 3 * width : 4 * width]),
        stacked(lambda attn, up, down: unspread(up[:rows])),
        stacked(lambda attn, up, down: unspread(down[:rows])),
        row_sums[:, :2],
        row_sums[:, 2:],
        upbias_grads,
    )
    there = ((1, 0, 2), (1, 0, 2), (1, 0, 2), (2, 0, 1)) + ((0, 1, 2),) * 2 + ((0, 1),)
    back = ((1, 0, 2), (1, 0, 2), (1, 0, 2), (1, 2, 0)) + ((0, 1, 2),) * 2 + ((0, 1),)

    def turned(arrays, orders):
        return tuple(jnp.transpose(array, order) for array, order in zip(arrays, orders))

    def handed_out(arrays):
        orders = ((1, 0, 2),) * 3 + ((2, 0, 1),)
        large = [
            array_layout.with_layout_constraint(
                array, array_layout.Layout(major_to_minor=order)
            )
            for array, order in zip(arrays, orders)
        ]
        return tuple(large) + tuple(arrays[len(orders) :])

    params = (w_qkv, w_out, w_up, w_down, norm_gains, bias_rows, up_bias)
    firsts = (first_qkv, first_out, first_up, first_down, first_gains, first_bias, first_upbias)
    seconds = (
        second_qkv, second_out, second_up, second_down, second_gains, second_bias, second_upbias,
    )
    states = [turned(arrays, there) for arrays in (params, firsts, seconds)]
    results = [
        adam_step(param, gradient, first, second)
        for param, gradient, first, second in zip(states[0], grads, states[1], states[2])
    ]
    grads = handed_out(turned(grads, back))
    return (
        (residual, grad_res)
        + grads
        + handed_out(turned([result[0] for result in results], back))
        + handed_out(turned([result[1] for result in results], back))
        + handed_out(turned([result[2] for result in results], back))
    )


def solution(mesh):
    in_specs = (
        P(("dp", "seq"), None),
        P(("dp", "seq")),
        P(("dp", "seq")),
        P(("dp", "seq"), None),
        P(None, ("dp", "seq"), None),
        P(None, ("dp", "seq"), None),
        P(None, ("dp", "seq"), None),
        P(None, None, ("dp", "seq")),
        P(None, None, ("dp", "seq")),
        P(None, None, ("dp", "seq")),
        P(),
        P(None, ("dp", "seq"), None),
        P(None, ("dp", "seq"), None),
        P(None, ("dp", "seq"), None),
        P(None, None, ("dp", "seq")),
        P(None, None, ("dp", "seq")),
        P(None, None, ("dp", "seq")),
        P(),
        P(None, ("dp", "seq"), None),
        P(None, ("dp", "seq"), None),
        P(None, ("dp", "seq"), None),
        P(None, None, ("dp", "seq")),
        P(None, None, ("dp", "seq")),
        P(None, None, ("dp", "seq")),
        P(),
    )
    out_specs = (
        P(("dp", "seq"), None),
        P(("dp", "seq"), None),
        P(None, ("dp", "seq"), None),
        P(None, ("dp", "seq"), None),
        P(None, ("dp", "seq"), None),
        P(None, None, ("dp", "seq")),
        P(None, None, ("dp", "seq")),
        P(None, None, ("dp", "seq")),
        P(),
        P(None, ("dp", "seq"), None),
        P(None, ("dp", "seq"), None),
        P(None, ("dp", "seq"), None),
        P(None, None, ("dp", "seq")),
        P(None, None, ("dp", "seq")),
        P(None, None, ("dp", "seq")),
        P(),
        P(None, ("dp", "seq"), None),
        P(None, ("dp", "seq"), None),
        P(None, ("dp", "seq"), None),
        P(None, None, ("dp", "seq")),
        P(None, None, ("dp", "seq")),
        P(None, None, ("dp", "seq")),
        P(),
        P(None, ("dp", "seq"), None),
        P(None, ("dp", "seq"), None),
        P(None, ("dp", "seq"), None),
        P(None, None, ("dp", "seq")),
        P(None, None, ("dp", "seq")),
        P(None, None, ("dp", "seq")),
        P(),
    )
    return jax.shard_map(
        per_device, mesh=mesh, in_specs=in_specs, out_specs=out_specs, check_vma=False
    )
```
